32 devices in a mesh: head: 2 (over core), seq: 16 (over z, y, x).
Axes of the slice: x: 2, y: 2, z: 4, core: 2. Of those that a mesh axis runs over, the one named last changes fastest.
Arguments:
- tokens: bfloat16 [2, 2048, 2048], P('head', 'seq'), may hold values from -6 to 6
- log_decay: float32 [2, 2048, 48], P(None, 'seq', 'head'), may hold values from -1 to 0
- norm_gain: bfloat16 [2048], P(('head', 'seq')), may hold values from 0.5 to 1.5
- qkv_proj: bfloat16 [2048, 1536], P(('head', 'seq')), may hold values from -0.125 to 0.125
- attn_proj: bfloat16 [1024, 2048], P(None, ('head', 'seq')), may hold values from -2 to 2
- inner_proj: bfloat16 [2048, 6704], P(('head', 'seq')), may hold values from -0.125 to 0.125
- conv_weight: bfloat16 [4, 3584], P(None, ('head', 'seq')), may hold values from -3 to 3
- conv_bias: bfloat16 [3584], P(('head', 'seq')), may hold values from -2 to 2
- step_bias: float32 [48], P('head'), may hold values from -4 to -1
- skip_gain: float32 [48], P('head'), may hold values from 0.5 to 8
- inner_gain: bfloat16 [3072], P(('head', 'seq')), may hold values from 0.5 to 1.5
- inner_out: bfloat16 [3072, 2048], P(None, ('head', 'seq')), may hold values from -0.109375 to 0.109375
- ff_gain: bfloat16 [2048], P(('head', 'seq')), may hold values from 0.5 to 1.5
- gate_up: bfloat16 [2048, 8192], P(('head', 'seq')), may hold values from -0.125 to 0.125
- down_proj: bfloat16 [4096, 2048], P(None, ('head', 'seq')), may hold values from -0.09375 to 0.09375
- cotangent: bfloat16 [2, 2048, 2048], P('head', 'seq'), may hold values from -6 to 6
Outputs:
- output: bfloat16 [2, 2048, 2048], P('head', 'seq')
- grad_tokens: float32 [2, 2048, 2048], P('head', 'seq')
- grad_norm_gain: float32 [2048], P(('head', 'seq'))
- grad_qkv_proj: float32 [2048, 1536], P(('head', 'seq'))
- grad_attn_proj: float32 [1024, 2048], P(None, ('head', 'seq'))
- grad_inner_proj: float32 [2048, 6704], P(('head', 'seq'))
- grad_conv_weight: float32 [4, 3584], P(None, ('head', 'seq'))
- grad_conv_bias: float32 [3584], P(('head', 'seq'))
- grad_step_bias: float32 [48], P('head')
- grad_skip_gain: float32 [48], P('head')
- grad_inner_gain: float32 [3072], P(('head', 'seq'))
- grad_inner_out: float32 [3072, 2048], P(None, ('head', 'seq'))
- grad_ff_gain: float32 [2048], P(('head', 'seq'))
- grad_gate_up: float32 [2048, 8192], P(('head', 'seq'))
- grad_down_proj: float32 [4096, 2048], P(None, ('head', 'seq'))
The draws below stay inside these ranges and needn't reach their ends.
All inputs are finite; a program needn't handle non-finite values.
Results may differ from the reference program's by a relative error of at most 0.033.
Values may be sent and summed in bfloat16 or wider, within the bound.
No kernel may reach another device: no remote copies, remote signals or barrier semaphores. Data moves between devices by JAX's collectives and lax.ppermute only.
A program may use at most 576 MiB of HBM per device.

```python
import math
import jax
import jax.numpy as jnp
from jax import lax

D = 2048
FF = 4096
QH = 8
KVH = 2
HD = 128
MH = 48
MP = 64
NS = 256
KC = 4
BLK = 128
SEQUENCE_COUNT = 2
SEQUENCE_LENGTH = 2048


def draw_log_decay(key, part):
    key = jax.random.fold_in(key, 7)
    random_subkeys = jax.random.split(key, 7)
    fast_share = 0.5
    fast_head = jax.random.uniform(random_subkeys[0], (MH,)) < fast_share
    fast_rate = jnp.exp(jax.random.uniform(random_subkeys[1], (MH,), minval=jnp.log(1.0 / 50.0), maxval=jnp.log(1.0 / 30.0)))
    slow_rate = jnp.exp(jax.random.uniform(random_subkeys[2], (MH,), minval=jnp.log(0.05), maxval=jnp.log(0.7))) / SEQUENCE_LENGTH
    baseline_rate = jnp.where(fast_head, fast_rate, slow_rate)
    block_count = SEQUENCE_LENGTH // BLK
    block_multiplier = jnp.exp(jax.random.uniform(random_subkeys[3], (SEQUENCE_COUNT, block_count, 1, MH), minval=-0.7, maxval=0.7))
    block_multiplier = jnp.broadcast_to(block_multiplier, (SEQUENCE_COUNT, block_count, BLK, MH)).reshape(SEQUENCE_COUNT, SEQUENCE_LENGTH, MH)
    token_multiplier = jax.random.uniform(random_subkeys[4], (SEQUENCE_COUNT, SEQUENCE_LENGTH, MH), minval=0.5, maxval=1.5)
    spike_mask = jax.random.uniform(random_subkeys[5], (SEQUENCE_COUNT, SEQUENCE_LENGTH, 1)) < 3.0 / SEQUENCE_LENGTH
    spike_loss_value = jax.random.uniform(random_subkeys[6], (SEQUENCE_COUNT, SEQUENCE_LENGTH, 1), minval=0.2, maxval=0.5)
    spike_logarithm = jnp.where(spike_mask, jnp.log(1.0 - spike_loss_value), 0.0)
    return (spike_logarithm - baseline_rate * block_multiplier * token_multiplier).astype(jnp.float32)


def level_of(key, shape, cuts, smallest, largest):
    factor_of = 1.0
    for position, shards_of in cuts:
        draws = jax.random.uniform(jax.random.fold_in(jax.random.fold_in(key, 6), position), (shards_of,), jnp.float32, smallest / len(cuts), largest / len(cuts))
        factor_of = factor_of * jnp.repeat(jnp.exp(draws), shape[position] // shards_of).reshape((-1,) + (1,) * (len(shape) - 1 - position))
    return factor_of


def noise(own_key, dims, scale, reach, shards=(), held_as=jnp.bfloat16):
    values = jax.random.normal(own_key, dims, jnp.float32) * scale
    if len(shards) > 0:
        values = level_of(own_key, dims, shards, -0.22, 0.18) * values
    return jnp.clip(values, min=-reach, max=reach).astype(held_as)


def setup_inputs(seed: int = 0) -> dict:
    key_of = jax.random.split(jax.random.key(seed), 17)
    tokens = noise(key_of[0], (SEQUENCE_COUNT, SEQUENCE_LENGTH, D), 1.0, 6.0, ((0, 2), (1, 16)))
    log_decay = draw_log_decay(jax.random.fold_in(key_of[16], 71), 0)
    norm_gain = jnp.clip(1.0 + 0.1 * jax.random.normal(key_of[2], (D,), jnp.float32), 0.5, 1.5).astype(jnp.bfloat16)
    qkv_proj = noise(key_of[3], (D, (QH + 2 * KVH) * HD), D ** -0.5, 0.125, ((0, 32),))
    attn_proj = noise(key_of[4], (QH * HD, D), (max(1, QH * HD * 16 // SEQUENCE_LENGTH)) ** -0.5, 2.0, ((1, 32),))
    inner_proj = noise(key_of[5], (D, 2 * MH * MP + 2 * NS + MH), D ** -0.5, 0.125, ((0, 32),))
    conv_weight = noise(key_of[6], (KC, MH * MP + 2 * NS), 0.5, 3.0, ((1, 32),))
    conv_bias = noise(key_of[7], (MH * MP + 2 * NS,), 0.3, 2.0, ((0, 32),))
    step_bias = jnp.clip(-4.0 + 3.0 * jax.random.uniform(key_of[8], (MH,), jnp.float32) ** level_of(key_of[8], (MH,), ((0, 2),), -0.2, 0.2), -4.0, -1.0)
    skip_gain = jnp.clip(jnp.exp(math.log(8.0) - 2.7725887 * jax.random.uniform(key_of[9], (MH,), jnp.float32) ** level_of(key_of[9], (MH,), ((0, 2),), -0.2, 0.2)), 0.5, 8.0)
    inner_gain = jnp.clip(1.0 + 0.1 * jax.random.normal(key_of[10], (MH * MP,), jnp.float32), 0.5, 1.5).astype(jnp.bfloat16)
    inner_out = noise(key_of[11], (MH * MP, D), (MH * MP) ** -0.5, 0.109375, ((1, 32),))
    ff_gain = jnp.clip(1.0 + 0.1 * jax.random.normal(key_of[12], (D,), jnp.float32), 0.5, 1.5).astype(jnp.bfloat16)
    gate_up = noise(key_of[13], (D, 2 * FF), D ** -0.5, 0.125, ((0, 32),))
    down_proj = noise(key_of[14], (FF, D), FF ** -0.5, 0.09375, ((1, 32),))
    cotangent = noise(key_of[15], (SEQUENCE_COUNT, SEQUENCE_LENGTH, D), 1.0, 6.0, ((0, 2), (1, 16)))
    return dict(tokens=tokens, log_decay=log_decay, norm_gain=norm_gain, qkv_proj=qkv_proj, attn_proj=attn_proj, inner_proj=inner_proj, conv_weight=conv_weight, conv_bias=conv_bias, step_bias=step_bias, skip_gain=skip_gain, inner_gain=inner_gain, inner_out=inner_out, ff_gain=ff_gain, gate_up=gate_up, down_proj=down_proj, cotangent=cotangent)


EPSILON = 1e-05
ROPE_BASE = 100000000000.0
NEGATIVE = -1e+30
HIGHEST = lax.Precision.HIGHEST

@jax.custom_vjp
def low(v):
    return lax.optimization_barrier(v.astype(jnp.bfloat16)).astype(jnp.float32)

@jax.custom_vjp
def low_back(v):
    return v

def low_keep(v):
    return (low(v), None)

def low_pass(kept, grad):
    return (grad,)

def back_keep(v):
    return (v, None)

def back_low(kept, grad):
    return (low(grad),)
low.defvjp(low_keep, low_pass)
low_back.defvjp(back_keep, back_low)

def rms_norm(value, gain):
    return value * lax.rsqrt(lax.optimization_barrier(jnp.mean(value * value, axis=-1, keepdims=True)) + EPSILON) * gain

def rotary(value, positions):
    halfway = value.shape[-1] // 2
    frequency = ROPE_BASE ** (-2.0 * jnp.arange(halfway, dtype=jnp.float32) / value.shape[-1])
    angle = positions[:, None] * frequency[None, :]
    cosine = jnp.cos(angle)[:, None, :]
    sine_part = jnp.sin(angle)[:, None, :]
    first = value[..., :halfway]
    second = value[..., halfway:]
    return jnp.concatenate([first * cosine - second * sine_part, second * cosine + first * sine_part], axis=-1)

def block_decay(log_decay):
    return jnp.exp(jnp.cumsum(log_decay, axis=1)[:, -1, :])

def inner_output(inner_x, step_in, state_maps, step_bias, skip_gain, state_in, log_decay):
    nstate = state_maps.shape[-1] // 2
    input_map = state_maps[..., :nstate]
    output_map = state_maps[..., nstate:]
    step_size = jax.nn.softplus(step_in + step_bias)
    cumulative = jnp.cumsum(log_decay, axis=1)
    scaled_x = inner_x * step_size[..., None]
    intersection = jnp.einsum('stn,sun->stu', output_map, input_map, precision=HIGHEST)
    length_blk = log_decay.shape[1]
    lower_mask = jnp.arange(length_blk)[:, None] >= jnp.arange(length_blk)[None, :]
    spread = cumulative[:, :, None, :] - cumulative[:, None, :, :]
    mixing = jnp.where(lower_mask[None, :, :, None], jnp.exp(jnp.minimum(spread, 0.0)), 0.0) * intersection[..., None]
    within = jnp.einsum('stuh,suhp->sthp', mixing, scaled_x, precision=HIGHEST)
    carried = jnp.einsum('shpn,stn->sthp', state_in, output_map, precision=HIGHEST) * jnp.exp(cumulative)[..., None]
    return within + carried + skip_gain[:, None] * inner_x

def inner_state(inner_x, step_in, state_maps, step_bias, log_decay):
    nstate = state_maps.shape[-1] // 2
    input_map = state_maps[..., :nstate]
    step_size = jax.nn.softplus(step_in + step_bias)
    cumulative = jnp.cumsum(log_decay, axis=1)
    tail_weight = jnp.exp(cumulative[:, -1:, :] - cumulative) * step_size
    return jnp.einsum('suh,suhp,sun->shpn', tail_weight, inner_x, input_map, precision=HIGHEST)

def attention(queries, key_rows, value_rows):
    length = queries.shape[0]
    block_rows = math.gcd(length, 1024)
    groups = QH // KVH
    score_scale = HD ** (-0.5)
    grouped = queries.reshape(length, KVH, groups, HD)
    key_pos = jnp.arange(length, dtype=jnp.int32)

    def attend_rows(block_index):
        query_blk = lax.dynamic_slice_in_dim(grouped, block_index * block_rows, block_rows, 0)
        query_pos = block_index * block_rows + jnp.arange(block_rows, dtype=jnp.int32)
        scores = low_back(jnp.einsum('qkgd,jkd->qkgj', query_blk, key_rows, precision=HIGHEST) * score_scale)
        allowed = (key_pos[None, :] <= query_pos[:, None])[:, None, None, :]
        masked = jnp.where(allowed, scores, NEGATIVE)
        row_top = lax.optimization_barrier(jnp.max(masked, axis=-1, keepdims=True))
        weights = jnp.where(allowed, jnp.exp(masked - row_top), 0.0)
        prob_rows = low(weights / lax.optimization_barrier(jnp.sum(weights, axis=-1, keepdims=True)))
        return jnp.einsum('qkgj,jkd->qkgd', prob_rows, value_rows, precision=HIGHEST)
    results = lax.map(jax.checkpoint(attend_rows), jnp.arange(length // block_rows, dtype=jnp.int32))
    return results.reshape(length, QH * HD)

def inner_scan(inner_x, step_in, state_maps, step_bias, skip_gain, log_decay):
    length = inner_x.shape[0]
    block_count = length // BLK
    pieces = (inner_x.reshape(block_count, 1, BLK, MH, MP), step_in.reshape(block_count, 1, BLK, MH), state_maps.reshape(block_count, 1, BLK, 2 * NS), log_decay.reshape(block_count, 1, BLK, MH))

    def advance(carried, piece):
        piece_x, piece_step, piece_maps, piece_decay = piece
        result = inner_output(piece_x, piece_step, piece_maps, step_bias, skip_gain, carried, piece_decay)
        fresh_state = inner_state(piece_x, piece_step, piece_maps, step_bias, piece_decay)
        block_fall = block_decay(piece_decay)
        return (block_fall[:, :, None, None] * carried + fresh_state, result)
    start_state = jnp.zeros((1, MH, MP, NS), jnp.float32)
    final_state, results = lax.scan(jax.checkpoint(advance), start_state, pieces)
    return results.reshape(length, MH, MP)

def layer(tokens_seq, decay_seq, norm_gain, qkv_proj, attn_proj, inner_proj, conv_weight, conv_bias, step_bias, skip_gain, inner_gain, inner_out, ff_gain, gate_up, down_proj):
    length = tokens_seq.shape[0]
    inner_width = MH * MP
    conv_width = inner_width + 2 * NS
    normed = low(rms_norm(tokens_seq, norm_gain))
    qkv_rows = low_back(jnp.dot(normed, qkv_proj, precision=HIGHEST))
    positions = jnp.arange(length, dtype=jnp.float32)
    queries = low_back(low(rotary(qkv_rows[:, :QH * HD].reshape(length, QH, HD), positions)))
    key_rows = low_back(low(rotary(qkv_rows[:, QH * HD:(QH + KVH) * HD].reshape(length, KVH, HD), positions)))
    value_rows = low_back(low(qkv_rows[:, (QH + KVH) * HD:].reshape(length, KVH, HD)))
    attended = low_back(low(attention(queries, key_rows, value_rows)))
    attn_branch = low_back(jnp.dot(attended, attn_proj, precision=HIGHEST))
    inner_raw = low_back(jnp.dot(normed, inner_proj, precision=HIGHEST))
    gate_z = inner_raw[:, :inner_width]
    conv_in = inner_raw[:, inner_width:inner_width + conv_width]
    step_raw = inner_raw[:, inner_width + conv_width:]
    padded = jnp.concatenate([jnp.zeros((KC - 1, conv_width), jnp.float32), conv_in], axis=0)
    conv_sum = conv_bias
    for conv_tap in range(KC):
        conv_sum = conv_sum + conv_weight[conv_tap] * padded[conv_tap:conv_tap + length]
    activated = low_back(low(jax.nn.silu(conv_sum)))
    inner_x = activated[:, :inner_width].reshape(length, MH, MP)
    state_maps = activated[:, inner_width:]
    step_in = low_back(low(step_raw))
    inner_y = low_back(low(inner_scan(inner_x, step_in, state_maps, step_bias, skip_gain, decay_seq)))
    gated_rows = inner_y.reshape(length, inner_width) * jax.nn.silu(gate_z)
    inner_normed = low(rms_norm(gated_rows, inner_gain))
    inner_branch = low_back(jnp.dot(inner_normed, inner_out, precision=HIGHEST))
    hidden = tokens_seq + attn_branch + inner_branch
    normed_ff = low(rms_norm(hidden, ff_gain))
    gate_vals = low_back(jnp.dot(normed_ff, gate_up, precision=HIGHEST))
    mixed_rows = low(jax.nn.silu(gate_vals[:, :FF]) * gate_vals[:, FF:])
    return hidden + low_back(jnp.dot(mixed_rows, down_proj, precision=HIGHEST))

def reference(tokens, log_decay, norm_gain, qkv_proj, attn_proj, inner_proj, conv_weight, conv_bias, step_bias, skip_gain, inner_gain, inner_out, ff_gain, gate_up, down_proj, cotangent):

    def forward(tokens_full, norm_g, qkv_w, attn_w, inner_w, conv_w, conv_b, step_b, skip_g, inner_g, out_w, ff_g, gate_w, down_w):

        def per_sequence(pair):
            return layer(pair[0], pair[1], norm_g, qkv_w, attn_w, inner_w, conv_w, conv_b, step_b, skip_g, inner_g, out_w, ff_g, gate_w, down_w)
        return lax.map(per_sequence, (tokens_full, log_decay))
    output, pullback = jax.vjp(forward, tokens.astype(jnp.float32), norm_gain.astype(jnp.float32), qkv_proj.astype(jnp.float32), attn_proj.astype(jnp.float32), inner_proj.astype(jnp.float32), conv_weight.astype(jnp.float32), conv_bias.astype(jnp.float32), step_bias.astype(jnp.float32), skip_gain.astype(jnp.float32), inner_gain.astype(jnp.float32), inner_out.astype(jnp.float32), ff_gain.astype(jnp.float32), gate_up.astype(jnp.float32), down_proj.astype(jnp.float32))
    grads = pullback(cotangent.astype(jnp.float32))
    return (output.astype(jnp.bfloat16), grads[0], grads[1], grads[2], grads[3], grads[4], grads[5], grads[6], grads[7], grads[8], grads[9], grads[10], grads[11], grads[12], grads[13])
```

```python
import functools
import math

import jax
import jax.numpy as jnp
from jax import lax
from jax.experimental import pallas as pl
from jax.experimental.pallas import tpu as pltpu
from jax.sharding import PartitionSpec as P

FF = 4096
QH = 8
KVH = 2
HD = 128
MH = 48
MP = 64
NS = 256
KC = 4


EPSILON = 1e-05
ROPE_BASE = 100000000000.0
NEGATIVE = -1e30
HIGHEST = lax.Precision.HIGHEST


def passed_along(value, axis, steps):
    count = lax.axis_size(axis)
    initial, last = (max(0, -steps), min(count, count - steps))
    return lax.ppermute(value, axis, [(source, source + steps) for source in range(initial, last)])


def carried_in(array, axis, combine, identity):
    count, mine = (lax.axis_size(axis), lax.axis_index(axis))
    everything = jax.tree.map(
        lambda part, kind: lax.all_gather(part.astype(kind), axis),
        array,
        (jnp.bfloat16, jnp.bfloat16),
    )
    start = jax.tree.map(
        lambda part, zero: jnp.broadcast_to(jnp.asarray(zero, part.dtype), part.shape),
        array,
        identity,
    )

    def carried_hop(k, before):
        reached = k < mine
        new = combine(
            before, jax.tree.map(lambda part, own: part[k].astype(own.dtype), everything, array)
        )
        return jax.tree.map(lambda a, b: jnp.where(reached, a, b), new, before)

    return lax.fori_loop(0, count, carried_hop, start)


def entering(array, axis, combine, identity):
    count, mine = (lax.axis_size(axis), lax.axis_index(axis))
    everything = jax.tree.map(
        lambda part, kind: lax.all_gather(part.astype(kind), axis),
        array,
        jax.tree.map(lambda a: jnp.bfloat16 if a.dtype == jnp.float32 else a.dtype, array),
    )
    start = jax.tree.map(
        lambda part, zero: jnp.broadcast_to(jnp.asarray(zero, part.dtype), part.shape),
        array,
        identity,
    )

    def entering_hop(k, before):
        at = count - 1 - k
        reached = at > mine
        new = combine(
            before, jax.tree.map(lambda part, own: part[at].astype(own.dtype), everything, array)
        )
        return jax.tree.map(lambda a, b: jnp.where(reached, a, b), new, before)

    return lax.fori_loop(0, count, entering_hop, start)


def shortened(array):
    return jax.tree.map(lambda a: a.astype(jnp.bfloat16) if a.dtype == jnp.float32 else a, array)


def rounded(value):
    return lax.optimization_barrier(value.astype(jnp.bfloat16)).astype(jnp.float32)


def rms_norm(value, gain):
    return value * lax.rsqrt(jnp.mean(value * value, axis=-1, keepdims=True) + EPSILON) * gain


def rotary(value, positions):
    halfway = value.shape[-1] // 2
    frequency = ROPE_BASE ** (-2.0 * jnp.arange(halfway, dtype=jnp.float32) / value.shape[-1])
    angle = positions[:, None] * frequency[None, :]
    cosine = jnp.cos(angle)[:, None, :]
    sine_part = jnp.sin(angle)[:, None, :]
    first = value[..., :halfway]
    second = value[..., halfway:]
    return jnp.concatenate(
        [first * cosine - second * sine_part, second * cosine + first * sine_part], axis=-1
    )


def block_decay(log_decay):
    return jnp.exp(jnp.cumsum(log_decay, axis=1)[:, -1, :])


def inner_output(inner_x, step_in, state_maps, step_bias, skip_gain, state_in, log_decay):
    nstate = state_maps.shape[-1] // 2
    input_map = state_maps[..., :nstate]
    output_map = state_maps[..., nstate:]
    step_size = jax.nn.softplus(step_in + step_bias)
    cumulative = jnp.cumsum(log_decay, axis=1)
    scaled_x = inner_x * step_size[..., None]
    intersection = jnp.einsum("stn,sun->stu", output_map, input_map, precision=HIGHEST)
    length_blk = log_decay.shape[1]
    lower_mask = jnp.arange(length_blk)[:, None] >= jnp.arange(length_blk)[None, :]
    spread = cumulative[:, :, None, :] - cumulative[:, None, :, :]
    mixing = (
        jnp.where(lower_mask[None, :, :, None], jnp.exp(jnp.minimum(spread, 0.0)), 0.0)
        * intersection[..., None]
    )
    within = jnp.einsum("stuh,suhp->sthp", mixing, scaled_x, precision=HIGHEST)
    carried = (
        jnp.einsum("shpn,stn->sthp", state_in, output_map, precision=HIGHEST)
        * jnp.exp(cumulative)[..., None]
    )
    return within + carried + skip_gain[:, None] * inner_x


def inner_state(inner_x, step_in, state_maps, step_bias, log_decay):
    nstate = state_maps.shape[-1] // 2
    input_map = state_maps[..., :nstate]
    step_size = jax.nn.softplus(step_in + step_bias)
    cumulative = jnp.cumsum(log_decay, axis=1)
    tail_weight = jnp.exp(cumulative[:, -1:, :] - cumulative) * step_size
    return jnp.einsum("suh,suhp,sun->shpn", tail_weight, inner_x, input_map, precision=HIGHEST)


def over_blocks(function, carried, arrays, offset, limit):
    row_count = arrays[0].shape[1]
    step_rows = math.gcd(row_count, 1024)

    def advance(number, running):
        pieces = tuple(
            (
                lax.dynamic_slice_in_dim(member, number * step_rows, step_rows, 1)
                for member in arrays
            )
        )
        return function(running, pieces, offset + number * step_rows)

    upper = (limit + step_rows - 1) // step_rows
    return lax.fori_loop(0, upper, advance, carried)


def attend_block(carried, pair, offset, queries, query_pos, score_scale):
    row_top, row_total, accumulated = carried
    key_blk, value_blk = pair
    scores = (
        jnp.einsum("sqkgd,sjkd->sqkgj", queries, key_blk, preferred_element_type=jnp.float32)
        * score_scale
    )
    key_pos = offset + jnp.arange(key_blk.shape[1])
    allowed = (key_pos[None, :] <= query_pos[:, None])[None, :, None, None, :]
    masked = jnp.where(allowed, scores, NEGATIVE)
    new_top = jnp.maximum(row_top, jnp.max(masked, axis=-1))
    factor = jnp.exp(row_top - new_top)
    weights = jnp.where(allowed, jnp.exp(masked - new_top[..., None]), 0.0)
    row_total = factor * row_total + jnp.sum(weights, axis=-1)
    accumulated = factor[..., None] * accumulated + jnp.einsum(
        "sqkgj,sjkd->sqkgd",
        weights.astype(jnp.bfloat16),
        value_blk,
        preferred_element_type=jnp.float32,
    )
    return (new_top, row_total, accumulated)


def score_grads(
    queries, grad_heads, log_total, row_delta, key_blk, value_blk, offset, query_pos, score_scale
):
    scores = (
        jnp.einsum("sqkgd,sjkd->sqkgj", queries, key_blk, preferred_element_type=jnp.float32)
        * score_scale
    )
    key_pos = offset + jnp.arange(key_blk.shape[1])
    allowed = (key_pos[None, :] <= query_pos[:, None])[None, :, None, None, :]
    prob_rows = jnp.where(allowed, jnp.exp(scores - log_total[..., None]), 0.0)
    grad_probs = jnp.einsum(
        "sqkgd,sjkd->sqkgj", grad_heads, value_blk, preferred_element_type=jnp.float32
    )
    grad_scores = (prob_rows * (grad_probs - row_delta[..., None])).astype(jnp.bfloat16)
    return (prob_rows.astype(jnp.bfloat16), grad_scores)


def body(
    tokens,
    log_decay,
    norm_gain,
    qkv_proj,
    attn_proj,
    inner_proj,
    conv_weight,
    conv_bias,
    step_bias,
    skip_gain,
    inner_gain,
    inner_out,
    ff_gain,
    gate_up,
    down_proj,
    cotangent,
):
    head_count = lax.axis_size("head")
    seq_index = lax.axis_index("seq")
    (
        gain_in,
        qkv_full,
        attn_full,
        inner_full,
        conv_full,
        conv_bias_full,
        inner_gain_full,
        out_full,
        ff_gain_full,
        gate_up_full,
        down_full,
    ) = (
        lax.all_gather(norm_gain, ("head", "seq"), axis=0, tiled=True),
        lax.all_gather(qkv_proj, ("head", "seq"), axis=0, tiled=True),
        lax.all_gather(attn_proj, ("head", "seq"), axis=1, tiled=True),
        lax.all_gather(inner_proj, ("head", "seq"), axis=0, tiled=True),
        lax.all_gather(conv_weight, ("head", "seq"), axis=1, tiled=True),
        lax.all_gather(conv_bias, ("head", "seq"), axis=0, tiled=True),
        lax.all_gather(inner_gain, ("head", "seq"), axis=0, tiled=True),
        lax.all_gather(inner_out, ("head", "seq"), axis=1, tiled=True),
        lax.all_gather(ff_gain, ("head", "seq"), axis=0, tiled=True),
        lax.all_gather(gate_up, ("head", "seq"), axis=0, tiled=True),
        lax.all_gather(down_proj, ("head", "seq"), axis=1, tiled=True),
    )
    local_seqs, block_rows, model_width = tokens.shape
    token_rows = local_seqs * block_rows
    inner_width = MH * MP
    conv_width = inner_width + 2 * NS
    groups = QH // KVH
    kv_local = KVH // head_count
    inner_local = MH // head_count
    all_seqs = local_seqs * head_count
    score_scale = HD ** (-0.5)
    key_limit = (seq_index + 1) * block_rows
    x_rows = tokens.astype(jnp.float32).reshape(token_rows, model_width)
    normed_f, norm_back = jax.vjp(rms_norm, x_rows, gain_in.astype(jnp.float32))
    normed = normed_f.astype(jnp.bfloat16)
    qkv_rows = jnp.dot(normed, qkv_full, preferred_element_type=jnp.float32).reshape(
        local_seqs, block_rows, -1
    )
    positions = (seq_index * block_rows + jnp.arange(block_rows)).astype(jnp.float32)
    query_send = rotary(
        qkv_rows[..., : QH * HD].reshape(local_seqs, block_rows, QH, HD), positions
    ).astype(jnp.bfloat16)
    key_send = rotary(
        qkv_rows[..., QH * HD : (QH + KVH) * HD].reshape(local_seqs, block_rows, KVH, HD), positions
    ).astype(jnp.bfloat16)
    value_send = qkv_rows[..., (QH + KVH) * HD :].astype(jnp.bfloat16)
    inner_raw = jnp.dot(normed, inner_full, preferred_element_type=jnp.float32).reshape(
        local_seqs, block_rows, -1
    )
    gate_z = inner_raw[..., :inner_width]
    conv_in = inner_raw[..., inner_width : inner_width + conv_width]
    step_send = inner_raw[..., inner_width + conv_width :].astype(jnp.bfloat16)
    rim_rows = passed_along(
        conv_in[:, block_rows - (KC - 1) :, :].astype(jnp.bfloat16), "seq", 1
    ).astype(jnp.float32)
    padded = jnp.concatenate([rim_rows, conv_in], axis=1)

    def convolve(padded_in, weight_taps, bias_taps):
        conv_sum = bias_taps
        for conv_tap in range(KC):
            conv_sum = (
                conv_sum + weight_taps[conv_tap] * padded_in[:, conv_tap : conv_tap + block_rows, :]
            )
        return jax.nn.silu(conv_sum)

    activated, conv_back = jax.vjp(
        convolve, padded, conv_full.astype(jnp.float32), conv_bias_full.astype(jnp.float32)
    )
    activated_send = activated.astype(jnp.bfloat16)

    def split_heads(value):
        return value.reshape(value.shape[:2] + (head_count, -1))

    map_copies = jnp.broadcast_to(
        activated_send[:, :, None, inner_width:], (local_seqs, block_rows, head_count, 2 * NS)
    )
    received = (
        lax.all_to_all(split_heads(query_send), "head", split_axis=2, concat_axis=0, tiled=True),
        lax.all_to_all(split_heads(key_send), "head", split_axis=2, concat_axis=0, tiled=True),
        lax.all_to_all(split_heads(value_send), "head", split_axis=2, concat_axis=0, tiled=True),
        lax.all_to_all(
            split_heads(activated_send[..., :inner_width]),
            "head",
            split_axis=2,
            concat_axis=0,
            tiled=True,
        ),
        lax.all_to_all(split_heads(step_send), "head", split_axis=2, concat_axis=0, tiled=True),
        lax.all_to_all(map_copies, "head", split_axis=2, concat_axis=0, tiled=True),
    )
    queries = received[0].reshape(all_seqs, block_rows, kv_local, groups, HD)
    key_heads = received[1]
    value_heads = received[2]
    inner_x = received[3].reshape(all_seqs, block_rows, inner_local, MP).astype(jnp.float32)
    step_in = received[4].reshape(all_seqs, block_rows, inner_local).astype(jnp.float32)
    state_maps = received[5].reshape(all_seqs, block_rows, 2 * NS).astype(jnp.float32)
    query_pos = seq_index * block_rows + jnp.arange(block_rows)
    key_all, value_all = (
        lax.all_gather(key_heads, "seq", axis=1, tiled=True),
        lax.all_gather(value_heads, "seq", axis=1, tiled=True),
    )

    def attend_step(carried, pair, offset):
        return attend_block(carried, pair, offset, queries, query_pos, score_scale)

    stat_shape = (all_seqs, block_rows, kv_local, groups)
    start_stats = (
        jnp.full(stat_shape, NEGATIVE, jnp.float32),
        jnp.zeros(stat_shape, jnp.float32),
        jnp.zeros(stat_shape + (HD,), jnp.float32),
    )
    row_top, row_total, accumulated = over_blocks(
        attend_step, start_stats, (key_all, value_all), 0, key_limit
    )
    attended_f = accumulated / row_total[..., None]
    log_total = row_top + jnp.log(row_total)

    def state_part(piece_x, piece_step, piece_maps, piece_bias):
        return inner_state(piece_x, piece_step, piece_maps, piece_bias, log_decay)

    def output_part(piece_x, piece_step, piece_maps, piece_bias, piece_skip, piece_state):
        return inner_output(
            piece_x, piece_step, piece_maps, piece_bias, piece_skip, piece_state, log_decay
        )

    fresh_state, state_back = jax.vjp(state_part, inner_x, step_in, state_maps, step_bias)
    block_fall = block_decay(log_decay)

    def chain_rule(earlier, later):
        return (earlier[0] * later[0], later[1] + later[0][:, :, None, None] * earlier[1])

    neutral = (jnp.ones_like(block_fall), jnp.zeros_like(fresh_state))
    state_in = carried_in((block_fall, fresh_state), "seq", chain_rule, neutral)[1]
    inner_y, output_back = jax.vjp(
        output_part, inner_x, step_in, state_maps, step_bias, skip_gain, state_in
    )
    returned = (
        lax.all_to_all(
            attended_f.astype(jnp.bfloat16).reshape(all_seqs, block_rows, 1, -1),
            "head",
            split_axis=0,
            concat_axis=2,
            tiled=True,
        ),
        lax.all_to_all(
            inner_y.astype(jnp.bfloat16).reshape(all_seqs, block_rows, 1, -1),
            "head",
            split_axis=0,
            concat_axis=2,
            tiled=True,
        ),
    )
    attended = returned[0].reshape(token_rows, QH * HD)
    inner_back_y = returned[1].reshape(local_seqs, block_rows, inner_width).astype(jnp.float32)

    def gated_norm(y_part, gate_part, gain_part):
        return rms_norm(y_part * jax.nn.silu(gate_part), gain_part)

    inner_normed_f, gated_back = jax.vjp(
        gated_norm, inner_back_y, gate_z, inner_gain_full.astype(jnp.float32)
    )
    inner_normed = inner_normed_f.astype(jnp.bfloat16).reshape(token_rows, inner_width)
    hidden = (
        x_rows
        + jnp.dot(attended, attn_full, preferred_element_type=jnp.float32)
        + jnp.dot(inner_normed, out_full, preferred_element_type=jnp.float32)
    )
    normed_ff_f, ff_back = jax.vjp(rms_norm, hidden, ff_gain_full.astype(jnp.float32))
    normed_ff = normed_ff_f.astype(jnp.bfloat16)
    gate_vals = jnp.dot(normed_ff, gate_up_full, preferred_element_type=jnp.float32)

    def swiglu(values_in):
        return jax.nn.silu(values_in[:, :FF]) * values_in[:, FF:]

    mixed_f, swiglu_back = jax.vjp(swiglu, gate_vals)
    mixed_rows = mixed_f.astype(jnp.bfloat16)
    output = (
        (hidden + jnp.dot(mixed_rows, down_full, preferred_element_type=jnp.float32))
        .astype(jnp.bfloat16)
        .reshape(tokens.shape)
    )
    grad_out = cotangent.reshape(token_rows, model_width)
    grad_down = jnp.einsum("rf,rd->fd", mixed_rows, grad_out, preferred_element_type=jnp.float32)
    grad_gate_vals = swiglu_back(
        jnp.einsum("rd,fd->rf", grad_out, down_full, preferred_element_type=jnp.float32)
    )[0].astype(jnp.bfloat16)
    grad_gate_up = jnp.einsum(
        "rd,re->de", normed_ff, grad_gate_vals, preferred_element_type=jnp.float32
    )
    grad_hidden_norm, grad_ff_gain = ff_back(
        jnp.einsum("re,de->rd", grad_gate_vals, gate_up_full, preferred_element_type=jnp.float32)
    )
    grad_hidden = grad_out.astype(jnp.float32) + grad_hidden_norm
    grad_branch = grad_hidden.astype(jnp.bfloat16)
    grad_attn = jnp.einsum("rc,rd->cd", attended, grad_branch, preferred_element_type=jnp.float32)
    grad_inner_out = jnp.einsum(
        "rc,rd->cd", inner_normed, grad_branch, preferred_element_type=jnp.float32
    )
    grad_attended = jnp.einsum(
        "rd,cd->rc", grad_branch, attn_full, preferred_element_type=jnp.float32
    ).astype(jnp.bfloat16)
    grad_y, grad_gate_z, grad_inner_gain = gated_back(
        jnp.einsum("rd,cd->rc", grad_branch, out_full, preferred_element_type=jnp.float32).reshape(
            local_seqs, block_rows, inner_width
        )
    )
    sent_grads = (
        lax.all_to_all(
            split_heads(grad_attended.reshape(local_seqs, block_rows, QH * HD)),
            "head",
            split_axis=2,
            concat_axis=0,
            tiled=True,
        ),
        lax.all_to_all(
            split_heads(grad_y.astype(jnp.bfloat16)),
            "head",
            split_axis=2,
            concat_axis=0,
            tiled=True,
        ),
    )
    grad_heads = sent_grads[0].reshape(all_seqs, block_rows, kv_local, groups, HD)
    grad_inner_y = sent_grads[1].reshape(all_seqs, block_rows, inner_local, MP).astype(jnp.float32)
    row_delta = jnp.sum(grad_heads.astype(jnp.float32) * attended_f, axis=-1)

    def query_step(carried, pair, offset):
        prob_rows, grad_scores = score_grads(
            queries,
            grad_heads,
            log_total,
            row_delta,
            pair[0],
            pair[1],
            offset,
            query_pos,
            score_scale,
        )
        return carried + jnp.einsum(
            "sqkgj,sjkd->sqkgd", grad_scores, pair[0], preferred_element_type=jnp.float32
        )

    grad_queries = (
        over_blocks(query_step, jnp.zeros_like(attended_f), (key_all, value_all), 0, key_limit)
        * score_scale
    )
    count = block_rows * lax.axis_size("seq")
    step_rows = math.gcd(count, 1024)
    term_shape = (step_rows, all_seqs, kv_local, 2 * HD)

    def compute_block(offset):
        key_blk = lax.dynamic_slice_in_dim(key_all, offset, step_rows, 1)
        value_blk = lax.dynamic_slice_in_dim(value_all, offset, step_rows, 1)
        prob_rows, grad_scores = score_grads(
            queries,
            grad_heads,
            log_total,
            row_delta,
            key_blk,
            value_blk,
            offset,
            query_pos,
            score_scale,
        )
        grad_keys = (
            jnp.einsum(
                "sqkgj,sqkgd->jskd", grad_scores, queries, preferred_element_type=jnp.float32
            )
            * score_scale
        )
        grad_values = jnp.einsum(
            "sqkgj,sqkgd->jskd", prob_rows, grad_heads, preferred_element_type=jnp.float32
        )
        return jnp.concatenate([grad_keys, grad_values], axis=-1)

    def one_block(offset):
        return lax.cond(
            offset < key_limit,
            compute_block,
            lambda unused: jnp.zeros(term_shape, jnp.float32),
            offset,
        )

    block_terms = lax.map(
        lambda number: one_block(number * step_rows), jnp.arange(count // step_rows)
    )
    key_grads = lax.psum_scatter(
        block_terms.reshape((count,) + block_terms.shape[2:]),
        "seq",
        scatter_dimension=0,
        tiled=True,
    )
    grad_key_heads = jnp.moveaxis(key_grads[..., :HD], 0, 1)
    grad_value_heads = jnp.moveaxis(key_grads[..., HD:], 0, 1)
    grad_x_a, grad_step_a, grad_maps_a, grad_bias_a, grad_skip, grad_state = output_back(
        grad_inner_y
    )
    grad_carry = entering((block_fall, grad_state), "seq", chain_rule, neutral)[1]
    grad_x_b, grad_step_b, grad_maps_b, grad_bias_b = state_back(grad_carry)
    grad_step_bias, grad_skip_gain = lax.psum((grad_bias_a + grad_bias_b, grad_skip), "seq")
    returned_grads = (
        lax.all_to_all(
            grad_queries.reshape(all_seqs, block_rows, 1, -1).astype(jnp.bfloat16),
            "head",
            split_axis=0,
            concat_axis=2,
            tiled=True,
        ).astype(jnp.float32),
        lax.all_to_all(
            grad_key_heads.astype(jnp.bfloat16), "head", split_axis=0, concat_axis=2, tiled=True
        ).astype(grad_key_heads.dtype),
        lax.all_to_all(
            grad_value_heads.astype(jnp.bfloat16), "head", split_axis=0, concat_axis=2, tiled=True
        ).astype(grad_value_heads.dtype),
        lax.all_to_all(
            (grad_x_a + grad_x_b).reshape(all_seqs, block_rows, 1, -1).astype(jnp.bfloat16),
            "head",
            split_axis=0,
            concat_axis=2,
            tiled=True,
        ).astype(jnp.float32),
        lax.all_to_all(
            (grad_step_a + grad_step_b).reshape(all_seqs, block_rows, 1, -1).astype(jnp.bfloat16),
            "head",
            split_axis=0,
            concat_axis=2,
            tiled=True,
        ).astype(jnp.float32),
        lax.all_to_all(
            (grad_maps_a + grad_maps_b)[:, :, None, :].astype(jnp.bfloat16),
            "head",
            split_axis=0,
            concat_axis=2,
            tiled=True,
        ).astype(jnp.float32),
    )
    grad_q = rounded(returned_grads[0].reshape(local_seqs, block_rows, QH, HD))
    grad_k = rounded(returned_grads[1])
    grad_v = returned_grads[2].reshape(token_rows, KVH * HD)
    grad_qkv_rows = jnp.concatenate(
        [
            rotary(grad_q, -positions).reshape(token_rows, -1),
            rotary(grad_k, -positions).reshape(token_rows, -1),
            grad_v,
        ],
        axis=-1,
    ).astype(jnp.bfloat16)
    grad_x_in = rounded(returned_grads[3].reshape(local_seqs, block_rows, inner_width))
    grad_step = rounded(returned_grads[4].reshape(token_rows, MH))
    grad_maps = rounded(jnp.sum(returned_grads[5], axis=2))
    grad_padded, grad_conv_weight, grad_conv_bias = conv_back(
        jnp.concatenate([grad_x_in, grad_maps], axis=-1)
    )
    rim_grad = passed_along(shortened(grad_padded[:, : KC - 1, :]), "seq", -1)
    grad_conv_in = grad_padded[:, KC - 1 :, :].at[:, block_rows - (KC - 1) :, :].add(rim_grad)
    grad_inner_rows = jnp.concatenate(
        [grad_gate_z.reshape(token_rows, -1), grad_conv_in.reshape(token_rows, -1), grad_step],
        axis=-1,
    ).astype(jnp.bfloat16)
    grad_qkv_weight = jnp.einsum(
        "rd,re->de", normed, grad_qkv_rows, preferred_element_type=jnp.float32
    )
    grad_inner_weight = jnp.einsum(
        "rd,re->de", normed, grad_inner_rows, preferred_element_type=jnp.float32
    )
    grad_normed = jnp.einsum(
        "re,de->rd", grad_qkv_rows, qkv_full, preferred_element_type=jnp.float32
    ) + jnp.einsum("re,de->rd", grad_inner_rows, inner_full, preferred_element_type=jnp.float32)
    grad_x_norm, grad_norm_gain = norm_back(grad_normed)
    grad_tokens = (grad_hidden + grad_x_norm).reshape(tokens.shape)
    weight_grads = (
        grad_norm_gain,
        grad_qkv_weight,
        grad_attn,
        grad_inner_weight,
        grad_conv_weight,
        grad_conv_bias,
        grad_inner_gain,
        grad_inner_out,
        grad_ff_gain,
        grad_gate_up,
        grad_down,
    )
    shares = (
        lax.psum_scatter(weight_grads[0], ("head", "seq"), scatter_dimension=0, tiled=True),
        lax.psum_scatter(weight_grads[1], ("head", "seq"), scatter_dimension=0, tiled=True),
        lax.psum_scatter(weight_grads[2], ("head", "seq"), scatter_dimension=1, tiled=True),
        lax.psum_scatter(weight_grads[3], ("head", "seq"), scatter_dimension=0, tiled=True),
        lax.psum_scatter(weight_grads[4], ("head", "seq"), scatter_dimension=1, tiled=True),
        lax.psum_scatter(weight_grads[5], ("head", "seq"), scatter_dimension=0, tiled=True),
        lax.psum_scatter(weight_grads[6], ("head", "seq"), scatter_dimension=0, tiled=True),
        lax.psum_scatter(weight_grads[7], ("head", "seq"), scatter_dimension=1, tiled=True),
        lax.psum_scatter(weight_grads[8], ("head", "seq"), scatter_dimension=0, tiled=True),
        lax.psum_scatter(weight_grads[9], ("head", "seq"), scatter_dimension=0, tiled=True),
        lax.psum_scatter(weight_grads[10], ("head", "seq"), scatter_dimension=1, tiled=True),
    )
    return (
        output,
        grad_tokens,
        shares[0],
        shares[1],
        shares[2],
        shares[3],
        shares[4],
        shares[5],
        grad_step_bias,
        grad_skip_gain,
        shares[6],
        shares[7],
        shares[8],
        shares[9],
        shares[10],
    )


BLOCK = 128
BIT_C, BIT_ZH, BIT_ZL, BIT_Y, BIT_X = 16, 8, 4, 2, 1
DEVICES = 32
BOTH = ("head", "seq")
CUBE_ORDERS = ((0, 1, 2), (1, 2, 0), (2, 0, 1))
CUBE_BITS = (BIT_ZL, BIT_Y, BIT_X)
bf16 = jnp.bfloat16
f32 = jnp.float32


def flip(value, mask):
    return lax.ppermute(value, BOTH, [(i, i ^ mask) for i in range(DEVICES)])


def swap_sequences(value):
    pairs = []
    for i in range(DEVICES):
        core, half = (i // BIT_C) % 2, (i // BIT_ZH) % 2
        pairs.append((i, i - core * BIT_C - half * BIT_ZH + half * BIT_C + core * BIT_ZH))
    return lax.ppermute(value, BOTH, pairs)


def column_parts(width):
    lanes = width // 128
    first = -(-lanes // 3)
    second = -(-(lanes - first) // 2)
    edges = (0, first * 128, (first + second) * 128, width)
    return [(edges[i], edges[i + 1]) for i in range(3)]


def joint(*values):
    return lax.optimization_barrier(values)


def column_parts(width):
    lanes = width // 128
    first = -(-lanes // 3)
    second = -(-(lanes - first) // 2)
    edges = (0, first * 128, (first + second) * 128, width)
    return [(edges[i], edges[i + 1]) for i in range(3)]


def assemble(pieces, moves, shape, info):
    count = len(pieces)

    def kernel(info_ref, *refs):
        out, sems = refs[count], refs[count + 1]
        copies = []
        for at, (number, source, target) in enumerate(moves):
            copies.append(
                pltpu.make_async_copy(
                    refs[number].at[source(info_ref)], out.at[target(info_ref)], sems.at[at]
                )
            )
        for copy in copies:
            copy.start()
        for copy in copies:
            copy.wait()

    size = math.prod(shape) * 2
    return pl.pallas_call(
        kernel,
        in_specs=[pl.BlockSpec(memory_space=pltpu.SMEM)]
        + [pl.BlockSpec(memory_space=pl.ANY)] * count,
        out_specs=pl.BlockSpec(memory_space=pltpu.VMEM),
        out_shape=jax.ShapeDtypeStruct(shape, bf16),
        scratch_shapes=[pltpu.SemaphoreType.DMA((len(moves),))],
        compiler_params=pltpu.CompilerParams(vmem_limit_bytes=2 * size + 8 * 1024 * 1024),
        cost_estimate=LITTLE,
        name="assemble",
    )(info, *pieces)


def fixed(row, rows, column, columns):
    return lambda info: (pl.ds(row, rows), pl.ds(column, columns))


class Gather:
    def __init__(self, value, edges):
        self.rows, self.step = value.shape[0], 0
        self.state = ([value[None, None, None, :, a:b] for a, b in edges], None)

    def hop(self):
        parts, received = self.state
        if received is not None:
            parts = [
                jnp.concatenate([part, got], axis=order[self.step - 1])
                for part, got, order in zip(parts, received, CUBE_ORDERS)
            ]
        sent = [
            flip(part, CUBE_BITS[order[self.step]]) for part, order in zip(parts, CUBE_ORDERS)
        ]
        self.state = (parts, sent)
        self.step += 1

    def pieces(self):
        while self.step < 3:
            self.hop()
        near, far = [[part.reshape(4 * self.rows, -1) for part in parts] for parts in self.state]
        crossed = [flip(jnp.concatenate(parts, axis=1), BIT_C) for parts in (near, far)]
        return near + far + crossed


def piece_blocks(part, far):
    last = CUBE_ORDERS[part][2]
    if last == 0:
        return [(0, 4 * far, 4)]
    if last == 1:
        return [(2 * z, 4 * z + 2 * far, 2) for z in range(2)]
    return [(i, 2 * i + far, 1) for i in range(4)]


def gathered(gather, width, info):
    rows = gather.rows
    pieces = gather.pieces()
    moves = []
    for group in range(4):
        half, far = group // 2, group % 2
        for part, (a, b) in enumerate(column_parts(width)):
            number = 3 * group + part if half == 0 else 6 + far
            for first, place, blocks in piece_blocks(part, far):
                moves.append(
                    (
                        number,
                        fixed(first * rows, blocks * rows, a * half, b - a),
                        fixed((half * 8 + place) * rows, blocks * rows, a, b - a),
                    )
                )
    return assemble(pieces, moves, (16 * rows, width), info)


def gather_start(value):
    return Gather(value, column_parts(value.shape[1]))


class Scatter:
    def __init__(self, own_half, other_half):
        self.total_rows, self.width = own_half.shape
        self.step = 0
        self.state = (own_half, flip(other_half.astype(bf16), BIT_C))

    def summed(self):
        kept, received = self.state
        if self.step == 0:
            value = kept.astype(f32) + received.astype(f32)
            shape = (2, 2, 2, self.total_rows // 8, self.width)
            value = value.reshape(shape)
            return [value[..., a:b] for a, b in column_parts(self.width)]
        return [near.astype(f32) + got.astype(f32) for near, got in zip(kept, received)]

    def hop(self):
        near, sent = [], []
        for part, order in zip(self.summed(), CUBE_ORDERS):
            axis = order[self.step]
            part = part.astype(bf16)
            near.append(lax.slice_in_dim(part, 0, 1, axis=axis))
            sent.append(flip(lax.slice_in_dim(part, 1, 2, axis=axis), CUBE_BITS[axis]))
        self.state = (near, sent)
        self.step += 1

    def result(self):
        while self.step < 3:
            self.hop()
        rows = self.total_rows // 8
        return jnp.concatenate([part.reshape(rows, -1) for part in self.summed()], axis=1)


def group_sum(value):
    for masks in ((BIT_C, BIT_X, BIT_C + BIT_X), (BIT_Y, BIT_ZL, BIT_Y + BIT_ZL)):
        first, second, third = [flip(value, mask) for mask in masks]
        value = (value + first) + (second + third)
    return value


def exchange(value):
    return lax.all_to_all(value, BOTH, split_axis=0, concat_axis=0, tiled=True)


def mm(a, b):
    return jnp.dot(a, b, preferred_element_type=f32)


def mm_nt(a, b):
    return lax.dot_general(a, b, (((1,), (1,)), ((), ())), preferred_element_type=f32)


def mm_tn(a, b):
    return lax.dot_general(a, b, (((0,), (0,)), ((), ())), preferred_element_type=f32)


VMEM_ASK = 40 * 1024 * 1024
LITTLE = pl.CostEstimate(flops=1000, bytes_accessed=1000, transcendentals=0)


def params():
    return pltpu.CompilerParams(
        dimension_semantics=("arbitrary",), vmem_limit_bytes=VMEM_ASK
    )


def k_nt(a, b, precision=None):
    return lax.dot_general(
        a, b, (((1,), (1,)), ((), ())), preferred_element_type=f32, precision=precision
    )


def k_tn(a, b):
    return lax.dot_general(a, b, (((0,), (0,)), ((), ())), preferred_element_type=f32)


def k_mm(a, b, precision=None):
    return lax.dot_general(
        a, b, (((1,), (0,)), ((), ())), preferred_element_type=f32, precision=precision
    )


def logistic(value):
    return 1.0 / (1.0 + jnp.exp(-value))


def by_head(columns, lane):
    spread = columns[:, 0:1]
    for head in range(1, HEADS_HERE):
        spread = jnp.where(lane >= head * MP, columns[:, head : head + 1], spread)
    return spread


def shifted_sum(padded, taps, start, step):
    total = None
    for tap in range(KC):
        at = start + step * tap
        term = taps[tap : tap + 1] * padded[at : at + BLOCK]
        total = term if total is None else total + term
    return total


HEADS_HERE = 3
OWN = HEADS_HERE * MP
TAIL = 8
KEYS_AT = 2 * NS


def block_decays(cum_col, cum_row, lane):
    cum = by_head(cum_col, lane)
    last = cum[BLOCK - 1 : BLOCK]
    row = lax.broadcasted_iota(jnp.int32, (BLOCK, BLOCK), 0)
    col = lax.broadcasted_iota(jnp.int32, (BLOCK, BLOCK), 1)
    reach = []
    for head in range(HEADS_HERE):
        spread = cum_col[:, head : head + 1] - cum_row[head : head + 1, :]
        reach.append(jnp.where(row >= col, jnp.exp(jnp.minimum(spread, 0.0)), 0.0))
    return cum, last, reach


def step_lanes(place, lane):
    source = lax.broadcasted_iota(jnp.int32, (128, OWN), 0)
    head = lax.broadcasted_iota(jnp.int32, (128, OWN), 1) // MP
    return jnp.where(source == place * HEADS_HERE + head, 1.0, 0.0)


def mix_forward(
    info,
    own_ref,
    s_ref,
    cos_ref,
    sin_ref,
    cum_col_ref,
    cum_row_ref,
    taps_x_ref,
    taps_m_ref,
    vec_ref,
    y_ref,
    gained_ref,
    square_ref,
    state_ref,
    q_ref,
    k_ref,
    v_ref,
    state,
    last_x,
    last_m,
):
    @pl.when(pl.program_id(0) == 0)
    def _():
        state[...] = jnp.zeros_like(state)
        last_x[...] = jnp.zeros_like(last_x)
        last_m[...] = jnp.zeros_like(last_m)

    lane = lax.broadcasted_iota(jnp.int32, (1, OWN), 1)
    gate = own_ref[:, :OWN]
    x_raw = own_ref[:, OWN : 2 * OWN]
    m_raw = s_ref[:, : 2 * NS]
    cosine, sine = cos_ref[...], sin_ref[...]

    def turned(value):
        return (value * cosine + pltpu.roll(value, HD // 2, 1) * sine).astype(bf16)

    q_ref[...] = turned(own_ref[:, 2 * OWN :])
    k_ref[...] = turned(s_ref[:, KEYS_AT : KEYS_AT + HD])
    v_ref[...] = s_ref[:, KEYS_AT + HD : KEYS_AT + 2 * HD].astype(bf16)

    s_x = shifted_sum(
        jnp.concatenate([last_x[...], x_raw], axis=0), taps_x_ref, TAIL - KC + 1, 1
    ) + taps_x_ref[KC : KC + 1]
    s_m = shifted_sum(
        jnp.concatenate([last_m[...], m_raw], axis=0), taps_m_ref, TAIL - KC + 1, 1
    ) + taps_m_ref[KC : KC + 1]
    last_x[...] = x_raw[BLOCK - TAIL :]
    last_m[...] = m_raw[BLOCK - TAIL :]
    x = (s_x * logistic(s_x)).astype(bf16).astype(f32)
    maps = (s_m * logistic(s_m)).astype(bf16)
    b_map, c_map = maps[:, :NS], maps[:, NS:]

    place = info[0]
    picked = k_mm(s_ref[:, KEYS_AT + 2 * HD :].astype(bf16), step_lanes(place, lane).astype(bf16))
    raised = picked + vec_ref[0:1]
    step = jnp.maximum(raised, 0.0) + jnp.log(1.0 + jnp.exp(-jnp.abs(raised)))
    cum, last, reach = block_decays(cum_col_ref[...], cum_row_ref[0], lane)
    scaled = step * x
    inter = k_nt(c_map, b_map)
    total = vec_ref[1:2] * x
    for head in range(HEADS_HERE):
        here = (lane >= head * MP) & (lane < (head + 1) * MP)
        total += k_mm(
            (reach[head] * inter).astype(bf16), jnp.where(here, scaled, 0.0).astype(bf16)
        )
    before = state[...]
    state_ref[0] = before.astype(bf16)
    total += jnp.exp(cum) * k_mm(c_map, before.astype(bf16))
    tail = (jnp.exp(last - cum) * scaled).astype(bf16)
    state[...] = jnp.exp(last) * before + k_tn(b_map, tail)
    y = total.astype(bf16)
    y_ref[...] = y
    gated = y.astype(f32) * (gate * logistic(gate))
    gained_ref[...] = (gated * vec_ref[2:3]).astype(bf16)
    square_ref[0] = k_nt(jnp.ones((8, OWN), f32), gated * gated, HIGHEST)


def mix_backward(
    info,
    own_ref,
    s_ref,
    own_tail_ref,
    s_tail_ref,
    cos_ref,
    sin_ref,
    cum_col_ref,
    cum_row_ref,
    taps_x_ref,
    taps_m_ref,
    vec_ref,
    lanes_ref,
    y_ref,
    g_inner_ref,
    scales_ref,
    state_ref,
    dq_ref,
    dk_ref,
    dv_ref,
    g_all_ref,
    acc_x_ref,
    acc_m_ref,
    acc_v_ref,
    acc_s_ref,
    g_state,
    next_x,
    next_m,
):
    step_id = pl.program_id(0)
    block = pl.num_programs(0) - 1 - step_id
    place = info[0]

    @pl.when(step_id == 0)
    def _():
        g_state[...] = jnp.zeros_like(g_state)
        next_x[...] = jnp.zeros_like(next_x)
        next_m[...] = jnp.zeros_like(next_m)
        acc_x_ref[...] = jnp.zeros_like(acc_x_ref)
        acc_m_ref[...] = jnp.zeros_like(acc_m_ref)
        acc_v_ref[...] = jnp.zeros_like(acc_v_ref)
        acc_s_ref[...] = jnp.zeros_like(acc_s_ref)

    lane = lax.broadcasted_iota(jnp.int32, (1, OWN), 1)
    cosine, sine = cos_ref[...], sin_ref[...]

    def unturned(value):
        return value * cosine - pltpu.roll(value, HD // 2, 1) * sine

    gate = own_ref[:, :OWN]
    x_raw = own_ref[:, OWN : 2 * OWN]
    m_raw = s_ref[:, : 2 * NS]
    first = block == 0
    x_pad = jnp.concatenate(
        [jnp.where(first, 0.0, own_tail_ref[:, OWN : 2 * OWN]), x_raw], axis=0
    )
    m_pad = jnp.concatenate([jnp.where(first, 0.0, s_tail_ref[:, : 2 * NS]), m_raw], axis=0)
    s_x = shifted_sum(x_pad, taps_x_ref, TAIL - KC + 1, 1) + taps_x_ref[KC : KC + 1]
    s_m = shifted_sum(m_pad, taps_m_ref, TAIL - KC + 1, 1) + taps_m_ref[KC : KC + 1]
    sig_x, sig_m = logistic(s_x), logistic(s_m)
    x = (s_x * sig_x).astype(bf16).astype(f32)
    maps = (s_m * sig_m).astype(bf16)
    b_map, c_map = maps[:, :NS], maps[:, NS:]
    select = step_lanes(place, lane)
    step_raw = s_ref[:, KEYS_AT + 2 * HD :].astype(bf16)
    raised = k_mm(step_raw, select.astype(bf16)) + vec_ref[0:1]
    step = jnp.maximum(raised, 0.0) + jnp.log(1.0 + jnp.exp(-jnp.abs(raised)))
    cum, last, reach = block_decays(cum_col_ref[...], cum_row_ref[0], lane)
    scaled = step * x

    inv, dots = scales_ref[:, 0:1], scales_ref[:, 1:2]
    y = y_ref[...].astype(f32)
    g_inner = g_inner_ref[...]
    gate_sig = logistic(gate)
    gate_silu = gate * gate_sig
    normed = y * gate_silu * inv
    g_gated = inv * (vec_ref[2:3] * g_inner - normed * dots)
    g_y = (g_gated * gate_silu).astype(bf16).astype(f32)
    g_z = g_gated * y * gate_sig * (1.0 + gate * (1.0 - gate_sig))

    inter = k_nt(c_map, b_map)
    g_inter = jnp.zeros((BLOCK, BLOCK), f32)
    g_scaled = jnp.zeros((BLOCK, OWN), f32)
    scaled_b = scaled.astype(bf16)
    for head in range(HEADS_HERE):
        here = (lane >= head * MP) & (lane < (head + 1) * MP)
        g_head = jnp.where(here, g_y, 0.0).astype(bf16)
        g_inter += reach[head] * k_nt(g_head, scaled_b)
        g_scaled += k_tn((reach[head] * inter).astype(bf16), g_head)
    before = state_ref[0]
    g_after = g_state[...]
    g_after_b = g_after.astype(bf16)
    tail_w = jnp.exp(last - cum)
    reached = (jnp.exp(cum) * g_y).astype(bf16)
    g_inter_b = g_inter.astype(bf16)
    g_c = k_mm(g_inter_b, b_map) + k_nt(reached, before)
    g_b = k_tn(g_inter_b, c_map) + k_nt((tail_w * scaled).astype(bf16), g_after_b)
    g_scaled += tail_w * k_mm(b_map, g_after_b)
    g_state[...] = jnp.exp(last) * g_after + k_tn(c_map, reached)
    g_x = step * g_scaled + vec_ref[1:2] * g_y
    g_step = k_nt(x * g_scaled, select, HIGHEST) * logistic(
        step_raw.astype(f32) + lanes_ref[0:1]
    )

    gs_x = g_x.astype(bf16).astype(f32) * (sig_x * (1.0 + s_x * (1.0 - sig_x)))
    g_maps = jnp.concatenate([g_b, g_c], axis=1).astype(bf16).astype(f32)
    gs_m = g_maps * (sig_m * (1.0 + s_m * (1.0 - sig_m)))
    gs_x_pad = jnp.concatenate([gs_x, next_x[...]], axis=0)
    gs_m_pad = jnp.concatenate([gs_m, next_m[...]], axis=0)
    g_x_raw = shifted_sum(gs_x_pad, taps_x_ref, KC - 1, -1)
    g_m_raw = shifted_sum(gs_m_pad, taps_m_ref, KC - 1, -1)
    next_x[...] = gs_x[:TAIL]
    next_m[...] = gs_m[:TAIL]
    for tap in range(KC):
        at = TAIL - KC + 1 + tap
        acc_x_ref[tap : tap + 1] += jnp.sum(gs_x * x_pad[at : at + BLOCK], axis=0, keepdims=True)
        acc_m_ref[tap : tap + 1] += jnp.sum(gs_m * m_pad[at : at + BLOCK], axis=0, keepdims=True)
    acc_x_ref[KC : KC + 1] += jnp.sum(gs_x, axis=0, keepdims=True)
    acc_m_ref[KC : KC + 1] += jnp.sum(gs_m, axis=0, keepdims=True)
    acc_v_ref[0:1] += jnp.sum(normed * g_inner, axis=0, keepdims=True)
    acc_v_ref[1:2] += jnp.sum(g_y * x, axis=0, keepdims=True)
    acc_s_ref[0:1] += jnp.sum(g_step, axis=0, keepdims=True)

    here = (block // 8) == info[1]
    g_q = jnp.where(here, unturned(dq_ref[...]), 0.0)
    at = 2 * OWN
    g_all_ref[:, :at] = jnp.concatenate([g_z, g_x_raw], axis=1).astype(bf16)
    for piece in (g_q, g_m_raw, unturned(dk_ref[...]), dv_ref[...], g_step):
        g_all_ref[:, at : at + piece.shape[1]] = piece.astype(bf16)
        at += piece.shape[1]


def masked_scores(info, keys, queries, length):
    scores = k_nt(keys, queries) * (HD**-0.5)
    start = (info[1] * 8 + pl.program_id(0)) * BLOCK
    key_at = lax.broadcasted_iota(jnp.int32, (length, BLOCK), 0)
    query_at = lax.broadcasted_iota(jnp.int32, (length, BLOCK), 1) + start
    return scores, key_at <= query_at


def attend_forward(info, q_ref, k_ref, v_ref, out_ref, out_f_ref, log_ref):
    scores, allowed = masked_scores(info, k_ref[...], q_ref[...], k_ref.shape[0])
    scores = jnp.where(allowed, scores, NEGATIVE)
    top = jnp.max(scores, axis=0, keepdims=True)
    weights = jnp.exp(scores - top)
    total = jnp.sum(weights, axis=0, keepdims=True)
    result = jnp.transpose(k_tn(v_ref[...], weights.astype(bf16)) / total)
    out_ref[...] = result.astype(bf16)
    out_f_ref[...] = result
    log_ref[0] = jnp.broadcast_to(top + jnp.log(total), (8, BLOCK))


def attend_backward(info, q_ref, k_ref, v_ref, out_f_ref, log_ref, g_ref, dq_ref, dk_ref, dv_ref):
    @pl.when(pl.program_id(0) == 0)
    def _():
        dk_ref[...] = jnp.zeros_like(dk_ref)
        dv_ref[...] = jnp.zeros_like(dv_ref)

    keys, queries, grads = k_ref[...], q_ref[...], g_ref[...]
    scores, allowed = masked_scores(info, keys, queries, k_ref.shape[0])
    probs = jnp.where(allowed, jnp.exp(scores - log_ref[0, 0:1]), 0.0)
    delta = k_nt(jnp.ones((8, HD), f32), grads.astype(f32) * out_f_ref[...], HIGHEST)[0:1]
    g_scores = (probs * (k_nt(v_ref[...], grads) - delta)).astype(bf16)
    dv_ref[...] += k_mm(probs.astype(bf16), grads)
    dk_ref[...] += k_mm(g_scores, queries) * (HD**-0.5)
    dq_ref[...] = (k_tn(g_scores, keys) * (HD**-0.5)).astype(bf16).astype(f32)


def rows_at(width, column=0):
    return pl.BlockSpec((BLOCK, width), lambda i, s: (i ^ s[0], column))


def rows_back(count, width, column=0):
    return pl.BlockSpec((BLOCK, width), lambda i, s: ((count - 1 - i) ^ s[0], column))


def whole(*shape):
    return pl.BlockSpec(shape, lambda i, s: (0,) * len(shape))


def run_mix_forward(info, own, shared, cosine, sine, cum_col, cum_row, taps_x, taps_m, vec):
    length = own.shape[0]
    count = length // BLOCK

    def plain(width):
        return pl.BlockSpec((BLOCK, width), lambda i, s: (i, 0))

    def plain3(rows, width):
        return pl.BlockSpec((1, rows, width), lambda i, s: (i, 0, 0))

    return pl.pallas_call(
        mix_forward,
        grid_spec=pltpu.PrefetchScalarGridSpec(
            num_scalar_prefetch=1,
            grid=(count,),
            in_specs=[
                rows_at(own.shape[1]),
                rows_at(shared.shape[1]),
                plain(HD),
                plain(HD),
                plain(8),
                plain3(8, BLOCK),
                whole(8, OWN),
                whole(8, 2 * NS),
                whole(8, OWN),
            ],
            out_specs=[
                rows_at(OWN),
                rows_at(OWN),
                plain3(8, BLOCK),
                plain3(NS, OWN),
                plain(HD),
                plain(HD),
                plain(HD),
            ],
            scratch_shapes=[
                pltpu.VMEM((NS, OWN), f32),
                pltpu.VMEM((TAIL, OWN), f32),
                pltpu.VMEM((TAIL, 2 * NS), f32),
            ],
        ),
        out_shape=[
            jax.ShapeDtypeStruct((length, OWN), bf16),
            jax.ShapeDtypeStruct((length, OWN), bf16),
            jax.ShapeDtypeStruct((count, 8, BLOCK), f32),
            jax.ShapeDtypeStruct((count, NS, OWN), bf16),
            jax.ShapeDtypeStruct((length, HD), bf16),
            jax.ShapeDtypeStruct((length, HD), bf16),
            jax.ShapeDtypeStruct((length, HD), bf16),
        ],
        compiler_params=params(),
        cost_estimate=LITTLE,
        name="mix_forward",
    )(info, own, shared, cosine, sine, cum_col, cum_row, taps_x, taps_m, vec)


def run_mix_backward(
    info,
    own,
    shared,
    cosine,
    sine,
    cum_col,
    cum_row,
    taps_x,
    taps_m,
    vec,
    lanes,
    y,
    g_inner,
    scales,
    states,
    dq,
    dk,
    dv,
):
    length = own.shape[0]
    count = length // BLOCK
    tails = BLOCK // TAIL
    all_width = own.shape[1] + shared.shape[1]

    def plain(width):
        return pl.BlockSpec((BLOCK, width), lambda i, s: (count - 1 - i, 0))

    def plain3(rows, width):
        return pl.BlockSpec((1, rows, width), lambda i, s: (count - 1 - i, 0, 0))

    def tail_of(width):
        def where(i, s):
            before = jnp.maximum(count - 2 - i, 0)
            return ((before ^ s[0]) * tails + tails - 1, 0)

        return pl.BlockSpec((TAIL, width), where)

    def query_rows(i, s):
        return ((count - 1 - i) % 8, 0)

    return pl.pallas_call(
        mix_backward,
        grid_spec=pltpu.PrefetchScalarGridSpec(
            num_scalar_prefetch=1,
            grid=(count,),
            in_specs=[
                rows_back(count, own.shape[1]),
                rows_back(count, shared.shape[1]),
                tail_of(own.shape[1]),
                tail_of(shared.shape[1]),
                plain(HD),
                plain(HD),
                plain(8),
                plain3(8, BLOCK),
                whole(8, OWN),
                whole(8, 2 * NS),
                whole(8, OWN),
                whole(8, 128),
                rows_back(count, OWN),
                rows_back(count, OWN),
                plain(8),
                plain3(NS, OWN),
                pl.BlockSpec((BLOCK, HD), query_rows),
                plain(HD),
                plain(HD),
            ],
            out_specs=[
                rows_back(count, all_width),
                whole(8, OWN),
                whole(8, 2 * NS),
                whole(8, OWN),
                whole(8, 128),
            ],
            scratch_shapes=[
                pltpu.VMEM((NS, OWN), f32),
                pltpu.VMEM((TAIL, OWN), f32),
                pltpu.VMEM((TAIL, 2 * NS), f32),
            ],
        ),
        out_shape=[
            jax.ShapeDtypeStruct((length, all_width), bf16),
            jax.ShapeDtypeStruct((8, OWN), f32),
            jax.ShapeDtypeStruct((8, 2 * NS), f32),
            jax.ShapeDtypeStruct((8, OWN), f32),
            jax.ShapeDtypeStruct((8, 128), f32),
        ],
        compiler_params=params(),
        cost_estimate=LITTLE,
        name="mix_backward",
    )(
        info,
        own,
        shared,
        own,
        shared,
        cosine,
        sine,
        cum_col,
        cum_row,
        taps_x,
        taps_m,
        vec,
        lanes,
        y,
        g_inner,
        scales,
        states,
        dq,
        dk,
        dv,
    )


def own_queries(width):
    return pl.BlockSpec((BLOCK, width), lambda i, s: (s[1] * 8 + i, 0))


def own_rows(width):
    return pl.BlockSpec((BLOCK, width), lambda i, s: (i ^ s[2], 0))


def run_attend_forward(info, queries, keys, values):
    length = keys.shape[0]
    half = length // 2
    count = half // BLOCK
    return pl.pallas_call(
        attend_forward,
        grid_spec=pltpu.PrefetchScalarGridSpec(
            num_scalar_prefetch=1,
            grid=(count,),
            in_specs=[own_queries(HD), whole(length, HD), whole(length, HD)],
            out_specs=[
                own_rows(HD),
                pl.BlockSpec((BLOCK, HD), lambda i, s: (i, 0)),
                pl.BlockSpec((1, 8, BLOCK), lambda i, s: (i, 0, 0)),
            ],
        ),
        out_shape=[
            jax.ShapeDtypeStruct((half, HD), bf16),
            jax.ShapeDtypeStruct((half, HD), f32),
            jax.ShapeDtypeStruct((count, 8, BLOCK), f32),
        ],
        compiler_params=params(),
        cost_estimate=LITTLE,
        name="attend_forward",
    )(info, queries, keys, values)


def run_attend_backward(info, queries, keys, values, out_f, logs, grads):
    length = keys.shape[0]
    half = length // 2
    count = half // BLOCK
    return pl.pallas_call(
        attend_backward,
        grid_spec=pltpu.PrefetchScalarGridSpec(
            num_scalar_prefetch=1,
            grid=(count,),
            in_specs=[
                own_queries(HD),
                whole(length, HD),
                whole(length, HD),
                pl.BlockSpec((BLOCK, HD), lambda i, s: (i, 0)),
                pl.BlockSpec((1, 8, BLOCK), lambda i, s: (i, 0, 0)),
                own_rows(HD),
            ],
            out_specs=[
                pl.BlockSpec((BLOCK, HD), lambda i, s: (i, 0)),
                whole(length, HD),
                whole(length, HD),
            ],
        ),
        out_shape=[
            jax.ShapeDtypeStruct((half, HD), f32),
            jax.ShapeDtypeStruct((length, HD), f32),
            jax.ShapeDtypeStruct((length, HD), f32),
        ],
        compiler_params=params(),
        cost_estimate=LITTLE,
        name="attend_backward",
    )(info, queries, keys, values, out_f, logs, grads)


def cube_body(
    tokens,
    log_decay,
    norm_gain,
    qkv_proj,
    attn_proj,
    inner_proj,
    conv_weight,
    conv_bias,
    step_bias,
    skip_gain,
    inner_gain,
    inner_out,
    ff_gain,
    gate_up,
    down_proj,
    cotangent,
):
    core = lax.axis_index("head")
    chip = lax.axis_index("seq")
    member = chip % 8
    bits = (member // 4, (member // 2) % 2, member % 2)
    zl = bits[0]
    place = core * 8 + member
    info = jnp.stack([place, core, member]).astype(jnp.int32)
    width = tokens.shape[-1]
    rows = tokens.shape[1]
    shard = width // DEVICES
    inner_width = MH * MP
    conv_width = inner_width + 2 * NS
    heads = MH // 16
    mine = heads * MP
    length = rows * 16
    half_rows = rows * 8
    ffc = FF // 16

    x_bf = swap_sequences(tokens[0])

    gain_rows = norm_gain.astype(f32)[:, None]
    qkv_s = (qkv_proj.astype(f32) * gain_rows).astype(bf16)
    inner_s = (inner_proj.astype(f32) * gain_rows).astype(bf16)
    gate_up_s = (gate_up.astype(f32) * ff_gain.astype(f32)[:, None]).astype(bf16)

    def to_places(value):
        return jnp.moveaxis(value.reshape(shard, 16, -1), 1, 0)

    def to_members(value):
        parts = jnp.moveaxis(value.reshape(shard, 8, -1), 1, 0)
        return jnp.concatenate([parts, parts], axis=0)

    def for_devices(value):
        split = value.reshape((2, 1, 8) + value.shape[1:])
        return jnp.broadcast_to(split, (2, 2, 8) + value.shape[1:]).reshape(
            (DEVICES,) + value.shape[1:]
        )

    kv_width = KVH * HD
    conv_shard = conv_weight.shape[1]
    smalls = jnp.concatenate([conv_weight.reshape(-1), conv_bias, inner_gain])
    decay_rows = jnp.moveaxis(log_decay, 1, 2).reshape(2, -1)
    decay_high = lax.optimization_barrier(decay_rows.astype(bf16))
    decay_low = (decay_rows - decay_high.astype(f32)).astype(bf16)
    decay_rows = jnp.concatenate([decay_high, decay_low], axis=1)
    extra_size = shard * 128
    extra_pad = jnp.zeros((extra_size - smalls.shape[0] - decay_rows.shape[1],), bf16)
    seq_half = chip // 8

    def shared_for(half):
        mine_rows = lax.dynamic_index_in_dim(decay_rows, half, 0, keepdims=False)
        extra = jnp.concatenate([smalls, mine_rows, extra_pad]).reshape(shard, 128)
        return jnp.concatenate([shared_send, extra], axis=1)

    shared_send = jnp.concatenate(
        [
            inner_s[:, 2 * inner_width : inner_width + conv_width],
            qkv_s[:, QH * HD : QH * HD + kv_width],
            inner_s[:, inner_width + conv_width :],
            jnp.zeros((shard, -MH % 128), bf16),
            qkv_s[:, QH * HD + kv_width :],
        ],
        axis=1,
    )
    shared_other = flip(shared_for(1 - seq_half), BIT_ZH)
    send_in = jnp.concatenate(
        [
            to_places(inner_s[:, :inner_width]),
            to_places(inner_s[:, inner_width : 2 * inner_width]),
            to_members(qkv_s[:, : QH * HD]),
        ],
        axis=2,
    )
    send_in, x_bf, shared_other = joint(for_devices(send_in), x_bf, shared_other)
    w_own = exchange(send_in).reshape(width, 2 * mine + HD)
    x_rows = x_bf.astype(f32)
    inv_in = lax.rsqrt(jnp.mean(x_rows * x_rows, axis=-1, keepdims=True) + EPSILON)
    shared_mine = shared_for(seq_half)
    shared_both = jnp.where(
        seq_half == 0,
        jnp.concatenate([shared_mine, shared_other], axis=0),
        jnp.concatenate([shared_other, shared_mine], axis=0),
    )
    normed_mine = (x_rows * inv_in).astype(bf16)
    shared_edges = ((0, 2 * NS), (2 * NS, 2 * NS + kv_width + 128), (2 * NS + kv_width + 128, None))
    lanes_all = (shared_both.shape[1] + width) // 128
    goals = (-(-lanes_all // 3), -(-lanes_all // 3), lanes_all - 2 * -(-lanes_all // 3))
    edges, normed_edges, joined, at, done = [], [], [], 0, 0
    for (a, b), lanes_here in zip(shared_edges, goals):
        part = shared_both[:, a:b]
        taken = lanes_here * 128 - part.shape[1]
        joined += [part, normed_mine[:, done : done + taken]]
        edges.append((at, at + lanes_here * 128))
        normed_edges.append((part.shape[1], done, taken))
        at += lanes_here * 128
        done += taken
    pieces = Gather(jnp.concatenate(joined, axis=1), edges).pieces()
    shared_width = 2 * NS + 2 * HD + 128
    picks = (
        ((0, 0, 0, 2 * NS),),
        ((0, HD, 2 * NS, HD), (kv_width, 0, 2 * NS + 2 * HD, 128)),
        ((0, HD, 2 * NS + HD, HD),),
    )
    moves, extra_moves, normed_moves = [], [], []
    for group in range(4):
        half, far = group // 2, group % 2
        for part in range(3):
            number = 3 * group + part if half == 0 else 6 + far
            start = edges[part][0] * half
            skip, normed_at, taken = normed_edges[part]
            for first, cube_place, count in piece_blocks(part, far):
                normed_moves.append(
                    (
                        number,
                        fixed(first * rows, count * rows, start + skip, taken),
                        fixed((half * 8 + cube_place) * rows, count * rows, normed_at, taken),
                    )
                )
                for block, zh in ((i, j) for i in range(count) for j in range(2)):
                    row = (first + block) * 2 * shard + zh * shard
                    position = half * 8 + cube_place + block

                    def goal(ref, position=position, zh=zh, target=0, columns=128):
                        place = ref[0] ^ position
                        to = (place // 8) * 16 + zh * 8 + place % 8
                        to = pl.multiple_of(to * shard, shard)
                        return (pl.ds(to, shard), pl.ds(target, columns))

                    for column, by_zl, target, columns in picks[part]:

                        def source(ref, row=row, at=start + column, by_zl=by_zl, columns=columns):
                            if by_zl:
                                at = pl.multiple_of(at + (ref[2] // 4) * by_zl, 128)
                            return (pl.ds(row, shard), pl.ds(at, columns))

                        moves.append(
                            (
                                number,
                                source,
                                functools.partial(goal, target=target, columns=columns),
                            )
                        )
                    if part == 2:
                        extra_moves.append(
                            (number, fixed(row, shard, start + kv_width, 128), goal)
                        )
    normed = assemble(pieces, normed_moves, (length, width), info)
    w_s = assemble(pieces, moves, (width, shared_width), info)
    small_got = assemble(pieces, extra_moves, (width, 128), info).reshape(DEVICES, -1)
    at = smalls.shape[0]
    decay = lax.dynamic_slice_in_dim(small_got[:, at : at + decay_rows.shape[1]], core * 16, 16, 0)
    decay = decay.astype(f32).reshape(16, 2, 8, heads, rows)
    decay = lax.dynamic_index_in_dim(decay[:, 0] + decay[:, 1], member, 1, keepdims=False)
    at = 0
    conv_w = jnp.moveaxis(
        small_got[:, at : at + KC * conv_shard].reshape(DEVICES, KC, conv_shard), 1, 0
    ).reshape(KC, conv_width)
    at += KC * conv_shard
    conv_b = small_got[:, at : at + conv_shard].reshape(1, conv_width)
    at += conv_shard
    gain_all = small_got[:, at : at + inner_gain.shape[0]].reshape(1, inner_width)
    conv_all = jnp.concatenate([conv_w, conv_b], axis=0).astype(f32)
    conv_all = jnp.concatenate([conv_all, jnp.zeros((8 - KC - 1, conv_width), f32)], axis=0)
    taps_x = lax.dynamic_slice_in_dim(conv_all[:, :inner_width], place * mine, mine, 1)
    taps_m = conv_all[:, inner_width:]
    gain_mine = lax.dynamic_slice_in_dim(gain_all, place * mine, mine, 1)[0].astype(f32)

    send_mix = jnp.concatenate(
        [to_places(inner_out.T), to_members(attn_proj.T)], axis=2
    )
    send_mix, w_own = joint(for_devices(send_mix), w_own)
    w_mix = exchange(send_mix).reshape(width, mine + HD)
    send_gu = jnp.concatenate([to_places(gate_up_s[:, :FF]), to_places(gate_up_s[:, FF:])], axis=2)
    send_down, w_mix = joint(for_devices(to_places(down_proj.T)), w_mix)
    w_down = exchange(send_down).reshape(width, ffc)
    send_gu, w_down = joint(for_devices(send_gu), w_down)
    w_gu = exchange(send_gu).reshape(width, 2 * ffc)

    bias_mine = lax.dynamic_slice_in_dim(step_bias, member * heads, heads, 0)
    skip_mine = lax.dynamic_slice_in_dim(skip_gain, member * heads, heads, 0)
    vec = jnp.concatenate(
        [
            jnp.repeat(bias_mine, MP)[None],
            jnp.repeat(skip_mine, MP)[None],
            gain_mine[None],
            jnp.zeros((5, mine), f32),
        ],
        axis=0,
    )
    lanes = lax.dynamic_update_slice(
        jnp.zeros((8, 128), f32), bias_mine[None], (0, place * heads)
    )
    cum_row = jnp.cumsum(decay, axis=2)
    cum_row = jnp.concatenate([cum_row, jnp.zeros((16, 8 - heads, rows), f32)], axis=1)
    cum_col = jnp.moveaxis(cum_row, 1, 2).reshape(length, 8)
    w_all = jnp.concatenate([w_own, w_s], axis=1)

    order = jnp.arange(16, dtype=jnp.int32) ^ place

    def reordered(value):
        return jnp.take(value, order, axis=0, unique_indices=True, mode="clip")

    cotangent_mine, normed = joint(cotangent[0], normed)
    g_out_bf = swap_sequences(cotangent_mine)
    raw_s = mm(normed, w_s)
    g_out_bf, raw_s = joint(g_out_bf, raw_s)
    g_out = gather_start(g_out_bf)
    g_out.hop()
    raw_own = mm(normed, w_own)
    raw_own, w_mix = joint(raw_own, w_mix)
    w_out, w_att = w_mix[:, :mine], w_mix[:, mine:]

    positions = jnp.arange(length, dtype=f32)
    frequency = ROPE_BASE ** (-2.0 * jnp.arange(HD // 2, dtype=f32) / HD)
    angle = positions[:, None] * frequency[None, :]
    cosine, sine = jnp.cos(angle), jnp.sin(angle)
    cosine = jnp.concatenate([cosine, cosine], axis=1)
    sine = jnp.concatenate([-sine, sine], axis=1)

    tables = (cosine, sine, cum_col, cum_row, taps_x, taps_m, vec)
    y, gained, squares, states, queries, keys, values = run_mix_forward(
        info, raw_own, raw_s, *tables
    )
    g_out.state, queries = joint(g_out.state, queries)
    g_out.hop()
    squares = group_sum(squares[:, 0])
    inv_mix = lax.rsqrt(squares / inner_width + EPSILON)
    inv_mix_rows = reordered(inv_mix).reshape(length, 1)
    keys, w_down = joint(keys, w_down)
    attended, attended_f, logs = run_attend_forward(info, queries, keys, values)
    g_out.state, attended = joint(g_out.state, attended)
    g_out.hop()
    part_other = inv_mix_rows[half_rows:] * mm_nt(gained[half_rows:], w_out)
    part_own = inv_mix_rows[:half_rows] * mm_nt(gained[:half_rows], w_out) + mm_nt(attended, w_att)
    sums = Scatter(part_own.astype(bf16), part_other)
    sums.hop()
    sums.state, w_gu = joint(sums.state, w_gu)
    hidden = x_rows + sums.result()
    g_out = gathered(g_out, width, info)

    inv_ff = lax.rsqrt(jnp.mean(hidden * hidden, axis=-1, keepdims=True) + EPSILON)
    normed_ff = gathered(gather_start((hidden * inv_ff).astype(bf16)), width, info)
    gate_vals = mm(normed_ff, w_gu)
    gate, up = gate_vals[:, :ffc], gate_vals[:, ffc:]
    sig = jax.nn.sigmoid(gate)
    mixed = (gate * sig * up).astype(bf16)
    g_mixed = mm(g_out, w_down)
    g_vals = jnp.concatenate(
        [g_mixed * up * sig * (1.0 + gate * (1.0 - sig)), g_mixed * gate * sig], axis=1
    ).astype(bf16)
    g_ff_other = mm_nt(g_vals[half_rows:], w_gu).astype(bf16)
    sums = Scatter(mm_nt(g_vals[:half_rows], w_gu).astype(bf16), g_ff_other)
    g_ff_own, g_ff_got = sums.state
    g_ff_own, mixed_late, g_vals_late = joint(g_ff_own, mixed, g_vals)
    sums.state = (g_ff_own, g_ff_got)
    out_other = mm_nt(mixed_late[half_rows:], w_down).astype(bf16)
    out_own = mm_nt(mixed_late[:half_rows], w_down).astype(bf16)
    d_gu = mm_tn(normed_ff, g_vals_late).astype(bf16)
    d_down = mm_tn(g_out, mixed_late).astype(bf16)
    sums.hop()
    sums.state, out_other, out_own, d_gu, d_down = joint(
        sums.state, out_other, out_own, d_gu, d_down
    )
    g_ff = sums.result()

    def to_owners(value):
        return exchange(value.astype(bf16).reshape(DEVICES, shard, -1))

    def owned(got):
        got = got.astype(f32).reshape((2, 2, 8) + got.shape[1:])
        return (got[:, 0] + got[:, 1]).reshape((16,) + got.shape[3:])

    def from_places(value):
        return jnp.moveaxis(value, 0, 1).reshape(shard, -1)

    g_hidden = (
        g_out_bf.astype(f32)
        + inv_ff * g_ff
        - hidden * inv_ff**3 * jnp.mean(hidden * g_ff, axis=-1, keepdims=True)
    )
    g_branch = gathered(gather_start(g_hidden.astype(bf16)), width, info)
    g_branch, d_gu, out_own, out_other = joint(g_branch, d_gu, out_own, out_other)
    d_gu_got = to_owners(d_gu)

    g_branch_own = g_branch[:half_rows]
    inner_normed = (gained.astype(f32) * inv_mix_rows).astype(bf16)
    g_inner = mm(g_branch, w_out)
    g_att = mm(g_branch_own, w_att).astype(bf16)
    dots = jnp.sum(inner_normed.astype(f32) * g_inner, axis=-1).reshape(16, rows)
    dots = group_sum(reordered(dots))
    d_out = mm_tn(g_branch, inner_normed).astype(bf16)
    d_att = mm_tn(g_branch_own, attended).astype(bf16)
    out_part = Scatter(out_own, out_other).result()

    d_q, d_k, d_v = run_attend_backward(
        info, queries, keys, values, attended_f, logs, g_att
    )
    scales = jnp.stack([inv_mix, dots / inner_width], axis=-1).reshape(length, 2)
    scales = jnp.concatenate([scales, jnp.zeros((length, 6), f32)], axis=1)
    scales, out_part = joint(scales, out_part)
    g_all, acc_x, acc_m, acc_v, acc_s = run_mix_backward(
        info,
        raw_own,
        raw_s,
        *tables,
        lanes,
        y,
        g_inner,
        scales,
        states,
        d_q,
        d_k,
        d_v,
    )
    output = swap_sequences((hidden + out_part).astype(bf16))[None]
    conv_grads = jnp.concatenate([acc_x[: KC + 1], acc_m[: KC + 1]], axis=1)
    g_bias = lax.dynamic_slice_in_dim(acc_s[0], place * heads, heads, 0)
    g_skip = jnp.sum(acc_v[1].reshape(heads, MP), axis=1)
    small_grads = jnp.concatenate([conv_grads.reshape(-1), acc_v[0], g_bias, g_skip])
    small_grads = jnp.pad(small_grads, (0, -small_grads.shape[0] % shard)).astype(bf16)
    small_grads = jnp.broadcast_to(
        small_grads.reshape(1, shard, -1), (DEVICES, shard, small_grads.shape[0] // shard)
    ).reshape(width, -1)
    d_mix = jnp.concatenate([d_down, d_out, d_att, small_grads], axis=1)
    d_mix, g_all, d_gu_got = joint(d_mix, g_all, d_gu_got)
    d_mix_got = to_owners(d_mix)
    g_in_other = mm_nt(g_all[half_rows:], w_all).astype(bf16)
    g_in_own = mm_nt(g_all[:half_rows], w_all).astype(bf16)
    g_late = g_all
    own_width = 2 * mine + HD
    d_own = mm_tn(normed, g_late[:, :own_width]).astype(bf16)
    d_own, d_mix_got = joint(d_own, d_mix_got)
    d_own_got = to_owners(d_own)
    d_shared = mm_tn(normed, g_late[:, own_width:]).astype(bf16)
    def only_mine(value):
        empty = jnp.zeros((width, KVH * HD), bf16)
        return lax.dynamic_update_slice_in_dim(empty, value, zl * HD, 1)

    d_shared = jnp.concatenate(
        [
            d_shared[:, : 2 * NS],
            only_mine(d_shared[:, 2 * NS : 2 * NS + HD]),
            only_mine(d_shared[:, 2 * NS + HD : 2 * NS + 2 * HD]),
            d_shared[:, 2 * NS + 2 * HD :],
        ],
        axis=1,
    )
    moves = []
    for block in range(DEVICES):

        def goal(ref, block=block):
            position = ref[0] ^ (block // 16 * 8 + block % 8)
            row = position * 2 + block // 8 % 2
            return (pl.ds(pl.multiple_of(row * shard, shard), shard), slice(None))

        moves.append((0, fixed(block * shard, shard, 0, d_shared.shape[1]), goal))
    d_shared = assemble([d_shared], moves, d_shared.shape, info)
    sums = Scatter(
        jnp.concatenate([g_in_own, d_shared[:half_rows]], axis=1),
        jnp.concatenate([g_in_other, d_shared[half_rows:]], axis=1),
    ).result()
    sums, d_mix_got = joint(sums, d_mix_got)
    g_in = sums[:, :width]
    d_cube = sums[:, width:].reshape(2, shard, -1)
    d_shared_own = lax.dynamic_index_in_dim(d_cube, seq_half, 0, keepdims=False) + flip(
        lax.dynamic_index_in_dim(d_cube, 1 - seq_half, 0, keepdims=False).astype(bf16), BIT_ZH
    ).astype(f32)
    d_gu_own = owned(d_gu_got)
    d_gate_up = jnp.concatenate(
        [from_places(d_gu_own[..., :ffc]), from_places(d_gu_own[..., ffc:])], axis=1
    )
    grad_gate_up = d_gate_up * ff_gain.astype(f32)[:, None]
    grad_ff_gain = jnp.sum(d_gate_up * gate_up.astype(f32), axis=1)
    d_mix_own = owned(d_mix_got)
    grad_down = jnp.moveaxis(d_mix_own[..., :ffc], 1, 2).reshape(FF, shard)
    grad_inner_out = jnp.moveaxis(d_mix_own[..., ffc : ffc + mine], 1, 2).reshape(
        inner_width, shard
    )
    at = ffc + mine + HD
    d_att = d_mix_own[..., ffc + mine : at].reshape(2, 8, shard, HD)
    grad_attn = jnp.moveaxis(d_att[0] + d_att[1], 1, 2).reshape(QH * HD, shard)
    d_own = owned(d_own_got)
    d_z = from_places(d_own[..., :mine])
    d_x = from_places(d_own[..., mine : 2 * mine])
    d_qw = d_own[..., 2 * mine :].reshape(2, 8, shard, HD)
    d_qw = from_places(d_qw[0] + d_qw[1])

    got = d_mix_own[..., at:].reshape(16, -1)
    at = 0
    taps_width = mine + 2 * NS
    conv_grads = got[:, at : at + (KC + 1) * taps_width].reshape(16, KC + 1, taps_width)
    at += (KC + 1) * taps_width
    conv_full = jnp.concatenate(
        [
            jnp.moveaxis(conv_grads[..., :mine], 0, 1).reshape(KC + 1, inner_width),
            jnp.sum(conv_grads[..., mine:], axis=0),
        ],
        axis=1,
    )
    device = core * 16 + chip
    conv_own = lax.dynamic_slice_in_dim(conv_full, device * conv_shard, conv_shard, 1)
    gain_full = got[:, at : at + mine].reshape(inner_width)
    gain_shard = inner_gain.shape[0]
    grad_inner_gain = lax.dynamic_slice_in_dim(gain_full, device * gain_shard, gain_shard, 0)
    at += mine
    local = lax.dynamic_slice_in_dim(got[:, at : at + 2 * heads], core * 8, 8, 0)
    grad_step_bias = local[:, :heads].reshape(-1)
    grad_skip_gain = local[:, heads:].reshape(-1)

    at = 2 * NS + 2 * kv_width
    d_qkv = jnp.concatenate([d_qw, d_shared_own[:, 2 * NS : at]], axis=1)
    d_inner = jnp.concatenate(
        [d_z, d_x, d_shared_own[:, : 2 * NS], d_shared_own[:, at : at + MH]], axis=1
    )
    grad_norm_gain = jnp.sum(d_qkv * qkv_proj.astype(f32), axis=1) + jnp.sum(
        d_inner * inner_proj.astype(f32), axis=1
    )
    g_x_rows = (
        inv_in * g_in - x_rows * inv_in**3 * jnp.mean(x_rows * g_in, axis=-1, keepdims=True)
    )
    grad_tokens = swap_sequences((g_hidden + g_x_rows).astype(bf16)).astype(f32)[None]
    return (
        output,
        grad_tokens,
        grad_norm_gain,
        d_qkv * gain_rows,
        grad_attn,
        d_inner * gain_rows,
        conv_own[:KC],
        conv_own[KC],
        grad_step_bias,
        grad_skip_gain,
        grad_inner_gain,
        grad_inner_out,
        grad_ff_gain,
        grad_gate_up,
        grad_down,
    )


def solution(mesh):
    return jax.shard_map(
        cube_body if mesh.shape["seq"] == 16 else body,
        mesh=mesh,
        in_specs=(
            P("head", "seq", None),
            P(None, "seq", "head"),
            P(("head", "seq")),
            P(("head", "seq"), None),
            P(None, ("head", "seq")),
            P(("head", "seq"), None),
            P(None, ("head", "seq")),
            P(("head", "seq")),
            P("head"),
            P("head"),
            P(("head", "seq")),
            P(None, ("head", "seq")),
            P(("head", "seq")),
            P(("head", "seq"), None),
            P(None, ("head", "seq")),
            P("head", "seq", None),
        ),
        out_specs=(
            P("head", "seq", None),
            P("head", "seq", None),
            P(("head", "seq")),
            P(("head", "seq"), None),
            P(None, ("head", "seq")),
            P(("head", "seq"), None),
            P(None, ("head", "seq")),
            P(("head", "seq")),
            P("head"),
            P("head"),
            P(("head", "seq")),
            P(None, ("head", "seq")),
            P(("head", "seq")),
            P(("head", "seq"), None),
            P(None, ("head", "seq")),
        ),
        check_vma=False,
    )
```

```python
import functools
import math

import jax
import jax.numpy as jnp
from jax import lax
from jax.experimental import pallas as pl
from jax.experimental.pallas import tpu as pltpu
from jax.sharding import PartitionSpec as P

FF = 4096
QH = 8
KVH = 2
HD = 128
MH = 48
MP = 64
NS = 256
KC = 4


EPSILON = 1e-05
ROPE_BASE = 100000000000.0
NEGATIVE = -1e30
HIGHEST = lax.Precision.HIGHEST


def passed_along(value, axis, steps):
    count = lax.axis_size(axis)
    initial, last = (max(0, -steps), min(count, count - steps))
    return lax.ppermute(value, axis, [(source, source + steps) for source in range(initial, last)])


def carried_in(array, axis, combine, identity):
    count, mine = (lax.axis_size(axis), lax.axis_index(axis))
    everything = jax.tree.map(
        lambda part, kind: lax.all_gather(part.astype(kind), axis),
        array,
        (jnp.bfloat16, jnp.bfloat16),
    )
    start = jax.tree.map(
        lambda part, zero: jnp.broadcast_to(jnp.asarray(zero, part.dtype), part.shape),
        array,
        identity,
    )

    def carried_hop(k, before):
        reached = k < mine
        new = combine(
            before, jax.tree.map(lambda part, own: part[k].astype(own.dtype), everything, array)
        )
        return jax.tree.map(lambda a, b: jnp.where(reached, a, b), new, before)

    return lax.fori_loop(0, count, carried_hop, start)


def entering(array, axis, combine, identity):
    count, mine = (lax.axis_size(axis), lax.axis_index(axis))
    everything = jax.tree.map(
        lambda part, kind: lax.all_gather(part.astype(kind), axis),
        array,
        jax.tree.map(lambda a: jnp.bfloat16 if a.dtype == jnp.float32 else a.dtype, array),
    )
    start = jax.tree.map(
        lambda part, zero: jnp.broadcast_to(jnp.asarray(zero, part.dtype), part.shape),
        array,
        identity,
    )

    def entering_hop(k, before):
        at = count - 1 - k
        reached = at > mine
        new = combine(
            before, jax.tree.map(lambda part, own: part[at].astype(own.dtype), everything, array)
        )
        return jax.tree.map(lambda a, b: jnp.where(reached, a, b), new, before)

    return lax.fori_loop(0, count, entering_hop, start)


def shortened(array):
    return jax.tree.map(lambda a: a.astype(jnp.bfloat16) if a.dtype == jnp.float32 else a, array)


def rounded(value):
    return lax.optimization_barrier(value.astype(jnp.bfloat16)).astype(jnp.float32)


def rms_norm(value, gain):
    return value * lax.rsqrt(jnp.mean(value * value, axis=-1, keepdims=True) + EPSILON) * gain


def rotary(value, positions):
    halfway = value.shape[-1] // 2
    frequency = ROPE_BASE ** (-2.0 * jnp.arange(halfway, dtype=jnp.float32) / value.shape[-1])
    angle = positions[:, None] * frequency[None, :]
    cosine = jnp.cos(angle)[:, None, :]
    sine_part = jnp.sin(angle)[:, None, :]
    first = value[..., :halfway]
    second = value[..., halfway:]
    return jnp.concatenate(
        [first * cosine - second * sine_part, second * cosine + first * sine_part], axis=-1
    )


def block_decay(log_decay):
    return jnp.exp(jnp.cumsum(log_decay, axis=1)[:, -1, :])


def inner_output(inner_x, step_in, state_maps, step_bias, skip_gain, state_in, log_decay):
    nstate = state_maps.shape[-1] // 2
    input_map = state_maps[..., :nstate]
    output_map = state_maps[..., nstate:]
    step_size = jax.nn.softplus(step_in + step_bias)
    cumulative = jnp.cumsum(log_decay, axis=1)
    scaled_x = inner_x * step_size[..., None]
    intersection = jnp.einsum("stn,sun->stu", output_map, input_map, precision=HIGHEST)
    length_blk = log_decay.shape[1]
    lower_mask = jnp.arange(length_blk)[:, None] >= jnp.arange(length_blk)[None, :]
    spread = cumulative[:, :, None, :] - cumulative[:, None, :, :]
    mixing = (
        jnp.where(lower_mask[None, :, :, None], jnp.exp(jnp.minimum(spread, 0.0)), 0.0)
        * intersection[..., None]
    )
    within = jnp.einsum("stuh,suhp->sthp", mixing, scaled_x, precision=HIGHEST)
    carried = (
        jnp.einsum("shpn,stn->sthp", state_in, output_map, precision=HIGHEST)
        * jnp.exp(cumulative)[..., None]
    )
    return within + carried + skip_gain[:, None] * inner_x


def inner_state(inner_x, step_in, state_maps, step_bias, log_decay):
    nstate = state_maps.shape[-1] // 2
    input_map = state_maps[..., :nstate]
    step_size = jax.nn.softplus(step_in + step_bias)
    cumulative = jnp.cumsum(log_decay, axis=1)
    tail_weight = jnp.exp(cumulative[:, -1:, :] - cumulative) * step_size
    return jnp.einsum("suh,suhp,sun->shpn", tail_weight, inner_x, input_map, precision=HIGHEST)


def over_blocks(function, carried, arrays, offset, limit):
    row_count = arrays[0].shape[1]
    step_rows = math.gcd(row_count, 1024)

    def advance(number, running):
        pieces = tuple(
            (
                lax.dynamic_slice_in_dim(member, number * step_rows, step_rows, 1)
                for member in arrays
            )
        )
        return function(running, pieces, offset + number * step_rows)

    upper = (limit + step_rows - 1) // step_rows
    return lax.fori_loop(0, upper, advance, carried)


def attend_block(carried, pair, offset, queries, query_pos, score_scale):
    row_top, row_total, accumulated = carried
    key_blk, value_blk = pair
    scores = (
        jnp.einsum("sqkgd,sjkd->sqkgj", queries, key_blk, preferred_element_type=jnp.float32)
        * score_scale
    )
    key_pos = offset + jnp.arange(key_blk.shape[1])
    allowed = (key_pos[None, :] <= query_pos[:, None])[None, :, None, None, :]
    masked = jnp.where(allowed, scores, NEGATIVE)
    new_top = jnp.maximum(row_top, jnp.max(masked, axis=-1))
    factor = jnp.exp(row_top - new_top)
    weights = jnp.where(allowed, jnp.exp(masked - new_top[..., None]), 0.0)
    row_total = factor * row_total + jnp.sum(weights, axis=-1)
    accumulated = factor[..., None] * accumulated + jnp.einsum(
        "sqkgj,sjkd->sqkgd",
        weights.astype(jnp.bfloat16),
        value_blk,
        preferred_element_type=jnp.float32,
    )
    return (new_top, row_total, accumulated)


def score_grads(
    queries, grad_heads, log_total, row_delta, key_blk, value_blk, offset, query_pos, score_scale
):
    scores = (
        jnp.einsum("sqkgd,sjkd->sqkgj", queries, key_blk, preferred_element_type=jnp.float32)
        * score_scale
    )
    key_pos = offset + jnp.arange(key_blk.shape[1])
    allowed = (key_pos[None, :] <= query_pos[:, None])[None, :, None, None, :]
    prob_rows = jnp.where(allowed, jnp.exp(scores - log_total[..., None]), 0.0)
    grad_probs = jnp.einsum(
        "sqkgd,sjkd->sqkgj", grad_heads, value_blk, preferred_element_type=jnp.float32
    )
    grad_scores = (prob_rows * (grad_probs - row_delta[..., None])).astype(jnp.bfloat16)
    return (prob_rows.astype(jnp.bfloat16), grad_scores)


def body(
    tokens,
    log_decay,
    norm_gain,
    qkv_proj,
    attn_proj,
    inner_proj,
    conv_weight,
    conv_bias,
    step_bias,
    skip_gain,
    inner_gain,
    inner_out,
    ff_gain,
    gate_up,
    down_proj,
    cotangent,
):
    head_count = lax.axis_size("head")
    seq_index = lax.axis_index("seq")
    (
        gain_in,
        qkv_full,
        attn_full,
        inner_full,
        conv_full,
        conv_bias_full,
        inner_gain_full,
        out_full,
        ff_gain_full,
        gate_up_full,
        down_full,
    ) = (
        lax.all_gather(norm_gain, ("head", "seq"), axis=0, tiled=True),
        lax.all_gather(qkv_proj, ("head", "seq"), axis=0, tiled=True),
        lax.all_gather(attn_proj, ("head", "seq"), axis=1, tiled=True),
        lax.all_gather(inner_proj, ("head", "seq"), axis=0, tiled=True),
        lax.all_gather(conv_weight, ("head", "seq"), axis=1, tiled=True),
        lax.all_gather(conv_bias, ("head", "seq"), axis=0, tiled=True),
        lax.all_gather(inner_gain, ("head", "seq"), axis=0, tiled=True),
        lax.all_gather(inner_out, ("head", "seq"), axis=1, tiled=True),
        lax.all_gather(ff_gain, ("head", "seq"), axis=0, tiled=True),
        lax.all_gather(gate_up, ("head", "seq"), axis=0, tiled=True),
        lax.all_gather(down_proj, ("head", "seq"), axis=1, tiled=True),
    )
    local_seqs, block_rows, model_width = tokens.shape
    token_rows = local_seqs * block_rows
    inner_width = MH * MP
    conv_width = inner_width + 2 * NS
    groups = QH // KVH
    kv_local = KVH // head_count
    inner_local = MH // head_count
    all_seqs = local_seqs * head_count
    score_scale = HD ** (-0.5)
    key_limit = (seq_index + 1) * block_rows
    x_rows = tokens.astype(jnp.float32).reshape(token_rows, model_width)
    normed_f, norm_back = jax.vjp(rms_norm, x_rows, gain_in.astype(jnp.float32))
    normed = normed_f.astype(jnp.bfloat16)
    qkv_rows = jnp.dot(normed, qkv_full, preferred_element_type=jnp.float32).reshape(
        local_seqs, block_rows, -1
    )
    positions = (seq_index * block_rows + jnp.arange(block_rows)).astype(jnp.float32)
    query_send = rotary(
        qkv_rows[..., : QH * HD].reshape(local_seqs, block_rows, QH, HD), positions
    ).astype(jnp.bfloat16)
    key_send = rotary(
        qkv_rows[..., QH * HD : (QH + KVH) * HD].reshape(local_seqs, block_rows, KVH, HD), positions
    ).astype(jnp.bfloat16)
    value_send = qkv_rows[..., (QH + KVH) * HD :].astype(jnp.bfloat16)
    inner_raw = jnp.dot(normed, inner_full, preferred_element_type=jnp.float32).reshape(
        local_seqs, block_rows, -1
    )
    gate_z = inner_raw[..., :inner_width]
    conv_in = inner_raw[..., inner_width : inner_width + conv_width]
    step_send = inner_raw[..., inner_width + conv_width :].astype(jnp.bfloat16)
    rim_rows = passed_along(
        conv_in[:, block_rows - (KC - 1) :, :].astype(jnp.bfloat16), "seq", 1
    ).astype(jnp.float32)
    padded = jnp.concatenate([rim_rows, conv_in], axis=1)

    def convolve(padded_in, weight_taps, bias_taps):
        conv_sum = bias_taps
        for conv_tap in range(KC):
            conv_sum = (
                conv_sum + weight_taps[conv_tap] * padded_in[:, conv_tap : conv_tap + block_rows, :]
            )
        return jax.nn.silu(conv_sum)

    activated, conv_back = jax.vjp(
        convolve, padded, conv_full.astype(jnp.float32), conv_bias_full.astype(jnp.float32)
    )
    activated_send = activated.astype(jnp.bfloat16)

    def split_heads(value):
        return value.reshape(value.shape[:2] + (head_count, -1))

    map_copies = jnp.broadcast_to(
        activated_send[:, :, None, inner_width:], (local_seqs, block_rows, head_count, 2 * NS)
    )
    received = (
        lax.all_to_all(split_heads(query_send), "head", split_axis=2, concat_axis=0, tiled=True),
        lax.all_to_all(split_heads(key_send), "head", split_axis=2, concat_axis=0, tiled=True),
        lax.all_to_all(split_heads(value_send), "head", split_axis=2, concat_axis=0, tiled=True),
        lax.all_to_all(
            split_heads(activated_send[..., :inner_width]),
            "head",
            split_axis=2,
            concat_axis=0,
            tiled=True,
        ),
        lax.all_to_all(split_heads(step_send), "head", split_axis=2, concat_axis=0, tiled=True),
        lax.all_to_all(map_copies, "head", split_axis=2, concat_axis=0, tiled=True),
    )
    queries = received[0].reshape(all_seqs, block_rows, kv_local, groups, HD)
    key_heads = received[1]
    value_heads = received[2]
    inner_x = received[3].reshape(all_seqs, block_rows, inner_local, MP).astype(jnp.float32)
    step_in = received[4].reshape(all_seqs, block_rows, inner_local).astype(jnp.float32)
    state_maps = received[5].reshape(all_seqs, block_rows, 2 * NS).astype(jnp.float32)
    query_pos = seq_index * block_rows + jnp.arange(block_rows)
    key_all, value_all = (
        lax.all_gather(key_heads, "seq", axis=1, tiled=True),
        lax.all_gather(value_heads, "seq", axis=1, tiled=True),
    )

    def attend_step(carried, pair, offset):
        return attend_block(carried, pair, offset, queries, query_pos, score_scale)

    stat_shape = (all_seqs, block_rows, kv_local, groups)
    start_stats = (
        jnp.full(stat_shape, NEGATIVE, jnp.float32),
        jnp.zeros(stat_shape, jnp.float32),
        jnp.zeros(stat_shape + (HD,), jnp.float32),
    )
    row_top, row_total, accumulated = over_blocks(
        attend_step, start_stats, (key_all, value_all), 0, key_limit
    )
    attended_f = accumulated / row_total[..., None]
    log_total = row_top + jnp.log(row_total)

    def state_part(piece_x, piece_step, piece_maps, piece_bias):
        return inner_state(piece_x, piece_step, piece_maps, piece_bias, log_decay)

    def output_part(piece_x, piece_step, piece_maps, piece_bias, piece_skip, piece_state):
        return inner_output(
            piece_x, piece_step, piece_maps, piece_bias, piece_skip, piece_state, log_decay
        )

    fresh_state, state_back = jax.vjp(state_part, inner_x, step_in, state_maps, step_bias)
    block_fall = block_decay(log_decay)

    def chain_rule(earlier, later):
        return (earlier[0] * later[0], later[1] + later[0][:, :, None, None] * earlier[1])

    neutral = (jnp.ones_like(block_fall), jnp.zeros_like(fresh_state))
    state_in = carried_in((block_fall, fresh_state), "seq", chain_rule, neutral)[1]
    inner_y, output_back = jax.vjp(
        output_part, inner_x, step_in, state_maps, step_bias, skip_gain, state_in
    )
    returned = (
        lax.all_to_all(
            attended_f.astype(jnp.bfloat16).reshape(all_seqs, block_rows, 1, -1),
            "head",
            split_axis=0,
            concat_axis=2,
            tiled=True,
        ),
        lax.all_to_all(
            inner_y.astype(jnp.bfloat16).reshape(all_seqs, block_rows, 1, -1),
            "head",
            split_axis=0,
            concat_axis=2,
            tiled=True,
        ),
    )
    attended = returned[0].reshape(token_rows, QH * HD)
    inner_back_y = returned[1].reshape(local_seqs, block_rows, inner_width).astype(jnp.float32)

    def gated_norm(y_part, gate_part, gain_part):
        return rms_norm(y_part * jax.nn.silu(gate_part), gain_part)

    inner_normed_f, gated_back = jax.vjp(
        gated_norm, inner_back_y, gate_z, inner_gain_full.astype(jnp.float32)
    )
    inner_normed = inner_normed_f.astype(jnp.bfloat16).reshape(token_rows, inner_width)
    hidden = (
        x_rows
        + jnp.dot(attended, attn_full, preferred_element_type=jnp.float32)
        + jnp.dot(inner_normed, out_full, preferred_element_type=jnp.float32)
    )
    normed_ff_f, ff_back = jax.vjp(rms_norm, hidden, ff_gain_full.astype(jnp.float32))
    normed_ff = normed_ff_f.astype(jnp.bfloat16)
    gate_vals = jnp.dot(normed_ff, gate_up_full, preferred_element_type=jnp.float32)

    def swiglu(values_in):
        return jax.nn.silu(values_in[:, :FF]) * values_in[:, FF:]

    mixed_f, swiglu_back = jax.vjp(swiglu, gate_vals)
    mixed_rows = mixed_f.astype(jnp.bfloat16)
    output = (
        (hidden + jnp.dot(mixed_rows, down_full, preferred_element_type=jnp.float32))
        .astype(jnp.bfloat16)
        .reshape(tokens.shape)
    )
    grad_out = cotangent.reshape(token_rows, model_width)
    grad_down = jnp.einsum("rf,rd->fd", mixed_rows, grad_out, preferred_element_type=jnp.float32)
    grad_gate_vals = swiglu_back(
        jnp.einsum("rd,fd->rf", grad_out, down_full, preferred_element_type=jnp.float32)
    )[0].astype(jnp.bfloat16)
    grad_gate_up = jnp.einsum(
        "rd,re->de", normed_ff, grad_gate_vals, preferred_element_type=jnp.float32
    )
    grad_hidden_norm, grad_ff_gain = ff_back(
        jnp.einsum("re,de->rd", grad_gate_vals, gate_up_full, preferred_element_type=jnp.float32)
    )
    grad_hidden = grad_out.astype(jnp.float32) + grad_hidden_norm
    grad_branch = grad_hidden.astype(jnp.bfloat16)
    grad_attn = jnp.einsum("rc,rd->cd", attended, grad_branch, preferred_element_type=jnp.float32)
    grad_inner_out = jnp.einsum(
        "rc,rd->cd", inner_normed, grad_branch, preferred_element_type=jnp.float32
    )
    grad_attended = jnp.einsum(
        "rd,cd->rc", grad_branch, attn_full, preferred_element_type=jnp.float32
    ).astype(jnp.bfloat16)
    grad_y, grad_gate_z, grad_inner_gain = gated_back(
        jnp.einsum("rd,cd->rc", grad_branch, out_full, preferred_element_type=jnp.float32).reshape(
            local_seqs, block_rows, inner_width
        )
    )
    sent_grads = (
        lax.all_to_all(
            split_heads(grad_attended.reshape(local_seqs, block_rows, QH * HD)),
            "head",
            split_axis=2,
            concat_axis=0,
            tiled=True,
        ),
        lax.all_to_all(
            split_heads(grad_y.astype(jnp.bfloat16)),
            "head",
            split_axis=2,
            concat_axis=0,
            tiled=True,
        ),
    )
    grad_heads = sent_grads[0].reshape(all_seqs, block_rows, kv_local, groups, HD)
    grad_inner_y = sent_grads[1].reshape(all_seqs, block_rows, inner_local, MP).astype(jnp.float32)
    row_delta = jnp.sum(grad_heads.astype(jnp.float32) * attended_f, axis=-1)

    def query_step(carried, pair, offset):
        prob_rows, grad_scores = score_grads(
            queries,
            grad_heads,
            log_total,
            row_delta,
            pair[0],
            pair[1],
            offset,
            query_pos,
            score_scale,
        )
        return carried + jnp.einsum(
            "sqkgj,sjkd->sqkgd", grad_scores, pair[0], preferred_element_type=jnp.float32
        )

    grad_queries = (
        over_blocks(query_step, jnp.zeros_like(attended_f), (key_all, value_all), 0, key_limit)
        * score_scale
    )
    count = block_rows * lax.axis_size("seq")
    step_rows = math.gcd(count, 1024)
    term_shape = (step_rows, all_seqs, kv_local, 2 * HD)

    def compute_block(offset):
        key_blk = lax.dynamic_slice_in_dim(key_all, offset, step_rows, 1)
        value_blk = lax.dynamic_slice_in_dim(value_all, offset, step_rows, 1)
        prob_rows, grad_scores = score_grads(
            queries,
            grad_heads,
            log_total,
            row_delta,
            key_blk,
            value_blk,
            offset,
            query_pos,
            score_scale,
        )
        grad_keys = (
            jnp.einsum(
                "sqkgj,sqkgd->jskd", grad_scores, queries, preferred_element_type=jnp.float32
            )
            * score_scale
        )
        grad_values = jnp.einsum(
            "sqkgj,sqkgd->jskd", prob_rows, grad_heads, preferred_element_type=jnp.float32
        )
        return jnp.concatenate([grad_keys, grad_values], axis=-1)

    def one_block(offset):
        return lax.cond(
            offset < key_limit,
            compute_block,
            lambda unused: jnp.zeros(term_shape, jnp.float32),
            offset,
        )

    block_terms = lax.map(
        lambda number: one_block(number * step_rows), jnp.arange(count // step_rows)
    )
    key_grads = lax.psum_scatter(
        block_terms.reshape((count,) + block_terms.shape[2:]),
        "seq",
        scatter_dimension=0,
        tiled=True,
    )
    grad_key_heads = jnp.moveaxis(key_grads[..., :HD], 0, 1)
    grad_value_heads = jnp.moveaxis(key_grads[..., HD:], 0, 1)
    grad_x_a, grad_step_a, grad_maps_a, grad_bias_a, grad_skip, grad_state = output_back(
        grad_inner_y
    )
    grad_carry = entering((block_fall, grad_state), "seq", chain_rule, neutral)[1]
    grad_x_b, grad_step_b, grad_maps_b, grad_bias_b = state_back(grad_carry)
    grad_step_bias, grad_skip_gain = lax.psum((grad_bias_a + grad_bias_b, grad_skip), "seq")
    returned_grads = (
        lax.all_to_all(
            grad_queries.reshape(all_seqs, block_rows, 1, -1).astype(jnp.bfloat16),
            "head",
            split_axis=0,
            concat_axis=2,
            tiled=True,
        ).astype(jnp.float32),
        lax.all_to_all(
            grad_key_heads.astype(jnp.bfloat16), "head", split_axis=0, concat_axis=2, tiled=True
        ).astype(grad_key_heads.dtype),
        lax.all_to_all(
            grad_value_heads.astype(jnp.bfloat16), "head", split_axis=0, concat_axis=2, tiled=True
        ).astype(grad_value_heads.dtype),
        lax.all_to_all(
            (grad_x_a + grad_x_b).reshape(all_seqs, block_rows, 1, -1).astype(jnp.bfloat16),
            "head",
            split_axis=0,
            concat_axis=2,
            tiled=True,
        ).astype(jnp.float32),
        lax.all_to_all(
            (grad_step_a + grad_step_b).reshape(all_seqs, block_rows, 1, -1).astype(jnp.bfloat16),
            "head",
            split_axis=0,
            concat_axis=2,
            tiled=True,
        ).astype(jnp.float32),
        lax.all_to_all(
            (grad_maps_a + grad_maps_b)[:, :, None, :].astype(jnp.bfloat16),
            "head",
            split_axis=0,
            concat_axis=2,
            tiled=True,
        ).astype(jnp.float32),
    )
    grad_q = rounded(returned_grads[0].reshape(local_seqs, block_rows, QH, HD))
    grad_k = rounded(returned_grads[1])
    grad_v = returned_grads[2].reshape(token_rows, KVH * HD)
    grad_qkv_rows = jnp.concatenate(
        [
            rotary(grad_q, -positions).reshape(token_rows, -1),
            rotary(grad_k, -positions).reshape(token_rows, -1),
            grad_v,
        ],
        axis=-1,
    ).astype(jnp.bfloat16)
    grad_x_in = rounded(returned_grads[3].reshape(local_seqs, block_rows, inner_width))
    grad_step = rounded(returned_grads[4].reshape(token_rows, MH))
    grad_maps = rounded(jnp.sum(returned_grads[5], axis=2))
    grad_padded, grad_conv_weight, grad_conv_bias = conv_back(
        jnp.concatenate([grad_x_in, grad_maps], axis=-1)
    )
    rim_grad = passed_along(shortened(grad_padded[:, : KC - 1, :]), "seq", -1)
    grad_conv_in = grad_padded[:, KC - 1 :, :].at[:, block_rows - (KC - 1) :, :].add(rim_grad)
    grad_inner_rows = jnp.concatenate(
        [grad_gate_z.reshape(token_rows, -1), grad_conv_in.reshape(token_rows, -1), grad_step],
        axis=-1,
    ).astype(jnp.bfloat16)
    grad_qkv_weight = jnp.einsum(
        "rd,re->de", normed, grad_qkv_rows, preferred_element_type=jnp.float32
    )
    grad_inner_weight = jnp.einsum(
        "rd,re->de", normed, grad_inner_rows, preferred_element_type=jnp.float32
    )
    grad_normed = jnp.einsum(
        "re,de->rd", grad_qkv_rows, qkv_full, preferred_element_type=jnp.float32
    ) + jnp.einsum("re,de->rd", grad_inner_rows, inner_full, preferred_element_type=jnp.float32)
    grad_x_norm, grad_norm_gain = norm_back(grad_normed)
    grad_tokens = (grad_hidden + grad_x_norm).reshape(tokens.shape)
    weight_grads = (
        grad_norm_gain,
        grad_qkv_weight,
        grad_attn,
        grad_inner_weight,
        grad_conv_weight,
        grad_conv_bias,
        grad_inner_gain,
        grad_inner_out,
        grad_ff_gain,
        grad_gate_up,
        grad_down,
    )
    shares = (
        lax.psum_scatter(weight_grads[0], ("head", "seq"), scatter_dimension=0, tiled=True),
        lax.psum_scatter(weight_grads[1], ("head", "seq"), scatter_dimension=0, tiled=True),
        lax.psum_scatter(weight_grads[2], ("head", "seq"), scatter_dimension=1, tiled=True),
        lax.psum_scatter(weight_grads[3], ("head", "seq"), scatter_dimension=0, tiled=True),
        lax.psum_scatter(weight_grads[4], ("head", "seq"), scatter_dimension=1, tiled=True),
        lax.psum_scatter(weight_grads[5], ("head", "seq"), scatter_dimension=0, tiled=True),
        lax.psum_scatter(weight_grads[6], ("head", "seq"), scatter_dimension=0, tiled=True),
        lax.psum_scatter(weight_grads[7], ("head", "seq"), scatter_dimension=1, tiled=True),
        lax.psum_scatter(weight_grads[8], ("head", "seq"), scatter_dimension=0, tiled=True),
        lax.psum_scatter(weight_grads[9], ("head", "seq"), scatter_dimension=0, tiled=True),
        lax.psum_scatter(weight_grads[10], ("head", "seq"), scatter_dimension=1, tiled=True),
    )
    return (
        output,
        grad_tokens,
        shares[0],
        shares[1],
        shares[2],
        shares[3],
        shares[4],
        shares[5],
        grad_step_bias,
        grad_skip_gain,
        shares[6],
        shares[7],
        shares[8],
        shares[9],
        shares[10],
    )


BLOCK = 128
BIT_C, BIT_ZH, BIT_ZL, BIT_Y, BIT_X = 16, 8, 4, 2, 1
DEVICES = 32
BOTH = ("head", "half", "cube")
GROUP = ("head", "cube")
CUBE_ORDERS = ((0, 1, 2), (1, 2, 0), (2, 0, 1))
CUBE_BITS = (BIT_ZL, BIT_Y, BIT_X)
bf16 = jnp.bfloat16
f32 = jnp.float32


def flip(value, mask):
    return lax.ppermute(value, BOTH, [(i, i ^ mask) for i in range(DEVICES)])


def swap_sequences(value):
    pairs = []
    for i in range(DEVICES):
        core, half = (i // BIT_C) % 2, (i // BIT_ZH) % 2
        if core != half:
            pairs.append((i, i ^ (BIT_C + BIT_ZH)))
    stays = lax.axis_index("head") == lax.axis_index("half")
    return jnp.where(stays, value, lax.ppermute(value, BOTH, pairs))


def joint(*values):
    return lax.optimization_barrier(values)


def column_parts(width):
    lanes = width // 128
    first = -(-lanes // 3)
    second = -(-(lanes - first) // 2)
    edges = (0, first * 128, (first + second) * 128, width)
    return [(edges[i], edges[i + 1]) for i in range(3)]


def assemble(pieces, outputs, info):
    count, made = len(pieces), len(outputs)
    moves = [(to, *move) for to, (_, _, out_moves) in enumerate(outputs) for move in out_moves]

    def kernel(info_ref, *refs):
        sems = refs[count + made]
        copies = []
        for at, (to, number, source, target) in enumerate(moves):
            copies.append(
                pltpu.make_async_copy(
                    refs[number].at[source(info_ref)],
                    refs[count + to].at[target(info_ref)],
                    sems.at[at],
                )
            )
        for copy in copies:
            copy.start()
        for copy in copies:
            copy.wait()

    size = sum(math.prod(shape) * jnp.dtype(kind).itemsize for shape, kind, _ in outputs)
    return pl.pallas_call(
        kernel,
        in_specs=[pl.BlockSpec(memory_space=pltpu.SMEM)]
        + [pl.BlockSpec(memory_space=pltpu.HBM)] * count,
        out_specs=[pl.BlockSpec(memory_space=pltpu.VMEM)] * made,
        out_shape=[jax.ShapeDtypeStruct(shape, kind) for shape, kind, _ in outputs],
        scratch_shapes=[pltpu.SemaphoreType.DMA((len(moves),))],
        compiler_params=pltpu.CompilerParams(vmem_limit_bytes=2 * size + 8 * 1024 * 1024),
        cost_estimate=LITTLE,
        name="assemble",
    )(info, *pieces)


def reordered_rows(value, info):
    moves = []
    for block in range(value.shape[0] // BLOCK):

        def goal(ref, block=block):
            row = pl.multiple_of((ref[2] ^ block) * BLOCK, BLOCK)
            return (pl.ds(row, BLOCK), slice(None))

        moves.append((0, fixed(block * BLOCK, BLOCK, 0, value.shape[1]), goal))
    return assemble([value], [(value.shape, value.dtype, moves)], info)[0]


def fixed(row, rows, column, columns):
    return lambda info: (pl.ds(row, rows), pl.ds(column, columns))


class Gather:
    def __init__(self, value, edges, info):
        self.rows, self.width, self.step = value.shape[0], value.shape[1], 0
        self.edges, self.info = edges, info
        self.joined = None
        self.state = ([value[:, a:b] for a, b in edges], None)

    def hop(self):
        parts, received = self.state
        if received is not None:
            parts = self.stacked(parts, received)
        sent = [
            flip(part, CUBE_BITS[order[self.step]]) for part, order in zip(parts, CUBE_ORDERS)
        ]
        self.state = (parts, sent)
        self.step += 1

    def stacked(self, parts, received):
        rows = parts[0].shape[0]
        outputs, side = [], []
        for i, (a, b) in enumerate(self.edges):
            own, got = fixed(0, rows, 0, b - a), fixed(rows, rows, 0, b - a)
            outputs.append(((2 * rows, b - a), bf16, [(i, own, own), (3 + i, own, got)]))
            side.append((i, own, fixed(0, rows, a, b - a)))
            side.append((3 + i, own, fixed(rows, rows, a, b - a)))
        if self.step == 2:
            outputs.append(((2 * rows, self.width), bf16, side))
        result = assemble(parts + received, outputs, self.info)
        if self.step == 2:
            self.joined = result[3]
        return list(result[:3])

    def pieces(self):
        while self.step < 3:
            self.hop()
        near, far = self.state
        side = [(i, fixed(0, 4 * self.rows, 0, b - a), fixed(0, 4 * self.rows, a, b - a)) for i, (a, b) in enumerate(self.edges)]
        (far_joined,) = assemble(
            far, [((4 * self.rows, self.width), bf16, side)], self.info
        )
        crossed = [flip(self.joined, BIT_C), flip(far_joined, BIT_C)]
        return near + far + crossed


def piece_blocks(part, far):
    axes = [CUBE_BITS[axis] for axis in CUBE_ORDERS[part]]
    return [
        (block, (block % 2) * axes[0] + (block // 2) * axes[1] + far * axes[2], 1)
        for block in range(4)
    ]


def gathered(gather, width, info):
    rows = gather.rows
    pieces = gather.pieces()
    moves = []
    for group in range(4):
        half, far = group // 2, group % 2
        for part, (a, b) in enumerate(column_parts(width)):
            number = 3 * group + part if half == 0 else 6 + far
            for first, place, blocks in piece_blocks(part, far):
                moves.append(
                    (
                        number,
                        fixed(first * rows, blocks * rows, a * half, b - a),
                        fixed((half * 8 + place) * rows, blocks * rows, a, b - a),
                    )
                )
    return assemble(pieces, [((16 * rows, width), bf16, moves)], info)[0]


def gather_start(value, info):
    return Gather(value, column_parts(value.shape[1]), info)


class Scatter:
    def __init__(self, own_half, other_half):
        self.total_rows, self.width = own_half.shape
        self.step = 0
        self.state = (own_half, flip(other_half.astype(bf16), BIT_C))

    def pairs(self):
        kept, received = self.state
        if self.step == 0:
            shape = (2, 2, 2, self.total_rows // 8, self.width)
            edges = column_parts(self.width)
            kept = [kept.reshape(shape)[..., a:b] for a, b in edges]
            received = [received.reshape(shape)[..., a:b] for a, b in edges]
        halves = []
        for part, got, order in zip(kept, received, CUBE_ORDERS):
            axis = order[self.step]
            halves.append(
                [
                    (
                        lax.slice_in_dim(part, i, i + 1, axis=axis).astype(f32)
                        + lax.slice_in_dim(got, i, i + 1, axis=axis).astype(f32)
                    ).astype(bf16)
                    for i in (0, 1)
                ]
            )
        return halves

    def hop(self):
        halves = self.pairs()
        sent = [
            flip(far, CUBE_BITS[order[self.step]])
            for (_, far), order in zip(halves, CUBE_ORDERS)
        ]
        self.state = ([near for near, _ in halves], sent)
        self.step += 1

    def then(self, *values):
        near, sent = self.state
        near, values = joint(near, values)
        self.state = (near, sent)
        return values

    def result(self):
        while self.step < 3:
            self.hop()
        rows = self.total_rows // 8
        return jnp.concatenate(
            [
                (near.astype(f32) + got.astype(f32)).reshape(rows, -1)
                for near, got in zip(*self.state)
            ],
            axis=1,
        )


def group_sum(value):
    for masks in ((BIT_C, BIT_X, BIT_C + BIT_X), (BIT_Y, BIT_ZL, BIT_Y + BIT_ZL)):
        first, second, third = [flip(value, mask) for mask in masks]
        value = (value + first) + (second + third)
    return value


def exchange(value):
    return lax.all_to_all(value, GROUP, split_axis=0, concat_axis=0, tiled=True)


def mm(a, b):
    return jnp.dot(a, b, preferred_element_type=f32)


def mm_nt(a, b):
    return lax.dot_general(a, b, (((1,), (1,)), ((), ())), preferred_element_type=f32)


def mm_tn(a, b):
    return lax.dot_general(a, b, (((0,), (0,)), ((), ())), preferred_element_type=f32)


VMEM_ASK = 40 * 1024 * 1024
LITTLE = pl.CostEstimate(flops=1000, bytes_accessed=1000, transcendentals=0)


def params():
    return pltpu.CompilerParams(
        dimension_semantics=("arbitrary",), vmem_limit_bytes=VMEM_ASK
    )


def k_nt(a, b, precision=None):
    return lax.dot_general(
        a, b, (((1,), (1,)), ((), ())), preferred_element_type=f32, precision=precision
    )


def k_tn(a, b):
    return lax.dot_general(a, b, (((0,), (0,)), ((), ())), preferred_element_type=f32)


def k_mm(a, b, precision=None):
    return lax.dot_general(
        a, b, (((1,), (0,)), ((), ())), preferred_element_type=f32, precision=precision
    )


def logistic(value):
    return 1.0 / (1.0 + jnp.exp(-value))


def by_head(columns, lane):
    spread = columns[:, 0:1]
    for head in range(1, HEADS_HERE):
        spread = jnp.where(lane >= head * MP, columns[:, head : head + 1], spread)
    return spread


def shifted_sum(padded, taps, start, step):
    total = None
    for tap in range(KC):
        at = start + step * tap
        term = taps[tap : tap + 1] * padded[at : at + BLOCK]
        total = term if total is None else total + term
    return total


HEADS_HERE = 3
OWN = HEADS_HERE * MP
TAIL = 8
KEYS_AT = 2 * NS


def block_decays(cum_col, cum_row, lane):
    cum = by_head(cum_col, lane)
    last = cum[BLOCK - 1 : BLOCK]
    row = lax.broadcasted_iota(jnp.int32, (BLOCK, BLOCK), 0)
    col = lax.broadcasted_iota(jnp.int32, (BLOCK, BLOCK), 1)
    reach = []
    for head in range(HEADS_HERE):
        spread = cum_col[:, head : head + 1] - cum_row[head : head + 1, :]
        reach.append(jnp.where(row >= col, jnp.exp(jnp.minimum(spread, 0.0)), 0.0))
    return cum, last, reach


def step_lanes(place, lane):
    source = lax.broadcasted_iota(jnp.int32, (128, OWN), 0)
    head = lax.broadcasted_iota(jnp.int32, (128, OWN), 1) // MP
    return jnp.where(source == place * HEADS_HERE + head, 1.0, 0.0)


def mix_forward(
    info,
    own_ref,
    s_ref,
    cos_ref,
    sin_ref,
    cum_col_ref,
    cum_row_ref,
    taps_x_ref,
    taps_m_ref,
    vec_ref,
    y_ref,
    gained_ref,
    square_ref,
    state_ref,
    q_ref,
    k_ref,
    v_ref,
    state,
    last_x,
    last_m,
):
    @pl.when(pl.program_id(0) == 0)
    def _():
        state[...] = jnp.zeros_like(state)
        last_x[...] = jnp.zeros_like(last_x)
        last_m[...] = jnp.zeros_like(last_m)

    lane = lax.broadcasted_iota(jnp.int32, (1, OWN), 1)
    gate = own_ref[:, :OWN]
    x_raw = own_ref[:, OWN : 2 * OWN]
    m_raw = s_ref[:, : 2 * NS]
    cosine, sine = cos_ref[...], sin_ref[...]

    def turned(value):
        return (value * cosine + pltpu.roll(value, HD // 2, 1) * sine).astype(bf16)

    q_ref[...] = turned(own_ref[:, 2 * OWN :])
    k_ref[...] = turned(s_ref[:, KEYS_AT : KEYS_AT + HD])
    v_ref[...] = s_ref[:, KEYS_AT + HD : KEYS_AT + 2 * HD].astype(bf16)

    s_x = shifted_sum(
        jnp.concatenate([last_x[...], x_raw], axis=0), taps_x_ref, TAIL - KC + 1, 1
    ) + taps_x_ref[KC : KC + 1]
    s_m = shifted_sum(
        jnp.concatenate([last_m[...], m_raw], axis=0), taps_m_ref, TAIL - KC + 1, 1
    ) + taps_m_ref[KC : KC + 1]
    last_x[...] = x_raw[BLOCK - TAIL :]
    last_m[...] = m_raw[BLOCK - TAIL :]
    x = (s_x * logistic(s_x)).astype(bf16).astype(f32)
    maps = (s_m * logistic(s_m)).astype(bf16)
    b_map, c_map = maps[:, :NS], maps[:, NS:]

    place = info[0]
    picked = k_mm(s_ref[:, KEYS_AT + 2 * HD :].astype(bf16), step_lanes(place, lane).astype(bf16))
    raised = picked + vec_ref[0:1]
    step = jnp.maximum(raised, 0.0) + jnp.log(1.0 + jnp.exp(-jnp.abs(raised)))
    cum, last, reach = block_decays(cum_col_ref[...], cum_row_ref[0], lane)
    scaled = step * x
    inter = k_nt(c_map, b_map)
    total = vec_ref[1:2] * x
    for head in range(HEADS_HERE):
        here = (lane >= head * MP) & (lane < (head + 1) * MP)
        total += k_mm(
            (reach[head] * inter).astype(bf16), jnp.where(here, scaled, 0.0).astype(bf16)
        )
    before = state[...]
    state_ref[0] = before.astype(bf16)
    total += jnp.exp(cum) * k_mm(c_map, before.astype(bf16))
    tail = (jnp.exp(last - cum) * scaled).astype(bf16)
    state[...] = jnp.exp(last) * before + k_tn(b_map, tail)
    y = total.astype(bf16)
    y_ref[...] = y
    gated = y.astype(f32) * (gate * logistic(gate))
    gained_ref[...] = (gated * vec_ref[2:3]).astype(bf16)
    square_ref[0] = k_nt(jnp.ones((8, OWN), f32), gated * gated, HIGHEST)


def mix_backward(
    info,
    own_ref,
    s_ref,
    own_tail_ref,
    s_tail_ref,
    cos_ref,
    sin_ref,
    cum_col_ref,
    cum_row_ref,
    taps_x_ref,
    taps_m_ref,
    vec_ref,
    lanes_ref,
    g_y_ref,
    g_z_ref,
    state_ref,
    dq_ref,
    dk_ref,
    dv_ref,
    g_all_ref,
    acc_x_ref,
    acc_m_ref,
    acc_v_ref,
    acc_s_ref,
    g_state,
    next_x,
    next_m,
):
    step_id = pl.program_id(0)
    block = pl.num_programs(0) - 1 - step_id
    place = info[0]

    @pl.when(step_id == 0)
    def _():
        g_state[...] = jnp.zeros_like(g_state)
        next_x[...] = jnp.zeros_like(next_x)
        next_m[...] = jnp.zeros_like(next_m)
        acc_x_ref[...] = jnp.zeros_like(acc_x_ref)
        acc_m_ref[...] = jnp.zeros_like(acc_m_ref)
        acc_v_ref[...] = jnp.zeros_like(acc_v_ref)
        acc_s_ref[...] = jnp.zeros_like(acc_s_ref)

    lane = lax.broadcasted_iota(jnp.int32, (1, OWN), 1)
    cosine, sine = cos_ref[...], sin_ref[...]

    def unturned(value):
        return value * cosine - pltpu.roll(value, HD // 2, 1) * sine

    x_raw = own_ref[:, OWN : 2 * OWN]
    m_raw = s_ref[:, : 2 * NS]
    first = block == 0
    x_pad = jnp.concatenate(
        [jnp.where(first, 0.0, own_tail_ref[:, OWN : 2 * OWN]), x_raw], axis=0
    )
    m_pad = jnp.concatenate([jnp.where(first, 0.0, s_tail_ref[:, : 2 * NS]), m_raw], axis=0)
    s_x = shifted_sum(x_pad, taps_x_ref, TAIL - KC + 1, 1) + taps_x_ref[KC : KC + 1]
    s_m = shifted_sum(m_pad, taps_m_ref, TAIL - KC + 1, 1) + taps_m_ref[KC : KC + 1]
    sig_x, sig_m = logistic(s_x), logistic(s_m)
    x = (s_x * sig_x).astype(bf16).astype(f32)
    maps = (s_m * sig_m).astype(bf16)
    b_map, c_map = maps[:, :NS], maps[:, NS:]
    select = step_lanes(place, lane)
    step_raw = s_ref[:, KEYS_AT + 2 * HD :].astype(bf16)
    raised = k_mm(step_raw, select.astype(bf16)) + vec_ref[0:1]
    step = jnp.maximum(raised, 0.0) + jnp.log(1.0 + jnp.exp(-jnp.abs(raised)))
    cum, last, reach = block_decays(cum_col_ref[...], cum_row_ref[0], lane)
    scaled = step * x

    g_y = g_y_ref[...].astype(f32)

    inter = k_nt(c_map, b_map)
    g_inter = jnp.zeros((BLOCK, BLOCK), f32)
    g_scaled = jnp.zeros((BLOCK, OWN), f32)
    scaled_b = scaled.astype(bf16)
    for head in range(HEADS_HERE):
        here = (lane >= head * MP) & (lane < (head + 1) * MP)
        g_head = jnp.where(here, g_y, 0.0).astype(bf16)
        g_inter += reach[head] * k_nt(g_head, scaled_b)
        g_scaled += k_tn((reach[head] * inter).astype(bf16), g_head)
    before = state_ref[0]
    g_after = g_state[...]
    g_after_b = g_after.astype(bf16)
    tail_w = jnp.exp(last - cum)
    reached = (jnp.exp(cum) * g_y).astype(bf16)
    g_inter_b = g_inter.astype(bf16)
    g_c = k_mm(g_inter_b, b_map) + k_nt(reached, before)
    g_b = k_tn(g_inter_b, c_map) + k_nt((tail_w * scaled).astype(bf16), g_after_b)
    g_scaled += tail_w * k_mm(b_map, g_after_b)
    g_state[...] = jnp.exp(last) * g_after + k_tn(c_map, reached)
    g_x = step * g_scaled + vec_ref[1:2] * g_y
    g_step = k_nt(x * g_scaled, select, HIGHEST) * logistic(
        step_raw.astype(f32) + lanes_ref[0:1]
    )

    gs_x = g_x.astype(bf16).astype(f32) * (sig_x * (1.0 + s_x * (1.0 - sig_x)))
    g_maps = jnp.concatenate([g_b, g_c], axis=1).astype(bf16).astype(f32)
    gs_m = g_maps * (sig_m * (1.0 + s_m * (1.0 - sig_m)))
    gs_x_pad = jnp.concatenate([gs_x, next_x[...]], axis=0)
    gs_m_pad = jnp.concatenate([gs_m, next_m[...]], axis=0)
    g_x_raw = shifted_sum(gs_x_pad, taps_x_ref, KC - 1, -1)
    g_m_raw = shifted_sum(gs_m_pad, taps_m_ref, KC - 1, -1)
    next_x[...] = gs_x[:TAIL]
    next_m[...] = gs_m[:TAIL]
    for tap in range(KC):
        at = TAIL - KC + 1 + tap
        acc_x_ref[tap : tap + 1] += jnp.sum(gs_x * x_pad[at : at + BLOCK], axis=0, keepdims=True)
        acc_m_ref[tap : tap + 1] += jnp.sum(gs_m * m_pad[at : at + BLOCK], axis=0, keepdims=True)
    acc_x_ref[KC : KC + 1] += jnp.sum(gs_x, axis=0, keepdims=True)
    acc_m_ref[KC : KC + 1] += jnp.sum(gs_m, axis=0, keepdims=True)
    acc_v_ref[0:1] += jnp.sum(g_y * x, axis=0, keepdims=True)
    acc_s_ref[0:1] += jnp.sum(g_step, axis=0, keepdims=True)

    here = (block // 8) == info[1]
    g_q = jnp.where(here, dq_ref[...].astype(f32), 0.0)
    at = 2 * OWN
    g_all_ref[:, :at] = jnp.concatenate([g_z_ref[...].astype(f32), g_x_raw], axis=1).astype(bf16)
    for piece in (g_q, g_m_raw, unturned(dk_ref[...]), dv_ref[...], g_step):
        g_all_ref[:, at : at + piece.shape[1]] = piece.astype(bf16)
        at += piece.shape[1]


def masked_scores(info, keys, queries, length):
    scores = k_nt(keys, queries) * (HD**-0.5)
    start = (info[1] * 8 + pl.program_id(0)) * BLOCK
    key_at = lax.broadcasted_iota(jnp.int32, (length, BLOCK), 0)
    query_at = lax.broadcasted_iota(jnp.int32, (length, BLOCK), 1) + start
    return scores, key_at <= query_at


def attend_forward(info, q_ref, k_ref, v_ref, out_ref, out_f_ref, log_ref):
    scores, allowed = masked_scores(info, k_ref[...], q_ref[...], k_ref.shape[0])
    scores = jnp.where(allowed, scores, NEGATIVE)
    top = jnp.max(scores, axis=0, keepdims=True)
    weights = jnp.exp(scores - top)
    total = jnp.sum(weights, axis=0, keepdims=True)
    result = jnp.transpose(k_tn(v_ref[...], weights.astype(bf16)) / total)
    out_ref[...] = result.astype(bf16)
    out_f_ref[...] = result
    log_ref[0] = jnp.broadcast_to(top + jnp.log(total), (8, BLOCK))


def attend_backward(
    info, q_ref, k_ref, v_ref, out_f_ref, log_ref, g_ref, cos_ref, sin_ref, dq_ref, dk_ref, dv_ref
):
    @pl.when(pl.program_id(0) == 0)
    def _():
        dk_ref[...] = jnp.zeros_like(dk_ref)
        dv_ref[...] = jnp.zeros_like(dv_ref)

    keys, queries, grads = k_ref[...], q_ref[...], g_ref[...]
    scores, allowed = masked_scores(info, keys, queries, k_ref.shape[0])
    probs = jnp.where(allowed, jnp.exp(scores - log_ref[0, 0:1]), 0.0)
    delta = k_nt(jnp.ones((8, HD), f32), grads.astype(f32) * out_f_ref[...], HIGHEST)[0:1]
    g_scores = (probs * (k_nt(v_ref[...], grads) - delta)).astype(bf16)
    dv_ref[...] += k_mm(probs.astype(bf16), grads)
    dk_ref[...] += k_mm(g_scores, queries) * (HD**-0.5)
    dq = (k_tn(g_scores, keys) * (HD**-0.5)).astype(bf16).astype(f32)
    dq_ref[...] = (dq * cos_ref[...] - pltpu.roll(dq, HD // 2, 1) * sin_ref[...]).astype(bf16)


def rows_at(width, column=0):
    return pl.BlockSpec((BLOCK, width), lambda i, s: (i ^ s[0], column))


def rows_back(count, width, column=0):
    return pl.BlockSpec((BLOCK, width), lambda i, s: ((count - 1 - i) ^ s[0], column))


def whole(*shape):
    return pl.BlockSpec(shape, lambda i, s: (0,) * len(shape))


def run_mix_forward(info, own, shared, cosine, sine, cum_col, cum_row, taps_x, taps_m, vec):
    length = own.shape[0]
    count = length // BLOCK

    def plain(width):
        return pl.BlockSpec((BLOCK, width), lambda i, s: (i, 0))

    def plain3(rows, width):
        return pl.BlockSpec((1, rows, width), lambda i, s: (i, 0, 0))

    return pl.pallas_call(
        mix_forward,
        grid_spec=pltpu.PrefetchScalarGridSpec(
            num_scalar_prefetch=1,
            grid=(count,),
            in_specs=[
                rows_at(own.shape[1]),
                rows_at(shared.shape[1]),
                plain(HD),
                plain(HD),
                plain(8),
                plain3(8, BLOCK),
                whole(8, OWN),
                whole(8, 2 * NS),
                whole(8, OWN),
            ],
            out_specs=[
                rows_at(OWN),
                rows_at(OWN),
                plain3(8, BLOCK),
                plain3(NS, OWN),
                plain(HD),
                plain(HD),
                plain(HD),
            ],
            scratch_shapes=[
                pltpu.VMEM((NS, OWN), f32),
                pltpu.VMEM((TAIL, OWN), f32),
                pltpu.VMEM((TAIL, 2 * NS), f32),
            ],
        ),
        out_shape=[
            jax.ShapeDtypeStruct((length, OWN), bf16),
            jax.ShapeDtypeStruct((length, OWN), bf16),
            jax.ShapeDtypeStruct((count, 8, BLOCK), f32),
            jax.ShapeDtypeStruct((count, NS, OWN), bf16),
            jax.ShapeDtypeStruct((length, HD), bf16),
            jax.ShapeDtypeStruct((length, HD), bf16),
            jax.ShapeDtypeStruct((length, HD), bf16),
        ],
        compiler_params=params(),
        cost_estimate=LITTLE,
        name="mix_forward",
    )(info, own, shared, cosine, sine, cum_col, cum_row, taps_x, taps_m, vec)


def run_mix_backward(
    info,
    own,
    shared,
    cosine,
    sine,
    cum_col,
    cum_row,
    taps_x,
    taps_m,
    vec,
    lanes,
    g_y,
    g_z,
    states,
    dq,
    dk,
    dv,
):
    length = own.shape[0]
    count = length // BLOCK
    tails = BLOCK // TAIL
    all_width = own.shape[1] + shared.shape[1]

    def plain(width):
        return pl.BlockSpec((BLOCK, width), lambda i, s: (count - 1 - i, 0))

    def plain3(rows, width):
        return pl.BlockSpec((1, rows, width), lambda i, s: (count - 1 - i, 0, 0))

    def tail_of(width):
        def where(i, s):
            before = jnp.maximum(count - 2 - i, 0)
            return ((before ^ s[0]) * tails + tails - 1, 0)

        return pl.BlockSpec((TAIL, width), where)

    def query_rows(i, s):
        return (((count - 1 - i) ^ s[0]) % 8, 0)

    return pl.pallas_call(
        mix_backward,
        grid_spec=pltpu.PrefetchScalarGridSpec(
            num_scalar_prefetch=1,
            grid=(count,),
            in_specs=[
                rows_back(count, own.shape[1]),
                rows_back(count, shared.shape[1]),
                tail_of(own.shape[1]),
                tail_of(shared.shape[1]),
                plain(HD),
                plain(HD),
                plain(8),
                plain3(8, BLOCK),
                whole(8, OWN),
                whole(8, 2 * NS),
                whole(8, OWN),
                whole(8, 128),
                rows_back(count, OWN),
                rows_back(count, OWN),
                plain3(NS, OWN),
                pl.BlockSpec((BLOCK, HD), query_rows),
                plain(HD),
                plain(HD),
            ],
            out_specs=[
                rows_back(count, all_width),
                whole(8, OWN),
                whole(8, 2 * NS),
                whole(8, OWN),
                whole(8, 128),
            ],
            scratch_shapes=[
                pltpu.VMEM((NS, OWN), f32),
                pltpu.VMEM((TAIL, OWN), f32),
                pltpu.VMEM((TAIL, 2 * NS), f32),
            ],
        ),
        out_shape=[
            jax.ShapeDtypeStruct((length, all_width), bf16),
            jax.ShapeDtypeStruct((8, OWN), f32),
            jax.ShapeDtypeStruct((8, 2 * NS), f32),
            jax.ShapeDtypeStruct((8, OWN), f32),
            jax.ShapeDtypeStruct((8, 128), f32),
        ],
        compiler_params=params(),
        cost_estimate=LITTLE,
        name="mix_backward",
    )(
        info,
        own,
        shared,
        own,
        shared,
        cosine,
        sine,
        cum_col,
        cum_row,
        taps_x,
        taps_m,
        vec,
        lanes,
        g_y,
        g_z,
        states,
        dq,
        dk,
        dv,
    )


def own_queries(width):
    return pl.BlockSpec((BLOCK, width), lambda i, s: (s[1] * 8 + i, 0))


def own_rows(width):
    return pl.BlockSpec((BLOCK, width), lambda i, s: (i ^ s[2], 0))


def run_attend_forward(info, queries, keys, values):
    length = keys.shape[0]
    half = length // 2
    count = half // BLOCK
    return pl.pallas_call(
        attend_forward,
        grid_spec=pltpu.PrefetchScalarGridSpec(
            num_scalar_prefetch=1,
            grid=(count,),
            in_specs=[own_queries(HD), whole(length, HD), whole(length, HD)],
            out_specs=[
                own_rows(HD),
                pl.BlockSpec((BLOCK, HD), lambda i, s: (i, 0)),
                pl.BlockSpec((1, 8, BLOCK), lambda i, s: (i, 0, 0)),
            ],
        ),
        out_shape=[
            jax.ShapeDtypeStruct((half, HD), bf16),
            jax.ShapeDtypeStruct((half, HD), f32),
            jax.ShapeDtypeStruct((count, 8, BLOCK), f32),
        ],
        compiler_params=params(),
        cost_estimate=LITTLE,
        name="attend_forward",
    )(info, queries, keys, values)


def run_attend_backward(info, queries, keys, values, out_f, logs, grads, cosine, sine):
    length = keys.shape[0]
    half = length // 2
    count = half // BLOCK
    return pl.pallas_call(
        attend_backward,
        grid_spec=pltpu.PrefetchScalarGridSpec(
            num_scalar_prefetch=1,
            grid=(count,),
            in_specs=[
                own_queries(HD),
                whole(length, HD),
                whole(length, HD),
                pl.BlockSpec((BLOCK, HD), lambda i, s: (i, 0)),
                pl.BlockSpec((1, 8, BLOCK), lambda i, s: (i, 0, 0)),
                own_rows(HD),
                own_queries(HD),
                own_queries(HD),
            ],
            out_specs=[
                own_rows(HD),
                whole(length, HD),
                whole(length, HD),
            ],
        ),
        out_shape=[
            jax.ShapeDtypeStruct((half, HD), bf16),
            jax.ShapeDtypeStruct((length, HD), f32),
            jax.ShapeDtypeStruct((length, HD), f32),
        ],
        compiler_params=params(),
        cost_estimate=LITTLE,
        name="attend_backward",
    )(info, queries, keys, values, out_f, logs, grads, cosine, sine)


def cube_body(
    tokens,
    log_decay,
    norm_gain,
    qkv_proj,
    attn_proj,
    inner_proj,
    conv_weight,
    conv_bias,
    step_bias,
    skip_gain,
    inner_gain,
    inner_out,
    ff_gain,
    gate_up,
    down_proj,
    cotangent,
):
    core = lax.axis_index("head")
    seq_half = lax.axis_index("half")
    member = lax.axis_index("cube")
    chip = seq_half * 8 + member
    bits = (member // 4, (member // 2) % 2, member % 2)
    zl = bits[0]
    place = core * 8 + member
    info = jnp.stack([place, core, member, seq_half]).astype(jnp.int32)
    width = tokens.shape[-1]
    rows = tokens.shape[1]
    shard = width // DEVICES
    inner_width = MH * MP
    conv_width = inner_width + 2 * NS
    heads = MH // 16
    mine = heads * MP
    length = rows * 16
    half_rows = rows * 8
    ffc = FF // 16

    def to_local(value):
        parts = [value[:, i * width // 4 : (i + 1) * width // 4] for i in range(4)]
        return jnp.where(
            seq_half == 0,
            jnp.concatenate([parts[i] for i in (0, 2, 1, 3)], axis=1),
            jnp.concatenate([parts[i] for i in (1, 3, 0, 2)], axis=1),
        )

    def to_natural(value):
        parts = [value[:, i * width // 4 : (i + 1) * width // 4] for i in range(4)]
        return jnp.where(
            seq_half == 0,
            jnp.concatenate([parts[i] for i in (0, 2, 1, 3)], axis=1),
            jnp.concatenate([parts[i] for i in (2, 0, 3, 1)], axis=1),
        )

    swapped = swap_sequences(jnp.concatenate([tokens[0], cotangent[0]], axis=0))
    x_bf, g_out_bf = to_local(swapped[:rows]), to_local(swapped[rows:])

    gain_rows = norm_gain.astype(f32)[:, None]
    qkv_s = (qkv_proj.astype(f32) * gain_rows).astype(bf16)
    inner_s = (inner_proj.astype(f32) * gain_rows).astype(bf16)
    gate_up_s = (gate_up.astype(f32) * ff_gain.astype(f32)[:, None]).astype(bf16)

    def to_places(value):
        return jnp.moveaxis(value.reshape(shard, 16, -1), 1, 0)

    def to_members(value):
        parts = jnp.moveaxis(value.reshape(shard, 8, -1), 1, 0)
        return jnp.concatenate([parts, parts], axis=0)

    def both_halves(value, other):
        return jnp.concatenate([value, other], axis=0)

    kv_width = KVH * HD
    conv_shard = conv_weight.shape[1]
    smalls = jnp.concatenate([conv_weight.reshape(-1), conv_bias, inner_gain])
    decay_rows = jnp.moveaxis(log_decay, 1, 2).reshape(2, -1)
    decay_high = lax.optimization_barrier(decay_rows.astype(bf16))
    decay_low = (decay_rows - decay_high.astype(f32)).astype(bf16)
    decay_rows = jnp.concatenate([decay_high, decay_low], axis=1)
    extra_size = shard * 128
    extra_pad = jnp.zeros((extra_size - smalls.shape[0] - decay_rows.shape[1],), bf16)

    def shared_for(half):
        mine_rows = lax.dynamic_index_in_dim(decay_rows, half, 0, keepdims=False)
        extra = jnp.concatenate([smalls, mine_rows, extra_pad]).reshape(shard, 128)
        return jnp.concatenate([shared_send, extra], axis=1)

    shared_send = jnp.concatenate(
        [
            inner_s[:, 2 * inner_width : inner_width + conv_width],
            qkv_s[:, QH * HD : QH * HD + kv_width],
            inner_s[:, inner_width + conv_width :],
            jnp.zeros((shard, -MH % 128), bf16),
            qkv_s[:, QH * HD + kv_width :],
        ],
        axis=1,
    )
    shared_other = flip(shared_for(1 - seq_half), BIT_ZH)
    send_own = jnp.concatenate(
        [
            to_places(inner_s[:, :inner_width]),
            to_places(inner_s[:, inner_width : 2 * inner_width]),
            to_members(qkv_s[:, : QH * HD]),
        ],
        axis=2,
    )
    got_own = exchange(send_own).reshape(width // 2, -1)
    x_rows = x_bf.astype(f32)
    inv_in = lax.rsqrt(jnp.mean(x_rows * x_rows, axis=-1, keepdims=True) + EPSILON)
    shared_mine = shared_for(seq_half)
    shared_both = jnp.concatenate([shared_mine, shared_other], axis=0)
    normed_mine = (x_rows * inv_in).astype(bf16)
    shared_edges = ((0, 2 * NS), (2 * NS, 2 * NS + kv_width + 128), (2 * NS + kv_width + 128, None))
    lanes_all = (shared_both.shape[1] + width) // 128
    goals = (-(-lanes_all // 3), -(-lanes_all // 3), lanes_all - 2 * -(-lanes_all // 3))
    edges, normed_edges, joined, at, done = [], [], [], 0, 0
    for (a, b), lanes_here in zip(shared_edges, goals):
        part = shared_both[:, a:b]
        taken = lanes_here * 128 - part.shape[1]
        joined += [part, normed_mine[:, done : done + taken]]
        edges.append((at, at + lanes_here * 128))
        normed_edges.append((part.shape[1], done, taken))
        at += lanes_here * 128
        done += taken
    first = Gather(jnp.concatenate(joined, axis=1), edges, info)
    first.state, got_own = joint(first.state, got_own)
    own_width = 2 * mine + HD
    other_own = [flip(got_own[:, : own_width // 2], BIT_ZH), None]
    first.hop()
    send_rest = jnp.concatenate(
        [
            to_places(inner_out.T),
            to_members(attn_proj.T),
            to_places(gate_up_s[:, :FF]),
            to_places(gate_up_s[:, FF:]),
            to_places(down_proj.T),
        ],
        axis=2,
    )
    positions = jnp.arange(length, dtype=f32)
    frequency = ROPE_BASE ** (-2.0 * jnp.arange(HD // 2, dtype=f32) / HD)
    angle = positions[:, None] * frequency[None, :]
    cosine, sine = jnp.cos(angle), jnp.sin(angle)
    cosine = jnp.concatenate([cosine, cosine], axis=1)
    sine = jnp.concatenate([-sine, sine], axis=1)
    first.hop()
    first.state, other_own[0], got_own = joint(first.state, other_own[0], got_own)
    other_own[1] = flip(got_own[:, own_width // 2 :], BIT_ZH)
    first.hop()
    first.state, send_rest, other_own[1], cosine, sine = joint(
        first.state, send_rest, other_own[1], cosine, sine
    )
    got = exchange(send_rest).reshape(width // 2, -1)
    pieces = first.pieces()
    shared_width = 2 * NS + 2 * HD + 128
    picks = (
        ((0, 0, 0, 2 * NS),),
        ((0, HD, 2 * NS, HD), (kv_width, 0, 2 * NS + 2 * HD, 128)),
        ((0, HD, 2 * NS + HD, HD),),
    )
    moves, extra_moves, normed_moves = [], [], []
    for group in range(4):
        half, far = group // 2, group % 2
        for part in range(3):
            number = 3 * group + part if half == 0 else 6 + far
            start = edges[part][0] * half
            skip, normed_at, taken = normed_edges[part]
            for begin, cube_place, count in piece_blocks(part, far):
                normed_moves.append(
                    (
                        number,
                        fixed(begin * rows, count * rows, start + skip, taken),
                        fixed((half * 8 + cube_place) * rows, count * rows, normed_at, taken),
                    )
                )
                for block, zh in ((i, j) for i in range(count) for j in range(2)):
                    row = (begin + block) * 2 * shard + zh * shard
                    position = half * 8 + cube_place + block

                    def goal(ref, position=position, zh=zh, target=0, columns=128):
                        to = zh * 16 + (ref[0] ^ position)
                        to = pl.multiple_of(to * shard, shard)
                        return (pl.ds(to, shard), pl.ds(target, columns))

                    def extra_goal(ref, position=position, zh=zh):
                        place = ref[0] ^ position
                        to = (place // 8) * 16 + (zh ^ ref[3]) * 8 + place % 8
                        to = pl.multiple_of(to * shard, shard)
                        return (pl.ds(to, shard), pl.ds(0, 128))

                    for column, by_zl, target, columns in picks[part]:

                        def source(ref, row=row, at=start + column, by_zl=by_zl, columns=columns):
                            if by_zl:
                                at = pl.multiple_of(at + (ref[2] // 4) * by_zl, 128)
                            return (pl.ds(row, shard), pl.ds(at, columns))

                        moves.append(
                            (
                                number,
                                source,
                                functools.partial(goal, target=target, columns=columns),
                            )
                        )
                    if part == 2:
                        extra_moves.append(
                            (number, fixed(row, shard, start + kv_width, 128), extra_goal)
                        )
    normed, w_s, small_got = assemble(
        pieces,
        [
            ((length, width), bf16, normed_moves),
            ((width, shared_width), bf16, moves),
            ((width, 128), bf16, extra_moves),
        ],
        info,
    )
    small_got = small_got.reshape(DEVICES, -1)
    at = smalls.shape[0]
    decay = lax.dynamic_slice_in_dim(small_got[:, at : at + decay_rows.shape[1]], core * 16, 16, 0)
    decay = decay.astype(f32).reshape(16, 2, 8, heads, rows)
    decay = lax.dynamic_index_in_dim(decay[:, 0] + decay[:, 1], member, 1, keepdims=False)
    at = 0
    conv_w = jnp.moveaxis(
        small_got[:, at : at + KC * conv_shard].reshape(DEVICES, KC, conv_shard), 1, 0
    ).reshape(KC, conv_width)
    at += KC * conv_shard
    conv_b = small_got[:, at : at + conv_shard].reshape(1, conv_width)
    at += conv_shard
    gain_all = small_got[:, at : at + inner_gain.shape[0]].reshape(1, inner_width)
    conv_all = jnp.concatenate([conv_w, conv_b], axis=0).astype(f32)
    conv_all = jnp.concatenate([conv_all, jnp.zeros((8 - KC - 1, conv_width), f32)], axis=0)
    taps_x = lax.dynamic_slice_in_dim(conv_all[:, :inner_width], place * mine, mine, 1)
    taps_m = conv_all[:, inner_width:]
    gain_mine = lax.dynamic_slice_in_dim(gain_all, place * mine, mine, 1)[0].astype(f32)

    (w_own,) = joint(both_halves(got_own, jnp.concatenate(other_own, axis=1)))
    bias_mine = lax.dynamic_slice_in_dim(step_bias, member * heads, heads, 0)
    skip_mine = lax.dynamic_slice_in_dim(skip_gain, member * heads, heads, 0)
    vec = jnp.concatenate(
        [
            jnp.repeat(bias_mine, MP)[None],
            jnp.repeat(skip_mine, MP)[None],
            gain_mine[None],
            jnp.zeros((5, mine), f32),
        ],
        axis=0,
    )
    lanes = lax.dynamic_update_slice(
        jnp.zeros((8, 128), f32), bias_mine[None], (0, place * heads)
    )
    cum_row = jnp.cumsum(decay, axis=2)
    cum_row = jnp.concatenate([cum_row, jnp.zeros((16, 8 - heads, rows), f32)], axis=1)
    cum_col = jnp.moveaxis(cum_row, 1, 2).reshape(length, 8)
    (w_all,) = joint(jnp.concatenate([w_own, w_s], axis=1))

    order = jnp.arange(16, dtype=jnp.int32) ^ place

    def reordered(value):
        return jnp.take(value, order, axis=0, unique_indices=True, mode="clip")

    g_out_bf, normed = joint(g_out_bf, normed)
    g_out = gather_start(g_out_bf, info)
    g_out.hop()
    raw_s = mm(normed, w_s)
    g_out.state, raw_s, got, normed = joint(g_out.state, raw_s, got, normed)
    cuts = [0, mine + HD] + [mine + HD + i * ffc for i in (1, 2, 3)]
    got = [got[:, a:b] for a, b in zip(cuts[:-1], cuts[1:])]
    other = [flip(got[0], BIT_ZH), None, None, None]
    g_out.hop()
    raw_own = mm(normed, w_own)
    g_out.state, raw_own = joint(g_out.state, raw_own)
    g_out.hop()

    tables = (cosine, sine, cum_col, cum_row, taps_x, taps_m, vec)
    y, gained, squares, states, queries, keys, values = run_mix_forward(
        info, raw_own, raw_s, *tables
    )
    squares, other[0] = joint(squares, other[0])
    other[3] = flip(got[3], BIT_ZH)
    (w_mix,) = joint(both_halves(got[0], other[0]))
    w_out, w_att = w_mix[:, :mine], w_mix[:, mine:]
    squares = group_sum(squares[:, 0])
    squares, queries, other[3], got[1] = joint(squares, queries, other[3], got[1])
    other[1] = flip(got[1], BIT_ZH)
    (w_down,) = joint(both_halves(got[3], other[3]))
    attended, attended_f, logs = run_attend_forward(info, queries, keys, values)
    inv_mix = lax.rsqrt(squares / inner_width + EPSILON)
    inv_mix_rows = reordered(inv_mix).reshape(length, 1)
    part_other = inv_mix_rows[half_rows:] * mm_nt(gained[half_rows:], w_out)
    part_own = inv_mix_rows[:half_rows] * mm_nt(gained[:half_rows], w_out) + mm_nt(attended, w_att)
    sums = Scatter(part_own.astype(bf16), part_other)
    sums.state, other[1], got[2] = joint(sums.state, other[1], got[2])
    other[2] = flip(got[2], BIT_ZH)
    sums.hop()
    sums.hop()
    sums.state, other[2] = joint(sums.state, other[2])
    (w_gu,) = joint(
        jnp.concatenate([both_halves(got[i], other[i]) for i in (1, 2)], axis=1)
    )
    hidden = x_rows + sums.result()
    g_out = gathered(g_out, width, info)

    inv_ff = lax.rsqrt(jnp.mean(hidden * hidden, axis=-1, keepdims=True) + EPSILON)
    gather = gather_start((hidden * inv_ff).astype(bf16), info)
    normed_ff = gathered(gather, width, info)
    gate_vals = mm(normed_ff, w_gu)
    gate, up = gate_vals[:, :ffc], gate_vals[:, ffc:]
    sig = jax.nn.sigmoid(gate)
    mixed = (gate * sig * up).astype(bf16)
    g_mixed = mm(g_out, w_down)
    g_vals = jnp.concatenate(
        [g_mixed * up * sig * (1.0 + gate * (1.0 - sig)), g_mixed * gate * sig], axis=1
    ).astype(bf16)
    g_ff_other = mm_nt(g_vals[half_rows:], w_gu).astype(bf16)
    sums = Scatter(mm_nt(g_vals[:half_rows], w_gu).astype(bf16), g_ff_other)
    sums.hop()
    def crossing(value):
        return flip(value[width // 2 :], BIT_ZH)

    def to_owners(values, crossed):
        total = [
            value[: width // 2].astype(f32) + got.astype(f32)
            for value, got in zip(values, crossed)
        ]
        total = jnp.concatenate([part.astype(bf16) for part in total], axis=1)
        return exchange(total.reshape(16, shard, -1))

    mixed_late, g_vals_late = sums.then(mixed, g_vals)
    mixed_cube = reordered_rows(mixed_late, info)
    out_other = mm_nt(mixed_cube[half_rows:], w_down).astype(bf16)
    out_own = mm_nt(mixed_cube[:half_rows], w_down).astype(bf16)
    d_gu = mm_tn(normed_ff, g_vals_late).astype(bf16)
    d_gate, d_up = d_gu[:, :ffc], d_gu[:, ffc:]
    sums.state, out_other, out_own, d_gate = joint(sums.state, out_other, out_own, d_gate)
    out_got = flip(out_other, BIT_C)
    gate_got = crossing(d_gate)
    sums.hop()
    mixed_late, g_out = sums.then(mixed_late, g_out)
    d_down = mm_tn(g_out, mixed_late).astype(bf16)
    sums.state, d_down = joint(sums.state, d_down)
    g_ff = sums.result()

    def from_places(value):
        return jnp.moveaxis(value, 0, 1).reshape(shard, -1)

    g_hidden = (
        g_out_bf.astype(f32)
        + inv_ff * g_ff
        - hidden * inv_ff**3 * jnp.mean(hidden * g_ff, axis=-1, keepdims=True)
    )
    gather = gather_start(g_hidden.astype(bf16), info)
    gather.state, gate_got, d_up = joint(gather.state, gate_got, d_up)
    up_got = crossing(d_up)
    gather.hop()
    gather.hop()
    out_sum = (out_own.astype(f32) + out_got.astype(f32)).astype(bf16)
    gather.state, up_got, d_down, out_sum, w_all = joint(
        gather.state, up_got, d_down, out_sum, w_all
    )
    down_got = crossing(d_down)
    g_branch = gathered(gather, width, info)

    inner_normed = (gained.astype(f32) * inv_mix_rows).astype(bf16)
    g_inner = mm(g_branch, w_out)
    g_branch_own = g_branch[:half_rows]
    g_att = mm(g_branch_own, w_att).astype(bf16)
    dots = jnp.sum(inner_normed.astype(f32) * g_inner, axis=-1).reshape(16, rows)
    dots = group_sum(reordered(dots))
    g_branch_own = g_branch[:half_rows]
    g_att = mm(g_branch_own, w_att).astype(bf16)
    d_mix_early = jnp.concatenate(
        [
            mm_tn(g_branch, inner_normed).astype(bf16),
            mm_tn(g_branch_own, attended).astype(bf16),
        ],
        axis=1,
    )
    d_mix_early, g_att = joint(d_mix_early, g_att)
    early_got = crossing(d_mix_early)
    d_q, d_k, d_v = run_attend_backward(
        info, queries, keys, values, attended_f, logs, g_att, cosine, sine
    )
    gate = raw_own[:, :mine]
    gate_sig = jax.nn.sigmoid(gate)
    y_rows = y.astype(f32)
    normed_mix = y_rows * (gate * gate_sig) * inv_mix_rows
    g_gated = inv_mix_rows * (
        gain_mine * g_inner - normed_mix * (reordered(dots).reshape(length, 1) / inner_width)
    )
    g_y = (g_gated * gate * gate_sig).astype(bf16)
    g_z = (g_gated * y_rows * gate_sig * (1.0 + gate * (1.0 - gate_sig))).astype(bf16)
    grad_gain_mine = jnp.sum(normed_mix * g_inner, axis=0)
    d_q, down_got, dots = joint(d_q, down_got, dots)
    d_ff_got = to_owners((d_gate, d_up, d_down), (gate_got, up_got, down_got))
    d_mix_late = jnp.concatenate(
        [
            mm_tn(normed, g_z).astype(bf16),
            mm_tn(normed[:half_rows], d_q).astype(bf16),
        ],
        axis=1,
    )
    d_mix_late, early_got = joint(d_mix_late, early_got)
    late_got = crossing(d_mix_late)
    g_y, d_ff_got, out_sum, d_mix_late = joint(g_y, d_ff_got, out_sum, d_mix_late)
    out_got = lax.all_to_all(
        out_sum.reshape(8, rows, width), "cube", split_axis=0, concat_axis=0, tiled=True
    )
    g_all, acc_x, acc_m, acc_v, acc_s = run_mix_backward(
        info,
        raw_own,
        raw_s,
        *tables,
        lanes,
        g_y,
        g_z,
        states,
        d_q,
        d_k,
        d_v,
    )
    conv_grads = jnp.concatenate([acc_x[: KC + 1], acc_m[: KC + 1]], axis=1)
    g_bias = lax.dynamic_slice_in_dim(acc_s[0], place * heads, heads, 0)
    g_skip = jnp.sum(acc_v[0].reshape(heads, MP), axis=1)
    small_grads = jnp.concatenate([conv_grads.reshape(-1), grad_gain_mine, g_bias, g_skip])
    small_grads = jnp.pad(small_grads, (0, -small_grads.shape[0] % shard)).astype(bf16)
    small_grads = jnp.broadcast_to(
        small_grads.reshape(1, shard, -1), (DEVICES, shard, small_grads.shape[0] // shard)
    ).reshape(width, -1)
    g_in_other = mm_nt(g_all[half_rows:], w_all).astype(bf16)
    sums = Scatter(mm_nt(g_all[:half_rows], w_all).astype(bf16), g_in_other)
    sums.state, out_got = joint(sums.state, out_got)
    sums.hop()
    (g_all,) = sums.then(g_all)
    d_own = mm_tn(normed, g_all[:, mine : 2 * mine]).astype(bf16)
    d_own = jnp.concatenate([d_own, small_grads], axis=1)
    d_shared = mm_tn(normed, g_all[:, own_width:]).astype(bf16)
    sums.state, d_own, d_shared = joint(sums.state, d_own, d_shared)
    sums.hop()
    d_shared, d_ff_got, out_got = sums.then(d_shared, d_ff_got, out_got)
    out_part = jnp.sum(out_got.astype(f32), axis=0)
    out_rows = (hidden + out_part).astype(bf16)

    def only_mine(value):
        empty = jnp.zeros((width, KVH * HD), bf16)
        return lax.dynamic_update_slice_in_dim(empty, value, zl * HD, 1)

    d_shared = jnp.concatenate(
        [
            d_shared[:, : 2 * NS],
            only_mine(d_shared[:, 2 * NS : 2 * NS + HD]),
            only_mine(d_shared[:, 2 * NS + HD : 2 * NS + 2 * HD]),
            d_shared[:, 2 * NS + 2 * HD :],
        ],
        axis=1,
    )
    moves = []
    for block in range(DEVICES):

        def goal(ref, block=block):
            row = (ref[0] ^ (block % 16)) * 2 + block // 16
            return (pl.ds(pl.multiple_of(row * shard, shard), shard), slice(None))

        moves.append((0, fixed(block * shard, shard, 0, d_shared.shape[1]), goal))
    d_shared = assemble([d_shared], [(d_shared.shape, bf16, moves)], info)[0]
    sums.state, d_shared = joint(sums.state, d_shared)
    shared_sums = Scatter(d_shared[:half_rows], d_shared[half_rows:])
    sums.hop()
    g_in, d_own = joint(sums.result(), d_own)
    own_back = crossing(d_own)
    g_x_rows = (
        inv_in * g_in - x_rows * inv_in**3 * jnp.mean(x_rows * g_in, axis=-1, keepdims=True)
    )
    both = jnp.concatenate(
        [to_natural(out_rows), to_natural((g_hidden + g_x_rows).astype(bf16))], axis=0
    )
    both = swap_sequences(both)
    output, grad_tokens = both[None, :rows], both[None, rows:].astype(f32)
    shared_sums.hop()
    shared_sums.state, own_back = joint(shared_sums.state, own_back)
    shared_sums.hop()
    shared_sums.hop()
    shared_sums.state, own_back, late_got, early_got = joint(
        shared_sums.state, own_back, late_got, early_got
    )
    d_own_got = to_owners((d_own, d_mix_late, d_mix_early), (own_back, late_got, early_got))
    d_cube = shared_sums.result().reshape(2, shard, -1)
    d_shared_own = d_cube[0] + flip(d_cube[1].astype(bf16), BIT_ZH).astype(f32)
    d_ff_own = d_ff_got.astype(f32)
    d_gate_up = jnp.concatenate(
        [from_places(d_ff_own[..., :ffc]), from_places(d_ff_own[..., ffc : 2 * ffc])], axis=1
    )
    grad_gate_up = d_gate_up * ff_gain.astype(f32)[:, None]
    grad_ff_gain = jnp.sum(d_gate_up * gate_up.astype(f32), axis=1)
    grad_down = jnp.moveaxis(d_ff_own[..., 2 * ffc : 3 * ffc], 1, 2).reshape(FF, shard)
    d_own = d_own_got.astype(f32)
    small_end = d_own.shape[-1] - 2 * mine - 2 * HD
    d_mix_own = d_own[..., small_end + mine + HD :]
    grad_inner_out = jnp.moveaxis(d_mix_own[..., :mine], 1, 2).reshape(inner_width, shard)
    d_att = d_mix_own[..., mine:].reshape(2, 8, shard, HD)
    grad_attn = jnp.moveaxis(d_att[0] + d_att[1], 1, 2).reshape(QH * HD, shard)
    d_x = from_places(d_own[..., :mine])
    d_z = from_places(d_own[..., small_end : small_end + mine])
    d_qw = d_own[..., small_end + mine : small_end + mine + HD].reshape(2, 8, shard, HD)
    d_qw = from_places(d_qw[0] + d_qw[1])

    got = d_own[..., mine:small_end].reshape(16, -1)
    at = 0
    taps_width = mine + 2 * NS
    conv_grads = got[:, at : at + (KC + 1) * taps_width].reshape(16, KC + 1, taps_width)
    at += (KC + 1) * taps_width
    conv_full = jnp.concatenate(
        [
            jnp.moveaxis(conv_grads[..., :mine], 0, 1).reshape(KC + 1, inner_width),
            jnp.sum(conv_grads[..., mine:], axis=0),
        ],
        axis=1,
    )
    device = core * 16 + chip
    conv_own = lax.dynamic_slice_in_dim(conv_full, device * conv_shard, conv_shard, 1)
    gain_full = got[:, at : at + mine].reshape(inner_width)
    gain_shard = inner_gain.shape[0]
    grad_inner_gain = lax.dynamic_slice_in_dim(gain_full, device * gain_shard, gain_shard, 0)
    at += mine
    local = lax.dynamic_slice_in_dim(got[:, at : at + 2 * heads], core * 8, 8, 0)
    grad_step_bias = local[:, :heads].reshape(-1)
    grad_skip_gain = local[:, heads:].reshape(-1)

    at = 2 * NS + 2 * kv_width
    d_qkv = jnp.concatenate([d_qw, d_shared_own[:, 2 * NS : at]], axis=1)
    d_inner = jnp.concatenate(
        [d_z, d_x, d_shared_own[:, : 2 * NS], d_shared_own[:, at : at + MH]], axis=1
    )
    grad_norm_gain = jnp.sum(d_qkv * qkv_proj.astype(f32), axis=1) + jnp.sum(
        d_inner * inner_proj.astype(f32), axis=1
    )
    return (
        output,
        grad_tokens,
        grad_norm_gain,
        d_qkv * gain_rows,
        grad_attn,
        d_inner * gain_rows,
        conv_own[:KC],
        conv_own[KC],
        grad_step_bias,
        grad_skip_gain,
        grad_inner_gain,
        grad_inner_out,
        grad_ff_gain,
        grad_gate_up,
        grad_down,
    )


def cube_solution(mesh):
    cubes = jax.sharding.Mesh(mesh.devices.reshape(2, 2, 8), BOTH)
    tokens = P("head", ("half", "cube"), None)
    lines = P(BOTH)
    rows = P(BOTH, None)
    columns = P(None, BOTH)
    head = P("head")
    return jax.shard_map(
        cube_body,
        mesh=cubes,
        in_specs=(
            tokens,
            P(None, ("half", "cube"), "head"),
            lines,
            rows,
            columns,
            rows,
            columns,
            lines,
            head,
            head,
            lines,
            columns,
            lines,
            rows,
            columns,
            tokens,
        ),
        out_specs=(
            tokens,
            tokens,
            lines,
            rows,
            columns,
            rows,
            columns,
            lines,
            head,
            head,
            lines,
            columns,
            lines,
            rows,
            columns,
        ),
        check_vma=False,
    )


def solution(mesh):
    if mesh.shape["seq"] == 16:
        return cube_solution(mesh)
    return jax.shard_map(
        body,
        mesh=mesh,
        in_specs=(
            P("head", "seq", None),
            P(None, "seq", "head"),
            P(("head", "seq")),
            P(("head", "seq"), None),
            P(None, ("head", "seq")),
            P(("head", "seq"), None),
            P(None, ("head", "seq")),
            P(("head", "seq")),
            P("head"),
            P("head"),
            P(("head", "seq")),
            P(None, ("head", "seq")),
            P(("head", "seq")),
            P(("head", "seq"), None),
            P(None, ("head", "seq")),
            P("head", "seq", None),
        ),
        out_specs=(
            P("head", "seq", None),
            P("head", "seq", None),
            P(("head", "seq")),
            P(("head", "seq"), None),
            P(None, ("head", "seq")),
            P(("head", "seq"), None),
            P(None, ("head", "seq")),
            P(("head", "seq")),
            P("head"),
            P("head"),
            P(("head", "seq")),
            P(None, ("head", "seq")),
            P(("head", "seq")),
            P(("head", "seq"), None),
            P(None, ("head", "seq")),
        ),
        check_vma=False,
    )
```

```python
import functools
import math

import jax
import jax.numpy as jnp
from jax import lax
from jax.experimental import pallas as pl
from jax.experimental.pallas import tpu as pltpu
from jax.sharding import PartitionSpec as P

FF = 4096
QH = 8
KVH = 2
HD = 128
MH = 48
MP = 64
NS = 256
KC = 4


EPSILON = 1e-05
ROPE_BASE = 100000000000.0
NEGATIVE = -1e30
HIGHEST = lax.Precision.HIGHEST


def passed_along(value, axis, steps):
    count = lax.axis_size(axis)
    initial, last = (max(0, -steps), min(count, count - steps))
    return lax.ppermute(value, axis, [(source, source + steps) for source in range(initial, last)])


def carried_in(array, axis, combine, identity):
    count, mine = (lax.axis_size(axis), lax.axis_index(axis))
    everything = jax.tree.map(
        lambda part, kind: lax.all_gather(part.astype(kind), axis),
        array,
        (jnp.bfloat16, jnp.bfloat16),
    )
    start = jax.tree.map(
        lambda part, zero: jnp.broadcast_to(jnp.asarray(zero, part.dtype), part.shape),
        array,
        identity,
    )

    def carried_hop(k, before):
        reached = k < mine
        new = combine(
            before, jax.tree.map(lambda part, own: part[k].astype(own.dtype), everything, array)
        )
        return jax.tree.map(lambda a, b: jnp.where(reached, a, b), new, before)

    return lax.fori_loop(0, count, carried_hop, start)


def entering(array, axis, combine, identity):
    count, mine = (lax.axis_size(axis), lax.axis_index(axis))
    everything = jax.tree.map(
        lambda part, kind: lax.all_gather(part.astype(kind), axis),
        array,
        jax.tree.map(lambda a: jnp.bfloat16 if a.dtype == jnp.float32 else a.dtype, array),
    )
    start = jax.tree.map(
        lambda part, zero: jnp.broadcast_to(jnp.asarray(zero, part.dtype), part.shape),
        array,
        identity,
    )

    def entering_hop(k, before):
        at = count - 1 - k
        reached = at > mine
        new = combine(
            before, jax.tree.map(lambda part, own: part[at].astype(own.dtype), everything, array)
        )
        return jax.tree.map(lambda a, b: jnp.where(reached, a, b), new, before)

    return lax.fori_loop(0, count, entering_hop, start)


def shortened(array):
    return jax.tree.map(lambda a: a.astype(jnp.bfloat16) if a.dtype == jnp.float32 else a, array)


def rounded(value):
    return lax.optimization_barrier(value.astype(jnp.bfloat16)).astype(jnp.float32)


def rms_norm(value, gain):
    return value * lax.rsqrt(jnp.mean(value * value, axis=-1, keepdims=True) + EPSILON) * gain


def rotary(value, positions):
    halfway = value.shape[-1] // 2
    frequency = ROPE_BASE ** (-2.0 * jnp.arange(halfway, dtype=jnp.float32) / value.shape[-1])
    angle = positions[:, None] * frequency[None, :]
    cosine = jnp.cos(angle)[:, None, :]
    sine_part = jnp.sin(angle)[:, None, :]
    first = value[..., :halfway]
    second = value[..., halfway:]
    return jnp.concatenate(
        [first * cosine - second * sine_part, second * cosine + first * sine_part], axis=-1
    )


def block_decay(log_decay):
    return jnp.exp(jnp.cumsum(log_decay, axis=1)[:, -1, :])


def inner_output(inner_x, step_in, state_maps, step_bias, skip_gain, state_in, log_decay):
    nstate = state_maps.shape[-1] // 2
    input_map = state_maps[..., :nstate]
    output_map = state_maps[..., nstate:]
    step_size = jax.nn.softplus(step_in + step_bias)
    cumulative = jnp.cumsum(log_decay, axis=1)
    scaled_x = inner_x * step_size[..., None]
    intersection = jnp.einsum("stn,sun->stu", output_map, input_map, precision=HIGHEST)
    length_blk = log_decay.shape[1]
    lower_mask = jnp.arange(length_blk)[:, None] >= jnp.arange(length_blk)[None, :]
    spread = cumulative[:, :, None, :] - cumulative[:, None, :, :]
    mixing = (
        jnp.where(lower_mask[None, :, :, None], jnp.exp(jnp.minimum(spread, 0.0)), 0.0)
        * intersection[..., None]
    )
    within = jnp.einsum("stuh,suhp->sthp", mixing, scaled_x, precision=HIGHEST)
    carried = (
        jnp.einsum("shpn,stn->sthp", state_in, output_map, precision=HIGHEST)
        * jnp.exp(cumulative)[..., None]
    )
    return within + carried + skip_gain[:, None] * inner_x


def inner_state(inner_x, step_in, state_maps, step_bias, log_decay):
    nstate = state_maps.shape[-1] // 2
    input_map = state_maps[..., :nstate]
    step_size = jax.nn.softplus(step_in + step_bias)
    cumulative = jnp.cumsum(log_decay, axis=1)
    tail_weight = jnp.exp(cumulative[:, -1:, :] - cumulative) * step_size
    return jnp.einsum("suh,suhp,sun->shpn", tail_weight, inner_x, input_map, precision=HIGHEST)


def over_blocks(function, carried, arrays, offset, limit):
    row_count = arrays[0].shape[1]
    step_rows = math.gcd(row_count, 1024)

    def advance(number, running):
        pieces = tuple(
            (
                lax.dynamic_slice_in_dim(member, number * step_rows, step_rows, 1)
                for member in arrays
            )
        )
        return function(running, pieces, offset + number * step_rows)

    upper = (limit + step_rows - 1) // step_rows
    return lax.fori_loop(0, upper, advance, carried)


def attend_block(carried, pair, offset, queries, query_pos, score_scale):
    row_top, row_total, accumulated = carried
    key_blk, value_blk = pair
    scores = (
        jnp.einsum("sqkgd,sjkd->sqkgj", queries, key_blk, preferred_element_type=jnp.float32)
        * score_scale
    )
    key_pos = offset + jnp.arange(key_blk.shape[1])
    allowed = (key_pos[None, :] <= query_pos[:, None])[None, :, None, None, :]
    masked = jnp.where(allowed, scores, NEGATIVE)
    new_top = jnp.maximum(row_top, jnp.max(masked, axis=-1))
    factor = jnp.exp(row_top - new_top)
    weights = jnp.where(allowed, jnp.exp(masked - new_top[..., None]), 0.0)
    row_total = factor * row_total + jnp.sum(weights, axis=-1)
    accumulated = factor[..., None] * accumulated + jnp.einsum(
        "sqkgj,sjkd->sqkgd",
        weights.astype(jnp.bfloat16),
        value_blk,
        preferred_element_type=jnp.float32,
    )
    return (new_top, row_total, accumulated)


def score_grads(
    queries, grad_heads, log_total, row_delta, key_blk, value_blk, offset, query_pos, score_scale
):
    scores = (
        jnp.einsum("sqkgd,sjkd->sqkgj", queries, key_blk, preferred_element_type=jnp.float32)
        * score_scale
    )
    key_pos = offset + jnp.arange(key_blk.shape[1])
    allowed = (key_pos[None, :] <= query_pos[:, None])[None, :, None, None, :]
    prob_rows = jnp.where(allowed, jnp.exp(scores - log_total[..., None]), 0.0)
    grad_probs = jnp.einsum(
        "sqkgd,sjkd->sqkgj", grad_heads, value_blk, preferred_element_type=jnp.float32
    )
    grad_scores = (prob_rows * (grad_probs - row_delta[..., None])).astype(jnp.bfloat16)
    return (prob_rows.astype(jnp.bfloat16), grad_scores)


def body(
    tokens,
    log_decay,
    norm_gain,
    qkv_proj,
    attn_proj,
    inner_proj,
    conv_weight,
    conv_bias,
    step_bias,
    skip_gain,
    inner_gain,
    inner_out,
    ff_gain,
    gate_up,
    down_proj,
    cotangent,
):
    head_count = lax.axis_size("head")
    seq_index = lax.axis_index("seq")
    (
        gain_in,
        qkv_full,
        attn_full,
        inner_full,
        conv_full,
        conv_bias_full,
        inner_gain_full,
        out_full,
        ff_gain_full,
        gate_up_full,
        down_full,
    ) = (
        lax.all_gather(norm_gain, ("head", "seq"), axis=0, tiled=True),
        lax.all_gather(qkv_proj, ("head", "seq"), axis=0, tiled=True),
        lax.all_gather(attn_proj, ("head", "seq"), axis=1, tiled=True),
        lax.all_gather(inner_proj, ("head", "seq"), axis=0, tiled=True),
        lax.all_gather(conv_weight, ("head", "seq"), axis=1, tiled=True),
        lax.all_gather(conv_bias, ("head", "seq"), axis=0, tiled=True),
        lax.all_gather(inner_gain, ("head", "seq"), axis=0, tiled=True),
        lax.all_gather(inner_out, ("head", "seq"), axis=1, tiled=True),
        lax.all_gather(ff_gain, ("head", "seq"), axis=0, tiled=True),
        lax.all_gather(gate_up, ("head", "seq"), axis=0, tiled=True),
        lax.all_gather(down_proj, ("head", "seq"), axis=1, tiled=True),
    )
    local_seqs, block_rows, model_width = tokens.shape
    token_rows = local_seqs * block_rows
    inner_width = MH * MP
    conv_width = inner_width + 2 * NS
    groups = QH // KVH
    kv_local = KVH // head_count
    inner_local = MH // head_count
    all_seqs = local_seqs * head_count
    score_scale = HD ** (-0.5)
    key_limit = (seq_index + 1) * block_rows
    x_rows = tokens.astype(jnp.float32).reshape(token_rows, model_width)
    normed_f, norm_back = jax.vjp(rms_norm, x_rows, gain_in.astype(jnp.float32))
    normed = normed_f.astype(jnp.bfloat16)
    qkv_rows = jnp.dot(normed, qkv_full, preferred_element_type=jnp.float32).reshape(
        local_seqs, block_rows, -1
    )
    positions = (seq_index * block_rows + jnp.arange(block_rows)).astype(jnp.float32)
    query_send = rotary(
        qkv_rows[..., : QH * HD].reshape(local_seqs, block_rows, QH, HD), positions
    ).astype(jnp.bfloat16)
    key_send = rotary(
        qkv_rows[..., QH * HD : (QH + KVH) * HD].reshape(local_seqs, block_rows, KVH, HD), positions
    ).astype(jnp.bfloat16)
    value_send = qkv_rows[..., (QH + KVH) * HD :].astype(jnp.bfloat16)
    inner_raw = jnp.dot(normed, inner_full, preferred_element_type=jnp.float32).reshape(
        local_seqs, block_rows, -1
    )
    gate_z = inner_raw[..., :inner_width]
    conv_in = inner_raw[..., inner_width : inner_width + conv_width]
    step_send = inner_raw[..., inner_width + conv_width :].astype(jnp.bfloat16)
    rim_rows = passed_along(
        conv_in[:, block_rows - (KC - 1) :, :].astype(jnp.bfloat16), "seq", 1
    ).astype(jnp.float32)
    padded = jnp.concatenate([rim_rows, conv_in], axis=1)

    def convolve(padded_in, weight_taps, bias_taps):
        conv_sum = bias_taps
        for conv_tap in range(KC):
            conv_sum = (
                conv_sum + weight_taps[conv_tap] * padded_in[:, conv_tap : conv_tap + block_rows, :]
            )
        return jax.nn.silu(conv_sum)

    activated, conv_back = jax.vjp(
        convolve, padded, conv_full.astype(jnp.float32), conv_bias_full.astype(jnp.float32)
    )
    activated_send = activated.astype(jnp.bfloat16)

    def split_heads(value):
        return value.reshape(value.shape[:2] + (head_count, -1))

    map_copies = jnp.broadcast_to(
        activated_send[:, :, None, inner_width:], (local_seqs, block_rows, head_count, 2 * NS)
    )
    received = (
        lax.all_to_all(split_heads(query_send), "head", split_axis=2, concat_axis=0, tiled=True),
        lax.all_to_all(split_heads(key_send), "head", split_axis=2, concat_axis=0, tiled=True),
        lax.all_to_all(split_heads(value_send), "head", split_axis=2, concat_axis=0, tiled=True),
        lax.all_to_all(
            split_heads(activated_send[..., :inner_width]),
            "head",
            split_axis=2,
            concat_axis=0,
            tiled=True,
        ),
        lax.all_to_all(split_heads(step_send), "head", split_axis=2, concat_axis=0, tiled=True),
        lax.all_to_all(map_copies, "head", split_axis=2, concat_axis=0, tiled=True),
    )
    queries = received[0].reshape(all_seqs, block_rows, kv_local, groups, HD)
    key_heads = received[1]
    value_heads = received[2]
    inner_x = received[3].reshape(all_seqs, block_rows, inner_local, MP).astype(jnp.float32)
    step_in = received[4].reshape(all_seqs, block_rows, inner_local).astype(jnp.float32)
    state_maps = received[5].reshape(all_seqs, block_rows, 2 * NS).astype(jnp.float32)
    query_pos = seq_index * block_rows + jnp.arange(block_rows)
    key_all, value_all = (
        lax.all_gather(key_heads, "seq", axis=1, tiled=True),
        lax.all_gather(value_heads, "seq", axis=1, tiled=True),
    )

    def attend_step(carried, pair, offset):
        return attend_block(carried, pair, offset, queries, query_pos, score_scale)

    stat_shape = (all_seqs, block_rows, kv_local, groups)
    start_stats = (
        jnp.full(stat_shape, NEGATIVE, jnp.float32),
        jnp.zeros(stat_shape, jnp.float32),
        jnp.zeros(stat_shape + (HD,), jnp.float32),
    )
    row_top, row_total, accumulated = over_blocks(
        attend_step, start_stats, (key_all, value_all), 0, key_limit
    )
    attended_f = accumulated / row_total[..., None]
    log_total = row_top + jnp.log(row_total)

    def state_part(piece_x, piece_step, piece_maps, piece_bias):
        return inner_state(piece_x, piece_step, piece_maps, piece_bias, log_decay)

    def output_part(piece_x, piece_step, piece_maps, piece_bias, piece_skip, piece_state):
        return inner_output(
            piece_x, piece_step, piece_maps, piece_bias, piece_skip, piece_state, log_decay
        )

    fresh_state, state_back = jax.vjp(state_part, inner_x, step_in, state_maps, step_bias)
    block_fall = block_decay(log_decay)

    def chain_rule(earlier, later):
        return (earlier[0] * later[0], later[1] + later[0][:, :, None, None] * earlier[1])

    neutral = (jnp.ones_like(block_fall), jnp.zeros_like(fresh_state))
    state_in = carried_in((block_fall, fresh_state), "seq", chain_rule, neutral)[1]
    inner_y, output_back = jax.vjp(
        output_part, inner_x, step_in, state_maps, step_bias, skip_gain, state_in
    )
    returned = (
        lax.all_to_all(
            attended_f.astype(jnp.bfloat16).reshape(all_seqs, block_rows, 1, -1),
            "head",
            split_axis=0,
            concat_axis=2,
            tiled=True,
        ),
        lax.all_to_all(
            inner_y.astype(jnp.bfloat16).reshape(all_seqs, block_rows, 1, -1),
            "head",
            split_axis=0,
            concat_axis=2,
            tiled=True,
        ),
    )
    attended = returned[0].reshape(token_rows, QH * HD)
    inner_back_y = returned[1].reshape(local_seqs, block_rows, inner_width).astype(jnp.float32)

    def gated_norm(y_part, gate_part, gain_part):
        return rms_norm(y_part * jax.nn.silu(gate_part), gain_part)

    inner_normed_f, gated_back = jax.vjp(
        gated_norm, inner_back_y, gate_z, inner_gain_full.astype(jnp.float32)
    )
    inner_normed = inner_normed_f.astype(jnp.bfloat16).reshape(token_rows, inner_width)
    hidden = (
        x_rows
        + jnp.dot(attended, attn_full, preferred_element_type=jnp.float32)
        + jnp.dot(inner_normed, out_full, preferred_element_type=jnp.float32)
    )
    normed_ff_f, ff_back = jax.vjp(rms_norm, hidden, ff_gain_full.astype(jnp.float32))
    normed_ff = normed_ff_f.astype(jnp.bfloat16)
    gate_vals = jnp.dot(normed_ff, gate_up_full, preferred_element_type=jnp.float32)

    def swiglu(values_in):
        return jax.nn.silu(values_in[:, :FF]) * values_in[:, FF:]

    mixed_f, swiglu_back = jax.vjp(swiglu, gate_vals)
    mixed_rows = mixed_f.astype(jnp.bfloat16)
    output = (
        (hidden + jnp.dot(mixed_rows, down_full, preferred_element_type=jnp.float32))
        .astype(jnp.bfloat16)
        .reshape(tokens.shape)
    )
    grad_out = cotangent.reshape(token_rows, model_width)
    grad_down = jnp.einsum("rf,rd->fd", mixed_rows, grad_out, preferred_element_type=jnp.float32)
    grad_gate_vals = swiglu_back(
        jnp.einsum("rd,fd->rf", grad_out, down_full, preferred_element_type=jnp.float32)
    )[0].astype(jnp.bfloat16)
    grad_gate_up = jnp.einsum(
        "rd,re->de", normed_ff, grad_gate_vals, preferred_element_type=jnp.float32
    )
    grad_hidden_norm, grad_ff_gain = ff_back(
        jnp.einsum("re,de->rd", grad_gate_vals, gate_up_full, preferred_element_type=jnp.float32)
    )
    grad_hidden = grad_out.astype(jnp.float32) + grad_hidden_norm
    grad_branch = grad_hidden.astype(jnp.bfloat16)
    grad_attn = jnp.einsum("rc,rd->cd", attended, grad_branch, preferred_element_type=jnp.float32)
    grad_inner_out = jnp.einsum(
        "rc,rd->cd", inner_normed, grad_branch, preferred_element_type=jnp.float32
    )
    grad_attended = jnp.einsum(
        "rd,cd->rc", grad_branch, attn_full, preferred_element_type=jnp.float32
    ).astype(jnp.bfloat16)
    grad_y, grad_gate_z, grad_inner_gain = gated_back(
        jnp.einsum("rd,cd->rc", grad_branch, out_full, preferred_element_type=jnp.float32).reshape(
            local_seqs, block_rows, inner_width
        )
    )
    sent_grads = (
        lax.all_to_all(
            split_heads(grad_attended.reshape(local_seqs, block_rows, QH * HD)),
            "head",
            split_axis=2,
            concat_axis=0,
            tiled=True,
        ),
        lax.all_to_all(
            split_heads(grad_y.astype(jnp.bfloat16)),
            "head",
            split_axis=2,
            concat_axis=0,
            tiled=True,
        ),
    )
    grad_heads = sent_grads[0].reshape(all_seqs, block_rows, kv_local, groups, HD)
    grad_inner_y = sent_grads[1].reshape(all_seqs, block_rows, inner_local, MP).astype(jnp.float32)
    row_delta = jnp.sum(grad_heads.astype(jnp.float32) * attended_f, axis=-1)

    def query_step(carried, pair, offset):
        prob_rows, grad_scores = score_grads(
            queries,
            grad_heads,
            log_total,
            row_delta,
            pair[0],
            pair[1],
            offset,
            query_pos,
            score_scale,
        )
        return carried + jnp.einsum(
            "sqkgj,sjkd->sqkgd", grad_scores, pair[0], preferred_element_type=jnp.float32
        )

    grad_queries = (
        over_blocks(query_step, jnp.zeros_like(attended_f), (key_all, value_all), 0, key_limit)
        * score_scale
    )
    count = block_rows * lax.axis_size("seq")
    step_rows = math.gcd(count, 1024)
    term_shape = (step_rows, all_seqs, kv_local, 2 * HD)

    def compute_block(offset):
        key_blk = lax.dynamic_slice_in_dim(key_all, offset, step_rows, 1)
        value_blk = lax.dynamic_slice_in_dim(value_all, offset, step_rows, 1)
        prob_rows, grad_scores = score_grads(
            queries,
            grad_heads,
            log_total,
            row_delta,
            key_blk,
            value_blk,
            offset,
            query_pos,
            score_scale,
        )
        grad_keys = (
            jnp.einsum(
                "sqkgj,sqkgd->jskd", grad_scores, queries, preferred_element_type=jnp.float32
            )
            * score_scale
        )
        grad_values = jnp.einsum(
            "sqkgj,sqkgd->jskd", prob_rows, grad_heads, preferred_element_type=jnp.float32
        )
        return jnp.concatenate([grad_keys, grad_values], axis=-1)

    def one_block(offset):
        return lax.cond(
            offset < key_limit,
            compute_block,
            lambda unused: jnp.zeros(term_shape, jnp.float32),
            offset,
        )

    block_terms = lax.map(
        lambda number: one_block(number * step_rows), jnp.arange(count // step_rows)
    )
    key_grads = lax.psum_scatter(
        block_terms.reshape((count,) + block_terms.shape[2:]),
        "seq",
        scatter_dimension=0,
        tiled=True,
    )
    grad_key_heads = jnp.moveaxis(key_grads[..., :HD], 0, 1)
    grad_value_heads = jnp.moveaxis(key_grads[..., HD:], 0, 1)
    grad_x_a, grad_step_a, grad_maps_a, grad_bias_a, grad_skip, grad_state = output_back(
        grad_inner_y
    )
    grad_carry = entering((block_fall, grad_state), "seq", chain_rule, neutral)[1]
    grad_x_b, grad_step_b, grad_maps_b, grad_bias_b = state_back(grad_carry)
    grad_step_bias, grad_skip_gain = lax.psum((grad_bias_a + grad_bias_b, grad_skip), "seq")
    returned_grads = (
        lax.all_to_all(
            grad_queries.reshape(all_seqs, block_rows, 1, -1).astype(jnp.bfloat16),
            "head",
            split_axis=0,
            concat_axis=2,
            tiled=True,
        ).astype(jnp.float32),
        lax.all_to_all(
            grad_key_heads.astype(jnp.bfloat16), "head", split_axis=0, concat_axis=2, tiled=True
        ).astype(grad_key_heads.dtype),
        lax.all_to_all(
            grad_value_heads.astype(jnp.bfloat16), "head", split_axis=0, concat_axis=2, tiled=True
        ).astype(grad_value_heads.dtype),
        lax.all_to_all(
            (grad_x_a + grad_x_b).reshape(all_seqs, block_rows, 1, -1).astype(jnp.bfloat16),
            "head",
            split_axis=0,
            concat_axis=2,
            tiled=True,
        ).astype(jnp.float32),
        lax.all_to_all(
            (grad_step_a + grad_step_b).reshape(all_seqs, block_rows, 1, -1).astype(jnp.bfloat16),
            "head",
            split_axis=0,
            concat_axis=2,
            tiled=True,
        ).astype(jnp.float32),
        lax.all_to_all(
            (grad_maps_a + grad_maps_b)[:, :, None, :].astype(jnp.bfloat16),
            "head",
            split_axis=0,
            concat_axis=2,
            tiled=True,
        ).astype(jnp.float32),
    )
    grad_q = rounded(returned_grads[0].reshape(local_seqs, block_rows, QH, HD))
    grad_k = rounded(returned_grads[1])
    grad_v = returned_grads[2].reshape(token_rows, KVH * HD)
    grad_qkv_rows = jnp.concatenate(
        [
            rotary(grad_q, -positions).reshape(token_rows, -1),
            rotary(grad_k, -positions).reshape(token_rows, -1),
            grad_v,
        ],
        axis=-1,
    ).astype(jnp.bfloat16)
    grad_x_in = rounded(returned_grads[3].reshape(local_seqs, block_rows, inner_width))
    grad_step = rounded(returned_grads[4].reshape(token_rows, MH))
    grad_maps = rounded(jnp.sum(returned_grads[5], axis=2))
    grad_padded, grad_conv_weight, grad_conv_bias = conv_back(
        jnp.concatenate([grad_x_in, grad_maps], axis=-1)
    )
    rim_grad = passed_along(shortened(grad_padded[:, : KC - 1, :]), "seq", -1)
    grad_conv_in = grad_padded[:, KC - 1 :, :].at[:, block_rows - (KC - 1) :, :].add(rim_grad)
    grad_inner_rows = jnp.concatenate(
        [grad_gate_z.reshape(token_rows, -1), grad_conv_in.reshape(token_rows, -1), grad_step],
        axis=-1,
    ).astype(jnp.bfloat16)
    grad_qkv_weight = jnp.einsum(
        "rd,re->de", normed, grad_qkv_rows, preferred_element_type=jnp.float32
    )
    grad_inner_weight = jnp.einsum(
        "rd,re->de", normed, grad_inner_rows, preferred_element_type=jnp.float32
    )
    grad_normed = jnp.einsum(
        "re,de->rd", grad_qkv_rows, qkv_full, preferred_element_type=jnp.float32
    ) + jnp.einsum("re,de->rd", grad_inner_rows, inner_full, preferred_element_type=jnp.float32)
    grad_x_norm, grad_norm_gain = norm_back(grad_normed)
    grad_tokens = (grad_hidden + grad_x_norm).reshape(tokens.shape)
    weight_grads = (
        grad_norm_gain,
        grad_qkv_weight,
        grad_attn,
        grad_inner_weight,
        grad_conv_weight,
        grad_conv_bias,
        grad_inner_gain,
        grad_inner_out,
        grad_ff_gain,
        grad_gate_up,
        grad_down,
    )
    shares = (
        lax.psum_scatter(weight_grads[0], ("head", "seq"), scatter_dimension=0, tiled=True),
        lax.psum_scatter(weight_grads[1], ("head", "seq"), scatter_dimension=0, tiled=True),
        lax.psum_scatter(weight_grads[2], ("head", "seq"), scatter_dimension=1, tiled=True),
        lax.psum_scatter(weight_grads[3], ("head", "seq"), scatter_dimension=0, tiled=True),
        lax.psum_scatter(weight_grads[4], ("head", "seq"), scatter_dimension=1, tiled=True),
        lax.psum_scatter(weight_grads[5], ("head", "seq"), scatter_dimension=0, tiled=True),
        lax.psum_scatter(weight_grads[6], ("head", "seq"), scatter_dimension=0, tiled=True),
        lax.psum_scatter(weight_grads[7], ("head", "seq"), scatter_dimension=1, tiled=True),
        lax.psum_scatter(weight_grads[8], ("head", "seq"), scatter_dimension=0, tiled=True),
        lax.psum_scatter(weight_grads[9], ("head", "seq"), scatter_dimension=0, tiled=True),
        lax.psum_scatter(weight_grads[10], ("head", "seq"), scatter_dimension=1, tiled=True),
    )
    return (
        output,
        grad_tokens,
        shares[0],
        shares[1],
        shares[2],
        shares[3],
        shares[4],
        shares[5],
        grad_step_bias,
        grad_skip_gain,
        shares[6],
        shares[7],
        shares[8],
        shares[9],
        shares[10],
    )


BLOCK = 128
BIT_C, BIT_ZH, BIT_ZL, BIT_Y, BIT_X = 16, 8, 4, 2, 1
DEVICES = 32
BOTH = ("head", "half", "cube")
GROUP = ("head", "cube")
CUBE_ORDERS = ((0, 1, 2), (1, 2, 0), (2, 0, 1))
CUBE_BITS = (BIT_ZL, BIT_Y, BIT_X)
bf16 = jnp.bfloat16
f32 = jnp.float32


def flip(value, mask):
    return lax.ppermute(value, BOTH, [(i, i ^ mask) for i in range(DEVICES)])


def swap_sequences(value):
    pairs = []
    for i in range(DEVICES):
        core, half = (i // BIT_C) % 2, (i // BIT_ZH) % 2
        if core != half:
            pairs.append((i, i ^ (BIT_C + BIT_ZH)))
    stays = lax.axis_index("head") == lax.axis_index("half")
    return jnp.where(stays, value, lax.ppermute(value, BOTH, pairs))


def joint(*values):
    return lax.optimization_barrier(values)


def column_parts(width):
    lanes = width // 128
    first = -(-lanes // 3)
    second = -(-(lanes - first) // 2)
    edges = (0, first * 128, (first + second) * 128, width)
    return [(edges[i], edges[i + 1]) for i in range(3)]


def assemble(pieces, outputs, info):
    count, made = len(pieces), len(outputs)
    moves = [(to, *move) for to, (_, _, out_moves) in enumerate(outputs) for move in out_moves]

    def kernel(info_ref, *refs):
        sems = refs[count + made]
        copies = []
        for at, (to, number, source, target) in enumerate(moves):
            copies.append(
                pltpu.make_async_copy(
                    refs[number].at[source(info_ref)],
                    refs[count + to].at[target(info_ref)],
                    sems.at[at],
                )
            )
        for copy in copies:
            copy.start()
        for copy in copies:
            copy.wait()

    size = sum(math.prod(shape) * jnp.dtype(kind).itemsize for shape, kind, _ in outputs)
    return pl.pallas_call(
        kernel,
        in_specs=[pl.BlockSpec(memory_space=pltpu.SMEM)]
        + [pl.BlockSpec(memory_space=pltpu.HBM)] * count,
        out_specs=[pl.BlockSpec(memory_space=pltpu.VMEM)] * made,
        out_shape=[jax.ShapeDtypeStruct(shape, kind) for shape, kind, _ in outputs],
        scratch_shapes=[pltpu.SemaphoreType.DMA((len(moves),))],
        compiler_params=pltpu.CompilerParams(vmem_limit_bytes=2 * size + 8 * 1024 * 1024),
        cost_estimate=LITTLE,
        name="assemble",
    )(info, *pieces)


def reordered_rows(value, info):
    moves = []
    for block in range(value.shape[0] // BLOCK):

        def goal(ref, block=block):
            row = pl.multiple_of((ref[2] ^ block) * BLOCK, BLOCK)
            return (pl.ds(row, BLOCK), slice(None))

        moves.append((0, fixed(block * BLOCK, BLOCK, 0, value.shape[1]), goal))
    return assemble([value], [(value.shape, value.dtype, moves)], info)[0]


def fixed(row, rows, column, columns):
    return lambda info: (pl.ds(row, rows), pl.ds(column, columns))


class Gather:
    def __init__(self, value, edges, info):
        self.rows, self.width, self.step = value.shape[0], value.shape[1], 0
        self.edges, self.info = edges, info
        self.joined = None
        self.state = ([value[:, a:b] for a, b in edges], None)

    def hop(self):
        parts, received = self.state
        if received is not None:
            parts = self.stacked(parts, received)
        sent = [
            flip(part, CUBE_BITS[order[self.step]]) for part, order in zip(parts, CUBE_ORDERS)
        ]
        self.state = (parts, sent)
        self.step += 1

    def stacked(self, parts, received):
        rows = parts[0].shape[0]
        outputs, side = [], []
        for i, (a, b) in enumerate(self.edges):
            own, got = fixed(0, rows, 0, b - a), fixed(rows, rows, 0, b - a)
            outputs.append(((2 * rows, b - a), bf16, [(i, own, own), (3 + i, own, got)]))
            side.append((i, own, fixed(0, rows, a, b - a)))
            side.append((3 + i, own, fixed(rows, rows, a, b - a)))
        if self.step == 2:
            outputs.append(((2 * rows, self.width), bf16, side))
        result = assemble(parts + received, outputs, self.info)
        if self.step == 2:
            self.joined = result[3]
        return list(result[:3])

    def pieces(self):
        while self.step < 3:
            self.hop()
        near, far = self.state
        side = [(i, fixed(0, 4 * self.rows, 0, b - a), fixed(0, 4 * self.rows, a, b - a)) for i, (a, b) in enumerate(self.edges)]
        (far_joined,) = assemble(
            far, [((4 * self.rows, self.width), bf16, side)], self.info
        )
        crossed = [flip(self.joined, BIT_C), flip(far_joined, BIT_C)]
        return near + far + crossed


def piece_blocks(part, far):
    axes = [CUBE_BITS[axis] for axis in CUBE_ORDERS[part]]
    return [
        (block, (block % 2) * axes[0] + (block // 2) * axes[1] + far * axes[2], 1)
        for block in range(4)
    ]


def gathered(gather, width, info):
    rows = gather.rows
    pieces = gather.pieces()
    moves = []
    for group in range(4):
        half, far = group // 2, group % 2
        for part, (a, b) in enumerate(column_parts(width)):
            number = 3 * group + part if half == 0 else 6 + far
            for first, place, blocks in piece_blocks(part, far):
                moves.append(
                    (
                        number,
                        fixed(first * rows, blocks * rows, a * half, b - a),
                        fixed((half * 8 + place) * rows, blocks * rows, a, b - a),
                    )
                )
    return assemble(pieces, [((16 * rows, width), bf16, moves)], info)[0]


def gather_start(value, info):
    return Gather(value, column_parts(value.shape[1]), info)


class Scatter:
    def __init__(self, own_half, other_half):
        self.total_rows, self.width = own_half.shape
        self.step = 0
        self.state = (own_half, flip(other_half.astype(bf16), BIT_C))

    def pairs(self):
        kept, received = self.state
        if self.step == 0:
            shape = (2, 2, 2, self.total_rows // 8, self.width)
            edges = column_parts(self.width)
            kept = [kept.reshape(shape)[..., a:b] for a, b in edges]
            received = [received.reshape(shape)[..., a:b] for a, b in edges]
        halves = []
        for part, got, order in zip(kept, received, CUBE_ORDERS):
            axis = order[self.step]
            halves.append(
                [
                    (
                        lax.slice_in_dim(part, i, i + 1, axis=axis).astype(f32)
                        + lax.slice_in_dim(got, i, i + 1, axis=axis).astype(f32)
                    ).astype(bf16)
                    for i in (0, 1)
                ]
            )
        return halves

    def hop(self):
        halves = self.pairs()
        sent = [
            flip(far, CUBE_BITS[order[self.step]])
            for (_, far), order in zip(halves, CUBE_ORDERS)
        ]
        self.state = ([near for near, _ in halves], sent)
        self.step += 1

    def then(self, *values):
        near, sent = self.state
        near, values = joint(near, values)
        self.state = (near, sent)
        return values

    def result(self):
        while self.step < 3:
            self.hop()
        rows = self.total_rows // 8
        return jnp.concatenate(
            [
                (near.astype(f32) + got.astype(f32)).reshape(rows, -1)
                for near, got in zip(*self.state)
            ],
            axis=1,
        )


def group_sum(value):
    for masks in ((BIT_C, BIT_X, BIT_C + BIT_X), (BIT_Y, BIT_ZL, BIT_Y + BIT_ZL)):
        first, second, third = [flip(value, mask) for mask in masks]
        value = (value + first) + (second + third)
    return value


def exchange(value):
    return lax.all_to_all(value, GROUP, split_axis=0, concat_axis=0, tiled=True)


def mm(a, b):
    return jnp.dot(a, b, preferred_element_type=f32)


def mm_nt(a, b):
    return lax.dot_general(a, b, (((1,), (1,)), ((), ())), preferred_element_type=f32)


def mm_tn(a, b):
    return lax.dot_general(a, b, (((0,), (0,)), ((), ())), preferred_element_type=f32)


VMEM_ASK = 40 * 1024 * 1024
LITTLE = pl.CostEstimate(flops=1000, bytes_accessed=1000, transcendentals=0)


def params():
    return pltpu.CompilerParams(
        dimension_semantics=("arbitrary",), vmem_limit_bytes=VMEM_ASK
    )


def k_nt(a, b, precision=None):
    return lax.dot_general(
        a, b, (((1,), (1,)), ((), ())), preferred_element_type=f32, precision=precision
    )


def k_tn(a, b):
    return lax.dot_general(a, b, (((0,), (0,)), ((), ())), preferred_element_type=f32)


def k_mm(a, b, precision=None):
    return lax.dot_general(
        a, b, (((1,), (0,)), ((), ())), preferred_element_type=f32, precision=precision
    )


def logistic(value):
    return 1.0 / (1.0 + jnp.exp(-value))


def by_head(columns, lane):
    spread = columns[:, 0:1]
    for head in range(1, HEADS_HERE):
        spread = jnp.where(lane >= head * MP, columns[:, head : head + 1], spread)
    return spread


def shifted_sum(padded, taps, start, step):
    total = None
    for tap in range(KC):
        at = start + step * tap
        term = taps[tap : tap + 1] * padded[at : at + BLOCK]
        total = term if total is None else total + term
    return total


HEADS_HERE = 3
OWN = HEADS_HERE * MP
TAIL = 16
KEYS_AT = 2 * NS


def block_decays(cum_col, cum_row, lane):
    cum = by_head(cum_col, lane)
    last = cum[BLOCK - 1 : BLOCK]
    row = lax.broadcasted_iota(jnp.int32, (BLOCK, BLOCK), 0)
    col = lax.broadcasted_iota(jnp.int32, (BLOCK, BLOCK), 1)
    reach = []
    for head in range(HEADS_HERE):
        spread = cum_col[:, head : head + 1] - cum_row[head : head + 1, :]
        reach.append(jnp.where(row >= col, jnp.exp(jnp.minimum(spread, 0.0)), 0.0))
    return cum, last, reach


def step_lanes(place, lane):
    source = lax.broadcasted_iota(jnp.int32, (128, OWN), 0)
    head = lax.broadcasted_iota(jnp.int32, (128, OWN), 1) // MP
    return jnp.where(source == place * HEADS_HERE + head, 1.0, 0.0)


def mix_forward(
    info,
    own_ref,
    s_ref,
    cos_ref,
    sin_ref,
    cum_col_ref,
    cum_row_ref,
    taps_x_ref,
    taps_m_ref,
    vec_ref,
    y_ref,
    gained_ref,
    square_ref,
    state_ref,
    q_ref,
    k_ref,
    v_ref,
    state,
    last_x,
    last_m,
):
    @pl.when(pl.program_id(0) == 0)
    def _():
        state[...] = jnp.zeros_like(state)
        last_x[...] = jnp.zeros_like(last_x)
        last_m[...] = jnp.zeros_like(last_m)

    lane = lax.broadcasted_iota(jnp.int32, (1, OWN), 1)
    gate = own_ref[:, :OWN].astype(f32)
    x_raw = own_ref[:, OWN : 2 * OWN].astype(f32)
    m_raw = s_ref[:, : 2 * NS].astype(f32)
    cosine, sine = cos_ref[...], sin_ref[...]

    def turned(value):
        return (value * cosine + pltpu.roll(value, HD // 2, 1) * sine).astype(bf16)

    q_ref[...] = turned(own_ref[:, 2 * OWN :].astype(f32))
    k_ref[...] = turned(s_ref[:, KEYS_AT : KEYS_AT + HD].astype(f32))
    v_ref[...] = s_ref[:, KEYS_AT + HD : KEYS_AT + 2 * HD].astype(bf16)

    s_x = shifted_sum(
        jnp.concatenate([last_x[...], x_raw], axis=0), taps_x_ref, TAIL - KC + 1, 1
    ) + taps_x_ref[KC : KC + 1]
    s_m = shifted_sum(
        jnp.concatenate([last_m[...], m_raw], axis=0), taps_m_ref, TAIL - KC + 1, 1
    ) + taps_m_ref[KC : KC + 1]
    last_x[...] = x_raw[BLOCK - TAIL :]
    last_m[...] = m_raw[BLOCK - TAIL :]
    x = (s_x * logistic(s_x)).astype(bf16).astype(f32)
    maps = (s_m * logistic(s_m)).astype(bf16)
    b_map, c_map = maps[:, :NS], maps[:, NS:]

    place = info[0]
    picked = k_mm(s_ref[:, KEYS_AT + 2 * HD :].astype(bf16), step_lanes(place, lane).astype(bf16))
    raised = picked + vec_ref[0:1]
    step = jnp.maximum(raised, 0.0) + jnp.log(1.0 + jnp.exp(-jnp.abs(raised)))
    cum, last, reach = block_decays(cum_col_ref[...], cum_row_ref[0], lane)
    scaled = step * x
    inter = k_nt(c_map, b_map)
    total = vec_ref[1:2] * x
    for head in range(HEADS_HERE):
        here = (lane >= head * MP) & (lane < (head + 1) * MP)
        total += k_mm(
            (reach[head] * inter).astype(bf16), jnp.where(here, scaled, 0.0).astype(bf16)
        )
    before = state[...]
    state_ref[0] = before.astype(bf16)
    total += jnp.exp(cum) * k_mm(c_map, before.astype(bf16))
    tail = (jnp.exp(last - cum) * scaled).astype(bf16)
    state[...] = jnp.exp(last) * before + k_tn(b_map, tail)
    y = total.astype(bf16)
    y_ref[...] = y
    gated = y.astype(f32) * (gate * logistic(gate))
    gained_ref[...] = (gated * vec_ref[2:3]).astype(bf16)
    square_ref[0] = k_nt(jnp.ones((8, OWN), f32), gated * gated, HIGHEST)


def mix_backward(
    info,
    own_ref,
    s_ref,
    own_tail_ref,
    s_tail_ref,
    cos_ref,
    sin_ref,
    cum_col_ref,
    cum_row_ref,
    taps_x_ref,
    taps_m_ref,
    vec_ref,
    lanes_ref,
    g_y_ref,
    g_z_ref,
    state_ref,
    dq_ref,
    dk_ref,
    dv_ref,
    g_all_ref,
    acc_x_ref,
    acc_m_ref,
    acc_v_ref,
    acc_s_ref,
    g_state,
    next_x,
    next_m,
):
    step_id = pl.program_id(0)
    block = pl.num_programs(0) - 1 - step_id
    place = info[0]

    @pl.when(step_id == 0)
    def _():
        g_state[...] = jnp.zeros_like(g_state)
        next_x[...] = jnp.zeros_like(next_x)
        next_m[...] = jnp.zeros_like(next_m)
        acc_x_ref[...] = jnp.zeros_like(acc_x_ref)
        acc_m_ref[...] = jnp.zeros_like(acc_m_ref)
        acc_v_ref[...] = jnp.zeros_like(acc_v_ref)
        acc_s_ref[...] = jnp.zeros_like(acc_s_ref)

    lane = lax.broadcasted_iota(jnp.int32, (1, OWN), 1)
    cosine, sine = cos_ref[...], sin_ref[...]

    def unturned(value):
        return value * cosine - pltpu.roll(value, HD // 2, 1) * sine

    x_raw = own_ref[:, OWN : 2 * OWN].astype(f32)
    m_raw = s_ref[:, : 2 * NS].astype(f32)
    first = block == 0
    x_pad = jnp.concatenate(
        [jnp.where(first, 0.0, own_tail_ref[:, OWN : 2 * OWN].astype(f32)), x_raw], axis=0
    )
    m_pad = jnp.concatenate([jnp.where(first, 0.0, s_tail_ref[:, : 2 * NS].astype(f32)), m_raw], axis=0)
    s_x = shifted_sum(x_pad, taps_x_ref, TAIL - KC + 1, 1) + taps_x_ref[KC : KC + 1]
    s_m = shifted_sum(m_pad, taps_m_ref, TAIL - KC + 1, 1) + taps_m_ref[KC : KC + 1]
    sig_x, sig_m = logistic(s_x), logistic(s_m)
    x = (s_x * sig_x).astype(bf16).astype(f32)
    maps = (s_m * sig_m).astype(bf16)
    b_map, c_map = maps[:, :NS], maps[:, NS:]
    select = step_lanes(place, lane)
    step_raw = s_ref[:, KEYS_AT + 2 * HD :].astype(bf16)
    raised = k_mm(step_raw, select.astype(bf16)) + vec_ref[0:1]
    step = jnp.maximum(raised, 0.0) + jnp.log(1.0 + jnp.exp(-jnp.abs(raised)))
    cum, last, reach = block_decays(cum_col_ref[...], cum_row_ref[0], lane)
    scaled = step * x

    g_y = g_y_ref[...].astype(f32)

    inter = k_nt(c_map, b_map)
    g_inter = jnp.zeros((BLOCK, BLOCK), f32)
    g_scaled = jnp.zeros((BLOCK, OWN), f32)
    scaled_b = scaled.astype(bf16)
    for head in range(HEADS_HERE):
        here = (lane >= head * MP) & (lane < (head + 1) * MP)
        g_head = jnp.where(here, g_y, 0.0).astype(bf16)
        g_inter += reach[head] * k_nt(g_head, scaled_b)
        g_scaled += k_tn((reach[head] * inter).astype(bf16), g_head)
    before = state_ref[0]
    g_after = g_state[...]
    g_after_b = g_after.astype(bf16)
    tail_w = jnp.exp(last - cum)
    reached = (jnp.exp(cum) * g_y).astype(bf16)
    g_inter_b = g_inter.astype(bf16)
    g_c = k_mm(g_inter_b, b_map) + k_nt(reached, before)
    g_b = k_tn(g_inter_b, c_map) + k_nt((tail_w * scaled).astype(bf16), g_after_b)
    g_scaled += tail_w * k_mm(b_map, g_after_b)
    g_state[...] = jnp.exp(last) * g_after + k_tn(c_map, reached)
    g_x = step * g_scaled + vec_ref[1:2] * g_y
    g_step = k_nt(x * g_scaled, select, HIGHEST) * logistic(
        step_raw.astype(f32) + lanes_ref[0:1]
    )

    gs_x = g_x.astype(bf16).astype(f32) * (sig_x * (1.0 + s_x * (1.0 - sig_x)))
    g_maps = jnp.concatenate([g_b, g_c], axis=1).astype(bf16).astype(f32)
    gs_m = g_maps * (sig_m * (1.0 + s_m * (1.0 - sig_m)))
    gs_x_pad = jnp.concatenate([gs_x, next_x[...]], axis=0)
    gs_m_pad = jnp.concatenate([gs_m, next_m[...]], axis=0)
    g_x_raw = shifted_sum(gs_x_pad, taps_x_ref, KC - 1, -1)
    g_m_raw = shifted_sum(gs_m_pad, taps_m_ref, KC - 1, -1)
    next_x[...] = gs_x[:TAIL]
    next_m[...] = gs_m[:TAIL]
    for tap in range(KC):
        at = TAIL - KC + 1 + tap
        acc_x_ref[tap : tap + 1] += jnp.sum(gs_x * x_pad[at : at + BLOCK], axis=0, keepdims=True)
        acc_m_ref[tap : tap + 1] += jnp.sum(gs_m * m_pad[at : at + BLOCK], axis=0, keepdims=True)
    acc_x_ref[KC : KC + 1] += jnp.sum(gs_x, axis=0, keepdims=True)
    acc_m_ref[KC : KC + 1] += jnp.sum(gs_m, axis=0, keepdims=True)
    acc_v_ref[0:1] += jnp.sum(g_y * x, axis=0, keepdims=True)
    acc_s_ref[0:1] += jnp.sum(g_step, axis=0, keepdims=True)

    here = (block // 8) == info[1]
    g_q = jnp.where(here, dq_ref[...].astype(f32), 0.0)
    at = 2 * OWN
    g_all_ref[:, :at] = jnp.concatenate([g_z_ref[...].astype(f32), g_x_raw], axis=1).astype(bf16)
    for piece in (g_q, g_m_raw, unturned(dk_ref[...]), dv_ref[...], g_step):
        g_all_ref[:, at : at + piece.shape[1]] = piece.astype(bf16)
        at += piece.shape[1]


def masked_scores(info, keys, queries, length):
    scores = k_nt(keys, queries) * (HD**-0.5)
    start = (info[1] * 8 + pl.program_id(0)) * BLOCK
    key_at = lax.broadcasted_iota(jnp.int32, (length, BLOCK), 0)
    query_at = lax.broadcasted_iota(jnp.int32, (length, BLOCK), 1) + start
    return scores, key_at <= query_at


def attend_forward(info, q_ref, k_ref, v_ref, out_ref, out_f_ref, log_ref):
    scores, allowed = masked_scores(info, k_ref[...], q_ref[...], k_ref.shape[0])
    scores = jnp.where(allowed, scores, NEGATIVE)
    top = jnp.max(scores, axis=0, keepdims=True)
    weights = jnp.exp(scores - top)
    total = jnp.sum(weights, axis=0, keepdims=True)
    result = jnp.transpose(k_tn(v_ref[...], weights.astype(bf16)) / total)
    out_ref[...] = result.astype(bf16)
    out_f_ref[...] = result
    log_ref[0] = jnp.broadcast_to(top + jnp.log(total), (8, BLOCK))


def attend_backward(
    info, q_ref, k_ref, v_ref, out_f_ref, log_ref, g_ref, cos_ref, sin_ref, dq_ref, dk_ref, dv_ref
):
    @pl.when(pl.program_id(0) == 0)
    def _():
        dk_ref[...] = jnp.zeros_like(dk_ref)
        dv_ref[...] = jnp.zeros_like(dv_ref)

    keys, queries, grads = k_ref[...], q_ref[...], g_ref[...]
    scores, allowed = masked_scores(info, keys, queries, k_ref.shape[0])
    probs = jnp.where(allowed, jnp.exp(scores - log_ref[0, 0:1]), 0.0)
    delta = k_nt(jnp.ones((8, HD), f32), grads.astype(f32) * out_f_ref[...], HIGHEST)[0:1]
    g_scores = (probs * (k_nt(v_ref[...], grads) - delta)).astype(bf16)
    dv_ref[...] += k_mm(probs.astype(bf16), grads)
    dk_ref[...] += k_mm(g_scores, queries) * (HD**-0.5)
    dq = (k_tn(g_scores, keys) * (HD**-0.5)).astype(bf16).astype(f32)
    dq_ref[...] = (dq * cos_ref[...] - pltpu.roll(dq, HD // 2, 1) * sin_ref[...]).astype(bf16)


def rows_at(width, column=0):
    return pl.BlockSpec((BLOCK, width), lambda i, s: (i ^ s[0], column))


def rows_back(count, width, column=0):
    return pl.BlockSpec((BLOCK, width), lambda i, s: ((count - 1 - i) ^ s[0], column))


def whole(*shape):
    return pl.BlockSpec(shape, lambda i, s: (0,) * len(shape))


def run_mix_forward(info, own, shared, cosine, sine, cum_col, cum_row, taps_x, taps_m, vec):
    length = own.shape[0]
    count = length // BLOCK

    def plain(width):
        return pl.BlockSpec((BLOCK, width), lambda i, s: (i, 0))

    def plain3(rows, width):
        return pl.BlockSpec((1, rows, width), lambda i, s: (i, 0, 0))

    return pl.pallas_call(
        mix_forward,
        grid_spec=pltpu.PrefetchScalarGridSpec(
            num_scalar_prefetch=1,
            grid=(count,),
            in_specs=[
                rows_at(own.shape[1]),
                rows_at(shared.shape[1]),
                plain(HD),
                plain(HD),
                plain(8),
                plain3(8, BLOCK),
                whole(8, OWN),
                whole(8, 2 * NS),
                whole(8, OWN),
            ],
            out_specs=[
                rows_at(OWN),
                rows_at(OWN),
                plain3(8, BLOCK),
                plain3(NS, OWN),
                plain(HD),
                plain(HD),
                plain(HD),
            ],
            scratch_shapes=[
                pltpu.VMEM((NS, OWN), f32),
                pltpu.VMEM((TAIL, OWN), f32),
                pltpu.VMEM((TAIL, 2 * NS), f32),
            ],
        ),
        out_shape=[
            jax.ShapeDtypeStruct((length, OWN), bf16),
            jax.ShapeDtypeStruct((length, OWN), bf16),
            jax.ShapeDtypeStruct((count, 8, BLOCK), f32),
            jax.ShapeDtypeStruct((count, NS, OWN), bf16),
            jax.ShapeDtypeStruct((length, HD), bf16),
            jax.ShapeDtypeStruct((length, HD), bf16),
            jax.ShapeDtypeStruct((length, HD), bf16),
        ],
        compiler_params=params(),
        cost_estimate=LITTLE,
        name="mix_forward",
    )(info, own, shared, cosine, sine, cum_col, cum_row, taps_x, taps_m, vec)


def run_mix_backward(
    info,
    own,
    shared,
    cosine,
    sine,
    cum_col,
    cum_row,
    taps_x,
    taps_m,
    vec,
    lanes,
    g_y,
    g_z,
    states,
    dq,
    dk,
    dv,
):
    length = own.shape[0]
    count = length // BLOCK
    tails = BLOCK // TAIL
    all_width = own.shape[1] + shared.shape[1]

    def plain(width):
        return pl.BlockSpec((BLOCK, width), lambda i, s: (count - 1 - i, 0))

    def plain3(rows, width):
        return pl.BlockSpec((1, rows, width), lambda i, s: (count - 1 - i, 0, 0))

    def tail_of(width):
        def where(i, s):
            before = jnp.maximum(count - 2 - i, 0)
            return ((before ^ s[0]) * tails + tails - 1, 0)

        return pl.BlockSpec((TAIL, width), where)

    def query_rows(i, s):
        return (((count - 1 - i) ^ s[0]) % 8, 0)

    return pl.pallas_call(
        mix_backward,
        grid_spec=pltpu.PrefetchScalarGridSpec(
            num_scalar_prefetch=1,
            grid=(count,),
            in_specs=[
                rows_back(count, own.shape[1]),
                rows_back(count, shared.shape[1]),
                tail_of(own.shape[1]),
                tail_of(shared.shape[1]),
                plain(HD),
                plain(HD),
                plain(8),
                plain3(8, BLOCK),
                whole(8, OWN),
                whole(8, 2 * NS),
                whole(8, OWN),
                whole(8, 128),
                rows_back(count, OWN),
                rows_back(count, OWN),
                plain3(NS, OWN),
                pl.BlockSpec((BLOCK, HD), query_rows),
                plain(HD),
                plain(HD),
            ],
            out_specs=[
                rows_back(count, all_width),
                whole(8, OWN),
                whole(8, 2 * NS),
                whole(8, OWN),
                whole(8, 128),
            ],
            scratch_shapes=[
                pltpu.VMEM((NS, OWN), f32),
                pltpu.VMEM((TAIL, OWN), f32),
                pltpu.VMEM((TAIL, 2 * NS), f32),
            ],
        ),
        out_shape=[
            jax.ShapeDtypeStruct((length, all_width), bf16),
            jax.ShapeDtypeStruct((8, OWN), f32),
            jax.ShapeDtypeStruct((8, 2 * NS), f32),
            jax.ShapeDtypeStruct((8, OWN), f32),
            jax.ShapeDtypeStruct((8, 128), f32),
        ],
        compiler_params=params(),
        cost_estimate=LITTLE,
        name="mix_backward",
    )(
        info,
        own,
        shared,
        own,
        shared,
        cosine,
        sine,
        cum_col,
        cum_row,
        taps_x,
        taps_m,
        vec,
        lanes,
        g_y,
        g_z,
        states,
        dq,
        dk,
        dv,
    )


def own_queries(width):
    return pl.BlockSpec((BLOCK, width), lambda i, s: (s[1] * 8 + i, 0))


def own_rows(width):
    return pl.BlockSpec((BLOCK, width), lambda i, s: (i ^ s[2], 0))


def run_attend_forward(info, queries, keys, values):
    length = keys.shape[0]
    half = length // 2
    count = half // BLOCK
    return pl.pallas_call(
        attend_forward,
        grid_spec=pltpu.PrefetchScalarGridSpec(
            num_scalar_prefetch=1,
            grid=(count,),
            in_specs=[own_queries(HD), whole(length, HD), whole(length, HD)],
            out_specs=[
                own_rows(HD),
                pl.BlockSpec((BLOCK, HD), lambda i, s: (i, 0)),
                pl.BlockSpec((1, 8, BLOCK), lambda i, s: (i, 0, 0)),
            ],
        ),
        out_shape=[
            jax.ShapeDtypeStruct((half, HD), bf16),
            jax.ShapeDtypeStruct((half, HD), f32),
            jax.ShapeDtypeStruct((count, 8, BLOCK), f32),
        ],
        compiler_params=params(),
        cost_estimate=LITTLE,
        name="attend_forward",
    )(info, queries, keys, values)


def run_attend_backward(info, queries, keys, values, out_f, logs, grads, cosine, sine):
    length = keys.shape[0]
    half = length // 2
    count = half // BLOCK
    return pl.pallas_call(
        attend_backward,
        grid_spec=pltpu.PrefetchScalarGridSpec(
            num_scalar_prefetch=1,
            grid=(count,),
            in_specs=[
                own_queries(HD),
                whole(length, HD),
                whole(length, HD),
                pl.BlockSpec((BLOCK, HD), lambda i, s: (i, 0)),
                pl.BlockSpec((1, 8, BLOCK), lambda i, s: (i, 0, 0)),
                own_rows(HD),
                own_queries(HD),
                own_queries(HD),
            ],
            out_specs=[
                own_rows(HD),
                whole(length, HD),
                whole(length, HD),
            ],
        ),
        out_shape=[
            jax.ShapeDtypeStruct((half, HD), bf16),
            jax.ShapeDtypeStruct((length, HD), f32),
            jax.ShapeDtypeStruct((length, HD), f32),
        ],
        compiler_params=params(),
        cost_estimate=LITTLE,
        name="attend_backward",
    )(info, queries, keys, values, out_f, logs, grads, cosine, sine)


def cube_body(
    tokens,
    log_decay,
    norm_gain,
    qkv_proj,
    attn_proj,
    inner_proj,
    conv_weight,
    conv_bias,
    step_bias,
    skip_gain,
    inner_gain,
    inner_out,
    ff_gain,
    gate_up,
    down_proj,
    cotangent,
):
    core = lax.axis_index("head")
    seq_half = lax.axis_index("half")
    member = lax.axis_index("cube")
    chip = seq_half * 8 + member
    bits = (member // 4, (member // 2) % 2, member % 2)
    zl = bits[0]
    place = core * 8 + member
    info = jnp.stack([place, core, member, seq_half]).astype(jnp.int32)
    width = tokens.shape[-1]
    rows = tokens.shape[1]
    shard = width // DEVICES
    inner_width = MH * MP
    conv_width = inner_width + 2 * NS
    heads = MH // 16
    mine = heads * MP
    length = rows * 16
    half_rows = rows * 8
    ffc = FF // 16

    def to_local(value):
        parts = [value[:, i * width // 4 : (i + 1) * width // 4] for i in range(4)]
        return jnp.where(
            seq_half == 0,
            jnp.concatenate([parts[i] for i in (0, 2, 1, 3)], axis=1),
            jnp.concatenate([parts[i] for i in (1, 3, 0, 2)], axis=1),
        )

    def to_natural(value):
        parts = [value[:, i * width // 4 : (i + 1) * width // 4] for i in range(4)]
        return jnp.where(
            seq_half == 0,
            jnp.concatenate([parts[i] for i in (0, 2, 1, 3)], axis=1),
            jnp.concatenate([parts[i] for i in (2, 0, 3, 1)], axis=1),
        )

    swapped = swap_sequences(jnp.concatenate([tokens[0], cotangent[0]], axis=0))
    x_bf, g_out_bf = to_local(swapped[:rows]), to_local(swapped[rows:])

    gain_rows = norm_gain.astype(f32)[:, None]
    qkv_s = (qkv_proj.astype(f32) * gain_rows).astype(bf16)
    inner_s = (inner_proj.astype(f32) * gain_rows).astype(bf16)
    gate_up_s = (gate_up.astype(f32) * ff_gain.astype(f32)[:, None]).astype(bf16)

    def to_places(value):
        return jnp.moveaxis(value.reshape(shard, 16, -1), 1, 0)

    def to_members(value):
        parts = jnp.moveaxis(value.reshape(shard, 8, -1), 1, 0)
        return jnp.concatenate([parts, parts], axis=0)

    def both_halves(value, other):
        return jnp.concatenate([value, other], axis=0)

    kv_width = KVH * HD
    conv_shard = conv_weight.shape[1]
    smalls = jnp.concatenate([conv_weight.reshape(-1), conv_bias, inner_gain])
    decay_rows = jnp.moveaxis(log_decay, 1, 2).reshape(2, -1)
    decay_high = lax.optimization_barrier(decay_rows.astype(bf16))
    decay_low = (decay_rows - decay_high.astype(f32)).astype(bf16)
    decay_rows = jnp.concatenate([decay_high, decay_low], axis=1)
    extra_size = shard * 128
    extra_pad = jnp.zeros((extra_size - smalls.shape[0] - decay_rows.shape[1],), bf16)

    def shared_for(half):
        mine_rows = lax.dynamic_index_in_dim(decay_rows, half, 0, keepdims=False)
        extra = jnp.concatenate([smalls, mine_rows, extra_pad]).reshape(shard, 128)
        return jnp.concatenate([shared_send, extra], axis=1)

    shared_send = jnp.concatenate(
        [
            inner_s[:, 2 * inner_width : inner_width + conv_width],
            qkv_s[:, QH * HD : QH * HD + kv_width],
            inner_s[:, inner_width + conv_width :],
            jnp.zeros((shard, -MH % 128), bf16),
            qkv_s[:, QH * HD + kv_width :],
        ],
        axis=1,
    )
    shared_other = flip(shared_for(1 - seq_half), BIT_ZH)
    send_own = jnp.concatenate(
        [
            to_places(inner_s[:, :inner_width]),
            to_places(inner_s[:, inner_width : 2 * inner_width]),
            to_members(qkv_s[:, : QH * HD]),
        ],
        axis=2,
    )
    got_own = exchange(send_own).reshape(width // 2, -1)
    x_rows = x_bf.astype(f32)
    inv_in = lax.rsqrt(jnp.mean(x_rows * x_rows, axis=-1, keepdims=True) + EPSILON)
    shared_mine = shared_for(seq_half)
    shared_both = jnp.concatenate([shared_mine, shared_other], axis=0)
    normed_mine = (x_rows * inv_in).astype(bf16)
    shared_edges = ((0, 2 * NS), (2 * NS, 2 * NS + kv_width + 128), (2 * NS + kv_width + 128, None))
    lanes_all = (shared_both.shape[1] + width) // 128
    goals = (-(-lanes_all // 3), -(-lanes_all // 3), lanes_all - 2 * -(-lanes_all // 3))
    edges, normed_edges, joined, at, done = [], [], [], 0, 0
    for (a, b), lanes_here in zip(shared_edges, goals):
        part = shared_both[:, a:b]
        taken = lanes_here * 128 - part.shape[1]
        joined += [part, normed_mine[:, done : done + taken]]
        edges.append((at, at + lanes_here * 128))
        normed_edges.append((part.shape[1], done, taken))
        at += lanes_here * 128
        done += taken
    first = Gather(jnp.concatenate(joined, axis=1), edges, info)
    first.state, got_own = joint(first.state, got_own)
    own_width = 2 * mine + HD
    other_own = [flip(got_own[:, : own_width // 2], BIT_ZH), None]
    first.hop()
    send_rest = jnp.concatenate(
        [
            to_places(inner_out.T),
            to_members(attn_proj.T),
            to_places(gate_up_s[:, :FF]),
            to_places(gate_up_s[:, FF:]),
            to_places(down_proj.T),
        ],
        axis=2,
    )
    positions = jnp.arange(length, dtype=f32)
    frequency = ROPE_BASE ** (-2.0 * jnp.arange(HD // 2, dtype=f32) / HD)
    angle = positions[:, None] * frequency[None, :]
    cosine, sine = jnp.cos(angle), jnp.sin(angle)
    cosine = jnp.concatenate([cosine, cosine], axis=1)
    sine = jnp.concatenate([-sine, sine], axis=1)
    first.hop()
    first.state, other_own[0], got_own = joint(first.state, other_own[0], got_own)
    other_own[1] = flip(got_own[:, own_width // 2 :], BIT_ZH)
    first.hop()
    first.state, send_rest, other_own[1], cosine, sine = joint(
        first.state, send_rest, other_own[1], cosine, sine
    )
    got = exchange(send_rest).reshape(width // 2, -1)
    pieces = first.pieces()
    shared_width = 2 * NS + 2 * HD + 128
    picks = (
        ((0, 0, 0, 2 * NS),),
        ((0, HD, 2 * NS, HD), (kv_width, 0, 2 * NS + 2 * HD, 128)),
        ((0, HD, 2 * NS + HD, HD),),
    )
    moves, extra_moves, normed_moves = [], [], []
    for group in range(4):
        half, far = group // 2, group % 2
        for part in range(3):
            number = 3 * group + part if half == 0 else 6 + far
            start = edges[part][0] * half
            skip, normed_at, taken = normed_edges[part]
            for begin, cube_place, count in piece_blocks(part, far):
                normed_moves.append(
                    (
                        number,
                        fixed(begin * rows, count * rows, start + skip, taken),
                        fixed((half * 8 + cube_place) * rows, count * rows, normed_at, taken),
                    )
                )
                for block, zh in ((i, j) for i in range(count) for j in range(2)):
                    row = (begin + block) * 2 * shard + zh * shard
                    position = half * 8 + cube_place + block

                    def goal(ref, position=position, zh=zh, target=0, columns=128):
                        to = zh * 16 + (ref[0] ^ position)
                        to = pl.multiple_of(to * shard, shard)
                        return (pl.ds(to, shard), pl.ds(target, columns))

                    def extra_goal(ref, position=position, zh=zh):
                        place = ref[0] ^ position
                        to = (place // 8) * 16 + (zh ^ ref[3]) * 8 + place % 8
                        to = pl.multiple_of(to * shard, shard)
                        return (pl.ds(to, shard), pl.ds(0, 128))

                    for column, by_zl, target, columns in picks[part]:

                        def source(ref, row=row, at=start + column, by_zl=by_zl, columns=columns):
                            if by_zl:
                                at = pl.multiple_of(at + (ref[2] // 4) * by_zl, 128)
                            return (pl.ds(row, shard), pl.ds(at, columns))

                        moves.append(
                            (
                                number,
                                source,
                                functools.partial(goal, target=target, columns=columns),
                            )
                        )
                    if part == 2:
                        extra_moves.append(
                            (number, fixed(row, shard, start + kv_width, 128), extra_goal)
                        )
    normed, w_s, small_got = assemble(
        pieces,
        [
            ((length, width), bf16, normed_moves),
            ((width, shared_width), bf16, moves),
            ((width, 128), bf16, extra_moves),
        ],
        info,
    )
    small_got = small_got.reshape(DEVICES, -1)
    at = smalls.shape[0]
    decay = lax.dynamic_slice_in_dim(small_got[:, at : at + decay_rows.shape[1]], core * 16, 16, 0)
    decay = decay.astype(f32).reshape(16, 2, 8, heads, rows)
    decay = lax.dynamic_index_in_dim(decay[:, 0] + decay[:, 1], member, 1, keepdims=False)
    at = 0
    conv_w = jnp.moveaxis(
        small_got[:, at : at + KC * conv_shard].reshape(DEVICES, KC, conv_shard), 1, 0
    ).reshape(KC, conv_width)
    at += KC * conv_shard
    conv_b = small_got[:, at : at + conv_shard].reshape(1, conv_width)
    at += conv_shard
    gain_all = small_got[:, at : at + inner_gain.shape[0]].reshape(1, inner_width)
    conv_all = jnp.concatenate([conv_w, conv_b], axis=0).astype(f32)
    conv_all = jnp.concatenate([conv_all, jnp.zeros((8 - KC - 1, conv_width), f32)], axis=0)
    taps_x = lax.dynamic_slice_in_dim(conv_all[:, :inner_width], place * mine, mine, 1)
    taps_m = conv_all[:, inner_width:]
    gain_mine = lax.dynamic_slice_in_dim(gain_all, place * mine, mine, 1)[0].astype(f32)

    (w_own,) = joint(both_halves(got_own, jnp.concatenate(other_own, axis=1)))
    bias_mine = lax.dynamic_slice_in_dim(step_bias, member * heads, heads, 0)
    skip_mine = lax.dynamic_slice_in_dim(skip_gain, member * heads, heads, 0)
    vec = jnp.concatenate(
        [
            jnp.repeat(bias_mine, MP)[None],
            jnp.repeat(skip_mine, MP)[None],
            gain_mine[None],
            jnp.zeros((5, mine), f32),
        ],
        axis=0,
    )
    lanes = lax.dynamic_update_slice(
        jnp.zeros((8, 128), f32), bias_mine[None], (0, place * heads)
    )
    cum_row = jnp.cumsum(decay, axis=2)
    cum_row = jnp.concatenate([cum_row, jnp.zeros((16, 8 - heads, rows), f32)], axis=1)
    cum_col = jnp.moveaxis(cum_row, 1, 2).reshape(length, 8)
    (w_all,) = joint(jnp.concatenate([w_own, w_s], axis=1))

    order = jnp.arange(16, dtype=jnp.int32) ^ place

    def reordered(value):
        return jnp.take(value, order, axis=0, unique_indices=True, mode="clip")

    g_out_bf, normed = joint(g_out_bf, normed)
    g_out = gather_start(g_out_bf, info)
    g_out.hop()
    raw_s = mm(normed, w_s).astype(bf16)
    g_out.state, raw_s, got, normed = joint(g_out.state, raw_s, got, normed)
    cuts = [0, mine + HD] + [mine + HD + i * ffc for i in (1, 2, 3)]
    got = [got[:, a:b] for a, b in zip(cuts[:-1], cuts[1:])]
    other = [flip(got[0], BIT_ZH), None, None, None]
    g_out.hop()
    raw_own = mm(normed, w_own).astype(bf16)
    g_out.state, raw_own = joint(g_out.state, raw_own)
    g_out.hop()

    tables = (cosine, sine, cum_col, cum_row, taps_x, taps_m, vec)
    y, gained, squares, states, queries, keys, values = run_mix_forward(
        info, raw_own, raw_s, *tables
    )
    squares, other[0] = joint(squares, other[0])
    other[3] = flip(got[3], BIT_ZH)
    (w_mix,) = joint(both_halves(got[0], other[0]))
    w_out, w_att = w_mix[:, :mine], w_mix[:, mine:]
    squares = group_sum(squares[:, 0])
    squares, queries, other[3], got[1] = joint(squares, queries, other[3], got[1])
    other[1] = flip(got[1], BIT_ZH)
    (w_down,) = joint(both_halves(got[3], other[3]))
    attended, attended_f, logs = run_attend_forward(info, queries, keys, values)
    inv_mix = lax.rsqrt(squares / inner_width + EPSILON)
    inv_mix_rows = reordered(inv_mix).reshape(length, 1)
    part_other = inv_mix_rows[half_rows:] * mm_nt(gained[half_rows:], w_out)
    part_own = inv_mix_rows[:half_rows] * mm_nt(gained[:half_rows], w_out) + mm_nt(attended, w_att)
    sums = Scatter(part_own.astype(bf16), part_other)
    sums.state, other[1], got[2] = joint(sums.state, other[1], got[2])
    other[2] = flip(got[2], BIT_ZH)
    sums.hop()
    sums.hop()
    sums.state, other[2] = joint(sums.state, other[2])
    (w_gu,) = joint(
        jnp.concatenate([both_halves(got[i], other[i]) for i in (1, 2)], axis=1)
    )
    hidden = x_rows + sums.result()
    g_out = gathered(g_out, width, info)

    inv_ff = lax.rsqrt(jnp.mean(hidden * hidden, axis=-1, keepdims=True) + EPSILON)
    gather = gather_start((hidden * inv_ff).astype(bf16), info)
    normed_ff = gathered(gather, width, info)
    gate_vals = mm(normed_ff, w_gu)
    gate, up = gate_vals[:, :ffc], gate_vals[:, ffc:]
    sig = jax.nn.sigmoid(gate)
    mixed = (gate * sig * up).astype(bf16)
    g_mixed = mm(g_out, w_down)
    g_vals = jnp.concatenate(
        [g_mixed * up * sig * (1.0 + gate * (1.0 - sig)), g_mixed * gate * sig], axis=1
    ).astype(bf16)
    g_ff_other = mm_nt(g_vals[half_rows:], w_gu).astype(bf16)
    sums = Scatter(mm_nt(g_vals[:half_rows], w_gu).astype(bf16), g_ff_other)
    sums.hop()
    def crossing(value):
        return flip(value[width // 2 :], BIT_ZH)

    def to_owners(values, crossed):
        total = [
            value[: width // 2].astype(f32) + got.astype(f32)
            for value, got in zip(values, crossed)
        ]
        total = jnp.concatenate([part.astype(bf16) for part in total], axis=1)
        return exchange(total.reshape(16, shard, -1))

    mixed_late, g_vals_late = sums.then(mixed, g_vals)
    mixed_cube = reordered_rows(mixed_late, info)
    out_other = mm_nt(mixed_cube[half_rows:], w_down).astype(bf16)
    out_own = mm_nt(mixed_cube[:half_rows], w_down).astype(bf16)
    d_gu = mm_tn(normed_ff, g_vals_late).astype(bf16)
    d_gate, d_up = d_gu[:, :ffc], d_gu[:, ffc:]
    sums.state, out_other, out_own, d_gate = joint(sums.state, out_other, out_own, d_gate)
    out_got = flip(out_other, BIT_C)
    gate_got = crossing(d_gate)
    sums.hop()
    mixed_late, g_out = sums.then(mixed_late, g_out)
    d_down = mm_tn(g_out, mixed_late).astype(bf16)
    sums.state, d_down = joint(sums.state, d_down)
    g_ff = sums.result()

    def from_places(value):
        return jnp.moveaxis(value, 0, 1).reshape(shard, -1)

    g_hidden = (
        g_out_bf.astype(f32)
        + inv_ff * g_ff
        - hidden * inv_ff**3 * jnp.mean(hidden * g_ff, axis=-1, keepdims=True)
    )
    gather = gather_start(g_hidden.astype(bf16), info)
    gather.state, gate_got, d_up = joint(gather.state, gate_got, d_up)
    up_got = crossing(d_up)
    gather.hop()
    gather.hop()
    out_sum = (out_own.astype(f32) + out_got.astype(f32)).astype(bf16)
    gather.state, up_got, d_down, out_sum, w_all = joint(
        gather.state, up_got, d_down, out_sum, w_all
    )
    down_got = crossing(d_down)
    g_branch = gathered(gather, width, info)

    inner_normed = (gained.astype(f32) * inv_mix_rows).astype(bf16)
    g_inner = mm(g_branch, w_out)
    g_branch_own = g_branch[:half_rows]
    g_att = mm(g_branch_own, w_att).astype(bf16)
    dots = jnp.sum(inner_normed.astype(f32) * g_inner, axis=-1).reshape(16, rows)
    dots = group_sum(reordered(dots))
    g_branch_own = g_branch[:half_rows]
    g_att = mm(g_branch_own, w_att).astype(bf16)
    d_mix_early = jnp.concatenate(
        [
            mm_tn(g_branch, inner_normed).astype(bf16),
            mm_tn(g_branch_own, attended).astype(bf16),
        ],
        axis=1,
    )
    d_mix_early, g_att = joint(d_mix_early, g_att)
    early_got = crossing(d_mix_early)
    d_q, d_k, d_v = run_attend_backward(
        info, queries, keys, values, attended_f, logs, g_att, cosine, sine
    )
    gate = raw_own[:, :mine].astype(f32)
    gate_sig = jax.nn.sigmoid(gate)
    y_rows = y.astype(f32)
    normed_mix = y_rows * (gate * gate_sig) * inv_mix_rows
    g_gated = inv_mix_rows * (
        gain_mine * g_inner - normed_mix * (reordered(dots).reshape(length, 1) / inner_width)
    )
    g_y = (g_gated * gate * gate_sig).astype(bf16)
    g_z = (g_gated * y_rows * gate_sig * (1.0 + gate * (1.0 - gate_sig))).astype(bf16)
    grad_gain_mine = jnp.sum(normed_mix * g_inner, axis=0)
    d_q, down_got, dots = joint(d_q, down_got, dots)
    d_ff_got = to_owners((d_gate, d_up, d_down), (gate_got, up_got, down_got))
    d_mix_late = jnp.concatenate(
        [
            mm_tn(normed, g_z).astype(bf16),
            mm_tn(normed[:half_rows], d_q).astype(bf16),
        ],
        axis=1,
    )
    d_mix_late, early_got = joint(d_mix_late, early_got)
    late_got = crossing(d_mix_late)
    g_y, d_ff_got, out_sum, d_mix_late = joint(g_y, d_ff_got, out_sum, d_mix_late)
    out_got = lax.all_to_all(
        out_sum.reshape(8, rows, width), "cube", split_axis=0, concat_axis=0, tiled=True
    )
    g_all, acc_x, acc_m, acc_v, acc_s = run_mix_backward(
        info,
        raw_own,
        raw_s,
        *tables,
        lanes,
        g_y,
        g_z,
        states,
        d_q,
        d_k,
        d_v,
    )
    conv_grads = jnp.concatenate([acc_x[: KC + 1], acc_m[: KC + 1]], axis=1)
    g_bias = lax.dynamic_slice_in_dim(acc_s[0], place * heads, heads, 0)
    g_skip = jnp.sum(acc_v[0].reshape(heads, MP), axis=1)
    small_grads = jnp.concatenate([conv_grads.reshape(-1), grad_gain_mine, g_bias, g_skip])
    small_grads = jnp.pad(small_grads, (0, -small_grads.shape[0] % shard)).astype(bf16)
    small_grads = jnp.broadcast_to(
        small_grads.reshape(1, shard, -1), (DEVICES, shard, small_grads.shape[0] // shard)
    ).reshape(width, -1)
    g_in_other = mm_nt(g_all[half_rows:], w_all).astype(bf16)
    sums = Scatter(mm_nt(g_all[:half_rows], w_all).astype(bf16), g_in_other)
    sums.state, out_got = joint(sums.state, out_got)
    sums.hop()
    (g_all,) = sums.then(g_all)
    d_own = mm_tn(normed, g_all[:, mine : 2 * mine]).astype(bf16)
    d_own = jnp.concatenate([d_own, small_grads], axis=1)
    d_shared = mm_tn(normed, g_all[:, own_width:]).astype(bf16)
    sums.state, d_own, d_shared = joint(sums.state, d_own, d_shared)
    sums.hop()
    d_shared, d_ff_got, out_got = sums.then(d_shared, d_ff_got, out_got)
    out_part = jnp.sum(out_got.astype(f32), axis=0)
    out_rows = (hidden + out_part).astype(bf16)

    def only_mine(value):
        empty = jnp.zeros((width, KVH * HD), bf16)
        return lax.dynamic_update_slice_in_dim(empty, value, zl * HD, 1)

    d_shared = jnp.concatenate(
        [
            d_shared[:, : 2 * NS],
            only_mine(d_shared[:, 2 * NS : 2 * NS + HD]),
            only_mine(d_shared[:, 2 * NS + HD : 2 * NS + 2 * HD]),
            d_shared[:, 2 * NS + 2 * HD :],
        ],
        axis=1,
    )
    moves = []
    for block in range(DEVICES):

        def goal(ref, block=block):
            row = (ref[0] ^ (block % 16)) * 2 + block // 16
            return (pl.ds(pl.multiple_of(row * shard, shard), shard), slice(None))

        moves.append((0, fixed(block * shard, shard, 0, d_shared.shape[1]), goal))
    d_shared = assemble([d_shared], [(d_shared.shape, bf16, moves)], info)[0]
    sums.state, d_shared = joint(sums.state, d_shared)
    shared_sums = Scatter(d_shared[:half_rows], d_shared[half_rows:])
    sums.hop()
    g_in, d_own = joint(sums.result(), d_own)
    own_back = crossing(d_own)
    g_x_rows = (
        inv_in * g_in - x_rows * inv_in**3 * jnp.mean(x_rows * g_in, axis=-1, keepdims=True)
    )
    both = jnp.concatenate(
        [to_natural(out_rows), to_natural((g_hidden + g_x_rows).astype(bf16))], axis=0
    )
    both = swap_sequences(both)
    output, grad_tokens = both[None, :rows], both[None, rows:].astype(f32)
    shared_sums.hop()
    shared_sums.hop()
    shared_sums.hop()
    shared_sums.state, own_back, late_got, early_got = joint(
        shared_sums.state, own_back, late_got, early_got
    )
    d_own_got = to_owners((d_own, d_mix_late, d_mix_early), (own_back, late_got, early_got))
    d_cube = shared_sums.result().reshape(2, shard, -1)
    d_shared_own = d_cube[0] + flip(d_cube[1].astype(bf16), BIT_ZH).astype(f32)
    d_ff_own = d_ff_got.astype(f32)
    d_gate_up = jnp.concatenate(
        [from_places(d_ff_own[..., :ffc]), from_places(d_ff_own[..., ffc : 2 * ffc])], axis=1
    )
    grad_gate_up = d_gate_up * ff_gain.astype(f32)[:, None]
    grad_ff_gain = jnp.sum(d_gate_up * gate_up.astype(f32), axis=1)
    grad_down = jnp.moveaxis(d_ff_own[..., 2 * ffc : 3 * ffc], 1, 2).reshape(FF, shard)
    d_own = d_own_got.astype(f32)
    small_end = d_own.shape[-1] - 2 * mine - 2 * HD
    d_mix_own = d_own[..., small_end + mine + HD :]
    grad_inner_out = jnp.moveaxis(d_mix_own[..., :mine], 1, 2).reshape(inner_width, shard)
    d_att = d_mix_own[..., mine:].reshape(2, 8, shard, HD)
    grad_attn = jnp.moveaxis(d_att[0] + d_att[1], 1, 2).reshape(QH * HD, shard)
    d_x = from_places(d_own[..., :mine])
    d_z = from_places(d_own[..., small_end : small_end + mine])
    d_qw = d_own[..., small_end + mine : small_end + mine + HD].reshape(2, 8, shard, HD)
    d_qw = from_places(d_qw[0] + d_qw[1])

    got = d_own[..., mine:small_end].reshape(16, -1)
    at = 0
    taps_width = mine + 2 * NS
    conv_grads = got[:, at : at + (KC + 1) * taps_width].reshape(16, KC + 1, taps_width)
    at += (KC + 1) * taps_width
    conv_full = jnp.concatenate(
        [
            jnp.moveaxis(conv_grads[..., :mine], 0, 1).reshape(KC + 1, inner_width),
            jnp.sum(conv_grads[..., mine:], axis=0),
        ],
        axis=1,
    )
    device = core * 16 + chip
    conv_own = lax.dynamic_slice_in_dim(conv_full, device * conv_shard, conv_shard, 1)
    gain_full = got[:, at : at + mine].reshape(inner_width)
    gain_shard = inner_gain.shape[0]
    grad_inner_gain = lax.dynamic_slice_in_dim(gain_full, device * gain_shard, gain_shard, 0)
    at += mine
    local = lax.dynamic_slice_in_dim(got[:, at : at + 2 * heads], core * 8, 8, 0)
    grad_step_bias = local[:, :heads].reshape(-1)
    grad_skip_gain = local[:, heads:].reshape(-1)

    at = 2 * NS + 2 * kv_width
    d_qkv = jnp.concatenate([d_qw, d_shared_own[:, 2 * NS : at]], axis=1)
    d_inner = jnp.concatenate(
        [d_z, d_x, d_shared_own[:, : 2 * NS], d_shared_own[:, at : at + MH]], axis=1
    )
    grad_norm_gain = jnp.sum(d_qkv * qkv_proj.astype(f32), axis=1) + jnp.sum(
        d_inner * inner_proj.astype(f32), axis=1
    )
    return (
        output,
        grad_tokens,
        grad_norm_gain,
        d_qkv * gain_rows,
        grad_attn,
        d_inner * gain_rows,
        conv_own[:KC],
        conv_own[KC],
        grad_step_bias,
        grad_skip_gain,
        grad_inner_gain,
        grad_inner_out,
        grad_ff_gain,
        grad_gate_up,
        grad_down,
    )


def cube_solution(mesh):
    cubes = jax.sharding.Mesh(mesh.devices.reshape(2, 2, 8), BOTH)
    tokens = P("head", ("half", "cube"), None)
    lines = P(BOTH)
    rows = P(BOTH, None)
    columns = P(None, BOTH)
    head = P("head")
    return jax.shard_map(
        cube_body,
        mesh=cubes,
        in_specs=(
            tokens,
            P(None, ("half", "cube"), "head"),
            lines,
            rows,
            columns,
            rows,
            columns,
            lines,
            head,
            head,
            lines,
            columns,
            lines,
            rows,
            columns,
            tokens,
        ),
        out_specs=(
            tokens,
            tokens,
            lines,
            rows,
            columns,
            rows,
            columns,
            lines,
            head,
            head,
            lines,
            columns,
            lines,
            rows,
            columns,
        ),
        check_vma=False,
    )


def solution(mesh):
    if mesh.shape["seq"] == 16:
        return cube_solution(mesh)
    return jax.shard_map(
        body,
        mesh=mesh,
        in_specs=(
            P("head", "seq", None),
            P(None, "seq", "head"),
            P(("head", "seq")),
            P(("head", "seq"), None),
            P(None, ("head", "seq")),
            P(("head", "seq"), None),
            P(None, ("head", "seq")),
            P(("head", "seq")),
            P("head"),
            P("head"),
            P(("head", "seq")),
            P(None, ("head", "seq")),
            P(("head", "seq")),
            P(("head", "seq"), None),
            P(None, ("head", "seq")),
            P("head", "seq", None),
        ),
        out_specs=(
            P("head", "seq", None),
            P("head", "seq", None),
            P(("head", "seq")),
            P(("head", "seq"), None),
            P(None, ("head", "seq")),
            P(("head", "seq"), None),
            P(None, ("head", "seq")),
            P(("head", "seq")),
            P("head"),
            P("head"),
            P(("head", "seq")),
            P(None, ("head", "seq")),
            P(("head", "seq")),
            P(("head", "seq"), None),
            P(None, ("head", "seq")),
        ),
        check_vma=False,
    )
```

```python
import functools
import math

import jax
import jax.numpy as jnp
from jax import lax
from jax.experimental import pallas as pl
from jax.experimental.pallas import tpu as pltpu
from jax.sharding import PartitionSpec as P

FF = 4096
QH = 8
KVH = 2
HD = 128
MH = 48
MP = 64
NS = 256
KC = 4


EPSILON = 1e-05
ROPE_BASE = 100000000000.0
NEGATIVE = -1e30
HIGHEST = lax.Precision.HIGHEST


def passed_along(value, axis, steps):
    count = lax.axis_size(axis)
    initial, last = (max(0, -steps), min(count, count - steps))
    return lax.ppermute(value, axis, [(source, source + steps) for source in range(initial, last)])


def carried_in(array, axis, combine, identity):
    count, mine = (lax.axis_size(axis), lax.axis_index(axis))
    everything = jax.tree.map(
        lambda part, kind: lax.all_gather(part.astype(kind), axis),
        array,
        (jnp.bfloat16, jnp.bfloat16),
    )
    start = jax.tree.map(
        lambda part, zero: jnp.broadcast_to(jnp.asarray(zero, part.dtype), part.shape),
        array,
        identity,
    )

    def carried_hop(k, before):
        reached = k < mine
        new = combine(
            before, jax.tree.map(lambda part, own: part[k].astype(own.dtype), everything, array)
        )
        return jax.tree.map(lambda a, b: jnp.where(reached, a, b), new, before)

    return lax.fori_loop(0, count, carried_hop, start)


def entering(array, axis, combine, identity):
    count, mine = (lax.axis_size(axis), lax.axis_index(axis))
    everything = jax.tree.map(
        lambda part, kind: lax.all_gather(part.astype(kind), axis),
        array,
        jax.tree.map(lambda a: jnp.bfloat16 if a.dtype == jnp.float32 else a.dtype, array),
    )
    start = jax.tree.map(
        lambda part, zero: jnp.broadcast_to(jnp.asarray(zero, part.dtype), part.shape),
        array,
        identity,
    )

    def entering_hop(k, before):
        at = count - 1 - k
        reached = at > mine
        new = combine(
            before, jax.tree.map(lambda part, own: part[at].astype(own.dtype), everything, array)
        )
        return jax.tree.map(lambda a, b: jnp.where(reached, a, b), new, before)

    return lax.fori_loop(0, count, entering_hop, start)


def shortened(array):
    return jax.tree.map(lambda a: a.astype(jnp.bfloat16) if a.dtype == jnp.float32 else a, array)


def rounded(value):
    return lax.optimization_barrier(value.astype(jnp.bfloat16)).astype(jnp.float32)


def rms_norm(value, gain):
    return value * lax.rsqrt(jnp.mean(value * value, axis=-1, keepdims=True) + EPSILON) * gain


def rotary(value, positions):
    halfway = value.shape[-1] // 2
    frequency = ROPE_BASE ** (-2.0 * jnp.arange(halfway, dtype=jnp.float32) / value.shape[-1])
    angle = positions[:, None] * frequency[None, :]
    cosine = jnp.cos(angle)[:, None, :]
    sine_part = jnp.sin(angle)[:, None, :]
    first = value[..., :halfway]
    second = value[..., halfway:]
    return jnp.concatenate(
        [first * cosine - second * sine_part, second * cosine + first * sine_part], axis=-1
    )


def block_decay(log_decay):
    return jnp.exp(jnp.cumsum(log_decay, axis=1)[:, -1, :])


def inner_output(inner_x, step_in, state_maps, step_bias, skip_gain, state_in, log_decay):
    nstate = state_maps.shape[-1] // 2
    input_map = state_maps[..., :nstate]
    output_map = state_maps[..., nstate:]
    step_size = jax.nn.softplus(step_in + step_bias)
    cumulative = jnp.cumsum(log_decay, axis=1)
    scaled_x = inner_x * step_size[..., None]
    intersection = jnp.einsum("stn,sun->stu", output_map, input_map, precision=HIGHEST)
    length_blk = log_decay.shape[1]
    lower_mask = jnp.arange(length_blk)[:, None] >= jnp.arange(length_blk)[None, :]
    spread = cumulative[:, :, None, :] - cumulative[:, None, :, :]
    mixing = (
        jnp.where(lower_mask[None, :, :, None], jnp.exp(jnp.minimum(spread, 0.0)), 0.0)
        * intersection[..., None]
    )
    within = jnp.einsum("stuh,suhp->sthp", mixing, scaled_x, precision=HIGHEST)
    carried = (
        jnp.einsum("shpn,stn->sthp", state_in, output_map, precision=HIGHEST)
        * jnp.exp(cumulative)[..., None]
    )
    return within + carried + skip_gain[:, None] * inner_x


def inner_state(inner_x, step_in, state_maps, step_bias, log_decay):
    nstate = state_maps.shape[-1] // 2
    input_map = state_maps[..., :nstate]
    step_size = jax.nn.softplus(step_in + step_bias)
    cumulative = jnp.cumsum(log_decay, axis=1)
    tail_weight = jnp.exp(cumulative[:, -1:, :] - cumulative) * step_size
    return jnp.einsum("suh,suhp,sun->shpn", tail_weight, inner_x, input_map, precision=HIGHEST)


def over_blocks(function, carried, arrays, offset, limit):
    row_count = arrays[0].shape[1]
    step_rows = math.gcd(row_count, 1024)

    def advance(number, running):
        pieces = tuple(
            (
                lax.dynamic_slice_in_dim(member, number * step_rows, step_rows, 1)
                for member in arrays
            )
        )
        return function(running, pieces, offset + number * step_rows)

    upper = (limit + step_rows - 1) // step_rows
    return lax.fori_loop(0, upper, advance, carried)


def attend_block(carried, pair, offset, queries, query_pos, score_scale):
    row_top, row_total, accumulated = carried
    key_blk, value_blk = pair
    scores = (
        jnp.einsum("sqkgd,sjkd->sqkgj", queries, key_blk, preferred_element_type=jnp.float32)
        * score_scale
    )
    key_pos = offset + jnp.arange(key_blk.shape[1])
    allowed = (key_pos[None, :] <= query_pos[:, None])[None, :, None, None, :]
    masked = jnp.where(allowed, scores, NEGATIVE)
    new_top = jnp.maximum(row_top, jnp.max(masked, axis=-1))
    factor = jnp.exp(row_top - new_top)
    weights = jnp.where(allowed, jnp.exp(masked - new_top[..., None]), 0.0)
    row_total = factor * row_total + jnp.sum(weights, axis=-1)
    accumulated = factor[..., None] * accumulated + jnp.einsum(
        "sqkgj,sjkd->sqkgd",
        weights.astype(jnp.bfloat16),
        value_blk,
        preferred_element_type=jnp.float32,
    )
    return (new_top, row_total, accumulated)


def score_grads(
    queries, grad_heads, log_total, row_delta, key_blk, value_blk, offset, query_pos, score_scale
):
    scores = (
        jnp.einsum("sqkgd,sjkd->sqkgj", queries, key_blk, preferred_element_type=jnp.float32)
        * score_scale
    )
    key_pos = offset + jnp.arange(key_blk.shape[1])
    allowed = (key_pos[None, :] <= query_pos[:, None])[None, :, None, None, :]
    prob_rows = jnp.where(allowed, jnp.exp(scores - log_total[..., None]), 0.0)
    grad_probs = jnp.einsum(
        "sqkgd,sjkd->sqkgj", grad_heads, value_blk, preferred_element_type=jnp.float32
    )
    grad_scores = (prob_rows * (grad_probs - row_delta[..., None])).astype(jnp.bfloat16)
    return (prob_rows.astype(jnp.bfloat16), grad_scores)


def body(
    tokens,
    log_decay,
    norm_gain,
    qkv_proj,
    attn_proj,
    inner_proj,
    conv_weight,
    conv_bias,
    step_bias,
    skip_gain,
    inner_gain,
    inner_out,
    ff_gain,
    gate_up,
    down_proj,
    cotangent,
):
    head_count = lax.axis_size("head")
    seq_index = lax.axis_index("seq")
    (
        gain_in,
        qkv_full,
        attn_full,
        inner_full,
        conv_full,
        conv_bias_full,
        inner_gain_full,
        out_full,
        ff_gain_full,
        gate_up_full,
        down_full,
    ) = (
        lax.all_gather(norm_gain, ("head", "seq"), axis=0, tiled=True),
        lax.all_gather(qkv_proj, ("head", "seq"), axis=0, tiled=True),
        lax.all_gather(attn_proj, ("head", "seq"), axis=1, tiled=True),
        lax.all_gather(inner_proj, ("head", "seq"), axis=0, tiled=True),
        lax.all_gather(conv_weight, ("head", "seq"), axis=1, tiled=True),
        lax.all_gather(conv_bias, ("head", "seq"), axis=0, tiled=True),
        lax.all_gather(inner_gain, ("head", "seq"), axis=0, tiled=True),
        lax.all_gather(inner_out, ("head", "seq"), axis=1, tiled=True),
        lax.all_gather(ff_gain, ("head", "seq"), axis=0, tiled=True),
        lax.all_gather(gate_up, ("head", "seq"), axis=0, tiled=True),
        lax.all_gather(down_proj, ("head", "seq"), axis=1, tiled=True),
    )
    local_seqs, block_rows, model_width = tokens.shape
    token_rows = local_seqs * block_rows
    inner_width = MH * MP
    conv_width = inner_width + 2 * NS
    groups = QH // KVH
    kv_local = KVH // head_count
    inner_local = MH // head_count
    all_seqs = local_seqs * head_count
    score_scale = HD ** (-0.5)
    key_limit = (seq_index + 1) * block_rows
    x_rows = tokens.astype(jnp.float32).reshape(token_rows, model_width)
    normed_f, norm_back = jax.vjp(rms_norm, x_rows, gain_in.astype(jnp.float32))
    normed = normed_f.astype(jnp.bfloat16)
    qkv_rows = jnp.dot(normed, qkv_full, preferred_element_type=jnp.float32).reshape(
        local_seqs, block_rows, -1
    )
    positions = (seq_index * block_rows + jnp.arange(block_rows)).astype(jnp.float32)
    query_send = rotary(
        qkv_rows[..., : QH * HD].reshape(local_seqs, block_rows, QH, HD), positions
    ).astype(jnp.bfloat16)
    key_send = rotary(
        qkv_rows[..., QH * HD : (QH + KVH) * HD].reshape(local_seqs, block_rows, KVH, HD), positions
    ).astype(jnp.bfloat16)
    value_send = qkv_rows[..., (QH + KVH) * HD :].astype(jnp.bfloat16)
    inner_raw = jnp.dot(normed, inner_full, preferred_element_type=jnp.float32).reshape(
        local_seqs, block_rows, -1
    )
    gate_z = inner_raw[..., :inner_width]
    conv_in = inner_raw[..., inner_width : inner_width + conv_width]
    step_send = inner_raw[..., inner_width + conv_width :].astype(jnp.bfloat16)
    rim_rows = passed_along(
        conv_in[:, block_rows - (KC - 1) :, :].astype(jnp.bfloat16), "seq", 1
    ).astype(jnp.float32)
    padded = jnp.concatenate([rim_rows, conv_in], axis=1)

    def convolve(padded_in, weight_taps, bias_taps):
        conv_sum = bias_taps
        for conv_tap in range(KC):
            conv_sum = (
                conv_sum + weight_taps[conv_tap] * padded_in[:, conv_tap : conv_tap + block_rows, :]
            )
        return jax.nn.silu(conv_sum)

    activated, conv_back = jax.vjp(
        convolve, padded, conv_full.astype(jnp.float32), conv_bias_full.astype(jnp.float32)
    )
    activated_send = activated.astype(jnp.bfloat16)

    def split_heads(value):
        return value.reshape(value.shape[:2] + (head_count, -1))

    map_copies = jnp.broadcast_to(
        activated_send[:, :, None, inner_width:], (local_seqs, block_rows, head_count, 2 * NS)
    )
    received = (
        lax.all_to_all(split_heads(query_send), "head", split_axis=2, concat_axis=0, tiled=True),
        lax.all_to_all(split_heads(key_send), "head", split_axis=2, concat_axis=0, tiled=True),
        lax.all_to_all(split_heads(value_send), "head", split_axis=2, concat_axis=0, tiled=True),
        lax.all_to_all(
            split_heads(activated_send[..., :inner_width]),
            "head",
            split_axis=2,
            concat_axis=0,
            tiled=True,
        ),
        lax.all_to_all(split_heads(step_send), "head", split_axis=2, concat_axis=0, tiled=True),
        lax.all_to_all(map_copies, "head", split_axis=2, concat_axis=0, tiled=True),
    )
    queries = received[0].reshape(all_seqs, block_rows, kv_local, groups, HD)
    key_heads = received[1]
    value_heads = received[2]
    inner_x = received[3].reshape(all_seqs, block_rows, inner_local, MP).astype(jnp.float32)
    step_in = received[4].reshape(all_seqs, block_rows, inner_local).astype(jnp.float32)
    state_maps = received[5].reshape(all_seqs, block_rows, 2 * NS).astype(jnp.float32)
    query_pos = seq_index * block_rows + jnp.arange(block_rows)
    key_all, value_all = (
        lax.all_gather(key_heads, "seq", axis=1, tiled=True),
        lax.all_gather(value_heads, "seq", axis=1, tiled=True),
    )

    def attend_step(carried, pair, offset):
        return attend_block(carried, pair, offset, queries, query_pos, score_scale)

    stat_shape = (all_seqs, block_rows, kv_local, groups)
    start_stats = (
        jnp.full(stat_shape, NEGATIVE, jnp.float32),
        jnp.zeros(stat_shape, jnp.float32),
        jnp.zeros(stat_shape + (HD,), jnp.float32),
    )
    row_top, row_total, accumulated = over_blocks(
        attend_step, start_stats, (key_all, value_all), 0, key_limit
    )
    attended_f = accumulated / row_total[..., None]
    log_total = row_top + jnp.log(row_total)

    def state_part(piece_x, piece_step, piece_maps, piece_bias):
        return inner_state(piece_x, piece_step, piece_maps, piece_bias, log_decay)

    def output_part(piece_x, piece_step, piece_maps, piece_bias, piece_skip, piece_state):
        return inner_output(
            piece_x, piece_step, piece_maps, piece_bias, piece_skip, piece_state, log_decay
        )

    fresh_state, state_back = jax.vjp(state_part, inner_x, step_in, state_maps, step_bias)
    block_fall = block_decay(log_decay)

    def chain_rule(earlier, later):
        return (earlier[0] * later[0], later[1] + later[0][:, :, None, None] * earlier[1])

    neutral = (jnp.ones_like(block_fall), jnp.zeros_like(fresh_state))
    state_in = carried_in((block_fall, fresh_state), "seq", chain_rule, neutral)[1]
    inner_y, output_back = jax.vjp(
        output_part, inner_x, step_in, state_maps, step_bias, skip_gain, state_in
    )
    returned = (
        lax.all_to_all(
            attended_f.astype(jnp.bfloat16).reshape(all_seqs, block_rows, 1, -1),
            "head",
            split_axis=0,
            concat_axis=2,
            tiled=True,
        ),
        lax.all_to_all(
            inner_y.astype(jnp.bfloat16).reshape(all_seqs, block_rows, 1, -1),
            "head",
            split_axis=0,
            concat_axis=2,
            tiled=True,
        ),
    )
    attended = returned[0].reshape(token_rows, QH * HD)
    inner_back_y = returned[1].reshape(local_seqs, block_rows, inner_width).astype(jnp.float32)

    def gated_norm(y_part, gate_part, gain_part):
        return rms_norm(y_part * jax.nn.silu(gate_part), gain_part)

    inner_normed_f, gated_back = jax.vjp(
        gated_norm, inner_back_y, gate_z, inner_gain_full.astype(jnp.float32)
    )
    inner_normed = inner_normed_f.astype(jnp.bfloat16).reshape(token_rows, inner_width)
    hidden = (
        x_rows
        + jnp.dot(attended, attn_full, preferred_element_type=jnp.float32)
        + jnp.dot(inner_normed, out_full, preferred_element_type=jnp.float32)
    )
    normed_ff_f, ff_back = jax.vjp(rms_norm, hidden, ff_gain_full.astype(jnp.float32))
    normed_ff = normed_ff_f.astype(jnp.bfloat16)
    gate_vals = jnp.dot(normed_ff, gate_up_full, preferred_element_type=jnp.float32)

    def swiglu(values_in):
        return jax.nn.silu(values_in[:, :FF]) * values_in[:, FF:]

    mixed_f, swiglu_back = jax.vjp(swiglu, gate_vals)
    mixed_rows = mixed_f.astype(jnp.bfloat16)
    output = (
        (hidden + jnp.dot(mixed_rows, down_full, preferred_element_type=jnp.float32))
        .astype(jnp.bfloat16)
        .reshape(tokens.shape)
    )
    grad_out = cotangent.reshape(token_rows, model_width)
    grad_down = jnp.einsum("rf,rd->fd", mixed_rows, grad_out, preferred_element_type=jnp.float32)
    grad_gate_vals = swiglu_back(
        jnp.einsum("rd,fd->rf", grad_out, down_full, preferred_element_type=jnp.float32)
    )[0].astype(jnp.bfloat16)
    grad_gate_up = jnp.einsum(
        "rd,re->de", normed_ff, grad_gate_vals, preferred_element_type=jnp.float32
    )
    grad_hidden_norm, grad_ff_gain = ff_back(
        jnp.einsum("re,de->rd", grad_gate_vals, gate_up_full, preferred_element_type=jnp.float32)
    )
    grad_hidden = grad_out.astype(jnp.float32) + grad_hidden_norm
    grad_branch = grad_hidden.astype(jnp.bfloat16)
    grad_attn = jnp.einsum("rc,rd->cd", attended, grad_branch, preferred_element_type=jnp.float32)
    grad_inner_out = jnp.einsum(
        "rc,rd->cd", inner_normed, grad_branch, preferred_element_type=jnp.float32
    )
    grad_attended = jnp.einsum(
        "rd,cd->rc", grad_branch, attn_full, preferred_element_type=jnp.float32
    ).astype(jnp.bfloat16)
    grad_y, grad_gate_z, grad_inner_gain = gated_back(
        jnp.einsum("rd,cd->rc", grad_branch, out_full, preferred_element_type=jnp.float32).reshape(
            local_seqs, block_rows, inner_width
        )
    )
    sent_grads = (
        lax.all_to_all(
            split_heads(grad_attended.reshape(local_seqs, block_rows, QH * HD)),
            "head",
            split_axis=2,
            concat_axis=0,
            tiled=True,
        ),
        lax.all_to_all(
            split_heads(grad_y.astype(jnp.bfloat16)),
            "head",
            split_axis=2,
            concat_axis=0,
            tiled=True,
        ),
    )
    grad_heads = sent_grads[0].reshape(all_seqs, block_rows, kv_local, groups, HD)
    grad_inner_y = sent_grads[1].reshape(all_seqs, block_rows, inner_local, MP).astype(jnp.float32)
    row_delta = jnp.sum(grad_heads.astype(jnp.float32) * attended_f, axis=-1)

    def query_step(carried, pair, offset):
        prob_rows, grad_scores = score_grads(
            queries,
            grad_heads,
            log_total,
            row_delta,
            pair[0],
            pair[1],
            offset,
            query_pos,
            score_scale,
        )
        return carried + jnp.einsum(
            "sqkgj,sjkd->sqkgd", grad_scores, pair[0], preferred_element_type=jnp.float32
        )

    grad_queries = (
        over_blocks(query_step, jnp.zeros_like(attended_f), (key_all, value_all), 0, key_limit)
        * score_scale
    )
    count = block_rows * lax.axis_size("seq")
    step_rows = math.gcd(count, 1024)
    term_shape = (step_rows, all_seqs, kv_local, 2 * HD)

    def compute_block(offset):
        key_blk = lax.dynamic_slice_in_dim(key_all, offset, step_rows, 1)
        value_blk = lax.dynamic_slice_in_dim(value_all, offset, step_rows, 1)
        prob_rows, grad_scores = score_grads(
            queries,
            grad_heads,
            log_total,
            row_delta,
            key_blk,
            value_blk,
            offset,
            query_pos,
            score_scale,
        )
        grad_keys = (
            jnp.einsum(
                "sqkgj,sqkgd->jskd", grad_scores, queries, preferred_element_type=jnp.float32
            )
            * score_scale
        )
        grad_values = jnp.einsum(
            "sqkgj,sqkgd->jskd", prob_rows, grad_heads, preferred_element_type=jnp.float32
        )
        return jnp.concatenate([grad_keys, grad_values], axis=-1)

    def one_block(offset):
        return lax.cond(
            offset < key_limit,
            compute_block,
            lambda unused: jnp.zeros(term_shape, jnp.float32),
            offset,
        )

    block_terms = lax.map(
        lambda number: one_block(number * step_rows), jnp.arange(count // step_rows)
    )
    key_grads = lax.psum_scatter(
        block_terms.reshape((count,) + block_terms.shape[2:]),
        "seq",
        scatter_dimension=0,
        tiled=True,
    )
    grad_key_heads = jnp.moveaxis(key_grads[..., :HD], 0, 1)
    grad_value_heads = jnp.moveaxis(key_grads[..., HD:], 0, 1)
    grad_x_a, grad_step_a, grad_maps_a, grad_bias_a, grad_skip, grad_state = output_back(
        grad_inner_y
    )
    grad_carry = entering((block_fall, grad_state), "seq", chain_rule, neutral)[1]
    grad_x_b, grad_step_b, grad_maps_b, grad_bias_b = state_back(grad_carry)
    grad_step_bias, grad_skip_gain = lax.psum((grad_bias_a + grad_bias_b, grad_skip), "seq")
    returned_grads = (
        lax.all_to_all(
            grad_queries.reshape(all_seqs, block_rows, 1, -1).astype(jnp.bfloat16),
            "head",
            split_axis=0,
            concat_axis=2,
            tiled=True,
        ).astype(jnp.float32),
        lax.all_to_all(
            grad_key_heads.astype(jnp.bfloat16), "head", split_axis=0, concat_axis=2, tiled=True
        ).astype(grad_key_heads.dtype),
        lax.all_to_all(
            grad_value_heads.astype(jnp.bfloat16), "head", split_axis=0, concat_axis=2, tiled=True
        ).astype(grad_value_heads.dtype),
        lax.all_to_all(
            (grad_x_a + grad_x_b).reshape(all_seqs, block_rows, 1, -1).astype(jnp.bfloat16),
            "head",
            split_axis=0,
            concat_axis=2,
            tiled=True,
        ).astype(jnp.float32),
        lax.all_to_all(
            (grad_step_a + grad_step_b).reshape(all_seqs, block_rows, 1, -1).astype(jnp.bfloat16),
            "head",
            split_axis=0,
            concat_axis=2,
            tiled=True,
        ).astype(jnp.float32),
        lax.all_to_all(
            (grad_maps_a + grad_maps_b)[:, :, None, :].astype(jnp.bfloat16),
            "head",
            split_axis=0,
            concat_axis=2,
            tiled=True,
        ).astype(jnp.float32),
    )
    grad_q = rounded(returned_grads[0].reshape(local_seqs, block_rows, QH, HD))
    grad_k = rounded(returned_grads[1])
    grad_v = returned_grads[2].reshape(token_rows, KVH * HD)
    grad_qkv_rows = jnp.concatenate(
        [
            rotary(grad_q, -positions).reshape(token_rows, -1),
            rotary(grad_k, -positions).reshape(token_rows, -1),
            grad_v,
        ],
        axis=-1,
    ).astype(jnp.bfloat16)
    grad_x_in = rounded(returned_grads[3].reshape(local_seqs, block_rows, inner_width))
    grad_step = rounded(returned_grads[4].reshape(token_rows, MH))
    grad_maps = rounded(jnp.sum(returned_grads[5], axis=2))
    grad_padded, grad_conv_weight, grad_conv_bias = conv_back(
        jnp.concatenate([grad_x_in, grad_maps], axis=-1)
    )
    rim_grad = passed_along(shortened(grad_padded[:, : KC - 1, :]), "seq", -1)
    grad_conv_in = grad_padded[:, KC - 1 :, :].at[:, block_rows - (KC - 1) :, :].add(rim_grad)
    grad_inner_rows = jnp.concatenate(
        [grad_gate_z.reshape(token_rows, -1), grad_conv_in.reshape(token_rows, -1), grad_step],
        axis=-1,
    ).astype(jnp.bfloat16)
    grad_qkv_weight = jnp.einsum(
        "rd,re->de", normed, grad_qkv_rows, preferred_element_type=jnp.float32
    )
    grad_inner_weight = jnp.einsum(
        "rd,re->de", normed, grad_inner_rows, preferred_element_type=jnp.float32
    )
    grad_normed = jnp.einsum(
        "re,de->rd", grad_qkv_rows, qkv_full, preferred_element_type=jnp.float32
    ) + jnp.einsum("re,de->rd", grad_inner_rows, inner_full, preferred_element_type=jnp.float32)
    grad_x_norm, grad_norm_gain = norm_back(grad_normed)
    grad_tokens = (grad_hidden + grad_x_norm).reshape(tokens.shape)
    weight_grads = (
        grad_norm_gain,
        grad_qkv_weight,
        grad_attn,
        grad_inner_weight,
        grad_conv_weight,
        grad_conv_bias,
        grad_inner_gain,
        grad_inner_out,
        grad_ff_gain,
        grad_gate_up,
        grad_down,
    )
    shares = (
        lax.psum_scatter(weight_grads[0], ("head", "seq"), scatter_dimension=0, tiled=True),
        lax.psum_scatter(weight_grads[1], ("head", "seq"), scatter_dimension=0, tiled=True),
        lax.psum_scatter(weight_grads[2], ("head", "seq"), scatter_dimension=1, tiled=True),
        lax.psum_scatter(weight_grads[3], ("head", "seq"), scatter_dimension=0, tiled=True),
        lax.psum_scatter(weight_grads[4], ("head", "seq"), scatter_dimension=1, tiled=True),
        lax.psum_scatter(weight_grads[5], ("head", "seq"), scatter_dimension=0, tiled=True),
        lax.psum_scatter(weight_grads[6], ("head", "seq"), scatter_dimension=0, tiled=True),
        lax.psum_scatter(weight_grads[7], ("head", "seq"), scatter_dimension=1, tiled=True),
        lax.psum_scatter(weight_grads[8], ("head", "seq"), scatter_dimension=0, tiled=True),
        lax.psum_scatter(weight_grads[9], ("head", "seq"), scatter_dimension=0, tiled=True),
        lax.psum_scatter(weight_grads[10], ("head", "seq"), scatter_dimension=1, tiled=True),
    )
    return (
        output,
        grad_tokens,
        shares[0],
        shares[1],
        shares[2],
        shares[3],
        shares[4],
        shares[5],
        grad_step_bias,
        grad_skip_gain,
        shares[6],
        shares[7],
        shares[8],
        shares[9],
        shares[10],
    )


BLOCK = 128
BIT_C, BIT_ZH, BIT_ZL, BIT_Y, BIT_X = 16, 8, 4, 2, 1
DEVICES = 32
BOTH = ("head", "half", "cube")
GROUP = ("head", "cube")
CUBE_ORDERS = ((0, 1, 2), (1, 2, 0), (2, 0, 1))
CUBE_BITS = (BIT_ZL, BIT_Y, BIT_X)
bf16 = jnp.bfloat16
f32 = jnp.float32


def flip(value, mask):
    return lax.ppermute(value, BOTH, [(i, i ^ mask) for i in range(DEVICES)])


def swap_sequences(value):
    pairs = []
    for i in range(DEVICES):
        core, half = (i // BIT_C) % 2, (i // BIT_ZH) % 2
        if core != half:
            pairs.append((i, i ^ (BIT_C + BIT_ZH)))
    stays = lax.axis_index("head") == lax.axis_index("half")
    return jnp.where(stays, value, lax.ppermute(value, BOTH, pairs))


def joint(*values):
    return lax.optimization_barrier(values)


def column_parts(width):
    lanes = width // 128
    first = -(-lanes // 3)
    second = -(-(lanes - first) // 2)
    edges = (0, first * 128, (first + second) * 128, width)
    return [(edges[i], edges[i + 1]) for i in range(3)]


def assemble(pieces, outputs, info):
    count, made = len(pieces), len(outputs)
    moves = [(to, *move) for to, (_, _, out_moves) in enumerate(outputs) for move in out_moves]

    def kernel(info_ref, *refs):
        sems = refs[count + made]
        copies = []
        for at, (to, number, source, target) in enumerate(moves):
            copies.append(
                pltpu.make_async_copy(
                    refs[number].at[source(info_ref)],
                    refs[count + to].at[target(info_ref)],
                    sems.at[at],
                )
            )
        for copy in copies:
            copy.start()
        for copy in copies:
            copy.wait()

    size = sum(math.prod(shape) * jnp.dtype(kind).itemsize for shape, kind, _ in outputs)
    return pl.pallas_call(
        kernel,
        in_specs=[pl.BlockSpec(memory_space=pltpu.SMEM)]
        + [pl.BlockSpec(memory_space=pltpu.HBM)] * count,
        out_specs=[pl.BlockSpec(memory_space=pltpu.VMEM)] * made,
        out_shape=[jax.ShapeDtypeStruct(shape, kind) for shape, kind, _ in outputs],
        scratch_shapes=[pltpu.SemaphoreType.DMA((len(moves),))],
        compiler_params=pltpu.CompilerParams(vmem_limit_bytes=2 * size + 8 * 1024 * 1024),
        cost_estimate=LITTLE,
        name="assemble",
    )(info, *pieces)


def reordered_rows(value, info):
    moves = []
    for block in range(value.shape[0] // BLOCK):

        def goal(ref, block=block):
            row = pl.multiple_of((ref[2] ^ block) * BLOCK, BLOCK)
            return (pl.ds(row, BLOCK), slice(None))

        moves.append((0, fixed(block * BLOCK, BLOCK, 0, value.shape[1]), goal))
    return assemble([value], [(value.shape, value.dtype, moves)], info)[0]


def fixed(row, rows, column, columns):
    return lambda info: (pl.ds(row, rows), pl.ds(column, columns))


class Gather:
    def __init__(self, value, edges, info):
        self.rows, self.width, self.step = value.shape[0], value.shape[1], 0
        self.edges, self.info = edges, info
        self.joined = None
        self.state = ([value[:, a:b] for a, b in edges], None)

    def hop(self):
        parts, received = self.state
        if received is not None:
            parts = self.stacked(parts, received)
        sent = [
            flip(part, CUBE_BITS[order[self.step]]) for part, order in zip(parts, CUBE_ORDERS)
        ]
        self.state = (parts, sent)
        self.step += 1

    def stacked(self, parts, received):
        rows = parts[0].shape[0]
        outputs, side = [], []
        for i, (a, b) in enumerate(self.edges):
            own, got = fixed(0, rows, 0, b - a), fixed(rows, rows, 0, b - a)
            outputs.append(((2 * rows, b - a), bf16, [(i, own, own), (3 + i, own, got)]))
            side.append((i, own, fixed(0, rows, a, b - a)))
            side.append((3 + i, own, fixed(rows, rows, a, b - a)))
        if self.step == 2:
            outputs.append(((2 * rows, self.width), bf16, side))
        result = assemble(parts + received, outputs, self.info)
        if self.step == 2:
            self.joined = result[3]
        return list(result[:3])

    def pieces(self):
        while self.step < 3:
            self.hop()
        near, far = self.state
        side = [(i, fixed(0, 4 * self.rows, 0, b - a), fixed(0, 4 * self.rows, a, b - a)) for i, (a, b) in enumerate(self.edges)]
        (far_joined,) = assemble(
            far, [((4 * self.rows, self.width), bf16, side)], self.info
        )
        crossed = [flip(self.joined, BIT_C), flip(far_joined, BIT_C)]
        return near + far + crossed


def piece_blocks(part, far):
    axes = [CUBE_BITS[axis] for axis in CUBE_ORDERS[part]]
    return [
        (block, (block % 2) * axes[0] + (block // 2) * axes[1] + far * axes[2], 1)
        for block in range(4)
    ]


def gathered(gather, width, info):
    rows = gather.rows
    pieces = gather.pieces()
    moves = []
    for group in range(4):
        half, far = group // 2, group % 2
        for part, (a, b) in enumerate(column_parts(width)):
            number = 3 * group + part if half == 0 else 6 + far
            for first, place, blocks in piece_blocks(part, far):
                moves.append(
                    (
                        number,
                        fixed(first * rows, blocks * rows, a * half, b - a),
                        fixed((half * 8 + place) * rows, blocks * rows, a, b - a),
                    )
                )
    return assemble(pieces, [((16 * rows, width), bf16, moves)], info)[0]


def gather_start(value, info):
    return Gather(value, column_parts(value.shape[1]), info)


class Scatter:
    def __init__(self, own_half, other_half):
        self.total_rows, self.width = own_half.shape
        self.step = 0
        self.state = (own_half, flip(other_half.astype(bf16), BIT_C))

    def pairs(self):
        kept, received = self.state
        if self.step == 0:
            shape = (2, 2, 2, self.total_rows // 8, self.width)
            edges = column_parts(self.width)
            kept = [kept.reshape(shape)[..., a:b] for a, b in edges]
            received = [received.reshape(shape)[..., a:b] for a, b in edges]
        halves = []
        for part, got, order in zip(kept, received, CUBE_ORDERS):
            axis = order[self.step]
            halves.append(
                [
                    (
                        lax.slice_in_dim(part, i, i + 1, axis=axis).astype(f32)
                        + lax.slice_in_dim(got, i, i + 1, axis=axis).astype(f32)
                    ).astype(bf16)
                    for i in (0, 1)
                ]
            )
        return halves

    def hop(self):
        halves = self.pairs()
        sent = [
            flip(far, CUBE_BITS[order[self.step]])
            for (_, far), order in zip(halves, CUBE_ORDERS)
        ]
        self.state = ([near for near, _ in halves], sent)
        self.step += 1

    def then(self, *values):
        near, sent = self.state
        near, values = joint(near, values)
        self.state = (near, sent)
        return values

    def result(self):
        while self.step < 3:
            self.hop()
        rows = self.total_rows // 8
        return jnp.concatenate(
            [
                (near.astype(f32) + got.astype(f32)).reshape(rows, -1)
                for near, got in zip(*self.state)
            ],
            axis=1,
        )


def group_sum(value):
    for masks in ((BIT_C, BIT_X, BIT_C + BIT_X), (BIT_Y, BIT_ZL, BIT_Y + BIT_ZL)):
        first, second, third = [flip(value, mask) for mask in masks]
        value = (value + first) + (second + third)
    return value


def exchange(value):
    return lax.all_to_all(value, GROUP, split_axis=0, concat_axis=0, tiled=True)


def mm(a, b):
    return jnp.dot(a, b, preferred_element_type=f32)


def mm_nt(a, b):
    return lax.dot_general(a, b, (((1,), (1,)), ((), ())), preferred_element_type=f32)


def mm_tn(a, b):
    return lax.dot_general(a, b, (((0,), (0,)), ((), ())), preferred_element_type=f32)


VMEM_ASK = 40 * 1024 * 1024
LITTLE = pl.CostEstimate(flops=1000, bytes_accessed=1000, transcendentals=0)


def params():
    return pltpu.CompilerParams(
        dimension_semantics=("arbitrary",), vmem_limit_bytes=VMEM_ASK
    )


def k_nt(a, b, precision=None):
    return lax.dot_general(
        a, b, (((1,), (1,)), ((), ())), preferred_element_type=f32, precision=precision
    )


def k_tn(a, b):
    return lax.dot_general(a, b, (((0,), (0,)), ((), ())), preferred_element_type=f32)


def k_mm(a, b, precision=None):
    return lax.dot_general(
        a, b, (((1,), (0,)), ((), ())), preferred_element_type=f32, precision=precision
    )


def logistic(value):
    return 1.0 / (1.0 + jnp.exp(-value))


def softplus(value):
    small = jnp.exp(-jnp.abs(value))
    series = small * (1.0 - small * (0.5 - small * (1.0 / 3.0 - 0.25 * small)))
    return jnp.maximum(value, 0.0) + jnp.where(small < 0.01, series, jnp.log(1.0 + small))


def by_head(columns, lane):
    spread = columns[:, 0:1]
    for head in range(1, HEADS_HERE):
        spread = jnp.where(lane >= head * MP, columns[:, head : head + 1], spread)
    return spread


def shifted_sum(padded, taps, start, step):
    total = None
    for tap in range(KC):
        at = start + step * tap
        term = taps[tap : tap + 1] * padded[at : at + BLOCK]
        total = term if total is None else total + term
    return total


HEADS_HERE = 3
OWN = HEADS_HERE * MP
TAIL = 16
KEYS_AT = 2 * NS


def block_decays(cum_col, cum_row, lane):
    cum = by_head(cum_col, lane)
    last = cum[BLOCK - 1 : BLOCK]
    row = lax.broadcasted_iota(jnp.int32, (BLOCK, BLOCK), 0)
    col = lax.broadcasted_iota(jnp.int32, (BLOCK, BLOCK), 1)
    reach = []
    for head in range(HEADS_HERE):
        spread = cum_col[:, head : head + 1] - cum_row[head : head + 1, :]
        reach.append(jnp.where(row >= col, jnp.exp(jnp.minimum(spread, 0.0)), 0.0))
    return cum, last, reach


def step_lanes(place, lane):
    source = lax.broadcasted_iota(jnp.int32, (128, OWN), 0)
    head = lax.broadcasted_iota(jnp.int32, (128, OWN), 1) // MP
    return jnp.where(source == place * HEADS_HERE + head, 1.0, 0.0)


def mix_forward(
    info,
    own_ref,
    s_ref,
    cos_ref,
    sin_ref,
    cum_col_ref,
    cum_row_ref,
    taps_x_ref,
    taps_m_ref,
    vec_ref,
    y_ref,
    gained_ref,
    square_ref,
    state_ref,
    q_ref,
    k_ref,
    v_ref,
    state,
    last_x,
    last_m,
):
    @pl.when(pl.program_id(0) == 0)
    def _():
        state[...] = jnp.zeros_like(state)
        last_x[...] = jnp.zeros_like(last_x)
        last_m[...] = jnp.zeros_like(last_m)

    lane = lax.broadcasted_iota(jnp.int32, (1, OWN), 1)
    gate = own_ref[:, :OWN].astype(f32)
    x_raw = own_ref[:, OWN : 2 * OWN].astype(f32)
    m_raw = s_ref[:, : 2 * NS].astype(f32)
    cosine, sine = cos_ref[...], sin_ref[...]

    def turned(value):
        return (value * cosine + pltpu.roll(value, HD // 2, 1) * sine).astype(bf16)

    q_ref[...] = turned(own_ref[:, 2 * OWN :].astype(f32))
    k_ref[...] = turned(s_ref[:, KEYS_AT : KEYS_AT + HD].astype(f32))
    v_ref[...] = s_ref[:, KEYS_AT + HD : KEYS_AT + 2 * HD].astype(bf16)

    s_x = shifted_sum(
        jnp.concatenate([last_x[...], x_raw], axis=0), taps_x_ref, TAIL - KC + 1, 1
    ) + taps_x_ref[KC : KC + 1]
    s_m = shifted_sum(
        jnp.concatenate([last_m[...], m_raw], axis=0), taps_m_ref, TAIL - KC + 1, 1
    ) + taps_m_ref[KC : KC + 1]
    last_x[...] = x_raw[BLOCK - TAIL :]
    last_m[...] = m_raw[BLOCK - TAIL :]
    x = (s_x * logistic(s_x)).astype(bf16).astype(f32)
    maps = (s_m * logistic(s_m)).astype(bf16)
    b_map, c_map = maps[:, :NS], maps[:, NS:]

    place = info[0]
    picked = k_mm(s_ref[:, KEYS_AT + 2 * HD :].astype(bf16), step_lanes(place, lane).astype(bf16))
    raised = picked + vec_ref[0:1]
    step = softplus(raised)
    cum, last, reach = block_decays(cum_col_ref[...], cum_row_ref[0], lane)
    scaled = step * x
    inter = k_nt(c_map, b_map)
    total = vec_ref[1:2] * x
    for head in range(HEADS_HERE):
        here = (lane >= head * MP) & (lane < (head + 1) * MP)
        total += k_mm(
            (reach[head] * inter).astype(bf16), jnp.where(here, scaled, 0.0).astype(bf16)
        )
    before = state[...]
    state_ref[0] = before.astype(bf16)
    total += jnp.exp(cum) * k_mm(c_map, before.astype(bf16))
    tail = (jnp.exp(last - cum) * scaled).astype(bf16)
    state[...] = jnp.exp(last) * before + k_tn(b_map, tail)
    y = total.astype(bf16)
    y_ref[...] = y
    gated = y.astype(f32) * (gate * logistic(gate))
    gained_ref[...] = (gated * vec_ref[2:3]).astype(bf16)
    square_ref[0] = k_nt(jnp.ones((8, OWN), f32), gated * gated, HIGHEST)


def mix_backward(
    info,
    own_ref,
    s_ref,
    own_tail_ref,
    s_tail_ref,
    cos_ref,
    sin_ref,
    cum_col_ref,
    cum_row_ref,
    taps_x_ref,
    taps_m_ref,
    vec_ref,
    lanes_ref,
    g_y_ref,
    g_z_ref,
    state_ref,
    dq_ref,
    dk_ref,
    dv_ref,
    g_all_ref,
    acc_x_ref,
    acc_m_ref,
    acc_v_ref,
    acc_s_ref,
    g_state,
    next_x,
    next_m,
):
    step_id = pl.program_id(0)
    block = pl.num_programs(0) - 1 - step_id
    place = info[0]

    @pl.when(step_id == 0)
    def _():
        g_state[...] = jnp.zeros_like(g_state)
        next_x[...] = jnp.zeros_like(next_x)
        next_m[...] = jnp.zeros_like(next_m)
        acc_x_ref[...] = jnp.zeros_like(acc_x_ref)
        acc_m_ref[...] = jnp.zeros_like(acc_m_ref)
        acc_v_ref[...] = jnp.zeros_like(acc_v_ref)
        acc_s_ref[...] = jnp.zeros_like(acc_s_ref)

    lane = lax.broadcasted_iota(jnp.int32, (1, OWN), 1)
    cosine, sine = cos_ref[...], sin_ref[...]

    def unturned(value):
        return value * cosine - pltpu.roll(value, HD // 2, 1) * sine

    x_raw = own_ref[:, OWN : 2 * OWN].astype(f32)
    m_raw = s_ref[:, : 2 * NS].astype(f32)
    first = block == 0
    x_pad = jnp.concatenate(
        [jnp.where(first, 0.0, own_tail_ref[:, OWN : 2 * OWN].astype(f32)), x_raw], axis=0
    )
    m_pad = jnp.concatenate([jnp.where(first, 0.0, s_tail_ref[:, : 2 * NS].astype(f32)), m_raw], axis=0)
    s_x = shifted_sum(x_pad, taps_x_ref, TAIL - KC + 1, 1) + taps_x_ref[KC : KC + 1]
    s_m = shifted_sum(m_pad, taps_m_ref, TAIL - KC + 1, 1) + taps_m_ref[KC : KC + 1]
    sig_x, sig_m = logistic(s_x), logistic(s_m)
    x = (s_x * sig_x).astype(bf16).astype(f32)
    maps = (s_m * sig_m).astype(bf16)
    b_map, c_map = maps[:, :NS], maps[:, NS:]
    select = step_lanes(place, lane)
    step_raw = s_ref[:, KEYS_AT + 2 * HD :].astype(bf16)
    raised = k_mm(step_raw, select.astype(bf16)) + vec_ref[0:1]
    step = softplus(raised)
    cum, last, reach = block_decays(cum_col_ref[...], cum_row_ref[0], lane)
    scaled = step * x

    g_y = g_y_ref[...].astype(f32)

    inter = k_nt(c_map, b_map)
    g_inter = jnp.zeros((BLOCK, BLOCK), f32)
    g_scaled = jnp.zeros((BLOCK, OWN), f32)
    scaled_b = scaled.astype(bf16)
    for head in range(HEADS_HERE):
        here = (lane >= head * MP) & (lane < (head + 1) * MP)
        g_head = jnp.where(here, g_y, 0.0).astype(bf16)
        g_inter += reach[head] * k_nt(g_head, scaled_b)
        g_scaled += k_tn((reach[head] * inter).astype(bf16), g_head)
    before = state_ref[0]
    g_after = g_state[...]
    g_after_b = g_after.astype(bf16)
    tail_w = jnp.exp(last - cum)
    reached = (jnp.exp(cum) * g_y).astype(bf16)
    g_inter_b = g_inter.astype(bf16)
    g_c = k_mm(g_inter_b, b_map) + k_nt(reached, before)
    g_b = k_tn(g_inter_b, c_map) + k_nt((tail_w * scaled).astype(bf16), g_after_b)
    g_scaled += tail_w * k_mm(b_map, g_after_b)
    g_state[...] = jnp.exp(last) * g_after + k_tn(c_map, reached)
    g_x = step * g_scaled + vec_ref[1:2] * g_y
    g_step = k_nt(x * g_scaled, select, HIGHEST) * logistic(
        step_raw.astype(f32) + lanes_ref[0:1]
    )

    gs_x = g_x.astype(bf16).astype(f32) * (sig_x * (1.0 + s_x * (1.0 - sig_x)))
    g_maps = jnp.concatenate([g_b, g_c], axis=1).astype(bf16).astype(f32)
    gs_m = g_maps * (sig_m * (1.0 + s_m * (1.0 - sig_m)))
    gs_x_pad = jnp.concatenate([gs_x, next_x[...]], axis=0)
    gs_m_pad = jnp.concatenate([gs_m, next_m[...]], axis=0)
    g_x_raw = shifted_sum(gs_x_pad, taps_x_ref, KC - 1, -1)
    g_m_raw = shifted_sum(gs_m_pad, taps_m_ref, KC - 1, -1)
    next_x[...] = gs_x[:TAIL]
    next_m[...] = gs_m[:TAIL]
    for tap in range(KC):
        at = TAIL - KC + 1 + tap
        acc_x_ref[tap : tap + 1] += jnp.sum(gs_x * x_pad[at : at + BLOCK], axis=0, keepdims=True)
        acc_m_ref[tap : tap + 1] += jnp.sum(gs_m * m_pad[at : at + BLOCK], axis=0, keepdims=True)
    acc_x_ref[KC : KC + 1] += jnp.sum(gs_x, axis=0, keepdims=True)
    acc_m_ref[KC : KC + 1] += jnp.sum(gs_m, axis=0, keepdims=True)
    acc_v_ref[0:1] += jnp.sum(g_y * x, axis=0, keepdims=True)
    acc_s_ref[0:1] += jnp.sum(g_step, axis=0, keepdims=True)

    here = (block // 8) == info[1]
    g_q = jnp.where(here, dq_ref[...].astype(f32), 0.0)
    at = 2 * OWN
    g_all_ref[:, :at] = jnp.concatenate([g_z_ref[...].astype(f32), g_x_raw], axis=1).astype(bf16)
    for piece in (g_q, g_m_raw, unturned(dk_ref[...]), dv_ref[...], g_step):
        g_all_ref[:, at : at + piece.shape[1]] = piece.astype(bf16)
        at += piece.shape[1]


def masked_scores(info, keys, queries, length):
    scores = k_nt(keys, queries) * (HD**-0.5)
    start = (info[1] * 8 + pl.program_id(0)) * BLOCK
    key_at = lax.broadcasted_iota(jnp.int32, (length, BLOCK), 0)
    query_at = lax.broadcasted_iota(jnp.int32, (length, BLOCK), 1) + start
    return scores, key_at <= query_at


def attend_forward(info, q_ref, k_ref, v_ref, out_ref, out_f_ref, log_ref):
    scores, allowed = masked_scores(info, k_ref[...], q_ref[...], k_ref.shape[0])
    scores = jnp.where(allowed, scores, NEGATIVE)
    top = jnp.max(scores, axis=0, keepdims=True)
    weights = jnp.exp(scores - top)
    total = jnp.sum(weights, axis=0, keepdims=True)
    result = jnp.transpose(k_tn(v_ref[...], weights.astype(bf16)) / total)
    out_ref[...] = result.astype(bf16)
    out_f_ref[...] = result
    log_ref[0] = jnp.broadcast_to(top + jnp.log(total), (8, BLOCK))


def attend_backward(
    info, q_ref, k_ref, v_ref, out_f_ref, log_ref, g_ref, cos_ref, sin_ref, dq_ref, dk_ref, dv_ref
):
    @pl.when(pl.program_id(0) == 0)
    def _():
        dk_ref[...] = jnp.zeros_like(dk_ref)
        dv_ref[...] = jnp.zeros_like(dv_ref)

    keys, queries, grads = k_ref[...], q_ref[...], g_ref[...]
    scores, allowed = masked_scores(info, keys, queries, k_ref.shape[0])
    probs = jnp.where(allowed, jnp.exp(scores - log_ref[0, 0:1]), 0.0)
    delta = k_nt(jnp.ones((8, HD), f32), grads.astype(f32) * out_f_ref[...], HIGHEST)[0:1]
    g_scores = (probs * (k_nt(v_ref[...], grads) - delta)).astype(bf16)
    dv_ref[...] += k_mm(probs.astype(bf16), grads)
    dk_ref[...] += k_mm(g_scores, queries) * (HD**-0.5)
    dq = (k_tn(g_scores, keys) * (HD**-0.5)).astype(bf16).astype(f32)
    dq_ref[...] = (dq * cos_ref[...] - pltpu.roll(dq, HD // 2, 1) * sin_ref[...]).astype(bf16)


def rows_at(width, column=0):
    return pl.BlockSpec((BLOCK, width), lambda i, s: (i ^ s[0], column))


def rows_back(count, width, column=0):
    return pl.BlockSpec((BLOCK, width), lambda i, s: ((count - 1 - i) ^ s[0], column))


def whole(*shape):
    return pl.BlockSpec(shape, lambda i, s: (0,) * len(shape))


def run_mix_forward(info, own, shared, cosine, sine, cum_col, cum_row, taps_x, taps_m, vec):
    length = own.shape[0]
    count = length // BLOCK

    def plain(width):
        return pl.BlockSpec((BLOCK, width), lambda i, s: (i, 0))

    def plain3(rows, width):
        return pl.BlockSpec((1, rows, width), lambda i, s: (i, 0, 0))

    return pl.pallas_call(
        mix_forward,
        grid_spec=pltpu.PrefetchScalarGridSpec(
            num_scalar_prefetch=1,
            grid=(count,),
            in_specs=[
                rows_at(own.shape[1]),
                rows_at(shared.shape[1]),
                plain(HD),
                plain(HD),
                plain(8),
                plain3(8, BLOCK),
                whole(8, OWN),
                whole(8, 2 * NS),
                whole(8, OWN),
            ],
            out_specs=[
                rows_at(OWN),
                rows_at(OWN),
                plain3(8, BLOCK),
                plain3(NS, OWN),
                plain(HD),
                plain(HD),
                plain(HD),
            ],
            scratch_shapes=[
                pltpu.VMEM((NS, OWN), f32),
                pltpu.VMEM((TAIL, OWN), f32),
                pltpu.VMEM((TAIL, 2 * NS), f32),
            ],
        ),
        out_shape=[
            jax.ShapeDtypeStruct((length, OWN), bf16),
            jax.ShapeDtypeStruct((length, OWN), bf16),
            jax.ShapeDtypeStruct((count, 8, BLOCK), f32),
            jax.ShapeDtypeStruct((count, NS, OWN), bf16),
            jax.ShapeDtypeStruct((length, HD), bf16),
            jax.ShapeDtypeStruct((length, HD), bf16),
            jax.ShapeDtypeStruct((length, HD), bf16),
        ],
        compiler_params=params(),
        cost_estimate=LITTLE,
        name="mix_forward",
    )(info, own, shared, cosine, sine, cum_col, cum_row, taps_x, taps_m, vec)


def run_mix_backward(
    info,
    own,
    shared,
    cosine,
    sine,
    cum_col,
    cum_row,
    taps_x,
    taps_m,
    vec,
    lanes,
    g_y,
    g_z,
    states,
    dq,
    dk,
    dv,
):
    length = own.shape[0]
    count = length // BLOCK
    tails = BLOCK // TAIL
    all_width = own.shape[1] + shared.shape[1]

    def plain(width):
        return pl.BlockSpec((BLOCK, width), lambda i, s: (count - 1 - i, 0))

    def plain3(rows, width):
        return pl.BlockSpec((1, rows, width), lambda i, s: (count - 1 - i, 0, 0))

    def tail_of(width):
        def where(i, s):
            before = jnp.maximum(count - 2 - i, 0)
            return ((before ^ s[0]) * tails + tails - 1, 0)

        return pl.BlockSpec((TAIL, width), where)

    def query_rows(i, s):
        return (((count - 1 - i) ^ s[0]) % 8, 0)

    return pl.pallas_call(
        mix_backward,
        grid_spec=pltpu.PrefetchScalarGridSpec(
            num_scalar_prefetch=1,
            grid=(count,),
            in_specs=[
                rows_back(count, own.shape[1]),
                rows_back(count, shared.shape[1]),
                tail_of(own.shape[1]),
                tail_of(shared.shape[1]),
                plain(HD),
                plain(HD),
                plain(8),
                plain3(8, BLOCK),
                whole(8, OWN),
                whole(8, 2 * NS),
                whole(8, OWN),
                whole(8, 128),
                rows_back(count, OWN),
                rows_back(count, OWN),
                plain3(NS, OWN),
                pl.BlockSpec((BLOCK, HD), query_rows),
                plain(HD),
                plain(HD),
            ],
            out_specs=[
                rows_back(count, all_width),
                whole(8, OWN),
                whole(8, 2 * NS),
                whole(8, OWN),
                whole(8, 128),
            ],
            scratch_shapes=[
                pltpu.VMEM((NS, OWN), f32),
                pltpu.VMEM((TAIL, OWN), f32),
                pltpu.VMEM((TAIL, 2 * NS), f32),
            ],
        ),
        out_shape=[
            jax.ShapeDtypeStruct((length, all_width), bf16),
            jax.ShapeDtypeStruct((8, OWN), f32),
            jax.ShapeDtypeStruct((8, 2 * NS), f32),
            jax.ShapeDtypeStruct((8, OWN), f32),
            jax.ShapeDtypeStruct((8, 128), f32),
        ],
        compiler_params=params(),
        cost_estimate=LITTLE,
        name="mix_backward",
    )(
        info,
        own,
        shared,
        own,
        shared,
        cosine,
        sine,
        cum_col,
        cum_row,
        taps_x,
        taps_m,
        vec,
        lanes,
        g_y,
        g_z,
        states,
        dq,
        dk,
        dv,
    )


def own_queries(width):
    return pl.BlockSpec((BLOCK, width), lambda i, s: (s[1] * 8 + i, 0))


def own_rows(width):
    return pl.BlockSpec((BLOCK, width), lambda i, s: (i ^ s[2], 0))


def run_attend_forward(info, queries, keys, values):
    length = keys.shape[0]
    half = length // 2
    count = half // BLOCK
    return pl.pallas_call(
        attend_forward,
        grid_spec=pltpu.PrefetchScalarGridSpec(
            num_scalar_prefetch=1,
            grid=(count,),
            in_specs=[own_queries(HD), whole(length, HD), whole(length, HD)],
            out_specs=[
                own_rows(HD),
                pl.BlockSpec((BLOCK, HD), lambda i, s: (i, 0)),
                pl.BlockSpec((1, 8, BLOCK), lambda i, s: (i, 0, 0)),
            ],
        ),
        out_shape=[
            jax.ShapeDtypeStruct((half, HD), bf16),
            jax.ShapeDtypeStruct((half, HD), f32),
            jax.ShapeDtypeStruct((count, 8, BLOCK), f32),
        ],
        compiler_params=params(),
        cost_estimate=LITTLE,
        name="attend_forward",
    )(info, queries, keys, values)


def run_attend_backward(info, queries, keys, values, out_f, logs, grads, cosine, sine):
    length = keys.shape[0]
    half = length // 2
    count = half // BLOCK
    return pl.pallas_call(
        attend_backward,
        grid_spec=pltpu.PrefetchScalarGridSpec(
            num_scalar_prefetch=1,
            grid=(count,),
            in_specs=[
                own_queries(HD),
                whole(length, HD),
                whole(length, HD),
                pl.BlockSpec((BLOCK, HD), lambda i, s: (i, 0)),
                pl.BlockSpec((1, 8, BLOCK), lambda i, s: (i, 0, 0)),
                own_rows(HD),
                own_queries(HD),
                own_queries(HD),
            ],
            out_specs=[
                own_rows(HD),
                whole(length, HD),
                whole(length, HD),
            ],
        ),
        out_shape=[
            jax.ShapeDtypeStruct((half, HD), bf16),
            jax.ShapeDtypeStruct((length, HD), f32),
            jax.ShapeDtypeStruct((length, HD), f32),
        ],
        compiler_params=params(),
        cost_estimate=LITTLE,
        name="attend_backward",
    )(info, queries, keys, values, out_f, logs, grads, cosine, sine)


def cube_body(
    tokens,
    log_decay,
    norm_gain,
    qkv_proj,
    attn_proj,
    inner_proj,
    conv_weight,
    conv_bias,
    step_bias,
    skip_gain,
    inner_gain,
    inner_out,
    ff_gain,
    gate_up,
    down_proj,
    cotangent,
):
    core = lax.axis_index("head")
    seq_half = lax.axis_index("half")
    member = lax.axis_index("cube")
    chip = seq_half * 8 + member
    bits = (member // 4, (member // 2) % 2, member % 2)
    zl = bits[0]
    place = core * 8 + member
    info = jnp.stack([place, core, member, seq_half]).astype(jnp.int32)
    width = tokens.shape[-1]
    rows = tokens.shape[1]
    shard = width // DEVICES
    inner_width = MH * MP
    conv_width = inner_width + 2 * NS
    heads = MH // 16
    mine = heads * MP
    length = rows * 16
    half_rows = rows * 8
    ffc = FF // 16

    def to_local(value):
        parts = [value[:, i * width // 4 : (i + 1) * width // 4] for i in range(4)]
        return jnp.where(
            seq_half == 0,
            jnp.concatenate([parts[i] for i in (0, 2, 1, 3)], axis=1),
            jnp.concatenate([parts[i] for i in (1, 3, 0, 2)], axis=1),
        )

    def to_natural(value):
        parts = [value[:, i * width // 4 : (i + 1) * width // 4] for i in range(4)]
        return jnp.where(
            seq_half == 0,
            jnp.concatenate([parts[i] for i in (0, 2, 1, 3)], axis=1),
            jnp.concatenate([parts[i] for i in (2, 0, 3, 1)], axis=1),
        )

    swapped = swap_sequences(jnp.concatenate([tokens[0], cotangent[0]], axis=0))
    x_bf, g_out_bf = to_local(swapped[:rows]), to_local(swapped[rows:])

    gain_rows = norm_gain.astype(f32)[:, None]
    qkv_s = (qkv_proj.astype(f32) * gain_rows).astype(bf16)
    inner_s = (inner_proj.astype(f32) * gain_rows).astype(bf16)
    gate_up_s = (gate_up.astype(f32) * ff_gain.astype(f32)[:, None]).astype(bf16)

    def to_places(value):
        return jnp.moveaxis(value.reshape(shard, 16, -1), 1, 0)

    def to_members(value):
        parts = jnp.moveaxis(value.reshape(shard, 8, -1), 1, 0)
        return jnp.concatenate([parts, parts], axis=0)

    def both_halves(value, other):
        return jnp.concatenate([value, other], axis=0)

    kv_width = KVH * HD
    conv_shard = conv_weight.shape[1]
    smalls = jnp.concatenate([conv_weight.reshape(-1), conv_bias, inner_gain])
    decay_rows = jnp.moveaxis(log_decay, 1, 2).reshape(2, -1)
    decay_high = lax.optimization_barrier(decay_rows.astype(bf16))
    decay_low = (decay_rows - decay_high.astype(f32)).astype(bf16)
    decay_rows = jnp.concatenate([decay_high, decay_low], axis=1)
    extra_size = shard * 128
    extra_pad = jnp.zeros((extra_size - smalls.shape[0] - decay_rows.shape[1],), bf16)

    def shared_for(half):
        mine_rows = lax.dynamic_index_in_dim(decay_rows, half, 0, keepdims=False)
        extra = jnp.concatenate([smalls, mine_rows, extra_pad]).reshape(shard, 128)
        return jnp.concatenate([shared_send, extra], axis=1)

    shared_send = jnp.concatenate(
        [
            inner_s[:, 2 * inner_width : inner_width + conv_width],
            qkv_s[:, QH * HD : QH * HD + kv_width],
            inner_s[:, inner_width + conv_width :],
            jnp.zeros((shard, -MH % 128), bf16),
            qkv_s[:, QH * HD + kv_width :],
        ],
        axis=1,
    )
    shared_other = flip(shared_for(1 - seq_half), BIT_ZH)
    send_own = jnp.concatenate(
        [
            to_places(inner_s[:, :inner_width]),
            to_places(inner_s[:, inner_width : 2 * inner_width]),
            to_members(qkv_s[:, : QH * HD]),
        ],
        axis=2,
    )
    got_own = exchange(send_own).reshape(width // 2, -1)
    x_rows = x_bf.astype(f32)
    inv_in = lax.rsqrt(jnp.mean(x_rows * x_rows, axis=-1, keepdims=True) + EPSILON)
    shared_mine = shared_for(seq_half)
    shared_both = jnp.concatenate([shared_mine, shared_other], axis=0)
    normed_mine = (x_rows * inv_in).astype(bf16)
    shared_edges = ((0, 2 * NS), (2 * NS, 2 * NS + kv_width + 128), (2 * NS + kv_width + 128, None))
    lanes_all = (shared_both.shape[1] + width) // 128
    goals = (-(-lanes_all // 3), -(-lanes_all // 3), lanes_all - 2 * -(-lanes_all // 3))
    edges, normed_edges, joined, at, done = [], [], [], 0, 0
    for (a, b), lanes_here in zip(shared_edges, goals):
        part = shared_both[:, a:b]
        taken = lanes_here * 128 - part.shape[1]
        joined += [part, normed_mine[:, done : done + taken]]
        edges.append((at, at + lanes_here * 128))
        normed_edges.append((part.shape[1], done, taken))
        at += lanes_here * 128
        done += taken
    first = Gather(jnp.concatenate(joined, axis=1), edges, info)
    first.state, got_own = joint(first.state, got_own)
    own_width = 2 * mine + HD
    other_own = [flip(got_own[:, : own_width // 2], BIT_ZH), None]
    first.hop()
    send_rest = jnp.concatenate(
        [
            to_places(inner_out.T),
            to_members(attn_proj.T),
            to_places(gate_up_s[:, :FF]),
            to_places(gate_up_s[:, FF:]),
            to_places(down_proj.T),
        ],
        axis=2,
    )
    positions = jnp.arange(length, dtype=f32)
    frequency = ROPE_BASE ** (-2.0 * jnp.arange(HD // 2, dtype=f32) / HD)
    angle = positions[:, None] * frequency[None, :]
    cosine, sine = jnp.cos(angle), jnp.sin(angle)
    cosine = jnp.concatenate([cosine, cosine], axis=1)
    sine = jnp.concatenate([-sine, sine], axis=1)
    first.hop()
    first.state, other_own[0], got_own = joint(first.state, other_own[0], got_own)
    other_own[1] = flip(got_own[:, own_width // 2 :], BIT_ZH)
    first.hop()
    first.state, send_rest, other_own[1], cosine, sine = joint(
        first.state, send_rest, other_own[1], cosine, sine
    )
    got = exchange(send_rest).reshape(width // 2, -1)
    pieces = first.pieces()
    shared_width = 2 * NS + 2 * HD + 128
    picks = (
        ((0, 0, 0, 2 * NS),),
        ((0, HD, 2 * NS, HD), (kv_width, 0, 2 * NS + 2 * HD, 128)),
        ((0, HD, 2 * NS + HD, HD),),
    )
    moves, extra_moves, normed_moves = [], [], []
    for group in range(4):
        half, far = group // 2, group % 2
        for part in range(3):
            number = 3 * group + part if half == 0 else 6 + far
            start = edges[part][0] * half
            skip, normed_at, taken = normed_edges[part]
            for begin, cube_place, count in piece_blocks(part, far):
                normed_moves.append(
                    (
                        number,
                        fixed(begin * rows, count * rows, start + skip, taken),
                        fixed((half * 8 + cube_place) * rows, count * rows, normed_at, taken),
                    )
                )
                for block, zh in ((i, j) for i in range(count) for j in range(2)):
                    row = (begin + block) * 2 * shard + zh * shard
                    position = half * 8 + cube_place + block

                    def goal(ref, position=position, zh=zh, target=0, columns=128):
                        to = zh * 16 + (ref[0] ^ position)
                        to = pl.multiple_of(to * shard, shard)
                        return (pl.ds(to, shard), pl.ds(target, columns))

                    def extra_goal(ref, position=position, zh=zh):
                        place = ref[0] ^ position
                        to = (place // 8) * 16 + (zh ^ ref[3]) * 8 + place % 8
                        to = pl.multiple_of(to * shard, shard)
                        return (pl.ds(to, shard), pl.ds(0, 128))

                    for column, by_zl, target, columns in picks[part]:

                        def source(ref, row=row, at=start + column, by_zl=by_zl, columns=columns):
                            if by_zl:
                                at = pl.multiple_of(at + (ref[2] // 4) * by_zl, 128)
                            return (pl.ds(row, shard), pl.ds(at, columns))

                        moves.append(
                            (
                                number,
                                source,
                                functools.partial(goal, target=target, columns=columns),
                            )
                        )
                    if part == 2:
                        extra_moves.append(
                            (number, fixed(row, shard, start + kv_width, 128), extra_goal)
                        )
    normed, w_s, small_got = assemble(
        pieces,
        [
            ((length, width), bf16, normed_moves),
            ((width, shared_width), bf16, moves),
            ((width, 128), bf16, extra_moves),
        ],
        info,
    )
    small_got = small_got.reshape(DEVICES, -1)
    at = smalls.shape[0]
    decay = lax.dynamic_slice_in_dim(small_got[:, at : at + decay_rows.shape[1]], core * 16, 16, 0)
    decay = decay.astype(f32).reshape(16, 2, 8, heads, rows)
    decay = lax.dynamic_index_in_dim(decay[:, 0] + decay[:, 1], member, 1, keepdims=False)
    at = 0
    conv_w = jnp.moveaxis(
        small_got[:, at : at + KC * conv_shard].reshape(DEVICES, KC, conv_shard), 1, 0
    ).reshape(KC, conv_width)
    at += KC * conv_shard
    conv_b = small_got[:, at : at + conv_shard].reshape(1, conv_width)
    at += conv_shard
    gain_all = small_got[:, at : at + inner_gain.shape[0]].reshape(1, inner_width)
    conv_all = jnp.concatenate([conv_w, conv_b], axis=0).astype(f32)
    conv_all = jnp.concatenate([conv_all, jnp.zeros((8 - KC - 1, conv_width), f32)], axis=0)
    taps_x = lax.dynamic_slice_in_dim(conv_all[:, :inner_width], place * mine, mine, 1)
    taps_m = conv_all[:, inner_width:]
    gain_mine = lax.dynamic_slice_in_dim(gain_all, place * mine, mine, 1)[0].astype(f32)

    (w_own,) = joint(both_halves(got_own, jnp.concatenate(other_own, axis=1)))
    bias_mine = lax.dynamic_slice_in_dim(step_bias, member * heads, heads, 0)
    skip_mine = lax.dynamic_slice_in_dim(skip_gain, member * heads, heads, 0)
    vec = jnp.concatenate(
        [
            jnp.repeat(bias_mine, MP)[None],
            jnp.repeat(skip_mine, MP)[None],
            gain_mine[None],
            jnp.zeros((5, mine), f32),
        ],
        axis=0,
    )
    lanes = lax.dynamic_update_slice(
        jnp.zeros((8, 128), f32), bias_mine[None], (0, place * heads)
    )
    cum_row = jnp.cumsum(decay, axis=2)
    cum_row = jnp.concatenate([cum_row, jnp.zeros((16, 8 - heads, rows), f32)], axis=1)
    cum_col = jnp.moveaxis(cum_row, 1, 2).reshape(length, 8)
    (w_all,) = joint(jnp.concatenate([w_own, w_s], axis=1))

    order = jnp.arange(16, dtype=jnp.int32) ^ place

    def reordered(value):
        return jnp.take(value, order, axis=0, unique_indices=True, mode="clip")

    g_out_bf, normed = joint(g_out_bf, normed)
    g_out = gather_start(g_out_bf, info)
    g_out.hop()
    raw_s = mm(normed, w_s).astype(bf16)
    g_out.state, raw_s, got, normed = joint(g_out.state, raw_s, got, normed)
    cuts = [0, mine + HD] + [mine + HD + i * ffc for i in (1, 2, 3)]
    got = [got[:, a:b] for a, b in zip(cuts[:-1], cuts[1:])]
    other = [flip(got[0], BIT_ZH), None, None, None]
    g_out.hop()
    raw_own = mm(normed, w_own).astype(bf16)
    g_out.state, raw_own = joint(g_out.state, raw_own)
    g_out.hop()

    tables = (cosine, sine, cum_col, cum_row, taps_x, taps_m, vec)
    y, gained, squares, states, queries, keys, values = run_mix_forward(
        info, raw_own, raw_s, *tables
    )
    squares, other[0] = joint(squares, other[0])
    other[3] = flip(got[3], BIT_ZH)
    (w_mix,) = joint(both_halves(got[0], other[0]))
    w_out, w_att = w_mix[:, :mine], w_mix[:, mine:]
    squares = group_sum(squares[:, 0])
    squares, queries, other[3], got[1] = joint(squares, queries, other[3], got[1])
    other[1] = flip(got[1], BIT_ZH)
    (w_down,) = joint(both_halves(got[3], other[3]))
    attended, attended_f, logs = run_attend_forward(info, queries, keys, values)
    inv_mix = lax.rsqrt(squares / inner_width + EPSILON)
    inv_mix_rows = reordered(inv_mix).reshape(length, 1)
    part_other = inv_mix_rows[half_rows:] * mm_nt(gained[half_rows:], w_out)
    part_own = inv_mix_rows[:half_rows] * mm_nt(gained[:half_rows], w_out) + mm_nt(attended, w_att)
    sums = Scatter(part_own.astype(bf16), part_other)
    sums.state, other[1], got[2] = joint(sums.state, other[1], got[2])
    other[2] = flip(got[2], BIT_ZH)
    sums.hop()
    sums.hop()
    sums.state, other[2] = joint(sums.state, other[2])
    (w_gu,) = joint(
        jnp.concatenate([both_halves(got[i], other[i]) for i in (1, 2)], axis=1)
    )
    hidden = x_rows + sums.result()
    g_out = gathered(g_out, width, info)

    inv_ff = lax.rsqrt(jnp.mean(hidden * hidden, axis=-1, keepdims=True) + EPSILON)
    gather = gather_start((hidden * inv_ff).astype(bf16), info)
    normed_ff = gathered(gather, width, info)
    gate_vals = mm(normed_ff, w_gu)
    gate, up = gate_vals[:, :ffc], gate_vals[:, ffc:]
    sig = jax.nn.sigmoid(gate)
    mixed = (gate * sig * up).astype(bf16)
    g_mixed = mm(g_out, w_down)
    g_vals = jnp.concatenate(
        [g_mixed * up * sig * (1.0 + gate * (1.0 - sig)), g_mixed * gate * sig], axis=1
    ).astype(bf16)
    g_ff_other = mm_nt(g_vals[half_rows:], w_gu).astype(bf16)
    sums = Scatter(mm_nt(g_vals[:half_rows], w_gu).astype(bf16), g_ff_other)
    sums.hop()
    def crossing(value):
        return flip(value[width // 2 :], BIT_ZH)

    def to_owners(values, crossed):
        total = [
            value[: width // 2].astype(f32) + got.astype(f32)
            for value, got in zip(values, crossed)
        ]
        total = jnp.concatenate([part.astype(bf16) for part in total], axis=1)
        return exchange(total.reshape(16, shard, -1))

    mixed_late, g_vals_late = sums.then(mixed, g_vals)
    mixed_cube = reordered_rows(mixed_late, info)
    out_other = mm_nt(mixed_cube[half_rows:], w_down).astype(bf16)
    out_own = mm_nt(mixed_cube[:half_rows], w_down).astype(bf16)
    d_gu = mm_tn(normed_ff, g_vals_late).astype(bf16)
    d_gate, d_up = d_gu[:, :ffc], d_gu[:, ffc:]
    sums.state, out_other, out_own, d_gate = joint(sums.state, out_other, out_own, d_gate)
    out_got = flip(out_other, BIT_C)
    gate_got = crossing(d_gate)
    sums.hop()
    mixed_late, g_out = sums.then(mixed_late, g_out)
    d_down = mm_tn(g_out, mixed_late).astype(bf16)
    sums.state, d_down = joint(sums.state, d_down)
    g_ff = sums.result()

    def from_places(value):
        return jnp.moveaxis(value, 0, 1).reshape(shard, -1)

    g_hidden = (
        g_out_bf.astype(f32)
        + inv_ff * g_ff
        - hidden * inv_ff**3 * jnp.mean(hidden * g_ff, axis=-1, keepdims=True)
    )
    gather = gather_start(g_hidden.astype(bf16), info)
    gather.state, gate_got, d_up = joint(gather.state, gate_got, d_up)
    up_got = crossing(d_up)
    gather.hop()
    gather.hop()
    out_sum = (out_own.astype(f32) + out_got.astype(f32)).astype(bf16)
    gather.state, up_got, d_down, out_sum, w_all = joint(
        gather.state, up_got, d_down, out_sum, w_all
    )
    down_got = crossing(d_down)
    g_branch = gathered(gather, width, info)

    inner_normed = (gained.astype(f32) * inv_mix_rows).astype(bf16)
    g_inner = mm(g_branch, w_out)
    g_branch_own = g_branch[:half_rows]
    g_att = mm(g_branch_own, w_att).astype(bf16)
    dots = jnp.sum(inner_normed.astype(f32) * g_inner, axis=-1).reshape(16, rows)
    dots = group_sum(reordered(dots))
    g_branch_own = g_branch[:half_rows]
    g_att = mm(g_branch_own, w_att).astype(bf16)
    d_mix_early = jnp.concatenate(
        [
            mm_tn(g_branch, inner_normed).astype(bf16),
            mm_tn(g_branch_own, attended).astype(bf16),
        ],
        axis=1,
    )
    d_mix_early, g_att = joint(d_mix_early, g_att)
    early_got = crossing(d_mix_early)
    d_q, d_k, d_v = run_attend_backward(
        info, queries, keys, values, attended_f, logs, g_att, cosine, sine
    )
    gate = raw_own[:, :mine].astype(f32)
    gate_sig = jax.nn.sigmoid(gate)
    y_rows = y.astype(f32)
    normed_mix = y_rows * (gate * gate_sig) * inv_mix_rows
    g_gated = inv_mix_rows * (
        gain_mine * g_inner - normed_mix * (reordered(dots).reshape(length, 1) / inner_width)
    )
    g_y = (g_gated * gate * gate_sig).astype(bf16)
    g_z = (g_gated * y_rows * gate_sig * (1.0 + gate * (1.0 - gate_sig))).astype(bf16)
    grad_gain_mine = jnp.sum(normed_mix * g_inner, axis=0)
    d_q, down_got, dots = joint(d_q, down_got, dots)
    d_ff_got = to_owners((d_gate, d_up, d_down), (gate_got, up_got, down_got))
    d_mix_late = jnp.concatenate(
        [
            mm_tn(normed, g_z).astype(bf16),
            mm_tn(normed[:half_rows], d_q).astype(bf16),
        ],
        axis=1,
    )
    d_mix_late, early_got = joint(d_mix_late, early_got)
    late_got = crossing(d_mix_late)
    g_y, d_ff_got, out_sum, d_mix_late = joint(g_y, d_ff_got, out_sum, d_mix_late)
    out_got = lax.all_to_all(
        out_sum.reshape(8, rows, width), "cube", split_axis=0, concat_axis=0, tiled=True
    )
    g_all, acc_x, acc_m, acc_v, acc_s = run_mix_backward(
        info,
        raw_own,
        raw_s,
        *tables,
        lanes,
        g_y,
        g_z,
        states,
        d_q,
        d_k,
        d_v,
    )
    conv_grads = jnp.concatenate([acc_x[: KC + 1], acc_m[: KC + 1]], axis=1)
    g_bias = lax.dynamic_slice_in_dim(acc_s[0], place * heads, heads, 0)
    g_skip = jnp.sum(acc_v[0].reshape(heads, MP), axis=1)
    small_grads = jnp.concatenate([conv_grads.reshape(-1), grad_gain_mine, g_bias, g_skip])
    small_grads = jnp.pad(small_grads, (0, -small_grads.shape[0] % shard)).astype(bf16)
    small_grads = jnp.broadcast_to(
        small_grads.reshape(1, shard, -1), (DEVICES, shard, small_grads.shape[0] // shard)
    ).reshape(width, -1)
    g_in_other = mm_nt(g_all[half_rows:], w_all).astype(bf16)
    sums = Scatter(mm_nt(g_all[:half_rows], w_all).astype(bf16), g_in_other)
    sums.state, out_got = joint(sums.state, out_got)
    sums.hop()
    (g_all,) = sums.then(g_all)
    d_own = mm_tn(normed, g_all[:, mine : 2 * mine]).astype(bf16)
    d_own = jnp.concatenate([d_own, small_grads], axis=1)
    d_shared = mm_tn(normed, g_all[:, own_width:]).astype(bf16)
    sums.state, d_own, d_shared = joint(sums.state, d_own, d_shared)
    sums.hop()
    d_shared, d_ff_got, out_got = sums.then(d_shared, d_ff_got, out_got)
    out_part = jnp.sum(out_got.astype(f32), axis=0)
    out_rows = (hidden + out_part).astype(bf16)

    def only_mine(value):
        empty = jnp.zeros((width, KVH * HD), bf16)
        return lax.dynamic_update_slice_in_dim(empty, value, zl * HD, 1)

    d_shared = jnp.concatenate(
        [
            d_shared[:, : 2 * NS],
            only_mine(d_shared[:, 2 * NS : 2 * NS + HD]),
            only_mine(d_shared[:, 2 * NS + HD : 2 * NS + 2 * HD]),
            d_shared[:, 2 * NS + 2 * HD :],
        ],
        axis=1,
    )
    moves = []
    for block in range(DEVICES):

        def goal(ref, block=block):
            row = (ref[0] ^ (block % 16)) * 2 + block // 16
            return (pl.ds(pl.multiple_of(row * shard, shard), shard), slice(None))

        moves.append((0, fixed(block * shard, shard, 0, d_shared.shape[1]), goal))
    d_shared = assemble([d_shared], [(d_shared.shape, bf16, moves)], info)[0]
    sums.state, d_shared = joint(sums.state, d_shared)
    shared_sums = Scatter(d_shared[:half_rows], d_shared[half_rows:])
    sums.hop()
    g_in, d_own = joint(sums.result(), d_own)
    own_back = crossing(d_own)
    g_x_rows = (
        inv_in * g_in - x_rows * inv_in**3 * jnp.mean(x_rows * g_in, axis=-1, keepdims=True)
    )
    both = jnp.concatenate(
        [to_natural(out_rows), to_natural((g_hidden + g_x_rows).astype(bf16))], axis=0
    )
    both = swap_sequences(both)
    output, grad_tokens = both[None, :rows], both[None, rows:].astype(f32)
    shared_sums.hop()
    shared_sums.hop()
    shared_sums.hop()
    shared_sums.state, own_back, late_got, early_got = joint(
        shared_sums.state, own_back, late_got, early_got
    )
    d_own_got = to_owners((d_own, d_mix_late, d_mix_early), (own_back, late_got, early_got))
    d_cube = shared_sums.result().reshape(2, shard, -1)
    d_shared_own = d_cube[0] + flip(d_cube[1].astype(bf16), BIT_ZH).astype(f32)
    d_ff_own = d_ff_got.astype(f32)
    d_gate_up = jnp.concatenate(
        [from_places(d_ff_own[..., :ffc]), from_places(d_ff_own[..., ffc : 2 * ffc])], axis=1
    )
    grad_gate_up = d_gate_up * ff_gain.astype(f32)[:, None]
    grad_ff_gain = jnp.sum(d_gate_up * gate_up.astype(f32), axis=1)
    grad_down = jnp.moveaxis(d_ff_own[..., 2 * ffc : 3 * ffc], 1, 2).reshape(FF, shard)
    d_own = d_own_got.astype(f32)
    small_end = d_own.shape[-1] - 2 * mine - 2 * HD
    d_mix_own = d_own[..., small_end + mine + HD :]
    grad_inner_out = jnp.moveaxis(d_mix_own[..., :mine], 1, 2).reshape(inner_width, shard)
    d_att = d_mix_own[..., mine:].reshape(2, 8, shard, HD)
    grad_attn = jnp.moveaxis(d_att[0] + d_att[1], 1, 2).reshape(QH * HD, shard)
    d_x = from_places(d_own[..., :mine])
    d_z = from_places(d_own[..., small_end : small_end + mine])
    d_qw = d_own[..., small_end + mine : small_end + mine + HD].reshape(2, 8, shard, HD)
    d_qw = from_places(d_qw[0] + d_qw[1])

    got = d_own[..., mine:small_end].reshape(16, -1)
    at = 0
    taps_width = mine + 2 * NS
    conv_grads = got[:, at : at + (KC + 1) * taps_width].reshape(16, KC + 1, taps_width)
    at += (KC + 1) * taps_width
    conv_full = jnp.concatenate(
        [
            jnp.moveaxis(conv_grads[..., :mine], 0, 1).reshape(KC + 1, inner_width),
            jnp.sum(conv_grads[..., mine:], axis=0),
        ],
        axis=1,
    )
    device = core * 16 + chip
    conv_own = lax.dynamic_slice_in_dim(conv_full, device * conv_shard, conv_shard, 1)
    gain_full = got[:, at : at + mine].reshape(inner_width)
    gain_shard = inner_gain.shape[0]
    grad_inner_gain = lax.dynamic_slice_in_dim(gain_full, device * gain_shard, gain_shard, 0)
    at += mine
    local = lax.dynamic_slice_in_dim(got[:, at : at + 2 * heads], core * 8, 8, 0)
    grad_step_bias = local[:, :heads].reshape(-1)
    grad_skip_gain = local[:, heads:].reshape(-1)

    at = 2 * NS + 2 * kv_width
    d_qkv = jnp.concatenate([d_qw, d_shared_own[:, 2 * NS : at]], axis=1)
    d_inner = jnp.concatenate(
        [d_z, d_x, d_shared_own[:, : 2 * NS], d_shared_own[:, at : at + MH]], axis=1
    )
    grad_norm_gain = jnp.sum(d_qkv * qkv_proj.astype(f32), axis=1) + jnp.sum(
        d_inner * inner_proj.astype(f32), axis=1
    )
    return (
        output,
        grad_tokens,
        grad_norm_gain,
        d_qkv * gain_rows,
        grad_attn,
        d_inner * gain_rows,
        conv_own[:KC],
        conv_own[KC],
        grad_step_bias,
        grad_skip_gain,
        grad_inner_gain,
        grad_inner_out,
        grad_ff_gain,
        grad_gate_up,
        grad_down,
    )


def cube_solution(mesh):
    cubes = jax.sharding.Mesh(mesh.devices.reshape(2, 2, 8), BOTH)
    tokens = P("head", ("half", "cube"), None)
    lines = P(BOTH)
    rows = P(BOTH, None)
    columns = P(None, BOTH)
    head = P("head")
    return jax.shard_map(
        cube_body,
        mesh=cubes,
        in_specs=(
            tokens,
            P(None, ("half", "cube"), "head"),
            lines,
            rows,
            columns,
            rows,
            columns,
            lines,
            head,
            head,
            lines,
            columns,
            lines,
            rows,
            columns,
            tokens,
        ),
        out_specs=(
            tokens,
            tokens,
            lines,
            rows,
            columns,
            rows,
            columns,
            lines,
            head,
            head,
            lines,
            columns,
            lines,
            rows,
            columns,
        ),
        check_vma=False,
    )


def solution(mesh):
    if mesh.shape["seq"] == 16:
        return cube_solution(mesh)
    return jax.shard_map(
        body,
        mesh=mesh,
        in_specs=(
            P("head", "seq", None),
            P(None, "seq", "head"),
            P(("head", "seq")),
            P(("head", "seq"), None),
            P(None, ("head", "seq")),
            P(("head", "seq"), None),
            P(None, ("head", "seq")),
            P(("head", "seq")),
            P("head"),
            P("head"),
            P(("head", "seq")),
            P(None, ("head", "seq")),
            P(("head", "seq")),
            P(("head", "seq"), None),
            P(None, ("head", "seq")),
            P("head", "seq", None),
        ),
        out_specs=(
            P("head", "seq", None),
            P("head", "seq", None),
            P(("head", "seq")),
            P(("head", "seq"), None),
            P(None, ("head", "seq")),
            P(("head", "seq"), None),
            P(None, ("head", "seq")),
            P(("head", "seq")),
            P("head"),
            P("head"),
            P(("head", "seq")),
            P(None, ("head", "seq")),
            P(("head", "seq")),
            P(("head", "seq"), None),
            P(None, ("head", "seq")),
        ),
        check_vma=False,
    )
```

```python
import functools
import math

import jax
import jax.numpy as jnp
from jax import lax
from jax.experimental import pallas as pl
from jax.experimental.pallas import tpu as pltpu
from jax.sharding import PartitionSpec as P

FF = 4096
QH = 8
KVH = 2
HD = 128
MH = 48
MP = 64
NS = 256
KC = 4


EPSILON = 1e-05
ROPE_BASE = 100000000000.0
NEGATIVE = -1e30
HIGHEST = lax.Precision.HIGHEST


def passed_along(value, axis, steps):
    count = lax.axis_size(axis)
    initial, last = (max(0, -steps), min(count, count - steps))
    return lax.ppermute(value, axis, [(source, source + steps) for source in range(initial, last)])


def carried_in(array, axis, combine, identity):
    count, mine = (lax.axis_size(axis), lax.axis_index(axis))
    everything = jax.tree.map(
        lambda part, kind: lax.all_gather(part.astype(kind), axis),
        array,
        (jnp.bfloat16, jnp.bfloat16),
    )
    start = jax.tree.map(
        lambda part, zero: jnp.broadcast_to(jnp.asarray(zero, part.dtype), part.shape),
        array,
        identity,
    )

    def carried_hop(k, before):
        reached = k < mine
        new = combine(
            before, jax.tree.map(lambda part, own: part[k].astype(own.dtype), everything, array)
        )
        return jax.tree.map(lambda a, b: jnp.where(reached, a, b), new, before)

    return lax.fori_loop(0, count, carried_hop, start)


def entering(array, axis, combine, identity):
    count, mine = (lax.axis_size(axis), lax.axis_index(axis))
    everything = jax.tree.map(
        lambda part, kind: lax.all_gather(part.astype(kind), axis),
        array,
        jax.tree.map(lambda a: jnp.bfloat16 if a.dtype == jnp.float32 else a.dtype, array),
    )
    start = jax.tree.map(
        lambda part, zero: jnp.broadcast_to(jnp.asarray(zero, part.dtype), part.shape),
        array,
        identity,
    )

    def entering_hop(k, before):
        at = count - 1 - k
        reached = at > mine
        new = combine(
            before, jax.tree.map(lambda part, own: part[at].astype(own.dtype), everything, array)
        )
        return jax.tree.map(lambda a, b: jnp.where(reached, a, b), new, before)

    return lax.fori_loop(0, count, entering_hop, start)


def shortened(array):
    return jax.tree.map(lambda a: a.astype(jnp.bfloat16) if a.dtype == jnp.float32 else a, array)


def rounded(value):
    return lax.optimization_barrier(value.astype(jnp.bfloat16)).astype(jnp.float32)


def rms_norm(value, gain):
    return value * lax.rsqrt(jnp.mean(value * value, axis=-1, keepdims=True) + EPSILON) * gain


def rotary(value, positions):
    halfway = value.shape[-1] // 2
    frequency = ROPE_BASE ** (-2.0 * jnp.arange(halfway, dtype=jnp.float32) / value.shape[-1])
    angle = positions[:, None] * frequency[None, :]
    cosine = jnp.cos(angle)[:, None, :]
    sine_part = jnp.sin(angle)[:, None, :]
    first = value[..., :halfway]
    second = value[..., halfway:]
    return jnp.concatenate(
        [first * cosine - second * sine_part, second * cosine + first * sine_part], axis=-1
    )


def block_decay(log_decay):
    return jnp.exp(jnp.cumsum(log_decay, axis=1)[:, -1, :])


def inner_output(inner_x, step_in, state_maps, step_bias, skip_gain, state_in, log_decay):
    nstate = state_maps.shape[-1] // 2
    input_map = state_maps[..., :nstate]
    output_map = state_maps[..., nstate:]
    step_size = jax.nn.softplus(step_in + step_bias)
    cumulative = jnp.cumsum(log_decay, axis=1)
    scaled_x = inner_x * step_size[..., None]
    intersection = jnp.einsum("stn,sun->stu", output_map, input_map, precision=HIGHEST)
    length_blk = log_decay.shape[1]
    lower_mask = jnp.arange(length_blk)[:, None] >= jnp.arange(length_blk)[None, :]
    spread = cumulative[:, :, None, :] - cumulative[:, None, :, :]
    mixing = (
        jnp.where(lower_mask[None, :, :, None], jnp.exp(jnp.minimum(spread, 0.0)), 0.0)
        * intersection[..., None]
    )
    within = jnp.einsum("stuh,suhp->sthp", mixing, scaled_x, precision=HIGHEST)
    carried = (
        jnp.einsum("shpn,stn->sthp", state_in, output_map, precision=HIGHEST)
        * jnp.exp(cumulative)[..., None]
    )
    return within + carried + skip_gain[:, None] * inner_x


def inner_state(inner_x, step_in, state_maps, step_bias, log_decay):
    nstate = state_maps.shape[-1] // 2
    input_map = state_maps[..., :nstate]
    step_size = jax.nn.softplus(step_in + step_bias)
    cumulative = jnp.cumsum(log_decay, axis=1)
    tail_weight = jnp.exp(cumulative[:, -1:, :] - cumulative) * step_size
    return jnp.einsum("suh,suhp,sun->shpn", tail_weight, inner_x, input_map, precision=HIGHEST)


def over_blocks(function, carried, arrays, offset, limit):
    row_count = arrays[0].shape[1]
    step_rows = math.gcd(row_count, 1024)

    def advance(number, running):
        pieces = tuple(
            (
                lax.dynamic_slice_in_dim(member, number * step_rows, step_rows, 1)
                for member in arrays
            )
        )
        return function(running, pieces, offset + number * step_rows)

    upper = (limit + step_rows - 1) // step_rows
    return lax.fori_loop(0, upper, advance, carried)


def attend_block(carried, pair, offset, queries, query_pos, score_scale):
    row_top, row_total, accumulated = carried
    key_blk, value_blk = pair
    scores = (
        jnp.einsum("sqkgd,sjkd->sqkgj", queries, key_blk, preferred_element_type=jnp.float32)
        * score_scale
    )
    key_pos = offset + jnp.arange(key_blk.shape[1])
    allowed = (key_pos[None, :] <= query_pos[:, None])[None, :, None, None, :]
    masked = jnp.where(allowed, scores, NEGATIVE)
    new_top = jnp.maximum(row_top, jnp.max(masked, axis=-1))
    factor = jnp.exp(row_top - new_top)
    weights = jnp.where(allowed, jnp.exp(masked - new_top[..., None]), 0.0)
    row_total = factor * row_total + jnp.sum(weights, axis=-1)
    accumulated = factor[..., None] * accumulated + jnp.einsum(
        "sqkgj,sjkd->sqkgd",
        weights.astype(jnp.bfloat16),
        value_blk,
        preferred_element_type=jnp.float32,
    )
    return (new_top, row_total, accumulated)


def score_grads(
    queries, grad_heads, log_total, row_delta, key_blk, value_blk, offset, query_pos, score_scale
):
    scores = (
        jnp.einsum("sqkgd,sjkd->sqkgj", queries, key_blk, preferred_element_type=jnp.float32)
        * score_scale
    )
    key_pos = offset + jnp.arange(key_blk.shape[1])
    allowed = (key_pos[None, :] <= query_pos[:, None])[None, :, None, None, :]
    prob_rows = jnp.where(allowed, jnp.exp(scores - log_total[..., None]), 0.0)
    grad_probs = jnp.einsum(
        "sqkgd,sjkd->sqkgj", grad_heads, value_blk, preferred_element_type=jnp.float32
    )
    grad_scores = (prob_rows * (grad_probs - row_delta[..., None])).astype(jnp.bfloat16)
    return (prob_rows.astype(jnp.bfloat16), grad_scores)


def body(
    tokens,
    log_decay,
    norm_gain,
    qkv_proj,
    attn_proj,
    inner_proj,
    conv_weight,
    conv_bias,
    step_bias,
    skip_gain,
    inner_gain,
    inner_out,
    ff_gain,
    gate_up,
    down_proj,
    cotangent,
):
    head_count = lax.axis_size("head")
    seq_index = lax.axis_index("seq")
    (
        gain_in,
        qkv_full,
        attn_full,
        inner_full,
        conv_full,
        conv_bias_full,
        inner_gain_full,
        out_full,
        ff_gain_full,
        gate_up_full,
        down_full,
    ) = (
        lax.all_gather(norm_gain, ("head", "seq"), axis=0, tiled=True),
        lax.all_gather(qkv_proj, ("head", "seq"), axis=0, tiled=True),
        lax.all_gather(attn_proj, ("head", "seq"), axis=1, tiled=True),
        lax.all_gather(inner_proj, ("head", "seq"), axis=0, tiled=True),
        lax.all_gather(conv_weight, ("head", "seq"), axis=1, tiled=True),
        lax.all_gather(conv_bias, ("head", "seq"), axis=0, tiled=True),
        lax.all_gather(inner_gain, ("head", "seq"), axis=0, tiled=True),
        lax.all_gather(inner_out, ("head", "seq"), axis=1, tiled=True),
        lax.all_gather(ff_gain, ("head", "seq"), axis=0, tiled=True),
        lax.all_gather(gate_up, ("head", "seq"), axis=0, tiled=True),
        lax.all_gather(down_proj, ("head", "seq"), axis=1, tiled=True),
    )
    local_seqs, block_rows, model_width = tokens.shape
    token_rows = local_seqs * block_rows
    inner_width = MH * MP
    conv_width = inner_width + 2 * NS
    groups = QH // KVH
    kv_local = KVH // head_count
    inner_local = MH // head_count
    all_seqs = local_seqs * head_count
    score_scale = HD ** (-0.5)
    key_limit = (seq_index + 1) * block_rows
    x_rows = tokens.astype(jnp.float32).reshape(token_rows, model_width)
    normed_f, norm_back = jax.vjp(rms_norm, x_rows, gain_in.astype(jnp.float32))
    normed = normed_f.astype(jnp.bfloat16)
    qkv_rows = jnp.dot(normed, qkv_full, preferred_element_type=jnp.float32).reshape(
        local_seqs, block_rows, -1
    )
    positions = (seq_index * block_rows + jnp.arange(block_rows)).astype(jnp.float32)
    query_send = rotary(
        qkv_rows[..., : QH * HD].reshape(local_seqs, block_rows, QH, HD), positions
    ).astype(jnp.bfloat16)
    key_send = rotary(
        qkv_rows[..., QH * HD : (QH + KVH) * HD].reshape(local_seqs, block_rows, KVH, HD), positions
    ).astype(jnp.bfloat16)
    value_send = qkv_rows[..., (QH + KVH) * HD :].astype(jnp.bfloat16)
    inner_raw = jnp.dot(normed, inner_full, preferred_element_type=jnp.float32).reshape(
        local_seqs, block_rows, -1
    )
    gate_z = inner_raw[..., :inner_width]
    conv_in = inner_raw[..., inner_width : inner_width + conv_width]
    step_send = inner_raw[..., inner_width + conv_width :].astype(jnp.bfloat16)
    rim_rows = passed_along(
        conv_in[:, block_rows - (KC - 1) :, :].astype(jnp.bfloat16), "seq", 1
    ).astype(jnp.float32)
    padded = jnp.concatenate([rim_rows, conv_in], axis=1)

    def convolve(padded_in, weight_taps, bias_taps):
        conv_sum = bias_taps
        for conv_tap in range(KC):
            conv_sum = (
                conv_sum + weight_taps[conv_tap] * padded_in[:, conv_tap : conv_tap + block_rows, :]
            )
        return jax.nn.silu(conv_sum)

    activated, conv_back = jax.vjp(
        convolve, padded, conv_full.astype(jnp.float32), conv_bias_full.astype(jnp.float32)
    )
    activated_send = activated.astype(jnp.bfloat16)

    def split_heads(value):
        return value.reshape(value.shape[:2] + (head_count, -1))

    map_copies = jnp.broadcast_to(
        activated_send[:, :, None, inner_width:], (local_seqs, block_rows, head_count, 2 * NS)
    )
    received = (
        lax.all_to_all(split_heads(query_send), "head", split_axis=2, concat_axis=0, tiled=True),
        lax.all_to_all(split_heads(key_send), "head", split_axis=2, concat_axis=0, tiled=True),
        lax.all_to_all(split_heads(value_send), "head", split_axis=2, concat_axis=0, tiled=True),
        lax.all_to_all(
            split_heads(activated_send[..., :inner_width]),
            "head",
            split_axis=2,
            concat_axis=0,
            tiled=True,
        ),
        lax.all_to_all(split_heads(step_send), "head", split_axis=2, concat_axis=0, tiled=True),
        lax.all_to_all(map_copies, "head", split_axis=2, concat_axis=0, tiled=True),
    )
    queries = received[0].reshape(all_seqs, block_rows, kv_local, groups, HD)
    key_heads = received[1]
    value_heads = received[2]
    inner_x = received[3].reshape(all_seqs, block_rows, inner_local, MP).astype(jnp.float32)
    step_in = received[4].reshape(all_seqs, block_rows, inner_local).astype(jnp.float32)
    state_maps = received[5].reshape(all_seqs, block_rows, 2 * NS).astype(jnp.float32)
    query_pos = seq_index * block_rows + jnp.arange(block_rows)
    key_all, value_all = (
        lax.all_gather(key_heads, "seq", axis=1, tiled=True),
        lax.all_gather(value_heads, "seq", axis=1, tiled=True),
    )

    def attend_step(carried, pair, offset):
        return attend_block(carried, pair, offset, queries, query_pos, score_scale)

    stat_shape = (all_seqs, block_rows, kv_local, groups)
    start_stats = (
        jnp.full(stat_shape, NEGATIVE, jnp.float32),
        jnp.zeros(stat_shape, jnp.float32),
        jnp.zeros(stat_shape + (HD,), jnp.float32),
    )
    row_top, row_total, accumulated = over_blocks(
        attend_step, start_stats, (key_all, value_all), 0, key_limit
    )
    attended_f = accumulated / row_total[..., None]
    log_total = row_top + jnp.log(row_total)

    def state_part(piece_x, piece_step, piece_maps, piece_bias):
        return inner_state(piece_x, piece_step, piece_maps, piece_bias, log_decay)

    def output_part(piece_x, piece_step, piece_maps, piece_bias, piece_skip, piece_state):
        return inner_output(
            piece_x, piece_step, piece_maps, piece_bias, piece_skip, piece_state, log_decay
        )

    fresh_state, state_back = jax.vjp(state_part, inner_x, step_in, state_maps, step_bias)
    block_fall = block_decay(log_decay)

    def chain_rule(earlier, later):
        return (earlier[0] * later[0], later[1] + later[0][:, :, None, None] * earlier[1])

    neutral = (jnp.ones_like(block_fall), jnp.zeros_like(fresh_state))
    state_in = carried_in((block_fall, fresh_state), "seq", chain_rule, neutral)[1]
    inner_y, output_back = jax.vjp(
        output_part, inner_x, step_in, state_maps, step_bias, skip_gain, state_in
    )
    returned = (
        lax.all_to_all(
            attended_f.astype(jnp.bfloat16).reshape(all_seqs, block_rows, 1, -1),
            "head",
            split_axis=0,
            concat_axis=2,
            tiled=True,
        ),
        lax.all_to_all(
            inner_y.astype(jnp.bfloat16).reshape(all_seqs, block_rows, 1, -1),
            "head",
            split_axis=0,
            concat_axis=2,
            tiled=True,
        ),
    )
    attended = returned[0].reshape(token_rows, QH * HD)
    inner_back_y = returned[1].reshape(local_seqs, block_rows, inner_width).astype(jnp.float32)

    def gated_norm(y_part, gate_part, gain_part):
        return rms_norm(y_part * jax.nn.silu(gate_part), gain_part)

    inner_normed_f, gated_back = jax.vjp(
        gated_norm, inner_back_y, gate_z, inner_gain_full.astype(jnp.float32)
    )
    inner_normed = inner_normed_f.astype(jnp.bfloat16).reshape(token_rows, inner_width)
    hidden = (
        x_rows
        + jnp.dot(attended, attn_full, preferred_element_type=jnp.float32)
        + jnp.dot(inner_normed, out_full, preferred_element_type=jnp.float32)
    )
    normed_ff_f, ff_back = jax.vjp(rms_norm, hidden, ff_gain_full.astype(jnp.float32))
    normed_ff = normed_ff_f.astype(jnp.bfloat16)
    gate_vals = jnp.dot(normed_ff, gate_up_full, preferred_element_type=jnp.float32)

    def swiglu(values_in):
        return jax.nn.silu(values_in[:, :FF]) * values_in[:, FF:]

    mixed_f, swiglu_back = jax.vjp(swiglu, gate_vals)
    mixed_rows = mixed_f.astype(jnp.bfloat16)
    output = (
        (hidden + jnp.dot(mixed_rows, down_full, preferred_element_type=jnp.float32))
        .astype(jnp.bfloat16)
        .reshape(tokens.shape)
    )
    grad_out = cotangent.reshape(token_rows, model_width)
    grad_down = jnp.einsum("rf,rd->fd", mixed_rows, grad_out, preferred_element_type=jnp.float32)
    grad_gate_vals = swiglu_back(
        jnp.einsum("rd,fd->rf", grad_out, down_full, preferred_element_type=jnp.float32)
    )[0].astype(jnp.bfloat16)
    grad_gate_up = jnp.einsum(
        "rd,re->de", normed_ff, grad_gate_vals, preferred_element_type=jnp.float32
    )
    grad_hidden_norm, grad_ff_gain = ff_back(
        jnp.einsum("re,de->rd", grad_gate_vals, gate_up_full, preferred_element_type=jnp.float32)
    )
    grad_hidden = grad_out.astype(jnp.float32) + grad_hidden_norm
    grad_branch = grad_hidden.astype(jnp.bfloat16)
    grad_attn = jnp.einsum("rc,rd->cd", attended, grad_branch, preferred_element_type=jnp.float32)
    grad_inner_out = jnp.einsum(
        "rc,rd->cd", inner_normed, grad_branch, preferred_element_type=jnp.float32
    )
    grad_attended = jnp.einsum(
        "rd,cd->rc", grad_branch, attn_full, preferred_element_type=jnp.float32
    ).astype(jnp.bfloat16)
    grad_y, grad_gate_z, grad_inner_gain = gated_back(
        jnp.einsum("rd,cd->rc", grad_branch, out_full, preferred_element_type=jnp.float32).reshape(
            local_seqs, block_rows, inner_width
        )
    )
    sent_grads = (
        lax.all_to_all(
            split_heads(grad_attended.reshape(local_seqs, block_rows, QH * HD)),
            "head",
            split_axis=2,
            concat_axis=0,
            tiled=True,
        ),
        lax.all_to_all(
            split_heads(grad_y.astype(jnp.bfloat16)),
            "head",
            split_axis=2,
            concat_axis=0,
            tiled=True,
        ),
    )
    grad_heads = sent_grads[0].reshape(all_seqs, block_rows, kv_local, groups, HD)
    grad_inner_y = sent_grads[1].reshape(all_seqs, block_rows, inner_local, MP).astype(jnp.float32)
    row_delta = jnp.sum(grad_heads.astype(jnp.float32) * attended_f, axis=-1)

    def query_step(carried, pair, offset):
        prob_rows, grad_scores = score_grads(
            queries,
            grad_heads,
            log_total,
            row_delta,
            pair[0],
            pair[1],
            offset,
            query_pos,
            score_scale,
        )
        return carried + jnp.einsum(
            "sqkgj,sjkd->sqkgd", grad_scores, pair[0], preferred_element_type=jnp.float32
        )

    grad_queries = (
        over_blocks(query_step, jnp.zeros_like(attended_f), (key_all, value_all), 0, key_limit)
        * score_scale
    )
    count = block_rows * lax.axis_size("seq")
    step_rows = math.gcd(count, 1024)
    term_shape = (step_rows, all_seqs, kv_local, 2 * HD)

    def compute_block(offset):
        key_blk = lax.dynamic_slice_in_dim(key_all, offset, step_rows, 1)
        value_blk = lax.dynamic_slice_in_dim(value_all, offset, step_rows, 1)
        prob_rows, grad_scores = score_grads(
            queries,
            grad_heads,
            log_total,
            row_delta,
            key_blk,
            value_blk,
            offset,
            query_pos,
            score_scale,
        )
        grad_keys = (
            jnp.einsum(
                "sqkgj,sqkgd->jskd", grad_scores, queries, preferred_element_type=jnp.float32
            )
            * score_scale
        )
        grad_values = jnp.einsum(
            "sqkgj,sqkgd->jskd", prob_rows, grad_heads, preferred_element_type=jnp.float32
        )
        return jnp.concatenate([grad_keys, grad_values], axis=-1)

    def one_block(offset):
        return lax.cond(
            offset < key_limit,
            compute_block,
            lambda unused: jnp.zeros(term_shape, jnp.float32),
            offset,
        )

    block_terms = lax.map(
        lambda number: one_block(number * step_rows), jnp.arange(count // step_rows)
    )
    key_grads = lax.psum_scatter(
        block_terms.reshape((count,) + block_terms.shape[2:]),
        "seq",
        scatter_dimension=0,
        tiled=True,
    )
    grad_key_heads = jnp.moveaxis(key_grads[..., :HD], 0, 1)
    grad_value_heads = jnp.moveaxis(key_grads[..., HD:], 0, 1)
    grad_x_a, grad_step_a, grad_maps_a, grad_bias_a, grad_skip, grad_state = output_back(
        grad_inner_y
    )
    grad_carry = entering((block_fall, grad_state), "seq", chain_rule, neutral)[1]
    grad_x_b, grad_step_b, grad_maps_b, grad_bias_b = state_back(grad_carry)
    grad_step_bias, grad_skip_gain = lax.psum((grad_bias_a + grad_bias_b, grad_skip), "seq")
    returned_grads = (
        lax.all_to_all(
            grad_queries.reshape(all_seqs, block_rows, 1, -1).astype(jnp.bfloat16),
            "head",
            split_axis=0,
            concat_axis=2,
            tiled=True,
        ).astype(jnp.float32),
        lax.all_to_all(
            grad_key_heads.astype(jnp.bfloat16), "head", split_axis=0, concat_axis=2, tiled=True
        ).astype(grad_key_heads.dtype),
        lax.all_to_all(
            grad_value_heads.astype(jnp.bfloat16), "head", split_axis=0, concat_axis=2, tiled=True
        ).astype(grad_value_heads.dtype),
        lax.all_to_all(
            (grad_x_a + grad_x_b).reshape(all_seqs, block_rows, 1, -1).astype(jnp.bfloat16),
            "head",
            split_axis=0,
            concat_axis=2,
            tiled=True,
        ).astype(jnp.float32),
        lax.all_to_all(
            (grad_step_a + grad_step_b).reshape(all_seqs, block_rows, 1, -1).astype(jnp.bfloat16),
            "head",
            split_axis=0,
            concat_axis=2,
            tiled=True,
        ).astype(jnp.float32),
        lax.all_to_all(
            (grad_maps_a + grad_maps_b)[:, :, None, :].astype(jnp.bfloat16),
            "head",
            split_axis=0,
            concat_axis=2,
            tiled=True,
        ).astype(jnp.float32),
    )
    grad_q = rounded(returned_grads[0].reshape(local_seqs, block_rows, QH, HD))
    grad_k = rounded(returned_grads[1])
    grad_v = returned_grads[2].reshape(token_rows, KVH * HD)
    grad_qkv_rows = jnp.concatenate(
        [
            rotary(grad_q, -positions).reshape(token_rows, -1),
            rotary(grad_k, -positions).reshape(token_rows, -1),
            grad_v,
        ],
        axis=-1,
    ).astype(jnp.bfloat16)
    grad_x_in = rounded(returned_grads[3].reshape(local_seqs, block_rows, inner_width))
    grad_step = rounded(returned_grads[4].reshape(token_rows, MH))
    grad_maps = rounded(jnp.sum(returned_grads[5], axis=2))
    grad_padded, grad_conv_weight, grad_conv_bias = conv_back(
        jnp.concatenate([grad_x_in, grad_maps], axis=-1)
    )
    rim_grad = passed_along(shortened(grad_padded[:, : KC - 1, :]), "seq", -1)
    grad_conv_in = grad_padded[:, KC - 1 :, :].at[:, block_rows - (KC - 1) :, :].add(rim_grad)
    grad_inner_rows = jnp.concatenate(
        [grad_gate_z.reshape(token_rows, -1), grad_conv_in.reshape(token_rows, -1), grad_step],
        axis=-1,
    ).astype(jnp.bfloat16)
    grad_qkv_weight = jnp.einsum(
        "rd,re->de", normed, grad_qkv_rows, preferred_element_type=jnp.float32
    )
    grad_inner_weight = jnp.einsum(
        "rd,re->de", normed, grad_inner_rows, preferred_element_type=jnp.float32
    )
    grad_normed = jnp.einsum(
        "re,de->rd", grad_qkv_rows, qkv_full, preferred_element_type=jnp.float32
    ) + jnp.einsum("re,de->rd", grad_inner_rows, inner_full, preferred_element_type=jnp.float32)
    grad_x_norm, grad_norm_gain = norm_back(grad_normed)
    grad_tokens = (grad_hidden + grad_x_norm).reshape(tokens.shape)
    weight_grads = (
        grad_norm_gain,
        grad_qkv_weight,
        grad_attn,
        grad_inner_weight,
        grad_conv_weight,
        grad_conv_bias,
        grad_inner_gain,
        grad_inner_out,
        grad_ff_gain,
        grad_gate_up,
        grad_down,
    )
    shares = (
        lax.psum_scatter(weight_grads[0], ("head", "seq"), scatter_dimension=0, tiled=True),
        lax.psum_scatter(weight_grads[1], ("head", "seq"), scatter_dimension=0, tiled=True),
        lax.psum_scatter(weight_grads[2], ("head", "seq"), scatter_dimension=1, tiled=True),
        lax.psum_scatter(weight_grads[3], ("head", "seq"), scatter_dimension=0, tiled=True),
        lax.psum_scatter(weight_grads[4], ("head", "seq"), scatter_dimension=1, tiled=True),
        lax.psum_scatter(weight_grads[5], ("head", "seq"), scatter_dimension=0, tiled=True),
        lax.psum_scatter(weight_grads[6], ("head", "seq"), scatter_dimension=0, tiled=True),
        lax.psum_scatter(weight_grads[7], ("head", "seq"), scatter_dimension=1, tiled=True),
        lax.psum_scatter(weight_grads[8], ("head", "seq"), scatter_dimension=0, tiled=True),
        lax.psum_scatter(weight_grads[9], ("head", "seq"), scatter_dimension=0, tiled=True),
        lax.psum_scatter(weight_grads[10], ("head", "seq"), scatter_dimension=1, tiled=True),
    )
    return (
        output,
        grad_tokens,
        shares[0],
        shares[1],
        shares[2],
        shares[3],
        shares[4],
        shares[5],
        grad_step_bias,
        grad_skip_gain,
        shares[6],
        shares[7],
        shares[8],
        shares[9],
        shares[10],
    )


BLOCK = 128
BIT_C, BIT_ZH, BIT_ZL, BIT_Y, BIT_X = 16, 8, 4, 2, 1
DEVICES = 32
BOTH = ("head", "half", "cube")
GROUP = ("head", "cube")
CUBE_ORDERS = ((0, 1, 2), (1, 2, 0), (2, 0, 1))
CUBE_BITS = (BIT_ZL, BIT_Y, BIT_X)
bf16 = jnp.bfloat16
f32 = jnp.float32


def flip(value, mask):
    return lax.ppermute(value, BOTH, [(i, i ^ mask) for i in range(DEVICES)])


def swap_sequences(value):
    pairs = []
    for i in range(DEVICES):
        core, half = (i // BIT_C) % 2, (i // BIT_ZH) % 2
        if core != half:
            pairs.append((i, i ^ (BIT_C + BIT_ZH)))
    stays = lax.axis_index("head") == lax.axis_index("half")
    return jnp.where(stays, value, lax.ppermute(value, BOTH, pairs))


def joint(*values):
    return lax.optimization_barrier(values)


def column_parts(width):
    lanes = width // 128
    first = -(-lanes // 3)
    second = -(-(lanes - first) // 2)
    edges = (0, first * 128, (first + second) * 128, width)
    return [(edges[i], edges[i + 1]) for i in range(3)]


def assemble(pieces, outputs, info):
    count, made = len(pieces), len(outputs)
    moves = [(to, *move) for to, (_, _, out_moves) in enumerate(outputs) for move in out_moves]

    def kernel(info_ref, *refs):
        sems = refs[count + made]
        copies = []
        for at, (to, number, source, target) in enumerate(moves):
            copies.append(
                pltpu.make_async_copy(
                    refs[number].at[source(info_ref)],
                    refs[count + to].at[target(info_ref)],
                    sems.at[at],
                )
            )
        for copy in copies:
            copy.start()
        for copy in copies:
            copy.wait()

    size = sum(math.prod(shape) * jnp.dtype(kind).itemsize for shape, kind, _ in outputs)
    return pl.pallas_call(
        kernel,
        in_specs=[pl.BlockSpec(memory_space=pltpu.SMEM)]
        + [pl.BlockSpec(memory_space=pltpu.HBM)] * count,
        out_specs=[pl.BlockSpec(memory_space=pltpu.VMEM)] * made,
        out_shape=[jax.ShapeDtypeStruct(shape, kind) for shape, kind, _ in outputs],
        scratch_shapes=[pltpu.SemaphoreType.DMA((len(moves),))],
        compiler_params=pltpu.CompilerParams(vmem_limit_bytes=2 * size + 8 * 1024 * 1024),
        cost_estimate=LITTLE,
        name="assemble",
    )(info, *pieces)


def reordered_rows(value, info):
    moves = []
    for block in range(value.shape[0] // BLOCK):

        def goal(ref, block=block):
            row = pl.multiple_of((ref[2] ^ block) * BLOCK, BLOCK)
            return (pl.ds(row, BLOCK), slice(None))

        moves.append((0, fixed(block * BLOCK, BLOCK, 0, value.shape[1]), goal))
    return assemble([value], [(value.shape, value.dtype, moves)], info)[0]


def fixed(row, rows, column, columns):
    return lambda info: (pl.ds(row, rows), pl.ds(column, columns))


class Gather:
    def __init__(self, value, edges, info):
        self.rows, self.width, self.step = value.shape[0], value.shape[1], 0
        self.edges, self.info = edges, info
        self.joined = None
        self.state = ([value[:, a:b] for a, b in edges], None)

    def hop(self):
        parts, received = self.state
        if received is not None:
            parts = self.stacked(parts, received)
        sent = [
            flip(part, CUBE_BITS[order[self.step]]) for part, order in zip(parts, CUBE_ORDERS)
        ]
        self.state = (parts, sent)
        self.step += 1

    def stacked(self, parts, received):
        rows = parts[0].shape[0]
        outputs, side = [], []
        for i, (a, b) in enumerate(self.edges):
            own, got = fixed(0, rows, 0, b - a), fixed(rows, rows, 0, b - a)
            outputs.append(((2 * rows, b - a), bf16, [(i, own, own), (3 + i, own, got)]))
            side.append((i, own, fixed(0, rows, a, b - a)))
            side.append((3 + i, own, fixed(rows, rows, a, b - a)))
        if self.step == 2:
            outputs.append(((2 * rows, self.width), bf16, side))
        result = assemble(parts + received, outputs, self.info)
        if self.step == 2:
            self.joined = result[3]
        return list(result[:3])

    def pieces(self):
        while self.step < 3:
            self.hop()
        near, far = self.state
        side = [(i, fixed(0, 4 * self.rows, 0, b - a), fixed(0, 4 * self.rows, a, b - a)) for i, (a, b) in enumerate(self.edges)]
        (far_joined,) = assemble(
            far, [((4 * self.rows, self.width), bf16, side)], self.info
        )
        crossed = [flip(self.joined, BIT_C), flip(far_joined, BIT_C)]
        return near + far + crossed


def piece_blocks(part, far):
    axes = [CUBE_BITS[axis] for axis in CUBE_ORDERS[part]]
    return [
        (block, (block % 2) * axes[0] + (block // 2) * axes[1] + far * axes[2], 1)
        for block in range(4)
    ]


def gathered(gather, width, info):
    rows = gather.rows
    pieces = gather.pieces()
    moves = []
    for group in range(4):
        half, far = group // 2, group % 2
        for part, (a, b) in enumerate(column_parts(width)):
            number = 3 * group + part if half == 0 else 6 + far
            for first, place, blocks in piece_blocks(part, far):
                moves.append(
                    (
                        number,
                        fixed(first * rows, blocks * rows, a * half, b - a),
                        fixed((half * 8 + place) * rows, blocks * rows, a, b - a),
                    )
                )
    return assemble(pieces, [((16 * rows, width), bf16, moves)], info)[0]


def gather_start(value, info):
    return Gather(value, column_parts(value.shape[1]), info)


class Scatter:
    def __init__(self, own_half, other_half):
        self.total_rows, self.width = own_half.shape
        self.step = 0
        self.state = (own_half, flip(other_half.astype(bf16), BIT_C))

    def pairs(self):
        kept, received = self.state
        if self.step == 0:
            shape = (2, 2, 2, self.total_rows // 8, self.width)
            edges = column_parts(self.width)
            kept = [kept.reshape(shape)[..., a:b] for a, b in edges]
            received = [received.reshape(shape)[..., a:b] for a, b in edges]
        halves = []
        for part, got, order in zip(kept, received, CUBE_ORDERS):
            axis = order[self.step]
            halves.append(
                [
                    (
                        lax.slice_in_dim(part, i, i + 1, axis=axis).astype(f32)
                        + lax.slice_in_dim(got, i, i + 1, axis=axis).astype(f32)
                    ).astype(bf16)
                    for i in (0, 1)
                ]
            )
        return halves

    def hop(self):
        halves = self.pairs()
        sent = [
            flip(far, CUBE_BITS[order[self.step]])
            for (_, far), order in zip(halves, CUBE_ORDERS)
        ]
        self.state = ([near for near, _ in halves], sent)
        self.step += 1

    def then(self, *values):
        near, sent = self.state
        near, values = joint(near, values)
        self.state = (near, sent)
        return values

    def result(self):
        while self.step < 3:
            self.hop()
        rows = self.total_rows // 8
        return jnp.concatenate(
            [
                (near.astype(f32) + got.astype(f32)).reshape(rows, -1)
                for near, got in zip(*self.state)
            ],
            axis=1,
        )


def group_sum(value):
    for masks in ((BIT_C, BIT_X, BIT_C + BIT_X), (BIT_Y, BIT_ZL, BIT_Y + BIT_ZL)):
        first, second, third = [flip(value, mask) for mask in masks]
        value = (value + first) + (second + third)
    return value


def exchange(value):
    return lax.all_to_all(value, GROUP, split_axis=0, concat_axis=0, tiled=True)


def mm(a, b):
    return jnp.dot(a, b, preferred_element_type=f32)


def mm_nt(a, b):
    return lax.dot_general(a, b, (((1,), (1,)), ((), ())), preferred_element_type=f32)


def mm_tn(a, b):
    return lax.dot_general(a, b, (((0,), (0,)), ((), ())), preferred_element_type=f32)


VMEM_ASK = 40 * 1024 * 1024
LITTLE = pl.CostEstimate(flops=1000, bytes_accessed=1000, transcendentals=0)


def params():
    return pltpu.CompilerParams(
        dimension_semantics=("arbitrary",), vmem_limit_bytes=VMEM_ASK
    )


def k_nt(a, b, precision=None):
    return lax.dot_general(
        a, b, (((1,), (1,)), ((), ())), preferred_element_type=f32, precision=precision
    )


def k_tn(a, b):
    return lax.dot_general(a, b, (((0,), (0,)), ((), ())), preferred_element_type=f32)


def k_mm(a, b, precision=None):
    return lax.dot_general(
        a, b, (((1,), (0,)), ((), ())), preferred_element_type=f32, precision=precision
    )


def logistic(value):
    return 1.0 / (1.0 + jnp.exp(-value))


def softplus(value):
    small = jnp.exp(-jnp.abs(value))
    series = small * (1.0 - small * (0.5 - small * (1.0 / 3.0 - 0.25 * small)))
    return jnp.maximum(value, 0.0) + jnp.where(small < 0.01, series, jnp.log(1.0 + small))


def by_head(columns, lane):
    spread = columns[:, 0:1]
    for head in range(1, HEADS_HERE):
        spread = jnp.where(lane >= head * MP, columns[:, head : head + 1], spread)
    return spread


def shifted_sum(padded, taps, start, step):
    total = None
    for tap in range(KC):
        at = start + step * tap
        term = taps[tap : tap + 1] * padded[at : at + BLOCK]
        total = term if total is None else total + term
    return total


HEADS_HERE = 3
OWN = HEADS_HERE * MP
TAIL = 16
KEYS_AT = 2 * NS


def block_decays(cum_col, cum_row, lane):
    cum = by_head(cum_col, lane)
    last = cum[BLOCK - 1 : BLOCK]
    row = lax.broadcasted_iota(jnp.int32, (BLOCK, BLOCK), 0)
    col = lax.broadcasted_iota(jnp.int32, (BLOCK, BLOCK), 1)
    reach = []
    for head in range(HEADS_HERE):
        spread = cum_col[:, head : head + 1] - cum_row[head : head + 1, :]
        reach.append(jnp.where(row >= col, jnp.exp(jnp.minimum(spread, 0.0)), 0.0))
    return cum, last, reach


def step_lanes(place, lane):
    source = lax.broadcasted_iota(jnp.int32, (128, OWN), 0)
    head = lax.broadcasted_iota(jnp.int32, (128, OWN), 1) // MP
    return jnp.where(source == place * HEADS_HERE + head, 1.0, 0.0)


def mix_forward(
    info,
    own_ref,
    s_ref,
    cos_ref,
    sin_ref,
    cum_col_ref,
    cum_row_ref,
    taps_x_ref,
    taps_m_ref,
    vec_ref,
    y_ref,
    gained_ref,
    square_ref,
    state_ref,
    q_ref,
    k_ref,
    v_ref,
    state,
    last_x,
    last_m,
):
    @pl.when(pl.program_id(0) == 0)
    def _():
        state[...] = jnp.zeros_like(state)
        last_x[...] = jnp.zeros_like(last_x)
        last_m[...] = jnp.zeros_like(last_m)

    lane = lax.broadcasted_iota(jnp.int32, (1, OWN), 1)
    gate = own_ref[:, :OWN].astype(f32)
    x_raw = own_ref[:, OWN : 2 * OWN].astype(f32)
    m_raw = s_ref[:, : 2 * NS].astype(f32)
    cosine, sine = cos_ref[...], sin_ref[...]

    def turned(value):
        return (value * cosine + pltpu.roll(value, HD // 2, 1) * sine).astype(bf16)

    q_ref[...] = turned(own_ref[:, 2 * OWN :].astype(f32))
    k_ref[...] = turned(s_ref[:, KEYS_AT : KEYS_AT + HD].astype(f32))
    v_ref[...] = s_ref[:, KEYS_AT + HD : KEYS_AT + 2 * HD].astype(bf16)

    s_x = shifted_sum(
        jnp.concatenate([last_x[...], x_raw], axis=0), taps_x_ref, TAIL - KC + 1, 1
    ) + taps_x_ref[KC : KC + 1]
    s_m = shifted_sum(
        jnp.concatenate([last_m[...], m_raw], axis=0), taps_m_ref, TAIL - KC + 1, 1
    ) + taps_m_ref[KC : KC + 1]
    last_x[...] = x_raw[BLOCK - TAIL :]
    last_m[...] = m_raw[BLOCK - TAIL :]
    x = (s_x * logistic(s_x)).astype(bf16).astype(f32)
    maps = (s_m * logistic(s_m)).astype(bf16)
    b_map, c_map = maps[:, :NS], maps[:, NS:]

    place = info[0]
    picked = k_mm(s_ref[:, KEYS_AT + 2 * HD :].astype(bf16), step_lanes(place, lane).astype(bf16))
    raised = picked + vec_ref[0:1]
    step = softplus(raised)
    cum, last, reach = block_decays(cum_col_ref[...], cum_row_ref[0], lane)
    scaled = step * x
    inter = k_nt(c_map, b_map)
    total = vec_ref[1:2] * x
    for head in range(HEADS_HERE):
        here = (lane >= head * MP) & (lane < (head + 1) * MP)
        total += k_mm(
            (reach[head] * inter).astype(bf16), jnp.where(here, scaled, 0.0).astype(bf16)
        )
    before = state[...]
    state_ref[0] = before.astype(bf16)
    total += jnp.exp(cum) * k_mm(c_map, before.astype(bf16))
    tail = (jnp.exp(last - cum) * scaled).astype(bf16)
    state[...] = jnp.exp(last) * before + k_tn(b_map, tail)
    y = total.astype(bf16)
    y_ref[...] = y
    gated = y.astype(f32) * (gate * logistic(gate))
    gained_ref[...] = (gated * vec_ref[2:3]).astype(bf16)
    square_ref[0] = k_nt(jnp.ones((8, OWN), f32), gated * gated, HIGHEST)


def mix_backward(
    info,
    own_ref,
    s_ref,
    own_tail_ref,
    s_tail_ref,
    cos_ref,
    sin_ref,
    cum_col_ref,
    cum_row_ref,
    taps_x_ref,
    taps_m_ref,
    vec_ref,
    lanes_ref,
    g_y_ref,
    g_z_ref,
    state_ref,
    dq_ref,
    dk_ref,
    dv_ref,
    g_all_ref,
    acc_x_ref,
    acc_m_ref,
    acc_v_ref,
    acc_s_ref,
    g_state,
    next_x,
    next_m,
):
    step_id = pl.program_id(0)
    block = pl.num_programs(0) - 1 - step_id
    place = info[0]

    @pl.when(step_id == 0)
    def _():
        g_state[...] = jnp.zeros_like(g_state)
        next_x[...] = jnp.zeros_like(next_x)
        next_m[...] = jnp.zeros_like(next_m)
        acc_x_ref[...] = jnp.zeros_like(acc_x_ref)
        acc_m_ref[...] = jnp.zeros_like(acc_m_ref)
        acc_v_ref[...] = jnp.zeros_like(acc_v_ref)
        acc_s_ref[...] = jnp.zeros_like(acc_s_ref)

    lane = lax.broadcasted_iota(jnp.int32, (1, OWN), 1)
    cosine, sine = cos_ref[...], sin_ref[...]

    def unturned(value):
        return value * cosine - pltpu.roll(value, HD // 2, 1) * sine

    x_raw = own_ref[:, OWN : 2 * OWN].astype(f32)
    m_raw = s_ref[:, : 2 * NS].astype(f32)
    first = block == 0
    x_pad = jnp.concatenate(
        [jnp.where(first, 0.0, own_tail_ref[:, OWN : 2 * OWN].astype(f32)), x_raw], axis=0
    )
    m_pad = jnp.concatenate([jnp.where(first, 0.0, s_tail_ref[:, : 2 * NS].astype(f32)), m_raw], axis=0)
    s_x = shifted_sum(x_pad, taps_x_ref, TAIL - KC + 1, 1) + taps_x_ref[KC : KC + 1]
    s_m = shifted_sum(m_pad, taps_m_ref, TAIL - KC + 1, 1) + taps_m_ref[KC : KC + 1]
    sig_x, sig_m = logistic(s_x), logistic(s_m)
    x = (s_x * sig_x).astype(bf16).astype(f32)
    maps = (s_m * sig_m).astype(bf16)
    b_map, c_map = maps[:, :NS], maps[:, NS:]
    select = step_lanes(place, lane)
    step_raw = s_ref[:, KEYS_AT + 2 * HD :].astype(bf16)
    raised = k_mm(step_raw, select.astype(bf16)) + vec_ref[0:1]
    step = softplus(raised)
    cum, last, reach = block_decays(cum_col_ref[...], cum_row_ref[0], lane)
    scaled = step * x

    g_y = g_y_ref[...].astype(f32)

    inter = k_nt(c_map, b_map)
    g_inter = jnp.zeros((BLOCK, BLOCK), f32)
    g_scaled = jnp.zeros((BLOCK, OWN), f32)
    scaled_b = scaled.astype(bf16)
    for head in range(HEADS_HERE):
        here = (lane >= head * MP) & (lane < (head + 1) * MP)
        g_head = jnp.where(here, g_y, 0.0).astype(bf16)
        g_inter += reach[head] * k_nt(g_head, scaled_b)
        g_scaled += k_tn((reach[head] * inter).astype(bf16), g_head)
    before = state_ref[0]
    g_after = g_state[...]
    g_after_b = g_after.astype(bf16)
    tail_w = jnp.exp(last - cum)
    reached = (jnp.exp(cum) * g_y).astype(bf16)
    g_inter_b = g_inter.astype(bf16)
    g_c = k_mm(g_inter_b, b_map) + k_nt(reached, before)
    g_b = k_tn(g_inter_b, c_map) + k_nt((tail_w * scaled).astype(bf16), g_after_b)
    g_scaled += tail_w * k_mm(b_map, g_after_b)
    g_state[...] = jnp.exp(last) * g_after + k_tn(c_map, reached)
    g_x = step * g_scaled + vec_ref[1:2] * g_y
    g_step = k_nt(x * g_scaled, select, HIGHEST) * logistic(
        step_raw.astype(f32) + lanes_ref[0:1]
    )

    gs_x = g_x.astype(bf16).astype(f32) * (sig_x * (1.0 + s_x * (1.0 - sig_x)))
    g_maps = jnp.concatenate([g_b, g_c], axis=1).astype(bf16).astype(f32)
    gs_m = g_maps * (sig_m * (1.0 + s_m * (1.0 - sig_m)))
    gs_x_pad = jnp.concatenate([gs_x, next_x[...]], axis=0)
    gs_m_pad = jnp.concatenate([gs_m, next_m[...]], axis=0)
    g_x_raw = shifted_sum(gs_x_pad, taps_x_ref, KC - 1, -1)
    g_m_raw = shifted_sum(gs_m_pad, taps_m_ref, KC - 1, -1)
    next_x[...] = gs_x[:TAIL]
    next_m[...] = gs_m[:TAIL]
    for tap in range(KC):
        at = TAIL - KC + 1 + tap
        acc_x_ref[tap : tap + 1] += jnp.sum(gs_x * x_pad[at : at + BLOCK], axis=0, keepdims=True)
        acc_m_ref[tap : tap + 1] += jnp.sum(gs_m * m_pad[at : at + BLOCK], axis=0, keepdims=True)
    acc_x_ref[KC : KC + 1] += jnp.sum(gs_x, axis=0, keepdims=True)
    acc_m_ref[KC : KC + 1] += jnp.sum(gs_m, axis=0, keepdims=True)
    acc_v_ref[0:1] += jnp.sum(g_y * x, axis=0, keepdims=True)
    acc_s_ref[0:1] += jnp.sum(g_step, axis=0, keepdims=True)

    here = (block // 8) == info[1]
    g_q = jnp.where(here, dq_ref[...].astype(f32), 0.0)
    at = 2 * OWN
    g_all_ref[:, :at] = jnp.concatenate([g_z_ref[...].astype(f32), g_x_raw], axis=1).astype(bf16)
    for piece in (g_q, g_m_raw, unturned(dk_ref[...]), dv_ref[...], g_step):
        g_all_ref[:, at : at + piece.shape[1]] = piece.astype(bf16)
        at += piece.shape[1]


def masked_scores(info, keys, queries, length):
    scores = k_nt(keys, queries) * (HD**-0.5)
    start = (info[1] * 8 + pl.program_id(0)) * BLOCK
    key_at = lax.broadcasted_iota(jnp.int32, (length, BLOCK), 0)
    query_at = lax.broadcasted_iota(jnp.int32, (length, BLOCK), 1) + start
    return scores, key_at <= query_at


def attend_forward(info, q_ref, k_ref, v_ref, out_ref, out_f_ref, log_ref):
    scores, allowed = masked_scores(info, k_ref[...], q_ref[...], k_ref.shape[0])
    scores = jnp.where(allowed, scores, NEGATIVE)
    top = jnp.max(scores, axis=0, keepdims=True)
    weights = jnp.exp(scores - top)
    total = jnp.sum(weights, axis=0, keepdims=True)
    result = jnp.transpose(k_tn(v_ref[...], weights.astype(bf16)) / total)
    out_ref[...] = result.astype(bf16)
    out_f_ref[...] = result
    log_ref[0] = jnp.broadcast_to(top + jnp.log(total), (8, BLOCK))


def attend_backward(
    info, q_ref, k_ref, v_ref, out_f_ref, log_ref, g_ref, cos_ref, sin_ref, dq_ref, dk_ref, dv_ref
):
    @pl.when(pl.program_id(0) == 0)
    def _():
        dk_ref[...] = jnp.zeros_like(dk_ref)
        dv_ref[...] = jnp.zeros_like(dv_ref)

    keys, queries, grads = k_ref[...], q_ref[...], g_ref[...]
    scores, allowed = masked_scores(info, keys, queries, k_ref.shape[0])
    probs = jnp.where(allowed, jnp.exp(scores - log_ref[0, 0:1]), 0.0)
    delta = k_nt(jnp.ones((8, HD), f32), grads.astype(f32) * out_f_ref[...], HIGHEST)[0:1]
    g_scores = (probs * (k_nt(v_ref[...], grads) - delta)).astype(bf16)
    dv_ref[...] += k_mm(probs.astype(bf16), grads)
    dk_ref[...] += k_mm(g_scores, queries) * (HD**-0.5)
    dq = (k_tn(g_scores, keys) * (HD**-0.5)).astype(bf16).astype(f32)
    dq_ref[...] = (dq * cos_ref[...] - pltpu.roll(dq, HD // 2, 1) * sin_ref[...]).astype(bf16)


def rows_at(width, column=0):
    return pl.BlockSpec((BLOCK, width), lambda i, s: (i ^ s[0], column))


def rows_back(count, width, column=0):
    return pl.BlockSpec((BLOCK, width), lambda i, s: ((count - 1 - i) ^ s[0], column))


def whole(*shape):
    return pl.BlockSpec(shape, lambda i, s: (0,) * len(shape))


def run_mix_forward(info, own, shared, cosine, sine, cum_col, cum_row, taps_x, taps_m, vec):
    length = own.shape[0]
    count = length // BLOCK

    def plain(width):
        return pl.BlockSpec((BLOCK, width), lambda i, s: (i, 0))

    def plain3(rows, width):
        return pl.BlockSpec((1, rows, width), lambda i, s: (i, 0, 0))

    return pl.pallas_call(
        mix_forward,
        grid_spec=pltpu.PrefetchScalarGridSpec(
            num_scalar_prefetch=1,
            grid=(count,),
            in_specs=[
                rows_at(own.shape[1]),
                rows_at(shared.shape[1]),
                plain(HD),
                plain(HD),
                plain(8),
                plain3(8, BLOCK),
                whole(8, OWN),
                whole(8, 2 * NS),
                whole(8, OWN),
            ],
            out_specs=[
                rows_at(OWN),
                rows_at(OWN),
                plain3(8, BLOCK),
                plain3(NS, OWN),
                plain(HD),
                plain(HD),
                plain(HD),
            ],
            scratch_shapes=[
                pltpu.VMEM((NS, OWN), f32),
                pltpu.VMEM((TAIL, OWN), f32),
                pltpu.VMEM((TAIL, 2 * NS), f32),
            ],
        ),
        out_shape=[
            jax.ShapeDtypeStruct((length, OWN), bf16),
            jax.ShapeDtypeStruct((length, OWN), bf16),
            jax.ShapeDtypeStruct((count, 8, BLOCK), f32),
            jax.ShapeDtypeStruct((count, NS, OWN), bf16),
            jax.ShapeDtypeStruct((length, HD), bf16),
            jax.ShapeDtypeStruct((length, HD), bf16),
            jax.ShapeDtypeStruct((length, HD), bf16),
        ],
        compiler_params=params(),
        cost_estimate=LITTLE,
        name="mix_forward",
    )(info, own, shared, cosine, sine, cum_col, cum_row, taps_x, taps_m, vec)


def run_mix_backward(
    info,
    own,
    shared,
    cosine,
    sine,
    cum_col,
    cum_row,
    taps_x,
    taps_m,
    vec,
    lanes,
    g_y,
    g_z,
    states,
    dq,
    dk,
    dv,
):
    length = own.shape[0]
    count = length // BLOCK
    tails = BLOCK // TAIL
    all_width = own.shape[1] + shared.shape[1]

    def plain(width):
        return pl.BlockSpec((BLOCK, width), lambda i, s: (count - 1 - i, 0))

    def plain3(rows, width):
        return pl.BlockSpec((1, rows, width), lambda i, s: (count - 1 - i, 0, 0))

    def tail_of(width):
        def where(i, s):
            before = jnp.maximum(count - 2 - i, 0)
            return ((before ^ s[0]) * tails + tails - 1, 0)

        return pl.BlockSpec((TAIL, width), where)

    def query_rows(i, s):
        return (((count - 1 - i) ^ s[0]) % 8, 0)

    return pl.pallas_call(
        mix_backward,
        grid_spec=pltpu.PrefetchScalarGridSpec(
            num_scalar_prefetch=1,
            grid=(count,),
            in_specs=[
                rows_back(count, own.shape[1]),
                rows_back(count, shared.shape[1]),
                tail_of(own.shape[1]),
                tail_of(shared.shape[1]),
                plain(HD),
                plain(HD),
                plain(8),
                plain3(8, BLOCK),
                whole(8, OWN),
                whole(8, 2 * NS),
                whole(8, OWN),
                whole(8, 128),
                rows_back(count, OWN),
                rows_back(count, OWN),
                plain3(NS, OWN),
                pl.BlockSpec((BLOCK, HD), query_rows),
                plain(HD),
                plain(HD),
            ],
            out_specs=[
                rows_back(count, all_width),
                whole(8, OWN),
                whole(8, 2 * NS),
                whole(8, OWN),
                whole(8, 128),
            ],
            scratch_shapes=[
                pltpu.VMEM((NS, OWN), f32),
                pltpu.VMEM((TAIL, OWN), f32),
                pltpu.VMEM((TAIL, 2 * NS), f32),
            ],
        ),
        out_shape=[
            jax.ShapeDtypeStruct((length, all_width), bf16),
            jax.ShapeDtypeStruct((8, OWN), f32),
            jax.ShapeDtypeStruct((8, 2 * NS), f32),
            jax.ShapeDtypeStruct((8, OWN), f32),
            jax.ShapeDtypeStruct((8, 128), f32),
        ],
        compiler_params=params(),
        cost_estimate=LITTLE,
        name="mix_backward",
    )(
        info,
        own,
        shared,
        own,
        shared,
        cosine,
        sine,
        cum_col,
        cum_row,
        taps_x,
        taps_m,
        vec,
        lanes,
        g_y,
        g_z,
        states,
        dq,
        dk,
        dv,
    )


def own_queries(width):
    return pl.BlockSpec((BLOCK, width), lambda i, s: (s[1] * 8 + i, 0))


def own_rows(width):
    return pl.BlockSpec((BLOCK, width), lambda i, s: (i ^ s[2], 0))


def run_attend_forward(info, queries, keys, values):
    length = keys.shape[0]
    half = length // 2
    count = half // BLOCK
    return pl.pallas_call(
        attend_forward,
        grid_spec=pltpu.PrefetchScalarGridSpec(
            num_scalar_prefetch=1,
            grid=(count,),
            in_specs=[own_queries(HD), whole(length, HD), whole(length, HD)],
            out_specs=[
                own_rows(HD),
                pl.BlockSpec((BLOCK, HD), lambda i, s: (i, 0)),
                pl.BlockSpec((1, 8, BLOCK), lambda i, s: (i, 0, 0)),
            ],
        ),
        out_shape=[
            jax.ShapeDtypeStruct((half, HD), bf16),
            jax.ShapeDtypeStruct((half, HD), f32),
            jax.ShapeDtypeStruct((count, 8, BLOCK), f32),
        ],
        compiler_params=params(),
        cost_estimate=LITTLE,
        name="attend_forward",
    )(info, queries, keys, values)


def run_attend_backward(info, queries, keys, values, out_f, logs, grads, cosine, sine):
    length = keys.shape[0]
    half = length // 2
    count = half // BLOCK
    return pl.pallas_call(
        attend_backward,
        grid_spec=pltpu.PrefetchScalarGridSpec(
            num_scalar_prefetch=1,
            grid=(count,),
            in_specs=[
                own_queries(HD),
                whole(length, HD),
                whole(length, HD),
                pl.BlockSpec((BLOCK, HD), lambda i, s: (i, 0)),
                pl.BlockSpec((1, 8, BLOCK), lambda i, s: (i, 0, 0)),
                own_rows(HD),
                own_queries(HD),
                own_queries(HD),
            ],
            out_specs=[
                own_rows(HD),
                whole(length, HD),
                whole(length, HD),
            ],
        ),
        out_shape=[
            jax.ShapeDtypeStruct((half, HD), bf16),
            jax.ShapeDtypeStruct((length, HD), f32),
            jax.ShapeDtypeStruct((length, HD), f32),
        ],
        compiler_params=params(),
        cost_estimate=LITTLE,
        name="attend_backward",
    )(info, queries, keys, values, out_f, logs, grads, cosine, sine)


def cube_body(
    tokens,
    log_decay,
    norm_gain,
    qkv_proj,
    attn_proj,
    inner_proj,
    conv_weight,
    conv_bias,
    step_bias,
    skip_gain,
    inner_gain,
    inner_out,
    ff_gain,
    gate_up,
    down_proj,
    cotangent,
):
    core = lax.axis_index("head")
    seq_half = lax.axis_index("half")
    member = lax.axis_index("cube")
    chip = seq_half * 8 + member
    bits = (member // 4, (member // 2) % 2, member % 2)
    zl = bits[0]
    place = core * 8 + member
    info = jnp.stack([place, core, member, seq_half]).astype(jnp.int32)
    width = tokens.shape[-1]
    rows = tokens.shape[1]
    shard = width // DEVICES
    inner_width = MH * MP
    conv_width = inner_width + 2 * NS
    heads = MH // 16
    mine = heads * MP
    length = rows * 16
    half_rows = rows * 8
    ffc = FF // 16

    def to_local(value):
        parts = [value[:, i * width // 4 : (i + 1) * width // 4] for i in range(4)]
        return jnp.where(
            seq_half == 0,
            jnp.concatenate([parts[i] for i in (0, 2, 1, 3)], axis=1),
            jnp.concatenate([parts[i] for i in (1, 3, 0, 2)], axis=1),
        )

    def to_natural(value):
        parts = [value[:, i * width // 4 : (i + 1) * width // 4] for i in range(4)]
        return jnp.where(
            seq_half == 0,
            jnp.concatenate([parts[i] for i in (0, 2, 1, 3)], axis=1),
            jnp.concatenate([parts[i] for i in (2, 0, 3, 1)], axis=1),
        )

    swapped = swap_sequences(jnp.concatenate([tokens[0], cotangent[0]], axis=0))
    x_bf, g_out_bf = to_local(swapped[:rows]), to_local(swapped[rows:])

    gain_rows = norm_gain.astype(f32)[:, None]
    qkv_s = (qkv_proj.astype(f32) * gain_rows).astype(bf16)
    inner_s = (inner_proj.astype(f32) * gain_rows).astype(bf16)
    gate_up_s = (gate_up.astype(f32) * ff_gain.astype(f32)[:, None]).astype(bf16)

    def to_places(value):
        return jnp.moveaxis(value.reshape(shard, 16, -1), 1, 0)

    def to_members(value):
        parts = jnp.moveaxis(value.reshape(shard, 8, -1), 1, 0)
        return jnp.concatenate([parts, parts], axis=0)

    def both_halves(value, other):
        return jnp.concatenate([value, other], axis=0)

    kv_width = KVH * HD
    conv_shard = conv_weight.shape[1]
    smalls = jnp.concatenate([conv_weight.reshape(-1), conv_bias, inner_gain])
    decay_rows = jnp.moveaxis(log_decay, 1, 2).reshape(2, -1)
    decay_high = lax.optimization_barrier(decay_rows.astype(bf16))
    decay_low = (decay_rows - decay_high.astype(f32)).astype(bf16)
    decay_rows = jnp.concatenate([decay_high, decay_low], axis=1)
    extra_size = shard * 128
    extra_pad = jnp.zeros((extra_size - smalls.shape[0] - decay_rows.shape[1],), bf16)

    def shared_for(half):
        mine_rows = lax.dynamic_index_in_dim(decay_rows, half, 0, keepdims=False)
        extra = jnp.concatenate([smalls, mine_rows, extra_pad]).reshape(shard, 128)
        return jnp.concatenate([shared_send, extra], axis=1)

    shared_send = jnp.concatenate(
        [
            inner_s[:, 2 * inner_width : inner_width + conv_width],
            qkv_s[:, QH * HD : QH * HD + kv_width],
            inner_s[:, inner_width + conv_width :],
            jnp.zeros((shard, -MH % 128), bf16),
            qkv_s[:, QH * HD + kv_width :],
        ],
        axis=1,
    )
    shared_other = flip(shared_for(1 - seq_half), BIT_ZH)
    send_own = jnp.concatenate(
        [
            to_places(inner_s[:, :inner_width]),
            to_places(inner_s[:, inner_width : 2 * inner_width]),
            to_members(qkv_s[:, : QH * HD]),
        ],
        axis=2,
    )
    got_own = exchange(send_own).reshape(width // 2, -1)
    x_rows = x_bf.astype(f32)
    inv_in = lax.rsqrt(jnp.mean(x_rows * x_rows, axis=-1, keepdims=True) + EPSILON)
    shared_mine = shared_for(seq_half)
    shared_both = jnp.concatenate([shared_mine, shared_other], axis=0)
    normed_mine = (x_rows * inv_in).astype(bf16)
    shared_edges = ((0, 2 * NS), (2 * NS, 2 * NS + kv_width + 128), (2 * NS + kv_width + 128, None))
    lanes_all = (shared_both.shape[1] + width) // 128
    goals = (-(-lanes_all // 3), -(-lanes_all // 3), lanes_all - 2 * -(-lanes_all // 3))
    edges, normed_edges, joined, at, done = [], [], [], 0, 0
    for (a, b), lanes_here in zip(shared_edges, goals):
        part = shared_both[:, a:b]
        taken = lanes_here * 128 - part.shape[1]
        joined += [part, normed_mine[:, done : done + taken]]
        edges.append((at, at + lanes_here * 128))
        normed_edges.append((part.shape[1], done, taken))
        at += lanes_here * 128
        done += taken
    first = Gather(jnp.concatenate(joined, axis=1), edges, info)
    first.state, got_own = joint(first.state, got_own)
    own_width = 2 * mine + HD
    other_own = [flip(got_own[:, : own_width // 2], BIT_ZH), None]
    first.hop()
    send_rest = jnp.concatenate(
        [
            to_places(inner_out.T),
            to_members(attn_proj.T),
            to_places(gate_up_s[:, :FF]),
            to_places(gate_up_s[:, FF:]),
            to_places(down_proj.T),
        ],
        axis=2,
    )
    positions = jnp.arange(length, dtype=f32)
    frequency = ROPE_BASE ** (-2.0 * jnp.arange(HD // 2, dtype=f32) / HD)
    angle = positions[:, None] * frequency[None, :]
    cosine, sine = jnp.cos(angle), jnp.sin(angle)
    cosine = jnp.concatenate([cosine, cosine], axis=1)
    sine = jnp.concatenate([-sine, sine], axis=1)
    first.hop()
    first.state, other_own[0], got_own = joint(first.state, other_own[0], got_own)
    other_own[1] = flip(got_own[:, own_width // 2 :], BIT_ZH)
    first.hop()
    first.state, send_rest, other_own[1], cosine, sine = joint(
        first.state, send_rest, other_own[1], cosine, sine
    )
    got = exchange(send_rest).reshape(width // 2, -1)
    pieces = first.pieces()
    shared_width = 2 * NS + 2 * HD + 128
    picks = (
        ((0, 0, 0, 2 * NS),),
        ((0, HD, 2 * NS, HD), (kv_width, 0, 2 * NS + 2 * HD, 128)),
        ((0, HD, 2 * NS + HD, HD),),
    )
    moves, extra_moves, normed_moves = [], [], []
    for group in range(4):
        half, far = group // 2, group % 2
        for part in range(3):
            number = 3 * group + part if half == 0 else 6 + far
            start = edges[part][0] * half
            skip, normed_at, taken = normed_edges[part]
            for begin, cube_place, count in piece_blocks(part, far):
                normed_moves.append(
                    (
                        number,
                        fixed(begin * rows, count * rows, start + skip, taken),
                        fixed((half * 8 + cube_place) * rows, count * rows, normed_at, taken),
                    )
                )
                for block, zh in ((i, j) for i in range(count) for j in range(2)):
                    row = (begin + block) * 2 * shard + zh * shard
                    position = half * 8 + cube_place + block

                    def goal(ref, position=position, zh=zh, target=0, columns=128):
                        to = zh * 16 + (ref[0] ^ position)
                        to = pl.multiple_of(to * shard, shard)
                        return (pl.ds(to, shard), pl.ds(target, columns))

                    def extra_goal(ref, position=position, zh=zh):
                        place = ref[0] ^ position
                        to = (place // 8) * 16 + (zh ^ ref[3]) * 8 + place % 8
                        to = pl.multiple_of(to * shard, shard)
                        return (pl.ds(to, shard), pl.ds(0, 128))

                    for column, by_zl, target, columns in picks[part]:

                        def source(ref, row=row, at=start + column, by_zl=by_zl, columns=columns):
                            if by_zl:
                                at = pl.multiple_of(at + (ref[2] // 4) * by_zl, 128)
                            return (pl.ds(row, shard), pl.ds(at, columns))

                        moves.append(
                            (
                                number,
                                source,
                                functools.partial(goal, target=target, columns=columns),
                            )
                        )
                    if part == 2:
                        extra_moves.append(
                            (number, fixed(row, shard, start + kv_width, 128), extra_goal)
                        )
    normed, w_s, small_got = assemble(
        pieces,
        [
            ((length, width), bf16, normed_moves),
            ((width, shared_width), bf16, moves),
            ((width, 128), bf16, extra_moves),
        ],
        info,
    )
    small_got = small_got.reshape(DEVICES, -1)
    at = smalls.shape[0]
    decay = lax.dynamic_slice_in_dim(small_got[:, at : at + decay_rows.shape[1]], core * 16, 16, 0)
    decay = decay.astype(f32).reshape(16, 2, 8, heads, rows)
    decay = lax.dynamic_index_in_dim(decay[:, 0] + decay[:, 1], member, 1, keepdims=False)
    at = 0
    conv_w = jnp.moveaxis(
        small_got[:, at : at + KC * conv_shard].reshape(DEVICES, KC, conv_shard), 1, 0
    ).reshape(KC, conv_width)
    at += KC * conv_shard
    conv_b = small_got[:, at : at + conv_shard].reshape(1, conv_width)
    at += conv_shard
    gain_all = small_got[:, at : at + inner_gain.shape[0]].reshape(1, inner_width)
    conv_all = jnp.concatenate([conv_w, conv_b], axis=0).astype(f32)
    conv_all = jnp.concatenate([conv_all, jnp.zeros((8 - KC - 1, conv_width), f32)], axis=0)
    taps_x = lax.dynamic_slice_in_dim(conv_all[:, :inner_width], place * mine, mine, 1)
    taps_m = conv_all[:, inner_width:]
    gain_mine = lax.dynamic_slice_in_dim(gain_all, place * mine, mine, 1)[0].astype(f32)

    (w_own,) = joint(both_halves(got_own, jnp.concatenate(other_own, axis=1)))
    bias_mine = lax.dynamic_slice_in_dim(step_bias, member * heads, heads, 0)
    skip_mine = lax.dynamic_slice_in_dim(skip_gain, member * heads, heads, 0)
    vec = jnp.concatenate(
        [
            jnp.repeat(bias_mine, MP)[None],
            jnp.repeat(skip_mine, MP)[None],
            gain_mine[None],
            jnp.zeros((5, mine), f32),
        ],
        axis=0,
    )
    lanes = lax.dynamic_update_slice(
        jnp.zeros((8, 128), f32), bias_mine[None], (0, place * heads)
    )
    cum_row = jnp.cumsum(decay, axis=2)
    cum_row = jnp.concatenate([cum_row, jnp.zeros((16, 8 - heads, rows), f32)], axis=1)
    cum_col = jnp.moveaxis(cum_row, 1, 2).reshape(length, 8)
    (w_all,) = joint(jnp.concatenate([w_own, w_s], axis=1))

    order = jnp.arange(16, dtype=jnp.int32) ^ place

    def reordered(value):
        return jnp.take(value, order, axis=0, unique_indices=True, mode="clip")

    g_out_bf, normed = joint(g_out_bf, normed)
    g_out = gather_start(g_out_bf, info)
    g_out.hop()
    raw_s = mm(normed, w_s).astype(bf16)
    g_out.state, raw_s, got, normed = joint(g_out.state, raw_s, got, normed)
    cuts = [0, mine + HD] + [mine + HD + i * ffc for i in (1, 2, 3)]
    got = [got[:, a:b] for a, b in zip(cuts[:-1], cuts[1:])]
    other = [flip(got[0], BIT_ZH), None, None, None]
    g_out.hop()
    raw_own = mm(normed, w_own).astype(bf16)
    g_out.state, raw_own = joint(g_out.state, raw_own)
    g_out.hop()

    tables = (cosine, sine, cum_col, cum_row, taps_x, taps_m, vec)
    y, gained, squares, states, queries, keys, values = run_mix_forward(
        info, raw_own, raw_s, *tables
    )
    squares, other[0] = joint(squares, other[0])
    other[3] = flip(got[3], BIT_ZH)
    (w_mix,) = joint(both_halves(got[0], other[0]))
    w_out, w_att = w_mix[:, :mine], w_mix[:, mine:]
    squares = group_sum(squares[:, 0])
    squares, queries, other[3], got[1] = joint(squares, queries, other[3], got[1])
    other[1] = flip(got[1], BIT_ZH)
    (w_down,) = joint(both_halves(got[3], other[3]))
    attended, attended_f, logs = run_attend_forward(info, queries, keys, values)
    inv_mix = lax.rsqrt(squares / inner_width + EPSILON)
    inv_mix_rows = reordered(inv_mix).reshape(length, 1)
    part_other = inv_mix_rows[half_rows:] * mm_nt(gained[half_rows:], w_out)
    part_own = inv_mix_rows[:half_rows] * mm_nt(gained[:half_rows], w_out) + mm_nt(attended, w_att)
    sums = Scatter(part_own.astype(bf16), part_other)
    sums.state, other[1], got[2] = joint(sums.state, other[1], got[2])
    other[2] = flip(got[2], BIT_ZH)
    sums.hop()
    sums.hop()
    sums.state, other[2] = joint(sums.state, other[2])
    (w_gu,) = joint(
        jnp.concatenate([both_halves(got[i], other[i]) for i in (1, 2)], axis=1)
    )
    hidden = x_rows + sums.result()
    g_out = gathered(g_out, width, info)

    inv_ff = lax.rsqrt(jnp.mean(hidden * hidden, axis=-1, keepdims=True) + EPSILON)
    gather = gather_start((hidden * inv_ff).astype(bf16), info)
    normed_ff = gathered(gather, width, info)
    gate_vals = mm(normed_ff, w_gu)
    gate, up = gate_vals[:, :ffc], gate_vals[:, ffc:]
    sig = jax.nn.sigmoid(gate)
    mixed = (gate * sig * up).astype(bf16)
    g_mixed = mm(g_out, w_down)
    g_vals = jnp.concatenate(
        [g_mixed * up * sig * (1.0 + gate * (1.0 - sig)), g_mixed * gate * sig], axis=1
    ).astype(bf16)
    g_ff_other = mm_nt(g_vals[half_rows:], w_gu).astype(bf16)
    sums = Scatter(mm_nt(g_vals[:half_rows], w_gu).astype(bf16), g_ff_other)
    sums.hop()
    def crossing(value):
        return flip(value[width // 2 :], BIT_ZH)

    def to_owners(values, crossed):
        total = [
            value[: width // 2].astype(f32) + got.astype(f32)
            for value, got in zip(values, crossed)
        ]
        total = jnp.concatenate([part.astype(bf16) for part in total], axis=1)
        return exchange(total.reshape(16, shard, -1))

    mixed_late, g_vals_late = sums.then(mixed, g_vals)
    mixed_cube = reordered_rows(mixed_late, info)
    out_other = mm_nt(mixed_cube[half_rows:], w_down).astype(bf16)
    out_own = mm_nt(mixed_cube[:half_rows], w_down).astype(bf16)
    d_gu = mm_tn(normed_ff, g_vals_late).astype(bf16)
    d_gate, d_up = d_gu[:, :ffc], d_gu[:, ffc:]
    sums.state, out_other, out_own, d_gate = joint(sums.state, out_other, out_own, d_gate)
    out_got = flip(out_other, BIT_C)
    gate_got = crossing(d_gate)
    sums.hop()
    mixed_late, g_out = sums.then(mixed_late, g_out)
    d_down = mm_tn(g_out, mixed_late).astype(bf16)
    sums.state, d_down = joint(sums.state, d_down)
    g_ff = sums.result()

    def from_places(value):
        return jnp.moveaxis(value, 0, 1).reshape(shard, -1)

    g_hidden = (
        g_out_bf.astype(f32)
        + inv_ff * g_ff
        - hidden * inv_ff**3 * jnp.mean(hidden * g_ff, axis=-1, keepdims=True)
    )
    gather = gather_start(g_hidden.astype(bf16), info)
    gather.state, gate_got, d_up = joint(gather.state, gate_got, d_up)
    up_got = crossing(d_up)
    gather.hop()
    gather.hop()
    out_sum = (out_own.astype(f32) + out_got.astype(f32)).astype(bf16)
    gather.state, up_got, d_down, out_sum, w_all = joint(
        gather.state, up_got, d_down, out_sum, w_all
    )
    down_got = crossing(d_down)
    g_branch = gathered(gather, width, info)

    inner_normed = (gained.astype(f32) * inv_mix_rows).astype(bf16)
    g_inner = mm(g_branch, w_out)
    g_branch_own = g_branch[:half_rows]
    g_att = mm(g_branch_own, w_att).astype(bf16)
    dots = jnp.sum(inner_normed.astype(f32) * g_inner, axis=-1).reshape(16, rows)
    dots = group_sum(reordered(dots))
    g_branch_own = g_branch[:half_rows]
    g_att = mm(g_branch_own, w_att).astype(bf16)
    d_mix_early = jnp.concatenate(
        [
            mm_tn(g_branch, inner_normed).astype(bf16),
            mm_tn(g_branch_own, attended).astype(bf16),
        ],
        axis=1,
    )
    d_mix_early, g_att = joint(d_mix_early, g_att)
    early_got = crossing(d_mix_early)
    d_q, d_k, d_v = run_attend_backward(
        info, queries, keys, values, attended_f, logs, g_att, cosine, sine
    )
    gate = raw_own[:, :mine].astype(f32)
    gate_sig = jax.nn.sigmoid(gate)
    y_rows = y.astype(f32)
    normed_mix = y_rows * (gate * gate_sig) * inv_mix_rows
    g_gated = inv_mix_rows * (
        gain_mine * g_inner - normed_mix * (reordered(dots).reshape(length, 1) / inner_width)
    )
    g_y = (g_gated * gate * gate_sig).astype(bf16)
    g_z = (g_gated * y_rows * gate_sig * (1.0 + gate * (1.0 - gate_sig))).astype(bf16)
    grad_gain_mine = jnp.sum(normed_mix * g_inner, axis=0)
    d_q, down_got, dots = joint(d_q, down_got, dots)
    d_ff_got = to_owners((d_gate, d_up, d_down), (gate_got, up_got, down_got))
    d_mix_late = jnp.concatenate(
        [
            mm_tn(normed, g_z).astype(bf16),
            mm_tn(normed[:half_rows], d_q).astype(bf16),
        ],
        axis=1,
    )
    d_mix_late, early_got = joint(d_mix_late, early_got)
    late_got = crossing(d_mix_late)
    g_y, d_ff_got, out_sum, d_mix_late = joint(g_y, d_ff_got, out_sum, d_mix_late)
    out_got = lax.all_to_all(
        out_sum.reshape(8, rows, width), "cube", split_axis=0, concat_axis=0, tiled=True
    )
    g_all, acc_x, acc_m, acc_v, acc_s = run_mix_backward(
        info,
        raw_own,
        raw_s,
        *tables,
        lanes,
        g_y,
        g_z,
        states,
        d_q,
        d_k,
        d_v,
    )
    conv_grads = jnp.concatenate([acc_x[: KC + 1], acc_m[: KC + 1]], axis=1)
    g_bias = lax.dynamic_slice_in_dim(acc_s[0], place * heads, heads, 0)
    g_skip = jnp.sum(acc_v[0].reshape(heads, MP), axis=1)
    small_grads = jnp.concatenate([conv_grads.reshape(-1), grad_gain_mine, g_bias, g_skip])
    small_grads = jnp.pad(small_grads, (0, -small_grads.shape[0] % shard)).astype(bf16)
    small_grads = jnp.broadcast_to(
        small_grads.reshape(1, shard, -1), (DEVICES, shard, small_grads.shape[0] // shard)
    ).reshape(width, -1)
    g_in_other = mm_nt(g_all[half_rows:], w_all).astype(bf16)
    sums = Scatter(mm_nt(g_all[:half_rows], w_all).astype(bf16), g_in_other)
    sums.state, out_got = joint(sums.state, out_got)
    sums.hop()
    (g_all,) = sums.then(g_all)
    d_shared = mm_tn(normed, g_all[:, own_width:]).astype(bf16)
    sums.state, d_shared, g_all = joint(sums.state, d_shared, g_all)
    sums.hop()
    d_shared, g_all, d_ff_got, out_got = sums.then(d_shared, g_all, d_ff_got, out_got)
    d_own = mm_tn(normed, g_all[:, mine : 2 * mine]).astype(bf16)
    d_own = jnp.concatenate([d_own, small_grads], axis=1)
    out_part = jnp.sum(out_got.astype(f32), axis=0)
    out_rows = (hidden + out_part).astype(bf16)

    def only_mine(value):
        empty = jnp.zeros((width, KVH * HD), bf16)
        return lax.dynamic_update_slice_in_dim(empty, value, zl * HD, 1)

    d_shared = jnp.concatenate(
        [
            d_shared[:, : 2 * NS],
            only_mine(d_shared[:, 2 * NS : 2 * NS + HD]),
            only_mine(d_shared[:, 2 * NS + HD : 2 * NS + 2 * HD]),
            d_shared[:, 2 * NS + 2 * HD :],
        ],
        axis=1,
    )
    moves = []
    for block in range(DEVICES):

        def goal(ref, block=block):
            row = (ref[0] ^ (block % 16)) * 2 + block // 16
            return (pl.ds(pl.multiple_of(row * shard, shard), shard), slice(None))

        moves.append((0, fixed(block * shard, shard, 0, d_shared.shape[1]), goal))
    d_shared = assemble([d_shared], [(d_shared.shape, bf16, moves)], info)[0]
    sums.state, d_shared, d_own = joint(sums.state, d_shared, d_own)
    shared_sums = Scatter(d_shared[:half_rows], d_shared[half_rows:])
    sums.hop()
    g_in, d_own = joint(sums.result(), d_own)
    own_back = crossing(d_own)
    g_x_rows = (
        inv_in * g_in - x_rows * inv_in**3 * jnp.mean(x_rows * g_in, axis=-1, keepdims=True)
    )
    both = jnp.concatenate(
        [to_natural(out_rows), to_natural((g_hidden + g_x_rows).astype(bf16))], axis=0
    )
    both = swap_sequences(both)
    output, grad_tokens = both[None, :rows], both[None, rows:].astype(f32)
    shared_sums.hop()
    shared_sums.hop()
    shared_sums.hop()
    shared_sums.state, own_back, late_got, early_got = joint(
        shared_sums.state, own_back, late_got, early_got
    )
    d_own_got = to_owners((d_own, d_mix_late, d_mix_early), (own_back, late_got, early_got))
    d_cube = shared_sums.result().reshape(2, shard, -1)
    d_shared_own = d_cube[0] + flip(d_cube[1].astype(bf16), BIT_ZH).astype(f32)
    d_ff_own = d_ff_got.astype(f32)
    d_gate_up = jnp.concatenate(
        [from_places(d_ff_own[..., :ffc]), from_places(d_ff_own[..., ffc : 2 * ffc])], axis=1
    )
    grad_gate_up = d_gate_up * ff_gain.astype(f32)[:, None]
    grad_ff_gain = jnp.sum(d_gate_up * gate_up.astype(f32), axis=1)
    grad_down = jnp.moveaxis(d_ff_own[..., 2 * ffc : 3 * ffc], 1, 2).reshape(FF, shard)
    d_own = d_own_got.astype(f32)
    small_end = d_own.shape[-1] - 2 * mine - 2 * HD
    d_mix_own = d_own[..., small_end + mine + HD :]
    grad_inner_out = jnp.moveaxis(d_mix_own[..., :mine], 1, 2).reshape(inner_width, shard)
    d_att = d_mix_own[..., mine:].reshape(2, 8, shard, HD)
    grad_attn = jnp.moveaxis(d_att[0] + d_att[1], 1, 2).reshape(QH * HD, shard)
    d_x = from_places(d_own[..., :mine])
    d_z = from_places(d_own[..., small_end : small_end + mine])
    d_qw = d_own[..., small_end + mine : small_end + mine + HD].reshape(2, 8, shard, HD)
    d_qw = from_places(d_qw[0] + d_qw[1])

    got = d_own[..., mine:small_end].reshape(16, -1)
    at = 0
    taps_width = mine + 2 * NS
    conv_grads = got[:, at : at + (KC + 1) * taps_width].reshape(16, KC + 1, taps_width)
    at += (KC + 1) * taps_width
    conv_full = jnp.concatenate(
        [
            jnp.moveaxis(conv_grads[..., :mine], 0, 1).reshape(KC + 1, inner_width),
            jnp.sum(conv_grads[..., mine:], axis=0),
        ],
        axis=1,
    )
    device = core * 16 + chip
    conv_own = lax.dynamic_slice_in_dim(conv_full, device * conv_shard, conv_shard, 1)
    gain_full = got[:, at : at + mine].reshape(inner_width)
    gain_shard = inner_gain.shape[0]
    grad_inner_gain = lax.dynamic_slice_in_dim(gain_full, device * gain_shard, gain_shard, 0)
    at += mine
    local = lax.dynamic_slice_in_dim(got[:, at : at + 2 * heads], core * 8, 8, 0)
    grad_step_bias = local[:, :heads].reshape(-1)
    grad_skip_gain = local[:, heads:].reshape(-1)

    at = 2 * NS + 2 * kv_width
    d_qkv = jnp.concatenate([d_qw, d_shared_own[:, 2 * NS : at]], axis=1)
    d_inner = jnp.concatenate(
        [d_z, d_x, d_shared_own[:, : 2 * NS], d_shared_own[:, at : at + MH]], axis=1
    )
    grad_norm_gain = jnp.sum(d_qkv * qkv_proj.astype(f32), axis=1) + jnp.sum(
        d_inner * inner_proj.astype(f32), axis=1
    )
    return (
        output,
        grad_tokens,
        grad_norm_gain,
        d_qkv * gain_rows,
        grad_attn,
        d_inner * gain_rows,
        conv_own[:KC],
        conv_own[KC],
        grad_step_bias,
        grad_skip_gain,
        grad_inner_gain,
        grad_inner_out,
        grad_ff_gain,
        grad_gate_up,
        grad_down,
    )


def cube_solution(mesh):
    cubes = jax.sharding.Mesh(mesh.devices.reshape(2, 2, 8), BOTH)
    tokens = P("head", ("half", "cube"), None)
    lines = P(BOTH)
    rows = P(BOTH, None)
    columns = P(None, BOTH)
    head = P("head")
    return jax.shard_map(
        cube_body,
        mesh=cubes,
        in_specs=(
            tokens,
            P(None, ("half", "cube"), "head"),
            lines,
            rows,
            columns,
            rows,
            columns,
            lines,
            head,
            head,
            lines,
            columns,
            lines,
            rows,
            columns,
            tokens,
        ),
        out_specs=(
            tokens,
            tokens,
            lines,
            rows,
            columns,
            rows,
            columns,
            lines,
            head,
            head,
            lines,
            columns,
            lines,
            rows,
            columns,
        ),
        check_vma=False,
    )


def solution(mesh):
    if mesh.shape["seq"] == 16:
        return cube_solution(mesh)
    return jax.shard_map(
        body,
        mesh=mesh,
        in_specs=(
            P("head", "seq", None),
            P(None, "seq", "head"),
            P(("head", "seq")),
            P(("head", "seq"), None),
            P(None, ("head", "seq")),
            P(("head", "seq"), None),
            P(None, ("head", "seq")),
            P(("head", "seq")),
            P("head"),
            P("head"),
            P(("head", "seq")),
            P(None, ("head", "seq")),
            P(("head", "seq")),
            P(("head", "seq"), None),
            P(None, ("head", "seq")),
            P("head", "seq", None),
        ),
        out_specs=(
            P("head", "seq", None),
            P("head", "seq", None),
            P(("head", "seq")),
            P(("head", "seq"), None),
            P(None, ("head", "seq")),
            P(("head", "seq"), None),
            P(None, ("head", "seq")),
            P(("head", "seq")),
            P("head"),
            P("head"),
            P(("head", "seq")),
            P(None, ("head", "seq")),
            P(("head", "seq")),
            P(("head", "seq"), None),
            P(None, ("head", "seq")),
        ),
        check_vma=False,
    )
```
